32 devices in a mesh: row: 4 (over x, core), col: 8 (over z, y).
Axes of the slice: x: 2, y: 2, z: 4, core: 2. Of those that a mesh axis runs over, the one named last changes fastest.
Arguments:
- queries: float32 [32, 16384], P(None, ('row', 'col'))
- block_spots: int32 [4, 8, 256], P('row', 'col'), may hold values from 0 to 511, as said below
- live_blocks: int32 [4, 8], P('row', 'col'), may hold values from 1 to 256, as said below
- neighbor_cols: int32 [4, 8, 256, 16, 128], P('row', 'col'), may hold values from 0 to 127
- neighbor_sims: bfloat16 [4, 8, 256, 16, 128], P('row', 'col'), may hold values from 0.099609375 to 1
Outputs:
- solution: float32 [32, 16384], P(None, ('row', 'col'))
- residual: float32 [32, 16384], P(None, ('row', 'col'))
The draws below stay inside these ranges and needn't reach their ends.
Inputs may be any that keep to these rules, and one draw needn't show every extreme that they name: `block_spots`: within each index of the first two dimensions the 256 spots are distinct. `live_blocks`: some index of the array holds exactly 256.
All inputs are finite; a program needn't handle non-finite values.
Results may differ from the reference program's by a relative error of at most 0.01.
Values may be sent and summed in bfloat16 or wider, within the bound.
No kernel may reach another device: no remote copies, remote signals or barrier semaphores. Data moves between devices by JAX's collectives and lax.ppermute only.
A program may use at most 128 MiB of HBM per device.

```python
import math
import jax
import jax.numpy as jnp
from jax import lax

Q = 32
SEG = 512
CAP = 256
KB = 16
ITERS = 2
NODES = 16384
N_ROW = 4
N_COL = 8


def draw_queries(key, part):
    key = jax.random.fold_in(key, 7)
    first_key, second_key, third_key = jax.random.split(key, 3)
    node_total = SEG * N_ROW * N_COL
    ramp = 1.0 + 2.0 * jnp.arange(node_total, dtype=jnp.float32) / (node_total - 1)
    row_scales = ramp * jnp.exp(jax.random.uniform(second_key, (node_total,), jnp.float32, 0.0, math.log(4.0)))
    col_scales = jnp.exp(jax.random.uniform(third_key, (Q, 1), jnp.float32, 0.0, math.log(2.0)))
    base_values = jax.random.normal(first_key, (Q, node_total), jnp.float32)
    return (0.25 * base_values * row_scales[None, :] * col_scales).astype(jnp.float32)


def pick_spots(device_key):
    per_seg = SEG // 128
    places = N_ROW * per_seg * N_COL * per_seg
    return jax.random.permutation(device_key, places)[:CAP]


def draw_block_spots(key, part):
    key = jax.random.fold_in(key, 11)
    device_keys = jax.random.split(key, N_ROW * N_COL)
    chosen = jax.vmap(pick_spots)(device_keys)
    return chosen.reshape(N_ROW, N_COL, CAP).astype(jnp.int32)


def draw_live_blocks(key, part):
    key = jax.random.fold_in(key, 12)
    count_key, busy_key = jax.random.split(key)
    counts = jax.random.randint(count_key, (N_ROW * N_COL,), CAP // 8, CAP // 2 + 1)
    busiest = jax.random.randint(busy_key, (), 0, N_ROW * N_COL)
    counts = jnp.where(jnp.arange(N_ROW * N_COL) == busiest, CAP, counts)
    return counts.reshape(N_ROW, N_COL).astype(jnp.int32)


def touch_ends(drawn, stream_key, low, high):
    dims = drawn.shape
    index_at = [jax.random.randint(jax.random.fold_in(stream_key, axis), (), 0, dims[axis]) for axis in range(len(dims))]
    drawn = drawn.at[tuple(index_at)].set(low)
    longest = dims.index(max(dims))
    index_at[longest] = (index_at[longest] + 1) % dims[longest]
    return drawn.at[tuple(index_at)].set(high)


def levels(key, shape, pieces, smallest, high):
    factor_of = 1.0
    for axis_at, parts in pieces:
        draws = jax.random.uniform(jax.random.fold_in(jax.random.fold_in(key, 6), axis_at), (parts,), jnp.float32, smallest / len(pieces), high / len(pieces))
        factor_of = factor_of * jnp.repeat(jnp.exp(draws), shape[axis_at] // parts).reshape((-1,) + (1,) * (len(shape) - 1 - axis_at))
    return factor_of


def setup_inputs(seed: int = 0) -> dict:
    splits = jax.random.split(jax.random.key(seed), 6)
    return {
        "queries": draw_queries(jax.random.fold_in(splits[5], 71), 0),
        "block_spots": draw_block_spots(jax.random.fold_in(splits[5], 71), 0),
        "live_blocks": draw_live_blocks(jax.random.fold_in(splits[5], 71), 0),
        "neighbor_cols": touch_ends(jax.random.randint(splits[3], (N_ROW, N_COL, CAP, KB, 128), 0, 128), jax.random.fold_in(splits[3], 1), 0, 127).astype(jnp.int32),
        "neighbor_sims": jnp.clip(jnp.exp(math.log(1.0) - 2.306499 * jax.random.uniform(splits[4], (N_ROW, N_COL, CAP, KB, 128), jnp.float32) ** levels(splits[4], (N_ROW, N_COL, CAP, KB, 128), ((0, 4), (1, 8)), -0.2, 0.2)), 0.099609375, 1.0).astype(jnp.bfloat16),
    }


graph_weight = 0.95

def fill_blocks(neighbor_idx, neighbor_val):
    lane_ids = jnp.arange(128, dtype=jnp.int32)
    running = jnp.zeros((neighbor_idx.shape[0], 128, 128), jnp.float32)
    for column_slot in range(neighbor_idx.shape[1]):
        matched = neighbor_idx[:, column_slot, :, None] == lane_ids
        running = running + jnp.where(matched, neighbor_val[:, column_slot, :, None].astype(jnp.float32), jnp.float32(0.0))
    return running.astype(jnp.bfloat16)

def spd_solve(matrix, right_side):
    factor = jnp.linalg.cholesky(matrix)
    partial_value = lax.linalg.triangular_solve(factor, right_side, left_side=True, lower=True)
    return lax.linalg.triangular_solve(factor, partial_value, left_side=True, lower=True, transpose_a=True)

def gram_matrix(first_rows, second_rows):
    return lax.dot_general(first_rows, second_rows, (((1,), (1,)), ((), ())), precision=lax.Precision.HIGHEST)

def symmetric(square):
    return 0.5 * (square + square.T)

def graph_product(vectors, block_spots, live_blocks, neighbor_cols, neighbor_sims):
    query_rows = vectors.shape[0]
    per_seg = SEG // 128
    col_span = N_COL * per_seg
    all_blocks = NODES // 128
    flattened = vectors.astype(jnp.float32).reshape(query_rows, all_blocks, 128)

    def device_step(totals, device):
        row_index = device // N_COL
        col_index = device % N_COL
        spot_list = block_spots[row_index, col_index]
        live_count = live_blocks[row_index, col_index]
        index_table = neighbor_cols[row_index, col_index]
        value_table = neighbor_sims[row_index, col_index]

        def group_turn(turn_index, partial_value):
            row_total, col_total = partial_value
            first_slot = turn_index * 16
            indices = lax.dynamic_slice_in_dim(index_table, first_slot, 16, 0)
            values = lax.dynamic_slice_in_dim(value_table, first_slot, 16, 0)
            placed = lax.dynamic_slice_in_dim(spot_list, first_slot, 16, 0)
            active = (first_slot + jnp.arange(16, dtype=jnp.int32) < live_count).astype(jnp.float32)
            blocks = fill_blocks(indices, values).astype(jnp.float32) * active[:, None, None]
            local_row = placed // col_span
            local_col = placed % col_span
            global_row = ((local_row // per_seg * N_COL + col_index) * per_seg + local_row % per_seg).astype(jnp.int32)
            global_col = ((row_index * N_COL + local_col // per_seg) * per_seg + local_col % per_seg).astype(jnp.int32)
            col_vecs = jnp.take(flattened, global_col, axis=1)
            row_vecs = jnp.take(flattened, global_row, axis=1)
            forward = jnp.einsum('sij,msj->msi', blocks, col_vecs, precision=lax.Precision.HIGHEST)
            backward = jnp.einsum('sij,msi->msj', blocks, row_vecs, precision=lax.Precision.HIGHEST)
            row_total = row_total.at[:, global_row].add(forward)
            col_total = col_total.at[:, global_col].add(backward)
            return (row_total, col_total)
        group_stop = ((live_count + 15) // 16).astype(jnp.int32)
        totals = lax.fori_loop(jnp.int32(0), group_stop, group_turn, totals)
        return (totals, None)
    zeroed = jnp.zeros((query_rows, all_blocks, 128), jnp.float32)
    (row_total, col_total), _ = lax.scan(device_step, (zeroed, zeroed), jnp.arange(N_ROW * N_COL, dtype=jnp.int32))
    return (0.5 * (row_total + col_total)).reshape(query_rows, NODES)

def reference(queries, block_spots, live_blocks, neighbor_cols, neighbor_sims):
    unit_vector = jnp.ones((1, NODES), jnp.bfloat16)
    degree = 1.0 + graph_product(unit_vector, block_spots, live_blocks, neighbor_cols, neighbor_sims)[0]
    scaling = 1.0 / jnp.sqrt(degree)

    def operator(vectors):
        scaled = (scaling * vectors).astype(jnp.bfloat16)
        return vectors - graph_weight * scaling * graph_product(scaled, block_spots, live_blocks, neighbor_cols, neighbor_sims)
    solution = jnp.zeros_like(queries)
    residual = queries
    direction = queries
    res_gram = symmetric(gram_matrix(residual, residual))
    for sweep_index in range(ITERS):
        applied = operator(direction)
        curvature = symmetric(gram_matrix(direction, applied))
        weights = spd_solve(curvature, res_gram)
        solution = solution + jnp.dot(weights.T, direction, precision=lax.Precision.HIGHEST)
        residual = residual - jnp.dot(weights.T, applied, precision=lax.Precision.HIGHEST)
        if sweep_index + 1 < ITERS:
            new_gram = symmetric(gram_matrix(residual, residual))
            mixing = spd_solve(res_gram, new_gram)
            direction = residual + jnp.dot(mixing.T, direction, precision=lax.Precision.HIGHEST)
            res_gram = new_gram
    return (solution, residual)
```

```python
import functools

import jax
import jax.numpy as jnp
from jax import lax
from jax.experimental import pallas as pl
from jax.experimental.pallas import tpu as pltpu
from jax.sharding import PartitionSpec as P

graph_weight = 0.95
GROUP = 16
VMEM_LIMIT = 48 * 1024 * 1024


def dot_plain(left, right, **kwargs):
    return lax.dot_general(
        left, right, (((1,), (0,)), ((), ())), preferred_element_type=jnp.float32, **kwargs
    )


def dot_across(left, right, **kwargs):
    return lax.dot_general(
        left, right, (((1,), (1,)), ((), ())), preferred_element_type=jnp.float32, **kwargs
    )


exact_plain = functools.partial(dot_plain, precision=lax.Precision.HIGHEST)
exact_across = functools.partial(dot_across, precision=lax.Precision.HIGHEST)


def build_kernel(
    col_blocks, spots_ref, live_ref, index_ref, value_ref, block_ref, row_ref, col_ref
):
    step = pl.program_id(0)
    live = live_ref[0]

    @pl.when(step == 0)
    def _():
        row_ref[...] = jnp.zeros_like(row_ref)
        col_ref[...] = jnp.zeros_like(col_ref)

    @pl.when(step * GROUP < live)
    def _():
        lanes = lax.broadcasted_iota(jnp.int32, (16, 128), 0).astype(jnp.float32)
        targets = [(lanes + 16.0 * part).astype(jnp.bfloat16) for part in range(8)]
        ones = jnp.ones((8, 128), jnp.bfloat16)
        zero = jnp.zeros((16, 128), jnp.bfloat16)
        row_sums = []
        col_sums = []
        for slot in range(GROUP):
            active = (step * GROUP + slot < live).astype(jnp.float32)
            index_f32 = index_ref[slot].astype(jnp.float32)
            value_f32 = value_ref[slot].astype(jnp.float32) * active
            sums = [zero] * 8
            for entry in range(16):
                index_row = jnp.broadcast_to(index_f32[entry : entry + 1], (16, 128)).astype(
                    jnp.bfloat16
                )
                value_row = jnp.broadcast_to(value_f32[entry : entry + 1], (16, 128)).astype(
                    jnp.bfloat16
                )
                for part in range(8):
                    sums[part] = sums[part] + jnp.where(
                        index_row == targets[part], value_row, zero
                    )
            block = jnp.concatenate(sums, axis=0)
            block_ref[slot] = block
            row_sums.append(dot_plain(ones, block))
            col_sums.append(dot_across(ones, block))
        for slot in range(GROUP):
            spot = spots_ref[step * GROUP + slot]
            row_ref[spot // col_blocks] += row_sums[slot]
            col_ref[spot % col_blocks] += col_sums[slot]


def build_blocks(spots, live, index_table, value_table, row_blocks, col_blocks):
    slots = index_table.shape[0]

    def clamp(step, spots_ref, live_ref):
        return (jnp.minimum(step, (live_ref[0] - 1) // GROUP), 0, 0)

    def whole(step, spots_ref, live_ref):
        return (0, 0, 0)

    return pl.pallas_call(
        functools.partial(build_kernel, col_blocks),
        grid_spec=pltpu.PrefetchScalarGridSpec(
            num_scalar_prefetch=2,
            grid=(slots // GROUP,),
            in_specs=[
                pl.BlockSpec((GROUP, 16, 128), clamp),
                pl.BlockSpec((GROUP, 16, 128), clamp),
            ],
            out_specs=[
                pl.BlockSpec((GROUP, 128, 128), clamp),
                pl.BlockSpec((row_blocks, 8, 128), whole),
                pl.BlockSpec((col_blocks, 8, 128), whole),
            ],
        ),
        out_shape=[
            jax.ShapeDtypeStruct((slots, 128, 128), jnp.bfloat16),
            jax.ShapeDtypeStruct((row_blocks, 8, 128), jnp.float32),
            jax.ShapeDtypeStruct((col_blocks, 8, 128), jnp.float32),
        ],
        compiler_params=pltpu.CompilerParams(vmem_limit_bytes=VMEM_LIMIT),
        name="build_blocks",
    )(spots, live, index_table, value_table)


def product_kernel(
    col_blocks,
    spots_ref,
    live_ref,
    block_ref,
    col_dir_ref,
    row_dir_ref,
    row_out_ref,
    col_out_ref,
    row_ref,
    col_ref,
):
    step = pl.program_id(0)
    live = live_ref[0]

    @pl.when(step == 0)
    def _():
        row_ref[...] = jnp.zeros_like(row_ref)
        col_ref[...] = jnp.zeros_like(col_ref)

    @pl.when(step * GROUP < live)
    def _():
        row_sums = []
        col_sums = []
        for slot in range(GROUP):
            spot = spots_ref[step * GROUP + slot]
            block = block_ref[slot]
            row_sums.append(dot_plain(col_dir_ref[spot % col_blocks], block))
            col_sums.append(dot_across(row_dir_ref[spot // col_blocks], block))
        for slot in range(GROUP):
            spot = spots_ref[step * GROUP + slot]
            row_ref[spot // col_blocks] += row_sums[slot]
            col_ref[spot % col_blocks] += col_sums[slot]

    @pl.when(step == pl.num_programs(0) - 1)
    def _():
        row_out_ref[...] = row_ref[...].astype(row_out_ref.dtype)
        col_out_ref[...] = col_ref[...].astype(col_out_ref.dtype)


def block_products(spots, live, blocks, col_dirs, row_dirs):
    slots = blocks.shape[0]

    def clamp(step, spots_ref, live_ref):
        return (jnp.minimum(step, (live_ref[0] - 1) // GROUP), 0, 0)

    def whole(step, spots_ref, live_ref):
        return (0, 0, 0)

    return pl.pallas_call(
        functools.partial(product_kernel, col_dirs.shape[0]),
        grid_spec=pltpu.PrefetchScalarGridSpec(
            num_scalar_prefetch=2,
            grid=(slots // GROUP,),
            in_specs=[
                pl.BlockSpec((GROUP, 128, 128), clamp),
                pl.BlockSpec(col_dirs.shape, whole),
                pl.BlockSpec(row_dirs.shape, whole),
            ],
            out_specs=[
                pl.BlockSpec(row_dirs.shape, whole),
                pl.BlockSpec(col_dirs.shape, whole),
            ],
            scratch_shapes=[
                pltpu.VMEM(row_dirs.shape, jnp.float32),
                pltpu.VMEM(col_dirs.shape, jnp.float32),
            ],
        ),
        out_shape=[
            jax.ShapeDtypeStruct(row_dirs.shape, jnp.bfloat16),
            jax.ShapeDtypeStruct(col_dirs.shape, jnp.bfloat16),
        ],
        compiler_params=pltpu.CompilerParams(vmem_limit_bytes=VMEM_LIMIT),
        name="block_products",
    )(spots, live, blocks, col_dirs, row_dirs)


def start_kernel(row_ref, col_ref, query_ref, scaling_ref, scaled_ref):
    degree = 1.0 + 0.5 * (jnp.sum(row_ref[...], axis=0) + jnp.sum(col_ref[...], axis=0))
    scaling = 1.0 / jnp.sqrt(degree)
    scaling_ref[...] = scaling
    for part in range(scaling.shape[0]):
        scaled_ref[part] = (
            scaling[part : part + 1] * query_ref[:, part * 128 : part * 128 + 128]
        ).astype(jnp.bfloat16)


def summed(ref, part):
    total = ref[0, part].astype(jnp.float32)
    for other in range(1, ref.shape[0]):
        total = total + ref[other, part].astype(jnp.float32)
    return total


def middle_kernel(row_ref, col_ref, scaling_ref, first_ref, scaled_ref):
    for part in range(scaling_ref.shape[0]):
        scaling = scaling_ref[part : part + 1]
        first = scaling * (0.5 * (summed(row_ref, part) + summed(col_ref, part)))
        first_ref[part] = first
        scaled_ref[part] = (scaling * first).astype(jnp.bfloat16)


def gram_kernel(row_ref, col_ref, scaling_ref, query_ref, first_ref, second_ref, gram_ref):
    per_seg = scaling_ref.shape[0]
    query_query = jnp.zeros((32, 32), jnp.float32)
    query_first = query_query
    first_first = query_query
    first_second = query_query
    for part in range(per_seg):
        scaling = scaling_ref[part : part + 1]
        second = scaling * (0.5 * (summed(row_ref, part) + summed(col_ref, part)))
        second_ref[part] = second
        first = first_ref[part]
        query = query_ref[:, part * 128 : part * 128 + 128]
        query_query += exact_across(query, query)
        query_first += exact_across(query, first)
        first_first += exact_across(first, first)
        first_second += exact_across(first, second)
    gram_ref[...] = jnp.concatenate([query_query, query_first, first_first, first_second], axis=1)


def tall(flat):
    rest = flat.shape[1] - flat.shape[0]
    return jnp.concatenate([flat, jnp.zeros((rest, flat.shape[1]), flat.dtype)], axis=0)


def flipped(flat):
    return tall(flat).T[: flat.shape[0]]


def times(left, right):
    return exact_plain(left, tall(right))


def beside(left, right):
    return left + pltpu.roll(right, left.shape[0], 1)


def stacked(upper, lower):
    rest = jnp.zeros((upper.shape[1] - 2 * upper.shape[0], upper.shape[1]), upper.dtype)
    return jnp.concatenate([upper, lower, rest], axis=0)


def sandwich(rows, middle):
    return exact_across(exact_plain(rows, middle), tall(rows))


def symmetric(flat):
    return 0.5 * (flat + flipped(flat))


def window(flat, place):
    size = flat.shape[0]
    if place:
        flat = pltpu.roll(flat, flat.shape[1] - place * size, 1)
    lanes = lax.broadcasted_iota(jnp.int32, flat.shape, 1)
    return jnp.where(lanes < size, flat, 0.0)


def solve_many(pairs):
    size = pairs[0][0].shape[0]
    systems = [matrix + pltpu.roll(side, size, 1) for matrix, side in pairs]
    sublanes = lax.broadcasted_iota(jnp.int32, systems[0].shape, 0)
    for pivot in range(size):
        updated = []
        for system in systems:
            column = system[:, pivot : pivot + 1]
            row = system[pivot : pivot + 1, :] / column[pivot : pivot + 1, :]
            updated.append(jnp.where(sublanes == pivot, row, system - column * row))
        systems = updated
    return [window(system, 1) for system in systems]


def close_kernel(gram_ref, query_ref, first_ref, second_ref, solution_ref, residual_ref):
    size = query_ref.shape[0]
    weight = graph_weight
    total = gram_ref[0]
    for other in range(1, gram_ref.shape[0]):
        total = total + gram_ref[other]
    g00 = symmetric(window(total, 0))
    g01 = window(total, 1)
    g11 = symmetric(window(total, 2))
    g12 = window(total, 3)
    eye = (
        lax.broadcasted_iota(jnp.int32, total.shape, 0)
        == lax.broadcasted_iota(jnp.int32, total.shape, 1)
    ).astype(jnp.float32)
    curve = symmetric(g00 - weight * g01)
    steps, inverse = solve_many([(curve, g00), (g00, eye)])
    steps_t = flipped(steps)
    plain_gram = stacked(beside(g00, g01), beside(flipped(g01), g11))
    through_gram = stacked(beside(g01, g11), beside(g11, g12))
    after_first = beside(eye - steps_t, weight * steps_t)
    new_gram = symmetric(sandwich(after_first, plain_gram))
    mixing = times(inverse, new_gram)
    direction = after_first + flipped(mixing)
    curve = symmetric(sandwich(direction, plain_gram - weight * through_gram))
    (steps,) = solve_many([(curve, new_gram)])
    steps_t2 = flipped(steps)
    applied = direction - weight * pltpu.roll(direction, size, 1)
    solution_rows = exact_plain(beside(eye, steps_t2), stacked(steps_t, direction))
    residual_rows = exact_plain(beside(eye, -steps_t2), stacked(after_first, applied))
    rows = jnp.concatenate([solution_rows, residual_rows], axis=0)
    for part in range(first_ref.shape[0]):
        lanes = slice(part * 128, part * 128 + 128)
        basis = jnp.concatenate(
            [query_ref[:, lanes], first_ref[part], second_ref[part], jnp.zeros_like(eye)], axis=0
        )
        values = exact_plain(rows, basis)
        solution_ref[:, lanes] = values[:size]
        residual_ref[:, lanes] = values[size:]


def exchange(parts, axis):
    return lax.all_to_all(parts, axis, 0, 0, tiled=True)


def spread(piece, axis):
    count = lax.axis_size(axis)
    return exchange(jnp.broadcast_to(piece[None], (count,) + piece.shape), axis)


def simple_call(kernel, shapes, name, *operands):
    return pl.pallas_call(
        kernel,
        out_shape=shapes,
        compiler_params=pltpu.CompilerParams(vmem_limit_bytes=VMEM_LIMIT),
        name=name,
    )(*operands)


def body(queries, block_spots, live_blocks, neighbor_cols, neighbor_sims):
    row_count = lax.axis_size("row")
    col_count = lax.axis_size("col")
    query_rows, seg_len = queries.shape
    per_seg = seg_len // 128
    row_blocks = row_count * per_seg
    col_blocks = col_count * per_seg
    spots = block_spots[0, 0]
    live = live_blocks[0]
    piece = (per_seg, query_rows, 128)
    wide = jax.ShapeDtypeStruct(piece, jnp.float32)
    narrow = jax.ShapeDtypeStruct(piece, jnp.bfloat16)

    blocks, row_sums, col_sums = build_blocks(
        spots, live, neighbor_cols[0, 0], neighbor_sims[0, 0], row_blocks, col_blocks
    )
    row_parts = exchange(row_sums[:, 0].reshape(row_count, per_seg, 128), "row")
    col_parts = exchange(col_sums[:, 0].reshape(col_count, per_seg, 128), "col")
    scaling, scaled = simple_call(
        start_kernel,
        [jax.ShapeDtypeStruct((per_seg, 128), jnp.float32), narrow],
        "start",
        row_parts,
        col_parts,
        queries,
    )

    def product(vectors):
        col_dirs = spread(vectors, "col").reshape(col_blocks, query_rows, 128)
        row_dirs = spread(vectors, "row").reshape(row_blocks, query_rows, 128)
        row_total, col_total = block_products(spots, live, blocks, col_dirs, row_dirs)
        return (
            exchange(row_total.reshape((row_count,) + piece), "row"),
            exchange(col_total.reshape((col_count,) + piece), "col"),
        )

    row_parts, col_parts = product(scaled)
    first, scaled = simple_call(
        middle_kernel, [wide, narrow], "middle", row_parts, col_parts, scaling
    )
    row_parts, col_parts = product(scaled)
    second, grams = simple_call(
        gram_kernel,
        [wide, jax.ShapeDtypeStruct((query_rows, 4 * query_rows), jnp.float32)],
        "grams",
        row_parts,
        col_parts,
        scaling,
        queries,
        first,
    )
    all_grams = spread(grams, ("row", "col"))
    flat = jax.ShapeDtypeStruct(queries.shape, jnp.float32)
    return tuple(
        simple_call(close_kernel, [flat, flat], "close", all_grams, queries, first, second)
    )


def solution(mesh):
    placed = (
        P(None, ("row", "col")),
        P("row", "col", None),
        P("row", "col"),
        P("row", "col", None, None, None),
        P("row", "col", None, None, None),
    )
    return jax.shard_map(
        body,
        mesh=mesh,
        in_specs=placed,
        out_specs=(P(None, ("row", "col")), P(None, ("row", "col"))),
        check_vma=False,
    )
```

```python
import functools

import jax
import jax.numpy as jnp
from jax import lax
from jax.experimental import pallas as pl
from jax.experimental.pallas import tpu as pltpu
from jax.sharding import PartitionSpec as P

graph_weight = 0.95
GROUP = 16
VMEM_LIMIT = 60 * 1024 * 1024


def dot_plain(left, right, **kwargs):
    return lax.dot_general(
        left, right, (((1,), (0,)), ((), ())), preferred_element_type=jnp.float32, **kwargs
    )


def dot_across(left, right, **kwargs):
    return lax.dot_general(
        left, right, (((1,), (1,)), ((), ())), preferred_element_type=jnp.float32, **kwargs
    )


exact_plain = functools.partial(dot_plain, precision=lax.Precision.HIGHEST)
exact_across = functools.partial(dot_across, precision=lax.Precision.HIGHEST)


def place_of(spots_ref, slot, col_blocks):
    spot = spots_ref[slot]
    return spot // col_blocks, spot % col_blocks


def build_kernel(row_count, col_count, per_seg, spots_ref, facts_ref, index_ref, value_ref, *refs):
    block_ref = refs[0]
    row_outs = refs[1 : 1 + row_count]
    col_outs = refs[1 + row_count : 1 + row_count + col_count]
    row_ref, col_ref = refs[1 + row_count + col_count :]
    col_blocks = col_count * per_seg
    step = pl.program_id(0)
    live = facts_ref[0]

    @pl.when(step == 0)
    def _():
        row_ref[...] = jnp.zeros_like(row_ref)
        col_ref[...] = jnp.zeros_like(col_ref)

    @pl.when(step * GROUP < live)
    def _():
        lanes = lax.broadcasted_iota(jnp.int32, (16, 128), 0).astype(jnp.float32)
        targets = [(lanes + 16.0 * part).astype(jnp.bfloat16) for part in range(8)]
        ones = jnp.ones((8, 128), jnp.bfloat16)
        zero = jnp.zeros((16, 128), jnp.bfloat16)
        row_sums = []
        col_sums = []
        for slot in range(GROUP):
            active = (step * GROUP + slot < live).astype(jnp.float32)
            index_f32 = index_ref[slot].astype(jnp.float32)
            value_f32 = value_ref[slot].astype(jnp.float32) * active
            sums = [zero] * 8
            for entry in range(16):
                index_row = jnp.broadcast_to(index_f32[entry : entry + 1], (16, 128)).astype(
                    jnp.bfloat16
                )
                value_row = jnp.broadcast_to(value_f32[entry : entry + 1], (16, 128)).astype(
                    jnp.bfloat16
                )
                for part in range(8):
                    sums[part] = sums[part] + jnp.where(
                        index_row == targets[part], value_row, zero
                    )
            block = jnp.concatenate(sums, axis=0)
            block_ref[slot] = block
            row_sums.append(dot_plain(ones, block))
            col_sums.append(dot_across(ones, block))
        for slot in range(GROUP):
            row_block, col_block = place_of(spots_ref, step * GROUP + slot, col_blocks)
            row_ref[row_block] += row_sums[slot]
            col_ref[col_block] += col_sums[slot]

    @pl.when(step == pl.num_programs(0) - 1)
    def _():
        for outs, total_ref, mine in ((row_outs, row_ref, facts_ref[1]), (col_outs, col_ref, facts_ref[2])):
            for ahead, out in enumerate(outs):
                first = lax.rem(mine + ahead, len(outs)) * per_seg
                for part in range(per_seg):
                    out[part : part + 1] = total_ref[first + part][:1]


def clamp_group(step, spots_ref, facts_ref):
    return (jnp.minimum(step, (facts_ref[0] - 1) // GROUP), 0, 0)


def whole_array(rank):
    return lambda step, spots_ref, facts_ref: (0,) * rank


def build_blocks(spots, facts, index_table, value_table, row_count, col_count, per_seg):
    slots = index_table.shape[0]
    devices = row_count + col_count
    return pl.pallas_call(
        functools.partial(build_kernel, row_count, col_count, per_seg),
        grid_spec=pltpu.PrefetchScalarGridSpec(
            num_scalar_prefetch=2,
            grid=(slots // GROUP,),
            in_specs=[
                pl.BlockSpec((GROUP, 16, 128), clamp_group),
                pl.BlockSpec((GROUP, 16, 128), clamp_group),
            ],
            out_specs=[pl.BlockSpec((GROUP, 128, 128), clamp_group)]
            + [pl.BlockSpec((per_seg, 128), whole_array(2))] * devices,
            scratch_shapes=[
                pltpu.VMEM((row_count * per_seg, 8, 128), jnp.float32),
                pltpu.VMEM((col_count * per_seg, 8, 128), jnp.float32),
            ],
        ),
        out_shape=[jax.ShapeDtypeStruct((slots, 128, 128), jnp.bfloat16)]
        + [jax.ShapeDtypeStruct((per_seg, 128), jnp.float32)] * devices,
        compiler_params=pltpu.CompilerParams(vmem_limit_bytes=VMEM_LIMIT),
        name="build_blocks",
    )(spots, facts, index_table, value_table)


def product_kernel(row_count, col_count, with_gram, spots_ref, facts_ref, block_ref, *refs):
    refs = list(refs)

    def take(count):
        taken = refs[:count]
        del refs[:count]
        return taken

    row_pieces = take(row_count)
    col_pieces = take(col_count)
    gram_in = take(1) if with_gram else None
    row_outs = take(row_count)
    col_outs = take(col_count)
    gram_out = take(1) if with_gram else None
    row_dir_ref, col_dir_ref, row_ref, col_ref = refs
    per_seg = row_pieces[0].shape[0]
    col_blocks = col_count * per_seg
    step = pl.program_id(0)
    live = facts_ref[0]

    @pl.when(step == 0)
    def _():
        row_ref[...] = jnp.zeros_like(row_ref)
        col_ref[...] = jnp.zeros_like(col_ref)
        for pieces, dir_ref, mine in (
            (row_pieces, row_dir_ref, facts_ref[1]),
            (col_pieces, col_dir_ref, facts_ref[2]),
        ):
            for behind, piece in enumerate(pieces):
                first = lax.rem(mine + (len(pieces) - behind), len(pieces)) * per_seg
                for part in range(per_seg):
                    dir_ref[first + part] = piece[part]

    @pl.when(step * GROUP < live)
    def _():
        row_sums = []
        col_sums = []
        for slot in range(GROUP):
            row_block, col_block = place_of(spots_ref, step * GROUP + slot, col_blocks)
            block = block_ref[slot]
            row_sums.append(dot_plain(col_dir_ref[col_block], block))
            col_sums.append(dot_across(row_dir_ref[row_block], block))
        for slot in range(GROUP):
            row_block, col_block = place_of(spots_ref, step * GROUP + slot, col_blocks)
            row_ref[row_block] += row_sums[slot]
            col_ref[col_block] += col_sums[slot]

    @pl.when(step == pl.num_programs(0) - 1)
    def _():
        for outs, total_ref, mine in (
            (row_outs, row_ref, facts_ref[1]),
            (col_outs, col_ref, facts_ref[2]),
        ):
            for ahead, out in enumerate(outs):
                first = lax.rem(mine + ahead, len(outs)) * per_seg
                for part in range(per_seg):
                    out[part] = total_ref[first + part].astype(out.dtype)
        if with_gram:
            size = row_ref.shape[1]

            def add_segment(segment, total):
                for part in range(per_seg):
                    col_block = segment * per_seg + part
                    values = col_ref[col_block]
                    high = values.astype(jnp.bfloat16)
                    low = (values - high.astype(jnp.float32)).astype(jnp.bfloat16)
                    total += dot_across(
                        jnp.concatenate([high, low], axis=0), tall(col_dir_ref[col_block])
                    )
                return total

            total = lax.fori_loop(
                0, col_count, add_segment, jnp.zeros((2 * size, 128), jnp.float32)
            )
            gram_out[0][...] = gram_in[0][...] + pltpu.roll(total[:size] + total[size:], 3 * size, 1)


def block_products(spots, facts, blocks, row_pieces, col_pieces, gram=None):
    slots = blocks.shape[0]
    piece = row_pieces[0]
    per_seg, rows, lanes = piece.shape
    devices = len(row_pieces) + len(col_pieces)
    grams = [] if gram is None else [gram]
    piece_specs = [pl.BlockSpec(piece.shape, whole_array(3))] * devices
    gram_specs = [pl.BlockSpec(item.shape, whole_array(2)) for item in grams]
    row_shape = (len(row_pieces) * per_seg, rows, lanes)
    col_shape = (len(col_pieces) * per_seg, rows, lanes)
    return pl.pallas_call(
        functools.partial(product_kernel, len(row_pieces), len(col_pieces), gram is not None),
        grid_spec=pltpu.PrefetchScalarGridSpec(
            num_scalar_prefetch=2,
            grid=(slots // GROUP,),
            in_specs=[pl.BlockSpec((GROUP, 128, 128), clamp_group)] + piece_specs + gram_specs,
            out_specs=piece_specs + gram_specs,
            scratch_shapes=[
                pltpu.VMEM(row_shape, jnp.bfloat16),
                pltpu.VMEM(col_shape, jnp.bfloat16),
                pltpu.VMEM(row_shape, jnp.float32),
                pltpu.VMEM(col_shape, jnp.float32),
            ],
        ),
        out_shape=[jax.ShapeDtypeStruct(piece.shape, jnp.bfloat16)] * devices
        + [jax.ShapeDtypeStruct(item.shape, jnp.float32) for item in grams],
        compiler_params=pltpu.CompilerParams(vmem_limit_bytes=VMEM_LIMIT),
        name="block_products",
    )(spots, facts, blocks, *row_pieces, *col_pieces, *grams)


def total_of(refs):
    total = refs[0][...].astype(jnp.float32)
    for ref in refs[1:]:
        total = total + ref[...].astype(jnp.float32)
    return total


def start_kernel(*refs):
    *degree_refs, query_ref, scaling_ref, scaled_ref = refs
    degree = 1.0 + 0.5 * total_of(degree_refs)
    scaling = 1.0 / jnp.sqrt(degree)
    scaling_ref[...] = scaling
    for part in range(scaling.shape[0]):
        scaled_ref[part] = (
            scaling[part : part + 1] * query_ref[:, part * 128 : part * 128 + 128]
        ).astype(jnp.bfloat16)


def scaled_sum(refs, scaling_ref, part):
    scaling = scaling_ref[part : part + 1]
    return scaling * (0.5 * total_of([ref.at[part] for ref in refs]))


def middle_kernel(*refs):
    *part_refs, scaling_ref, query_ref, first_ref, scaled_ref, gram_ref = refs
    size = query_ref.shape[0]
    pair_gram = jnp.zeros((2 * size, 128), jnp.float32)
    for part in range(scaling_ref.shape[0]):
        first = scaled_sum(part_refs, scaling_ref, part)
        first_ref[part] = first
        scaled_ref[part] = (scaling_ref[part : part + 1] * first).astype(jnp.bfloat16)
        pair = jnp.concatenate(
            [query_ref[:, part * 128 : part * 128 + 128], first], axis=0
        )
        pair_gram += exact_across(pair, tall(pair))
    gram_ref[...] = beside(
        pair_gram[:size], pltpu.roll(window(pair_gram[size:], 1), size, 1)
    )


def tall(flat):
    rest = flat.shape[1] - flat.shape[0]
    return jnp.concatenate([flat, jnp.zeros((rest, flat.shape[1]), flat.dtype)], axis=0)


def flipped(flat):
    return tall(flat).T[: flat.shape[0]]


def times(left, right):
    return exact_plain(left, tall(right))


def beside(left, right):
    return left + pltpu.roll(right, left.shape[0], 1)


def stacked(upper, lower):
    rest = jnp.zeros((upper.shape[1] - 2 * upper.shape[0], upper.shape[1]), upper.dtype)
    return jnp.concatenate([upper, lower, rest], axis=0)


def sandwich(rows, middle):
    return exact_across(exact_plain(rows, middle), tall(rows))


def symmetric(flat):
    return 0.5 * (flat + flipped(flat))


def window(flat, place):
    size = flat.shape[0]
    if place:
        flat = pltpu.roll(flat, flat.shape[1] - place * size, 1)
    lanes = lax.broadcasted_iota(jnp.int32, flat.shape, 1)
    return jnp.where(lanes < size, flat, 0.0)


def solve_many(pairs):
    size = pairs[0][0].shape[0]
    systems = [matrix + pltpu.roll(side, size, 1) for matrix, side in pairs]
    sublanes = lax.broadcasted_iota(jnp.int32, systems[0].shape, 0)
    for pivot in range(size):
        updated = []
        for system in systems:
            column = system[:, pivot : pivot + 1]
            row = system[pivot : pivot + 1, :] / column[pivot : pivot + 1, :]
            updated.append(jnp.where(sublanes == pivot, row, system - column * row))
        systems = updated
    return [window(system, 1) for system in systems]


def close_kernel(piece_count, *refs):
    part_refs = refs[:piece_count]
    *gram_refs, scaling_ref, query_ref, first_ref, solution_ref, residual_ref = refs[piece_count:]
    size = query_ref.shape[0]
    weight = graph_weight
    total = total_of(gram_refs)
    g00 = symmetric(window(total, 0))
    g01 = window(total, 1)
    g11 = symmetric(window(total, 2))
    g12 = symmetric(window(total, 3))
    eye = (
        lax.broadcasted_iota(jnp.int32, total.shape, 0)
        == lax.broadcasted_iota(jnp.int32, total.shape, 1)
    ).astype(jnp.float32)
    curve = symmetric(g00 - weight * g01)
    steps, inverse = solve_many([(curve, g00), (g00, eye)])
    steps_t = flipped(steps)
    plain_gram = stacked(beside(g00, g01), beside(flipped(g01), g11))
    through_gram = stacked(beside(g01, g11), beside(g11, g12))
    after_first = beside(eye - steps_t, weight * steps_t)
    new_gram = symmetric(sandwich(after_first, plain_gram))
    mixing = times(inverse, new_gram)
    direction = after_first + flipped(mixing)
    curve = symmetric(sandwich(direction, plain_gram - weight * through_gram))
    (steps,) = solve_many([(curve, new_gram)])
    steps_t2 = flipped(steps)
    applied = direction - weight * pltpu.roll(direction, size, 1)
    solution_rows = exact_plain(beside(eye, steps_t2), stacked(steps_t, direction))
    residual_rows = exact_plain(beside(eye, -steps_t2), stacked(after_first, applied))
    rows = jnp.concatenate([solution_rows, residual_rows], axis=0)
    for part in range(first_ref.shape[0]):
        lanes = slice(part * 128, part * 128 + 128)
        basis = jnp.concatenate(
            [
                query_ref[:, lanes],
                first_ref[part],
                scaled_sum(part_refs, scaling_ref, part),
                jnp.zeros_like(eye),
            ],
            axis=0,
        )
        values = exact_plain(rows, basis)
        solution_ref[:, lanes] = values[:size]
        residual_ref[:, lanes] = values[size:]


def pass_around(pieces, axis):
    count = len(pieces)
    return [pieces[0]] + [
        lax.ppermute(pieces[ahead], axis, [(at, (at + ahead) % count) for at in range(count)])
        for ahead in range(1, count)
    ]


def spread(piece, axis):
    return pass_around([piece] * lax.axis_size(axis), axis)


def simple_call(kernel, shapes, name, *operands):
    return pl.pallas_call(
        kernel,
        out_shape=shapes,
        compiler_params=pltpu.CompilerParams(vmem_limit_bytes=VMEM_LIMIT),
        name=name,
    )(*operands)


def sum_kernel(*refs):
    refs[-1][...] = total_of(refs[:-1])


def body(queries, block_spots, live_blocks, neighbor_cols, neighbor_sims):
    row_count = lax.axis_size("row")
    col_count = lax.axis_size("col")
    query_rows, seg_len = queries.shape
    per_seg = seg_len // 128
    spots = block_spots[0, 0]
    facts = jnp.stack([live_blocks[0, 0], lax.axis_index("row"), lax.axis_index("col")])
    piece = (per_seg, query_rows, 128)
    wide = jax.ShapeDtypeStruct(piece, jnp.float32)
    narrow = jax.ShapeDtypeStruct(piece, jnp.bfloat16)
    gram_shape = jax.ShapeDtypeStruct((query_rows, 128), jnp.float32)

    blocks, *sums = build_blocks(
        spots, facts, neighbor_cols[0, 0], neighbor_sims[0, 0], row_count, col_count, per_seg
    )
    row_parts = pass_around(sums[:row_count], "row")
    col_parts = pass_around(sums[row_count:], "col")
    scaling, scaled = simple_call(
        start_kernel,
        [jax.ShapeDtypeStruct((per_seg, 128), jnp.float32), narrow],
        "start",
        *row_parts,
        *col_parts,
        queries,
    )

    def product(vectors, gram=None):
        totals = block_products(
            spots, facts, blocks, spread(vectors, "row"), spread(vectors, "col"), gram
        )
        devices = row_count + col_count
        parts = pass_around(totals[:row_count], "row")
        parts += pass_around(totals[row_count:devices], "col")
        return parts, totals[devices:]

    parts, _ = product(scaled)
    first, scaled, gram = simple_call(
        middle_kernel, [wide, narrow, gram_shape], "middle", *parts, scaling, queries
    )
    parts, (gram,) = product(scaled, gram)
    (gram,) = simple_call(sum_kernel, [gram_shape], "gram_sum", *spread(gram, "row"))
    flat = jax.ShapeDtypeStruct(queries.shape, jnp.float32)
    return tuple(
        simple_call(
            functools.partial(close_kernel, len(parts)),
            [flat, flat],
            "close",
            *parts,
            *spread(gram, "col"),
            scaling,
            queries,
            first,
        )
    )


def solution(mesh):
    placed = (
        P(None, ("row", "col")),
        P("row", "col", None),
        P("row", "col"),
        P("row", "col", None, None, None),
        P("row", "col", None, None, None),
    )
    return jax.shard_map(
        body,
        mesh=mesh,
        in_specs=placed,
        out_specs=(P(None, ("row", "col")), P(None, ("row", "col"))),
        check_vma=False,
    )
```

```python
import functools

import jax
import jax.numpy as jnp
from jax import lax
from jax.experimental import pallas as pl
from jax.experimental.pallas import tpu as pltpu
from jax.sharding import PartitionSpec as P

graph_weight = 0.95
GROUP = 16
VMEM_LIMIT = 60 * 1024 * 1024


def dot_plain(left, right, **kwargs):
    return lax.dot_general(
        left, right, (((1,), (0,)), ((), ())), preferred_element_type=jnp.float32, **kwargs
    )


def dot_across(left, right, **kwargs):
    return lax.dot_general(
        left, right, (((1,), (1,)), ((), ())), preferred_element_type=jnp.float32, **kwargs
    )


exact_plain = functools.partial(dot_plain, precision=lax.Precision.HIGHEST)
exact_across = functools.partial(dot_across, precision=lax.Precision.HIGHEST)


def place_of(spots_ref, slot, col_blocks):
    spot = spots_ref[slot]
    return spot // col_blocks, spot % col_blocks


def build_kernel(row_count, col_count, per_seg, spots_ref, facts_ref, index_ref, value_ref, *refs):
    block_ref = refs[0]
    row_outs = refs[1 : 1 + row_count]
    col_out_ref, row_ref, col_ref = refs[1 + row_count :]
    col_blocks = col_count * per_seg
    step = pl.program_id(0)
    live = facts_ref[0]

    @pl.when(step == 0)
    def _():
        row_ref[...] = jnp.zeros_like(row_ref)
        col_ref[...] = jnp.zeros_like(col_ref)

    @pl.when(step * GROUP < live)
    def _():
        lanes = lax.broadcasted_iota(jnp.int32, (16, 128), 0).astype(jnp.float32)
        targets = [(lanes + 16.0 * part).astype(jnp.bfloat16) for part in range(8)]
        ones = jnp.ones((8, 128), jnp.bfloat16)
        zero = jnp.zeros((16, 128), jnp.bfloat16)
        row_sums = []
        col_sums = []
        for slot in range(GROUP):
            active = (step * GROUP + slot < live).astype(jnp.float32)
            index_f32 = index_ref[slot].astype(jnp.float32)
            value_f32 = value_ref[slot].astype(jnp.float32) * active
            sums = [zero] * 8
            for entry in range(16):
                index_row = jnp.broadcast_to(index_f32[entry : entry + 1], (16, 128)).astype(
                    jnp.bfloat16
                )
                value_row = jnp.broadcast_to(value_f32[entry : entry + 1], (16, 128)).astype(
                    jnp.bfloat16
                )
                for part in range(8):
                    sums[part] = sums[part] + jnp.where(
                        index_row == targets[part], value_row, zero
                    )
            block = jnp.concatenate(sums, axis=0)
            block_ref[slot] = block
            row_sums.append(dot_plain(ones, block))
            col_sums.append(dot_across(ones, block))
        for slot in range(GROUP):
            row_block, col_block = place_of(spots_ref, step * GROUP + slot, col_blocks)
            row_ref[row_block] += row_sums[slot]
            col_ref[col_block] += col_sums[slot]

    @pl.when(step == pl.num_programs(0) - 1)
    def _():
        for ahead, out in enumerate(row_outs):
            first = lax.rem(facts_ref[1] + ahead, row_count) * per_seg
            for part in range(per_seg):
                out[part : part + 1] = row_ref[first + part][:1]
        for col_block in range(col_blocks):
            col_out_ref[col_block : col_block + 1] = col_ref[col_block][:1]


def clamp_group(step, spots_ref, facts_ref):
    return (jnp.minimum(step, (facts_ref[0] - 1) // GROUP), 0, 0)


def whole_array(rank):
    return lambda step, spots_ref, facts_ref: (0,) * rank


def build_blocks(spots, facts, index_table, value_table, row_count, col_count, per_seg):
    slots = index_table.shape[0]
    row_shapes = [(per_seg, 128)] * row_count
    sum_shapes = row_shapes + [(col_count * per_seg, 128)]
    return pl.pallas_call(
        functools.partial(build_kernel, row_count, col_count, per_seg),
        grid_spec=pltpu.PrefetchScalarGridSpec(
            num_scalar_prefetch=2,
            grid=(slots // GROUP,),
            in_specs=[
                pl.BlockSpec((GROUP, 16, 128), clamp_group),
                pl.BlockSpec((GROUP, 16, 128), clamp_group),
            ],
            out_specs=[pl.BlockSpec((GROUP, 128, 128), clamp_group)]
            + [pl.BlockSpec(shape, whole_array(2)) for shape in sum_shapes],
            scratch_shapes=[
                pltpu.VMEM((row_count * per_seg, 8, 128), jnp.float32),
                pltpu.VMEM((col_count * per_seg, 8, 128), jnp.float32),
            ],
        ),
        out_shape=[jax.ShapeDtypeStruct((slots, 128, 128), jnp.bfloat16)]
        + [jax.ShapeDtypeStruct(shape, jnp.float32) for shape in sum_shapes],
        compiler_params=pltpu.CompilerParams(vmem_limit_bytes=VMEM_LIMIT),
        name="build_blocks",
    )(spots, facts, index_table, value_table)


def backward_kernel(col_blocks, spots_ref, facts_ref, block_ref, *refs):
    *row_pieces, col_out_ref, row_dir_ref, col_ref = refs
    per_seg = row_pieces[0].shape[0]
    step = pl.program_id(0)

    @pl.when(step == 0)
    def _():
        col_ref[...] = jnp.zeros_like(col_ref)
        fill_directions(row_pieces, row_dir_ref, facts_ref[1], per_seg)

    @pl.when(step * GROUP < facts_ref[0])
    def _():
        sums = []
        for slot in range(GROUP):
            row_block, _ = place_of(spots_ref, step * GROUP + slot, col_blocks)
            sums.append(dot_across(row_dir_ref[row_block], block_ref[slot]))
        for slot in range(GROUP):
            _, col_block = place_of(spots_ref, step * GROUP + slot, col_blocks)
            col_ref[col_block] += sums[slot]

    @pl.when(step == pl.num_programs(0) - 1)
    def _():
        col_out_ref[...] = col_ref[...].astype(col_out_ref.dtype)


def fill_directions(pieces, dir_ref, mine, per_seg):
    for behind, piece in enumerate(pieces):
        first = lax.rem(mine + (len(pieces) - behind), len(pieces)) * per_seg
        for part in range(per_seg):
            dir_ref[first + part] = piece[part]


def forward_kernel(row_count, with_gram, spots_ref, facts_ref, block_ref, col_dir_ref, *refs):
    refs = list(refs)

    def take(count):
        taken = refs[:count]
        del refs[:count]
        return taken

    row_pieces = take(row_count if with_gram else 0)
    gram_in = take(int(with_gram))
    row_outs = take(row_count)
    gram_out = take(int(with_gram))
    row_ref = refs[0]
    col_blocks = col_dir_ref.shape[0]
    per_seg, size, _ = row_outs[0].shape
    step = pl.program_id(0)

    @pl.when(step == 0)
    def _():
        row_ref[...] = jnp.zeros_like(row_ref)

    @pl.when(step * GROUP < facts_ref[0])
    def _():
        sums = []
        for slot in range(GROUP):
            _, col_block = place_of(spots_ref, step * GROUP + slot, col_blocks)
            sums.append(dot_plain(col_dir_ref[col_block], block_ref[slot]))
        for slot in range(GROUP):
            row_block, _ = place_of(spots_ref, step * GROUP + slot, col_blocks)
            row_ref[row_block] += sums[slot]

    @pl.when(step == pl.num_programs(0) - 1)
    def _():
        gram = jnp.zeros((2 * size, 128), jnp.float32)
        for ahead, out in enumerate(row_outs):
            first = lax.rem(facts_ref[1] + ahead, row_count) * per_seg
            for part in range(per_seg):
                values = row_ref[first + part]
                high = values.astype(out.dtype)
                out[part] = high
                if with_gram:
                    low = (values - high.astype(jnp.float32)).astype(out.dtype)
                    piece = row_pieces[(row_count - ahead) % row_count]
                    gram += dot_across(jnp.concatenate([high, low], axis=0), tall(piece[part]))
        if with_gram:
            gram = gram[:size] + gram[size:]
            gram_out[0][...] = gram_in[0][...] + pltpu.roll(gram, 3 * size, 1)


def over_blocks(kernel, name, spots, facts, blocks, inputs, outputs, scratch):
    slots = blocks.shape[0]
    return pl.pallas_call(
        kernel,
        grid_spec=pltpu.PrefetchScalarGridSpec(
            num_scalar_prefetch=2,
            grid=(slots // GROUP,),
            in_specs=[pl.BlockSpec((GROUP, 128, 128), clamp_group)]
            + [pl.BlockSpec(item.shape, whole_array(item.ndim)) for item in inputs],
            out_specs=[pl.BlockSpec(item.shape, whole_array(len(item.shape))) for item in outputs],
            scratch_shapes=scratch,
        ),
        out_shape=outputs,
        compiler_params=pltpu.CompilerParams(vmem_limit_bytes=VMEM_LIMIT),
        cost_estimate=pl.CostEstimate(
            flops=2 * slots * 32 * 128 * 128, bytes_accessed=2 * blocks.size, transcendentals=0
        ),
        name=name,
    )(spots, facts, blocks, *inputs)


def backward_product(spots, facts, blocks, row_pieces, col_count):
    per_seg, rows, lanes = row_pieces[0].shape
    col_shape = (col_count * per_seg, rows, lanes)
    (total,) = over_blocks(
        functools.partial(backward_kernel, col_shape[0]),
        "backward_product",
        spots,
        facts,
        blocks,
        row_pieces,
        [jax.ShapeDtypeStruct(col_shape, jnp.bfloat16)],
        [
            pltpu.VMEM((len(row_pieces) * per_seg, rows, lanes), jnp.bfloat16),
            pltpu.VMEM(col_shape, jnp.float32),
        ],
    )
    return total


def forward_product(spots, facts, blocks, col_dirs, row_pieces, gram=None):
    piece = row_pieces[0]
    inputs = [col_dirs]
    outputs = [jax.ShapeDtypeStruct(piece.shape, jnp.bfloat16)] * len(row_pieces)
    if gram is not None:
        inputs += [*row_pieces, gram]
        outputs += [jax.ShapeDtypeStruct(gram.shape, jnp.float32)]
    row_shape = (len(row_pieces) * piece.shape[0],) + piece.shape[1:]
    return over_blocks(
        functools.partial(forward_kernel, len(row_pieces), gram is not None),
        "forward_product",
        spots,
        facts,
        blocks,
        inputs,
        outputs,
        [pltpu.VMEM(row_shape, jnp.float32)],
    )


def total_of(values):
    total = values[0].astype(jnp.float32)
    for value in values[1:]:
        total = total + value.astype(jnp.float32)
    return total


def leading(ref):
    return [ref.at[index] for index in range(ref.shape[0])]


def start_kernel(*refs):
    *row_refs, col_ref, query_ref, scaling_ref, scaled_ref, copies_ref = refs
    degree = 1.0 + 0.5 * total_of([ref[...] for ref in [*row_refs, *leading(col_ref)]])
    scaling = 1.0 / jnp.sqrt(degree)
    scaling_ref[...] = scaling
    for part in range(scaling.shape[0]):
        scaled = (
            scaling[part : part + 1] * query_ref[:, part * 128 : part * 128 + 128]
        ).astype(jnp.bfloat16)
        scaled_ref[part] = scaled
        for copy in range(copies_ref.shape[0]):
            copies_ref[copy, part] = scaled


def scaled_sum(row_refs, col_ref, scaling_ref, part):
    scaling = scaling_ref[part : part + 1]
    total = total_of([ref[part] for ref in [*row_refs, *leading(col_ref)]])
    return scaling * (0.5 * total)


def middle_kernel(*refs):
    *row_refs, col_ref, scaling_ref, query_ref, first_ref, scaled_ref, copies_ref, gram_ref = refs
    size = query_ref.shape[0]
    pair_gram = jnp.zeros((2 * size, 128), jnp.float32)
    for part in range(scaling_ref.shape[0]):
        first = scaled_sum(row_refs, col_ref, scaling_ref, part)
        first_ref[part] = first
        scaled = (scaling_ref[part : part + 1] * first).astype(jnp.bfloat16)
        scaled_ref[part] = scaled
        for copy in range(copies_ref.shape[0]):
            copies_ref[copy, part] = scaled
        pair = jnp.concatenate(
            [query_ref[:, part * 128 : part * 128 + 128], first], axis=0
        )
        pair_gram += exact_across(pair, tall(pair))
    gram_ref[...] = beside(
        pair_gram[:size], pltpu.roll(window(pair_gram[size:], 1), size, 1)
    )


def tall(flat):
    rest = flat.shape[1] - flat.shape[0]
    return jnp.concatenate([flat, jnp.zeros((rest, flat.shape[1]), flat.dtype)], axis=0)


def flipped(flat):
    return tall(flat).T[: flat.shape[0]]


def times(left, right):
    return exact_plain(left, tall(right))


def beside(left, right):
    return left + pltpu.roll(right, left.shape[0], 1)


def stacked(upper, lower):
    rest = jnp.zeros((upper.shape[1] - 2 * upper.shape[0], upper.shape[1]), upper.dtype)
    return jnp.concatenate([upper, lower, rest], axis=0)


def sandwich(rows, middle):
    return exact_across(exact_plain(rows, middle), tall(rows))


def symmetric(flat):
    return 0.5 * (flat + flipped(flat))


def window(flat, place):
    size = flat.shape[0]
    if place:
        flat = pltpu.roll(flat, flat.shape[1] - place * size, 1)
    lanes = lax.broadcasted_iota(jnp.int32, flat.shape, 1)
    return jnp.where(lanes < size, flat, 0.0)


def solve_many(pairs):
    size = pairs[0][0].shape[0]
    systems = [matrix + pltpu.roll(side, size, 1) for matrix, side in pairs]
    sublanes = lax.broadcasted_iota(jnp.int32, systems[0].shape, 0)
    for pivot in range(size):
        updated = []
        for system in systems:
            column = system[:, pivot : pivot + 1]
            row = system[pivot : pivot + 1, :] / column[pivot : pivot + 1, :]
            updated.append(jnp.where(sublanes == pivot, row, system - column * row))
        systems = updated
    return [window(system, 1) for system in systems]


def close_kernel(*refs):
    *row_refs, col_ref, gram_ref, scaling_ref, query_ref, first_ref = refs[:-2]
    solution_ref, residual_ref = refs[-2:]
    size = query_ref.shape[0]
    weight = graph_weight
    total = total_of([ref[...] for ref in leading(gram_ref)])
    g00 = symmetric(window(total, 0))
    g01 = window(total, 1)
    g11 = symmetric(window(total, 2))
    g12 = symmetric(window(total, 3))
    eye = (
        lax.broadcasted_iota(jnp.int32, total.shape, 0)
        == lax.broadcasted_iota(jnp.int32, total.shape, 1)
    ).astype(jnp.float32)
    curve = symmetric(g00 - weight * g01)
    steps, inverse = solve_many([(curve, g00), (g00, eye)])
    steps_t = flipped(steps)
    plain_gram = stacked(beside(g00, g01), beside(flipped(g01), g11))
    through_gram = stacked(beside(g01, g11), beside(g11, g12))
    after_first = beside(eye - steps_t, weight * steps_t)
    new_gram = symmetric(sandwich(after_first, plain_gram))
    mixing = times(inverse, new_gram)
    direction = after_first + flipped(mixing)
    curve = symmetric(sandwich(direction, plain_gram - weight * through_gram))
    (steps,) = solve_many([(curve, new_gram)])
    steps_t2 = flipped(steps)
    applied = direction - weight * pltpu.roll(direction, size, 1)
    solution_rows = exact_plain(beside(eye, steps_t2), stacked(steps_t, direction))
    residual_rows = exact_plain(beside(eye, -steps_t2), stacked(after_first, applied))
    rows = jnp.concatenate([solution_rows, residual_rows], axis=0)
    for part in range(first_ref.shape[0]):
        lanes = slice(part * 128, part * 128 + 128)
        basis = jnp.concatenate(
            [
                query_ref[:, lanes],
                first_ref[part],
                scaled_sum(row_refs, col_ref, scaling_ref, part),
                jnp.zeros_like(eye),
            ],
            axis=0,
        )
        values = exact_plain(rows, basis)
        solution_ref[:, lanes] = values[:size]
        residual_ref[:, lanes] = values[size:]


def pass_around(pieces, axis):
    count = len(pieces)
    return [pieces[0]] + [
        lax.ppermute(pieces[ahead], axis, [(at, (at + ahead) % count) for at in range(count)])
        for ahead in range(1, count)
    ]


def exchange(pieces, axis):
    return lax.all_to_all(pieces, axis, 0, 0, tiled=True)


def simple_call(kernel, shapes, name, *operands):
    return pl.pallas_call(
        kernel,
        out_shape=shapes,
        compiler_params=pltpu.CompilerParams(vmem_limit_bytes=VMEM_LIMIT),
        name=name,
    )(*operands)


def sum_kernel(*refs):
    *piece_refs, copies_ref = refs
    total = total_of([ref[...] for ref in piece_refs])
    for copy in range(copies_ref.shape[0]):
        copies_ref[copy] = total


def body(queries, block_spots, live_blocks, neighbor_cols, neighbor_sims):
    row_count = lax.axis_size("row")
    col_count = lax.axis_size("col")
    query_rows, seg_len = queries.shape
    per_seg = seg_len // 128
    spots = block_spots[0, 0]
    facts = jnp.stack([live_blocks[0, 0], lax.axis_index("row"), lax.axis_index("col")])
    piece = (per_seg, query_rows, 128)
    wide = jax.ShapeDtypeStruct(piece, jnp.float32)
    narrow = jax.ShapeDtypeStruct(piece, jnp.bfloat16)
    copies = jax.ShapeDtypeStruct((col_count,) + piece, jnp.bfloat16)
    gram_shape = jax.ShapeDtypeStruct((query_rows, 128), jnp.float32)
    gram_copies = jax.ShapeDtypeStruct((col_count, query_rows, 128), jnp.float32)

    blocks, *row_sums, col_sums = build_blocks(
        spots, facts, neighbor_cols[0, 0], neighbor_sims[0, 0], row_count, col_count, per_seg
    )
    col_part = exchange(col_sums.reshape(col_count, per_seg, 128), "col")
    row_parts = pass_around(row_sums, "row")
    scaling, scaled, scaled_copies = simple_call(
        start_kernel,
        [jax.ShapeDtypeStruct((per_seg, 128), jnp.float32), narrow, copies],
        "start",
        *row_parts,
        col_part,
        queries,
    )

    def product(vectors, vector_copies, gram=None):
        col_dirs = exchange(vector_copies, "col").reshape((col_count * per_seg,) + piece[1:])
        row_pieces = pass_around([vectors] * row_count, "row")
        total = backward_product(spots, facts, blocks, row_pieces, col_count)
        col_part = exchange(total.reshape((col_count,) + piece), "col")
        totals = forward_product(spots, facts, blocks, col_dirs, row_pieces, gram)
        row_parts = pass_around(totals[:row_count], "row")
        return row_parts, col_part, totals[row_count:]

    row_parts, col_part, _ = product(scaled, scaled_copies)
    first, scaled, scaled_copies, gram = simple_call(
        middle_kernel,
        [wide, narrow, copies, gram_shape],
        "middle",
        *row_parts,
        col_part,
        scaling,
        queries,
    )
    row_parts, col_part, (gram,) = product(scaled, scaled_copies, gram)
    (grams,) = simple_call(
        sum_kernel, [gram_copies], "gram_sum", *pass_around([gram] * row_count, "row")
    )
    flat = jax.ShapeDtypeStruct(queries.shape, jnp.float32)
    return tuple(
        simple_call(
            close_kernel,
            [flat, flat],
            "close",
            *row_parts,
            col_part,
            exchange(grams, "col"),
            scaling,
            queries,
            first,
        )
    )


def solution(mesh):
    placed = (
        P(None, ("row", "col")),
        P("row", "col", None),
        P("row", "col"),
        P("row", "col", None, None, None),
        P("row", "col", None, None, None),
    )
    return jax.shard_map(
        body,
        mesh=mesh,
        in_specs=placed,
        out_specs=(P(None, ("row", "col")), P(None, ("row", "col"))),
        check_vma=False,
    )
```

```python
import functools

import jax
import jax.numpy as jnp
from jax import lax
from jax.experimental import pallas as pl
from jax.experimental.pallas import tpu as pltpu
from jax.sharding import PartitionSpec as P

graph_weight = 0.95
GROUP = 16
BATCH = 32
VMEM_LIMIT = 60 * 1024 * 1024


def dot_plain(left, right, **kwargs):
    return lax.dot_general(
        left, right, (((1,), (0,)), ((), ())), preferred_element_type=jnp.float32, **kwargs
    )


def dot_across(left, right, **kwargs):
    return lax.dot_general(
        left, right, (((1,), (1,)), ((), ())), preferred_element_type=jnp.float32, **kwargs
    )


exact_plain = functools.partial(dot_plain, precision=lax.Precision.HIGHEST)
exact_across = functools.partial(dot_across, precision=lax.Precision.HIGHEST)


LIVE, ROW, COL, PLACES = 0, 1, 2, 4


def group_count(facts_ref, group):
    return (facts_ref[LIVE] + group - 1) // group


def group_copy(source, target, sems, index, group):
    window = pl.ds(index * group, group)
    return pltpu.make_async_copy(source.at[window], target.at[window], sems.at[index])


def build_kernel(row_count, facts_ref, index_hbm, value_hbm, block_hbm, *refs):
    row_outs = refs[:row_count]
    (
        col_out_ref,
        index_ref,
        value_ref,
        block_ref,
        row_ref,
        col_ref,
        index_sems,
        value_sems,
        block_sems,
    ) = refs[row_count:]
    slots = index_ref.shape[0]
    per_seg = row_outs[0].shape[0]
    groups = group_count(facts_ref, BATCH) * (BATCH // GROUP)

    def start_copies(index, _):
        group_copy(index_hbm, index_ref, index_sems, index, GROUP).start()
        group_copy(value_hbm, value_ref, value_sems, index, GROUP).start()
        return 0

    lax.fori_loop(0, groups, start_copies, 0)
    row_ref[...] = jnp.zeros_like(row_ref)
    col_ref[...] = jnp.zeros_like(col_ref)
    rows_16 = lax.broadcasted_iota(jnp.int32, (16, 128), 0).astype(jnp.float32)
    ones = jnp.ones((8, 128), jnp.bfloat16)
    zero = jnp.zeros((16, 128), jnp.bfloat16)

    def build_group(index, _):
        group_copy(index_hbm, index_ref, index_sems, index, GROUP).wait()
        group_copy(value_hbm, value_ref, value_sems, index, GROUP).wait()
        targets = [(rows_16 + 16.0 * part).astype(jnp.bfloat16) for part in range(8)]
        row_sums = []
        col_sums = []
        for inside in range(GROUP):
            slot = index * GROUP + inside
            active = (slot < facts_ref[LIVE]).astype(jnp.float32)
            index_f32 = index_ref[slot].astype(jnp.float32)
            value_f32 = value_ref[slot].astype(jnp.float32) * active
            sums = [zero] * 8
            for entry in range(16):
                index_row = jnp.broadcast_to(index_f32[entry : entry + 1], (16, 128)).astype(
                    jnp.bfloat16
                )
                value_row = jnp.broadcast_to(value_f32[entry : entry + 1], (16, 128)).astype(
                    jnp.bfloat16
                )
                for part in range(8):
                    sums[part] = sums[part] + jnp.where(
                        index_row == targets[part], value_row, zero
                    )
            block = jnp.concatenate(sums, axis=0)
            block_ref[slot] = block
            row_sums.append(dot_plain(ones, block))
            col_sums.append(dot_across(ones, block))
        group_copy(block_ref, block_hbm, block_sems, index, GROUP).start()
        for inside in range(GROUP):
            slot = index * GROUP + inside
            row_ref[facts_ref[PLACES + slot]] += row_sums[inside]
            col_ref[facts_ref[PLACES + slots + slot]] += col_sums[inside]
        return 0

    lax.fori_loop(0, groups, build_group, 0)
    for ahead, out in enumerate(row_outs):
        first = lax.rem(facts_ref[ROW] + ahead, row_count) * per_seg
        for part in range(per_seg):
            out[part : part + 1] = row_ref[first + part][:1]
    for col_block in range(col_out_ref.shape[0]):
        col_out_ref[col_block : col_block + 1] = col_ref[col_block][:1]

    def finish_copies(index, _):
        group_copy(block_ref, block_hbm, block_sems, index, GROUP).wait()
        return 0

    lax.fori_loop(0, groups, finish_copies, 0)


SCALARS = pl.BlockSpec(memory_space=pltpu.SMEM)
ANYWHERE = pl.BlockSpec(memory_space=pl.ANY)
IN_VMEM = pl.BlockSpec(memory_space=pltpu.VMEM)


def build_blocks(facts, index_table, value_table, row_count, col_count, per_seg):
    slots = index_table.shape[0]
    groups = slots // GROUP
    sum_shapes = [(per_seg, 128)] * row_count + [(col_count * per_seg, 128)]
    return pl.pallas_call(
        functools.partial(build_kernel, row_count),
        in_specs=[SCALARS, ANYWHERE, ANYWHERE],
        out_specs=[ANYWHERE] + [IN_VMEM] * len(sum_shapes),
        out_shape=[jax.ShapeDtypeStruct((slots, 128, 128), jnp.bfloat16)]
        + [jax.ShapeDtypeStruct(shape, jnp.float32) for shape in sum_shapes],
        scratch_shapes=[
            pltpu.VMEM(index_table.shape, index_table.dtype),
            pltpu.VMEM(value_table.shape, value_table.dtype),
            pltpu.VMEM((slots, 128, 128), jnp.bfloat16),
            pltpu.VMEM((row_count * per_seg, 8, 128), jnp.float32),
            pltpu.VMEM((col_count * per_seg, 8, 128), jnp.float32),
            pltpu.SemaphoreType.DMA((groups,)),
            pltpu.SemaphoreType.DMA((groups,)),
            pltpu.SemaphoreType.DMA((groups,)),
        ],
        compiler_params=pltpu.CompilerParams(vmem_limit_bytes=VMEM_LIMIT),
        name="build_blocks",
    )(facts, index_table, value_table)


def each_group(facts_ref, block_hbm, block_ref, sems, prepare, run_group):
    groups = group_count(facts_ref, BATCH)

    def start_copy(index, _):
        group_copy(block_hbm, block_ref, sems, index, BATCH).start()
        return 0

    lax.fori_loop(0, groups, start_copy, 0)
    prepare()

    def one_group(index, _):
        group_copy(block_hbm, block_ref, sems, index, BATCH).wait()
        run_group(index * BATCH)
        return 0

    lax.fori_loop(0, groups, one_group, 0)


def add_products(dot, facts_ref, first_slot, block_ref, dir_ref, sources, total_refs, targets):
    sums = []
    for inside in range(BATCH):
        slot = first_slot + inside
        sums.append(dot(dir_ref[facts_ref[sources + slot]], block_ref[slot]))
    for inside in range(BATCH):
        total_ref = total_refs[inside % len(total_refs)]
        total_ref[facts_ref[targets + first_slot + inside]] += sums[inside]


def fill_directions(pieces, dir_ref, mine, per_seg):
    for behind, piece in enumerate(pieces):
        first = lax.rem(mine + (len(pieces) - behind), len(pieces)) * per_seg
        for part in range(per_seg):
            dir_ref[first + part] = piece[part]


def backward_kernel(facts_ref, block_hbm, *refs):
    *row_pieces, col_out_ref, block_ref, row_dir_ref, even_ref, odd_ref, sems = refs
    per_seg = row_pieces[0].shape[0]
    slots = block_ref.shape[0]

    def prepare():
        even_ref[...] = jnp.zeros_like(even_ref)
        odd_ref[...] = jnp.zeros_like(odd_ref)
        fill_directions(row_pieces, row_dir_ref, facts_ref[ROW], per_seg)

    def run_group(first_slot):
        add_products(
            dot_across,
            facts_ref,
            first_slot,
            block_ref,
            row_dir_ref,
            PLACES,
            [even_ref, odd_ref],
            PLACES + slots,
        )

    each_group(facts_ref, block_hbm, block_ref, sems, prepare, run_group)
    col_out_ref[...] = (even_ref[...] + odd_ref[...]).astype(col_out_ref.dtype)


def forward_kernel(row_count, with_gram, facts_ref, block_hbm, col_dir_ref, *refs):
    refs = list(refs)

    def take(count):
        taken = refs[:count]
        del refs[:count]
        return taken

    row_pieces = take(row_count if with_gram else 0)
    gram_in = take(int(with_gram))
    row_outs = take(row_count)
    gram_out = take(int(with_gram))
    block_ref, even_ref, odd_ref, sems = refs
    per_seg, size, _ = row_outs[0].shape
    slots = block_ref.shape[0]

    def prepare():
        even_ref[...] = jnp.zeros_like(even_ref)
        odd_ref[...] = jnp.zeros_like(odd_ref)

    def run_group(first_slot):
        add_products(
            dot_plain,
            facts_ref,
            first_slot,
            block_ref,
            col_dir_ref,
            PLACES + slots,
            [even_ref, odd_ref],
            PLACES,
        )

    each_group(facts_ref, block_hbm, block_ref, sems, prepare, run_group)
    gram = jnp.zeros((2 * size, 128), jnp.float32)
    for ahead, out in enumerate(row_outs):
        first = lax.rem(facts_ref[ROW] + ahead, row_count) * per_seg
        for part in range(per_seg):
            values = even_ref[first + part] + odd_ref[first + part]
            high = values.astype(out.dtype)
            out[part] = high
            if with_gram:
                low = (values - high.astype(jnp.float32)).astype(out.dtype)
                piece = row_pieces[(row_count - ahead) % row_count]
                gram += dot_across(jnp.concatenate([high, low], axis=0), tall(piece[part]))
    if with_gram:
        gram = gram[:size] + gram[size:]
        gram_out[0][...] = gram_in[0][...] + pltpu.roll(gram, 3 * size, 1)


def over_blocks(kernel, name, facts, blocks, inputs, outputs, scratch):
    slots = blocks.shape[0]
    return pl.pallas_call(
        kernel,
        in_specs=[SCALARS, ANYWHERE] + [IN_VMEM] * len(inputs),
        out_specs=[IN_VMEM] * len(outputs),
        out_shape=outputs,
        scratch_shapes=[pltpu.VMEM(blocks.shape, blocks.dtype)]
        + scratch
        + [pltpu.SemaphoreType.DMA((slots // BATCH,))],
        compiler_params=pltpu.CompilerParams(vmem_limit_bytes=VMEM_LIMIT),
        cost_estimate=pl.CostEstimate(
            flops=2 * slots * 32 * 128 * 128, bytes_accessed=2 * blocks.size, transcendentals=0
        ),
        name=name,
    )(facts, blocks, *inputs)


def backward_product(facts, blocks, row_pieces, col_count):
    per_seg, rows, lanes = row_pieces[0].shape
    col_shape = (col_count * per_seg, rows, lanes)
    (total,) = over_blocks(
        backward_kernel,
        "backward_product",
        facts,
        blocks,
        row_pieces,
        [jax.ShapeDtypeStruct(col_shape, jnp.bfloat16)],
        [
            pltpu.VMEM((len(row_pieces) * per_seg, rows, lanes), jnp.bfloat16),
            pltpu.VMEM(col_shape, jnp.float32),
            pltpu.VMEM(col_shape, jnp.float32),
        ],
    )
    return total


def forward_product(facts, blocks, col_dirs, row_pieces, gram=None):
    piece = row_pieces[0]
    inputs = [col_dirs]
    outputs = [jax.ShapeDtypeStruct(piece.shape, jnp.bfloat16)] * len(row_pieces)
    if gram is not None:
        inputs += [*row_pieces, gram]
        outputs += [jax.ShapeDtypeStruct(gram.shape, jnp.float32)]
    row_shape = (len(row_pieces) * piece.shape[0],) + piece.shape[1:]
    return over_blocks(
        functools.partial(forward_kernel, len(row_pieces), gram is not None),
        "forward_product",
        facts,
        blocks,
        inputs,
        outputs,
        [pltpu.VMEM(row_shape, jnp.float32), pltpu.VMEM(row_shape, jnp.float32)],
    )


def total_of(values):
    total = values[0].astype(jnp.float32)
    for value in values[1:]:
        total = total + value.astype(jnp.float32)
    return total


def leading(ref):
    return [ref.at[index] for index in range(ref.shape[0])]


def start_kernel(*refs):
    *row_refs, col_ref, query_ref, scaling_ref, scaled_ref, copies_ref = refs
    degree = 1.0 + 0.5 * total_of([ref[...] for ref in [*row_refs, *leading(col_ref)]])
    scaling = 1.0 / jnp.sqrt(degree)
    scaling_ref[...] = scaling
    for part in range(scaling.shape[0]):
        scaled = (
            scaling[part : part + 1] * query_ref[:, part * 128 : part * 128 + 128]
        ).astype(jnp.bfloat16)
        scaled_ref[part] = scaled
        for copy in range(copies_ref.shape[0]):
            copies_ref[copy, part] = scaled


def scaled_sum(row_refs, col_ref, scaling_ref, part):
    scaling = scaling_ref[part : part + 1]
    total = total_of([ref[part] for ref in [*row_refs, *leading(col_ref)]])
    return scaling * (0.5 * total)


def middle_kernel(*refs):
    *row_refs, col_ref, scaling_ref, query_ref, first_ref, scaled_ref, copies_ref, gram_ref = refs
    size = query_ref.shape[0]
    pair_gram = jnp.zeros((2 * size, 128), jnp.float32)
    for part in range(scaling_ref.shape[0]):
        first = scaled_sum(row_refs, col_ref, scaling_ref, part)
        first_ref[part] = first
        scaled = (scaling_ref[part : part + 1] * first).astype(jnp.bfloat16)
        scaled_ref[part] = scaled
        for copy in range(copies_ref.shape[0]):
            copies_ref[copy, part] = scaled
        pair = jnp.concatenate(
            [query_ref[:, part * 128 : part * 128 + 128], first], axis=0
        )
        pair_gram += exact_across(pair, tall(pair))
    gram_ref[...] = beside(
        pair_gram[:size], pltpu.roll(window(pair_gram[size:], 1), size, 1)
    )


def tall(flat):
    rest = flat.shape[1] - flat.shape[0]
    return jnp.concatenate([flat, jnp.zeros((rest, flat.shape[1]), flat.dtype)], axis=0)


def flipped(flat):
    return tall(flat).T[: flat.shape[0]]


def times(left, right):
    return exact_plain(left, tall(right))


def beside(left, right):
    return left + pltpu.roll(right, left.shape[0], 1)


def stacked(upper, lower):
    rest = jnp.zeros((upper.shape[1] - 2 * upper.shape[0], upper.shape[1]), upper.dtype)
    return jnp.concatenate([upper, lower, rest], axis=0)


def sandwich(rows, middle):
    return exact_across(exact_plain(rows, middle), tall(rows))


def symmetric(flat):
    return 0.5 * (flat + flipped(flat))


def window(flat, place):
    size = flat.shape[0]
    if place:
        flat = pltpu.roll(flat, flat.shape[1] - place * size, 1)
    lanes = lax.broadcasted_iota(jnp.int32, flat.shape, 1)
    return jnp.where(lanes < size, flat, 0.0)


def solve_many(pairs):
    size = pairs[0][0].shape[0]
    systems = [matrix + pltpu.roll(side, size, 1) for matrix, side in pairs]
    sublanes = lax.broadcasted_iota(jnp.int32, systems[0].shape, 0)
    for pivot in range(0, size, 2):
        updated = []
        for system in systems:
            upper, lower = system[pivot : pivot + 1, :], system[pivot + 1 : pivot + 2, :]
            left, right = system[:, pivot : pivot + 1], system[:, pivot + 1 : pivot + 2]
            inverse = 1.0 / left[pivot : pivot + 1, :]
            upper = upper * inverse
            ratio = left[pivot + 1 : pivot + 2, :]
            across = right[pivot : pivot + 1, :] * inverse
            inverse = 1.0 / (right[pivot + 1 : pivot + 2, :] - ratio * across)
            new_lower = (lower - ratio * upper) * inverse
            new_upper = upper - across * new_lower
            rest = system - left * new_upper - right * new_lower
            rest = jnp.where(sublanes == pivot, new_upper, rest)
            updated.append(jnp.where(sublanes == pivot + 1, new_lower, rest))
        systems = updated
    return [window(system, 1) for system in systems]


def close_kernel(*refs):
    *row_refs, col_ref, gram_ref, scaling_ref, query_ref, first_ref = refs[:-2]
    solution_ref, residual_ref = refs[-2:]
    size = query_ref.shape[0]
    weight = graph_weight
    total = total_of([ref[...] for ref in leading(gram_ref)])
    g00 = symmetric(window(total, 0))
    g01 = window(total, 1)
    g11 = symmetric(window(total, 2))
    g12 = symmetric(window(total, 3))
    eye = (
        lax.broadcasted_iota(jnp.int32, total.shape, 0)
        == lax.broadcasted_iota(jnp.int32, total.shape, 1)
    ).astype(jnp.float32)
    curve = symmetric(g00 - weight * g01)
    steps, inverse = solve_many([(curve, g00), (g00, eye)])
    steps_t = flipped(steps)
    plain_gram = stacked(beside(g00, g01), beside(flipped(g01), g11))
    through_gram = stacked(beside(g01, g11), beside(g11, g12))
    after_first = beside(eye - steps_t, weight * steps_t)
    new_gram = symmetric(sandwich(after_first, plain_gram))
    mixing = times(inverse, new_gram)
    direction = after_first + flipped(mixing)
    curve = symmetric(sandwich(direction, plain_gram - weight * through_gram))
    (steps,) = solve_many([(curve, new_gram)])
    steps_t2 = flipped(steps)
    applied = direction - weight * pltpu.roll(direction, size, 1)
    solution_rows = exact_plain(beside(eye, steps_t2), stacked(steps_t, direction))
    residual_rows = exact_plain(beside(eye, -steps_t2), stacked(after_first, applied))
    rows = jnp.concatenate([solution_rows, residual_rows], axis=0)
    for part in range(first_ref.shape[0]):
        lanes = slice(part * 128, part * 128 + 128)
        basis = jnp.concatenate(
            [
                query_ref[:, lanes],
                first_ref[part],
                scaled_sum(row_refs, col_ref, scaling_ref, part),
                jnp.zeros_like(eye),
            ],
            axis=0,
        )
        values = exact_plain(rows, basis)
        solution_ref[:, lanes] = values[:size]
        residual_ref[:, lanes] = values[size:]


def pass_around(pieces, axis):
    count = len(pieces)
    return [pieces[0]] + [
        lax.ppermute(pieces[ahead], axis, [(at, (at + ahead) % count) for at in range(count)])
        for ahead in range(1, count)
    ]


def exchange(pieces, axis):
    return lax.all_to_all(pieces, axis, 0, 0, tiled=True)


def simple_call(kernel, shapes, name, *operands):
    return pl.pallas_call(
        kernel,
        out_shape=shapes,
        compiler_params=pltpu.CompilerParams(vmem_limit_bytes=VMEM_LIMIT),
        name=name,
    )(*operands)


def sum_kernel(*refs):
    *piece_refs, copies_ref = refs
    total = total_of([ref[...] for ref in piece_refs])
    for copy in range(copies_ref.shape[0]):
        copies_ref[copy] = total


def body(queries, block_spots, live_blocks, neighbor_cols, neighbor_sims):
    row_count = lax.axis_size("row")
    col_count = lax.axis_size("col")
    query_rows, seg_len = queries.shape
    per_seg = seg_len // 128
    spots = block_spots[0, 0]
    col_blocks = col_count * per_seg
    heads = [live_blocks[0, 0], lax.axis_index("row"), lax.axis_index("col"), 0]
    facts = jnp.concatenate(
        [jnp.stack(heads).astype(jnp.int32), spots // col_blocks, spots % col_blocks]
    )
    piece = (per_seg, query_rows, 128)
    wide = jax.ShapeDtypeStruct(piece, jnp.float32)
    narrow = jax.ShapeDtypeStruct(piece, jnp.bfloat16)
    copies = jax.ShapeDtypeStruct((col_count,) + piece, jnp.bfloat16)
    gram_shape = jax.ShapeDtypeStruct((query_rows, 128), jnp.float32)
    gram_copies = jax.ShapeDtypeStruct((col_count, query_rows, 128), jnp.float32)

    blocks, *row_sums, col_sums = build_blocks(
        facts, neighbor_cols[0, 0], neighbor_sims[0, 0], row_count, col_count, per_seg
    )
    col_part = exchange(col_sums.reshape(col_count, per_seg, 128), "col")
    row_parts = pass_around(row_sums, "row")
    scaling, scaled, scaled_copies = simple_call(
        start_kernel,
        [jax.ShapeDtypeStruct((per_seg, 128), jnp.float32), narrow, copies],
        "start",
        *row_parts,
        col_part,
        queries,
    )

    def product(vectors, vector_copies, gram=None):
        col_dirs = exchange(vector_copies, "col").reshape((col_count * per_seg,) + piece[1:])
        row_pieces = pass_around([vectors] * row_count, "row")
        total = backward_product(facts, blocks, row_pieces, col_count)
        col_part = exchange(total.reshape((col_count,) + piece), "col")
        totals = forward_product(facts, blocks, col_dirs, row_pieces, gram)
        row_parts = pass_around(totals[:row_count], "row")
        return row_parts, col_part, totals[row_count:]

    row_parts, col_part, _ = product(scaled, scaled_copies)
    first, scaled, scaled_copies, gram = simple_call(
        middle_kernel,
        [wide, narrow, copies, gram_shape],
        "middle",
        *row_parts,
        col_part,
        scaling,
        queries,
    )
    row_parts, col_part, (gram,) = product(scaled, scaled_copies, gram)
    (grams,) = simple_call(
        sum_kernel, [gram_copies], "gram_sum", *pass_around([gram] * row_count, "row")
    )
    flat = jax.ShapeDtypeStruct(queries.shape, jnp.float32)
    return tuple(
        simple_call(
            close_kernel,
            [flat, flat],
            "close",
            *row_parts,
            col_part,
            exchange(grams, "col"),
            scaling,
            queries,
            first,
        )
    )


def solution(mesh):
    placed = (
        P(None, ("row", "col")),
        P("row", "col", None),
        P("row", "col"),
        P("row", "col", None, None, None),
        P("row", "col", None, None, None),
    )
    return jax.shard_map(
        body,
        mesh=mesh,
        in_specs=placed,
        out_specs=(P(None, ("row", "col")), P(None, ("row", "col"))),
        check_vma=False,
    )
```

```python
import functools

import jax
import jax.numpy as jnp
from jax import lax
from jax.experimental import pallas as pl
from jax.experimental.pallas import tpu as pltpu
from jax.sharding import PartitionSpec as P

graph_weight = 0.95
GROUP = 16
BATCH = 64
GRAM_TERMS = 3
VMEM_LIMIT = 60 * 1024 * 1024


def dot_plain(left, right, **kwargs):
    return lax.dot_general(
        left, right, (((1,), (0,)), ((), ())), preferred_element_type=jnp.float32, **kwargs
    )


def dot_across(left, right, **kwargs):
    return lax.dot_general(
        left, right, (((1,), (1,)), ((), ())), preferred_element_type=jnp.float32, **kwargs
    )


exact_plain = functools.partial(dot_plain, precision=lax.Precision.HIGHEST)
exact_across = functools.partial(dot_across, precision=lax.Precision.HIGHEST)


def place_of(spots_ref, slot, col_blocks):
    spot = spots_ref[0, 0, slot]
    if col_blocks & (col_blocks - 1):
        return lax.div(spot, col_blocks), lax.rem(spot, col_blocks)
    return spot >> (col_blocks.bit_length() - 1), spot & (col_blocks - 1)


def group_count(live_ref, group):
    return (live_ref[0, 0] + group - 1) // group


def group_copy(source, target, sems, index, group):
    window = pl.ds(index * group, group)
    return pltpu.make_async_copy(source.at[window], target.at[window], sems.at[index])


def build_kernel(row_count, spots_ref, live_ref, index_hbm, value_hbm, block_hbm, *refs):
    row_outs = refs[:row_count]
    (
        col_out_ref,
        index_ref,
        value_ref,
        block_ref,
        row_ref,
        col_ref,
        index_sems,
        value_sems,
        block_sems,
    ) = refs[row_count:]
    per_seg = row_outs[0].shape[0]
    col_blocks = col_out_ref.shape[0]
    groups = group_count(live_ref, BATCH) * (BATCH // GROUP)

    def start_copies(index, _):
        group_copy(index_hbm, index_ref, index_sems, index, GROUP).start()
        group_copy(value_hbm, value_ref, value_sems, index, GROUP).start()
        return 0

    lax.fori_loop(0, groups, start_copies, 0)
    row_ref[...] = jnp.zeros_like(row_ref)
    col_ref[...] = jnp.zeros_like(col_ref)
    rows_16 = lax.broadcasted_iota(jnp.int32, (16, 128), 0)
    ones = jnp.ones((8, 128), jnp.bfloat16)
    zero = jnp.zeros((16, 128), jnp.bfloat16)

    def build_group(index, _):
        group_copy(index_hbm, index_ref, index_sems, index, GROUP).wait()
        group_copy(value_hbm, value_ref, value_sems, index, GROUP).wait()
        targets = [(rows_16 + 16 * part).astype(jnp.int16) for part in range(8)]
        row_sums = []
        col_sums = []
        for inside in range(GROUP):
            slot = index * GROUP + inside
            active = (slot < live_ref[0, 0]).astype(jnp.float32)
            index_i32 = index_ref[slot]
            value_f32 = value_ref[slot].astype(jnp.float32) * active
            sums = [zero] * 8
            for entry in range(16):
                index_row = jnp.broadcast_to(index_i32[entry : entry + 1], (16, 128)).astype(
                    jnp.int16
                )
                value_row = jnp.broadcast_to(value_f32[entry : entry + 1], (16, 128)).astype(
                    jnp.bfloat16
                )
                for part in range(8):
                    sums[part] = sums[part] + jnp.where(
                        index_row == targets[part], value_row, zero
                    )
            block = jnp.concatenate(sums, axis=0)
            block_ref[slot] = block
            row_sums.append(dot_plain(ones, block))
            col_sums.append(dot_across(ones, block))
        group_copy(block_ref, block_hbm, block_sems, index, GROUP).start()
        for inside in range(GROUP):
            slot = index * GROUP + inside
            row_block, col_block = place_of(spots_ref, slot, col_blocks)
            row_ref[row_block] += row_sums[inside]
            col_ref[col_block] += col_sums[inside]
        return 0

    lax.fori_loop(0, groups, build_group, 0)
    for ahead, out in enumerate(row_outs):
        first = lax.rem(lax.axis_index("row") + ahead, row_count) * per_seg
        for part in range(per_seg):
            out[part : part + 1] = row_ref[first + part][:1]
    for col_block in range(col_blocks):
        col_out_ref[col_block : col_block + 1] = col_ref[col_block][:1]

    def finish_copies(index, _):
        group_copy(block_ref, block_hbm, block_sems, index, GROUP).wait()
        return 0

    lax.fori_loop(0, groups, finish_copies, 0)


SCALARS = pl.BlockSpec(memory_space=pltpu.SMEM)
ANYWHERE = pl.BlockSpec(memory_space=pl.ANY)
IN_VMEM = pl.BlockSpec(memory_space=pltpu.VMEM)


def build_blocks(spots, live, index_table, value_table, row_count, col_count, per_seg):
    slots = index_table.shape[0]
    groups = slots // GROUP
    sum_shapes = [(per_seg, 128)] * row_count + [(col_count * per_seg, 128)]
    return pl.pallas_call(
        functools.partial(build_kernel, row_count),
        in_specs=[SCALARS, SCALARS, ANYWHERE, ANYWHERE],
        out_specs=[ANYWHERE] + [IN_VMEM] * len(sum_shapes),
        out_shape=[jax.ShapeDtypeStruct((slots, 128, 128), jnp.bfloat16)]
        + [jax.ShapeDtypeStruct(shape, jnp.float32) for shape in sum_shapes],
        scratch_shapes=[
            pltpu.VMEM(index_table.shape, index_table.dtype),
            pltpu.VMEM(value_table.shape, value_table.dtype),
            pltpu.VMEM((slots, 128, 128), jnp.bfloat16),
            pltpu.VMEM((row_count * per_seg, 8, 128), jnp.float32),
            pltpu.VMEM((col_count * per_seg, 8, 128), jnp.float32),
            pltpu.SemaphoreType.DMA((groups,)),
            pltpu.SemaphoreType.DMA((groups,)),
            pltpu.SemaphoreType.DMA((groups,)),
        ],
        compiler_params=pltpu.CompilerParams(vmem_limit_bytes=VMEM_LIMIT),
        name="build_blocks",
    )(spots, live, index_table, value_table)


def each_group(live_ref, block_hbm, block_ref, sems, prepare, run_group):
    groups = group_count(live_ref, BATCH)

    def start_copy(index, _):
        group_copy(block_hbm, block_ref, sems, index, BATCH).start()
        return 0

    lax.fori_loop(0, groups, start_copy, 0)
    prepare()

    def one_group(index, _):
        group_copy(block_hbm, block_ref, sems, index, BATCH).wait()
        run_group(index * BATCH)
        return 0

    lax.fori_loop(0, groups, one_group, 0)


def add_products(dot, places, first_slot, block_ref, dir_ref, total_refs):
    sums = []
    for inside in range(BATCH):
        slot = first_slot + inside
        sums.append(dot(dir_ref[places(slot)[0]], block_ref[slot]))
    for inside in range(BATCH):
        total_ref = total_refs[inside % len(total_refs)]
        total_ref[places(first_slot + inside)[1]] += sums[inside]


def fill_directions(pieces, dir_ref, mine, per_seg):
    for behind, piece in enumerate(pieces):
        first = lax.rem(mine + (len(pieces) - behind), len(pieces)) * per_seg
        for part in range(per_seg):
            dir_ref[first + part] = piece[part]


def backward_kernel(spots_ref, live_ref, block_hbm, *refs):
    *row_pieces, col_out_ref, block_ref, row_dir_ref, even_ref, odd_ref, sems = refs
    per_seg = row_pieces[0].shape[0]
    col_blocks = even_ref.shape[0]

    def prepare():
        even_ref[...] = jnp.zeros_like(even_ref)
        odd_ref[...] = jnp.zeros_like(odd_ref)
        fill_directions(row_pieces, row_dir_ref, lax.axis_index("row"), per_seg)

    def run_group(first_slot):
        add_products(
            dot_across,
            lambda slot: place_of(spots_ref, slot, col_blocks),
            first_slot,
            block_ref,
            row_dir_ref,
            [even_ref, odd_ref],
        )

    each_group(live_ref, block_hbm, block_ref, sems, prepare, run_group)
    col_out_ref[...] = (even_ref[...] + odd_ref[...]).astype(col_out_ref.dtype)


def forward_kernel(row_count, with_gram, spots_ref, live_ref, block_hbm, col_dir_ref, *refs):
    refs = list(refs)

    def take(count):
        taken = refs[:count]
        del refs[:count]
        return taken

    row_pieces = take(row_count if with_gram else 0)
    gram_in = take(int(with_gram))
    row_outs = take(row_count)
    block_ref, even_ref, odd_ref, sems = refs
    _, size, _ = row_outs[0].shape
    per_seg = even_ref.shape[0] // row_count
    col_blocks = col_dir_ref.shape[0]

    def prepare():
        even_ref[...] = jnp.zeros_like(even_ref)
        odd_ref[...] = jnp.zeros_like(odd_ref)

    def run_group(first_slot):
        add_products(
            dot_plain,
            lambda slot: place_of(spots_ref, slot, col_blocks)[::-1],
            first_slot,
            block_ref,
            col_dir_ref,
            [even_ref, odd_ref],
        )

    each_group(live_ref, block_hbm, block_ref, sems, prepare, run_group)
    gram = jnp.zeros((2 * size, 128), jnp.float32)
    for ahead, out in enumerate(row_outs):
        first = lax.rem(lax.axis_index("row") + ahead, row_count) * per_seg
        for part in range(per_seg):
            values = even_ref[first + part] + odd_ref[first + part]
            high = values.astype(out.dtype)
            out[part] = high
            if with_gram:
                low = (values - high.astype(jnp.float32)).astype(out.dtype)
                piece = row_pieces[(row_count - ahead) % row_count]
                gram += dot_across(jnp.concatenate([high, low], axis=0), tall(piece[part]))
    if with_gram:
        gram = gram_in[0][...] + pltpu.roll(gram[:size] + gram[size:], 3 * size, 1)
        for term in range(GRAM_TERMS):
            rounded = gram.astype(jnp.bfloat16)
            gram = gram - rounded.astype(jnp.float32)
            for out in row_outs:
                out[per_seg + term] = rounded


def over_blocks(kernel, name, places, blocks, inputs, outputs, scratch):
    slots = blocks.shape[0]
    return pl.pallas_call(
        kernel,
        in_specs=[SCALARS, SCALARS, ANYWHERE] + [IN_VMEM] * len(inputs),
        out_specs=[IN_VMEM] * len(outputs),
        out_shape=outputs,
        scratch_shapes=[pltpu.VMEM(blocks.shape, blocks.dtype)]
        + scratch
        + [pltpu.SemaphoreType.DMA((slots // BATCH,))],
        compiler_params=pltpu.CompilerParams(vmem_limit_bytes=VMEM_LIMIT),
        cost_estimate=pl.CostEstimate(
            flops=2 * slots * 32 * 128 * 128, bytes_accessed=2 * blocks.size, transcendentals=0
        ),
        name=name,
    )(*places, blocks, *inputs)


def backward_product(places, blocks, row_pieces, col_count):
    per_seg, rows, lanes = row_pieces[0].shape
    col_shape = (col_count * per_seg, rows, lanes)
    (total,) = over_blocks(
        backward_kernel,
        "backward_product",
        places,
        blocks,
        row_pieces,
        [jax.ShapeDtypeStruct(col_shape, jnp.bfloat16)],
        [
            pltpu.VMEM((len(row_pieces) * per_seg, rows, lanes), jnp.bfloat16),
            pltpu.VMEM(col_shape, jnp.float32),
            pltpu.VMEM(col_shape, jnp.float32),
        ],
    )
    return total


def forward_product(places, blocks, col_dirs, row_pieces, gram=None):
    piece = row_pieces[0]
    inputs = [col_dirs]
    sent = piece.shape[0]
    if gram is not None:
        inputs += [*row_pieces, gram]
        sent += GRAM_TERMS
    outputs = [jax.ShapeDtypeStruct((sent,) + piece.shape[1:], jnp.bfloat16)] * len(row_pieces)
    row_shape = (len(row_pieces) * piece.shape[0],) + piece.shape[1:]
    return over_blocks(
        functools.partial(forward_kernel, len(row_pieces), gram is not None),
        "forward_product",
        places,
        blocks,
        inputs,
        outputs,
        [pltpu.VMEM(row_shape, jnp.float32), pltpu.VMEM(row_shape, jnp.float32)],
    )


def total_of(values):
    total = values[0].astype(jnp.float32)
    for value in values[1:]:
        total = total + value.astype(jnp.float32)
    return total


def leading(ref):
    return [ref.at[index] for index in range(ref.shape[0])]


def start_kernel(*refs):
    *row_refs, col_ref, query_ref, scaling_ref, scaled_ref, copies_ref = refs
    degree = 1.0 + 0.5 * total_of([ref[...] for ref in [*row_refs, *leading(col_ref)]])
    scaling = 1.0 / jnp.sqrt(degree)
    scaling_ref[...] = scaling
    for part in range(scaling.shape[0]):
        scaled = (
            scaling[part : part + 1] * query_ref[:, part * 128 : part * 128 + 128]
        ).astype(jnp.bfloat16)
        scaled_ref[part] = scaled
        for copy in range(copies_ref.shape[0]):
            copies_ref[copy, part] = scaled


def scaled_sum(row_refs, col_ref, scaling_ref, part):
    scaling = scaling_ref[part : part + 1]
    total = total_of([ref[part] for ref in [*row_refs, *leading(col_ref)]])
    return scaling * (0.5 * total)


def middle_kernel(*refs):
    *row_refs, col_ref, scaling_ref, query_ref, first_ref, scaled_ref, copies_ref, gram_ref = refs
    size = query_ref.shape[0]
    pair_gram = jnp.zeros((2 * size, 128), jnp.float32)
    for part in range(scaling_ref.shape[0]):
        first = scaled_sum(row_refs, col_ref, scaling_ref, part)
        first_ref[part] = first
        scaled = (scaling_ref[part : part + 1] * first).astype(jnp.bfloat16)
        scaled_ref[part] = scaled
        for copy in range(copies_ref.shape[0]):
            copies_ref[copy, part] = scaled
        pair = jnp.concatenate(
            [query_ref[:, part * 128 : part * 128 + 128], first], axis=0
        )
        pair_gram += exact_across(pair, tall(pair))
    gram_ref[...] = beside(
        pair_gram[:size], pltpu.roll(window(pair_gram[size:], 1), size, 1)
    )


def tall(flat):
    rest = flat.shape[1] - flat.shape[0]
    return jnp.concatenate([flat, jnp.zeros((rest, flat.shape[1]), flat.dtype)], axis=0)


def flipped(flat):
    return tall(flat).T[: flat.shape[0]]


def times(left, right):
    return exact_plain(left, tall(right))


def beside(left, right):
    return left + pltpu.roll(right, left.shape[0], 1)


def stacked(upper, lower):
    rest = jnp.zeros((upper.shape[1] - 2 * upper.shape[0], upper.shape[1]), upper.dtype)
    return jnp.concatenate([upper, lower, rest], axis=0)


def sandwich(rows, middle):
    return exact_across(exact_plain(rows, middle), tall(rows))


def symmetric(flat):
    return 0.5 * (flat + flipped(flat))


def window(flat, place):
    size = flat.shape[0]
    if place:
        flat = pltpu.roll(flat, flat.shape[1] - place * size, 1)
    lanes = lax.broadcasted_iota(jnp.int32, flat.shape, 1)
    return jnp.where(lanes < size, flat, 0.0)


def solve_many(pairs):
    size = pairs[0][0].shape[0]
    systems = [matrix + pltpu.roll(side, size, 1) for matrix, side in pairs]
    sublanes = lax.broadcasted_iota(jnp.int32, systems[0].shape, 0)
    for pivot in range(size):
        updated = []
        for system in systems:
            column = system[:, pivot : pivot + 1]
            row = system[pivot : pivot + 1, :] / column[pivot : pivot + 1, :]
            updated.append(jnp.where(sublanes == pivot, row, system - column * row))
        systems = updated
    return [window(system, 1) for system in systems]


def close_kernel(*refs):
    *row_refs, col_ref, gram_ref, scaling_ref, query_ref, first_ref = refs[:-2]
    solution_ref, residual_ref = refs[-2:]
    size = query_ref.shape[0]
    weight = graph_weight
    total = total_of([ref[...] for ref in leading(gram_ref)])
    g00 = symmetric(window(total, 0))
    g01 = window(total, 1)
    g11 = symmetric(window(total, 2))
    g12 = symmetric(window(total, 3))
    eye = (
        lax.broadcasted_iota(jnp.int32, total.shape, 0)
        == lax.broadcasted_iota(jnp.int32, total.shape, 1)
    ).astype(jnp.float32)
    curve = symmetric(g00 - weight * g01)
    steps, inverse = solve_many([(curve, g00), (g00, eye)])
    steps_t = flipped(steps)
    plain_gram = stacked(beside(g00, g01), beside(flipped(g01), g11))
    through_gram = stacked(beside(g01, g11), beside(g11, g12))
    after_first = beside(eye - steps_t, weight * steps_t)
    new_gram = symmetric(sandwich(after_first, plain_gram))
    mixing = times(inverse, new_gram)
    direction = after_first + flipped(mixing)
    curve = symmetric(sandwich(direction, plain_gram - weight * through_gram))
    (steps,) = solve_many([(curve, new_gram)])
    steps_t2 = flipped(steps)
    applied = direction - weight * pltpu.roll(direction, size, 1)
    solution_rows = exact_plain(beside(eye, steps_t2), stacked(steps_t, direction))
    residual_rows = exact_plain(beside(eye, -steps_t2), stacked(after_first, applied))
    rows = jnp.concatenate([solution_rows, residual_rows], axis=0)
    for part in range(first_ref.shape[0]):
        lanes = slice(part * 128, part * 128 + 128)
        basis = jnp.concatenate(
            [
                query_ref[:, lanes],
                first_ref[part],
                scaled_sum(row_refs, col_ref, scaling_ref, part),
                jnp.zeros_like(eye),
            ],
            axis=0,
        )
        values = exact_plain(rows, basis)
        solution_ref[:, lanes] = values[:size]
        residual_ref[:, lanes] = values[size:]


def pass_around(pieces, axis):
    count = len(pieces)
    return [pieces[0]] + [
        lax.ppermute(pieces[ahead], axis, [(at, (at + ahead) % count) for at in range(count)])
        for ahead in range(1, count)
    ]


def exchange(pieces, axis):
    return lax.all_to_all(pieces, axis, 0, 0, tiled=True)


def simple_call(kernel, shapes, name, *operands):
    return pl.pallas_call(
        kernel,
        out_shape=shapes,
        compiler_params=pltpu.CompilerParams(vmem_limit_bytes=VMEM_LIMIT),
        name=name,
    )(*operands)


def sum_kernel(*refs):
    *piece_refs, copies_ref = refs
    first = piece_refs[0].shape[0] - GRAM_TERMS
    total = total_of(
        [ref[first + term] for term in range(GRAM_TERMS) for ref in piece_refs]
    )
    for copy in range(copies_ref.shape[0]):
        copies_ref[copy] = total


def body(queries, block_spots, live_blocks, neighbor_cols, neighbor_sims):
    row_count = lax.axis_size("row")
    col_count = lax.axis_size("col")
    query_rows, seg_len = queries.shape
    per_seg = seg_len // 128
    places = (block_spots, live_blocks)
    piece = (per_seg, query_rows, 128)
    wide = jax.ShapeDtypeStruct(piece, jnp.float32)
    narrow = jax.ShapeDtypeStruct(piece, jnp.bfloat16)
    copies = jax.ShapeDtypeStruct((col_count,) + piece, jnp.bfloat16)
    gram_shape = jax.ShapeDtypeStruct((query_rows, 128), jnp.float32)
    gram_copies = jax.ShapeDtypeStruct((col_count, query_rows, 128), jnp.float32)

    blocks, *row_sums, col_sums = build_blocks(
        *places, neighbor_cols[0, 0], neighbor_sims[0, 0], row_count, col_count, per_seg
    )
    col_part = exchange(col_sums.reshape(col_count, per_seg, 128), "col")
    row_parts = pass_around(row_sums, "row")
    scaling, scaled, scaled_copies = simple_call(
        start_kernel,
        [jax.ShapeDtypeStruct((per_seg, 128), jnp.float32), narrow, copies],
        "start",
        *row_parts,
        col_part,
        queries,
    )

    def product(vectors, vector_copies, gram=None):
        col_dirs = exchange(vector_copies, "col").reshape((col_count * per_seg,) + piece[1:])
        row_pieces = pass_around([vectors] * row_count, "row")
        total = backward_product(places, blocks, row_pieces, col_count)
        col_part = exchange(total.reshape((col_count,) + piece), "col")
        totals = forward_product(places, blocks, col_dirs, row_pieces, gram)
        return pass_around(totals, "row"), col_part

    row_parts, col_part = product(scaled, scaled_copies)
    first, scaled, scaled_copies, gram = simple_call(
        middle_kernel,
        [wide, narrow, copies, gram_shape],
        "middle",
        *row_parts,
        col_part,
        scaling,
        queries,
    )
    row_parts, col_part = product(scaled, scaled_copies, gram)
    (grams,) = simple_call(sum_kernel, [gram_copies], "gram_sum", *row_parts)
    flat = jax.ShapeDtypeStruct(queries.shape, jnp.float32)
    return tuple(
        simple_call(
            close_kernel,
            [flat, flat],
            "close",
            *row_parts,
            col_part,
            exchange(grams, "col"),
            scaling,
            queries,
            first,
        )
    )


def solution(mesh):
    placed = (
        P(None, ("row", "col")),
        P("row", "col", None),
        P("row", "col"),
        P("row", "col", None, None, None),
        P("row", "col", None, None, None),
    )
    return jax.shard_map(
        body,
        mesh=mesh,
        in_specs=placed,
        out_specs=(P(None, ("row", "col")), P(None, ("row", "col"))),
        check_vma=False,
    )
```

```python
import functools

import jax
import jax.numpy as jnp
from jax import lax
from jax.experimental import pallas as pl
from jax.experimental.pallas import tpu as pltpu
from jax.sharding import PartitionSpec as P

graph_weight = 0.95
GROUP = 16
BATCH = 64
GRAM_TERMS = 3
VMEM_LIMIT = 24 * 1024 * 1024


def dot_plain(left, right, **kwargs):
    return lax.dot_general(
        left, right, (((1,), (0,)), ((), ())), preferred_element_type=jnp.float32, **kwargs
    )


def dot_across(left, right, **kwargs):
    return lax.dot_general(
        left, right, (((1,), (1,)), ((), ())), preferred_element_type=jnp.float32, **kwargs
    )


exact_plain = functools.partial(dot_plain, precision=lax.Precision.HIGHEST)
exact_across = functools.partial(dot_across, precision=lax.Precision.HIGHEST)


def place_of(spots_ref, slot, col_blocks):
    spot = spots_ref[0, 0, slot]
    if col_blocks & (col_blocks - 1):
        return lax.div(spot, col_blocks), lax.rem(spot, col_blocks)
    return spot >> (col_blocks.bit_length() - 1), spot & (col_blocks - 1)


def group_count(live_ref, group):
    return (live_ref[0, 0] + group - 1) // group


def group_copy(source, target, sems, index, group):
    window = pl.ds(index * group, group)
    return pltpu.make_async_copy(source.at[window], target.at[window], sems.at[index])


def build_kernel(row_count, spots_ref, live_ref, index_hbm, value_hbm, block_ref, *refs):
    row_outs = refs[:row_count]
    (
        col_out_ref,
        index_ref,
        value_ref,
        wide_ref,
        row_ref,
        col_ref,
        index_sems,
        value_sems,
    ) = refs[row_count:]
    per_seg = row_outs[0].shape[0]
    col_blocks = col_out_ref.shape[0]
    groups = group_count(live_ref, BATCH) * (BATCH // GROUP)

    def start_copies(index, _):
        group_copy(index_hbm, index_ref, index_sems, index, GROUP).start()
        group_copy(value_hbm, value_ref, value_sems, index, GROUP).start()
        return 0

    lax.fori_loop(0, groups, start_copies, 0)
    row_ref[...] = jnp.zeros_like(row_ref)
    col_ref[...] = jnp.zeros_like(col_ref)
    rows_16 = lax.broadcasted_iota(jnp.int32, (16, 128), 0)
    ones = jnp.ones((8, 128), jnp.bfloat16)
    zero = jnp.zeros((16, 128), jnp.bfloat16)

    def build_group(index, _):
        group_copy(index_hbm, index_ref, index_sems, index, GROUP).wait()
        group_copy(value_hbm, value_ref, value_sems, index, GROUP).wait()
        targets = [(rows_16 + 16 * part).astype(jnp.int16) for part in range(8)]
        row_sums = []
        for inside in range(GROUP):
            slot = index * GROUP + inside
            active = (slot < live_ref[0, 0]).astype(jnp.float32)
            value_f32 = value_ref[slot].astype(jnp.float32) * active
            wide_ref[inside] = value_f32
            row_sums.append(value_f32[:8] + value_f32[8:])
        col_sums = []
        for inside in range(GROUP):
            slot = index * GROUP + inside
            sums = [zero] * 8
            for entry in range(16):
                index_row = jnp.broadcast_to(
                    index_ref[slot, entry : entry + 1, :], (16, 128)
                ).astype(jnp.int16)
                value_row = jnp.broadcast_to(
                    wide_ref[inside, entry : entry + 1, :], (16, 128)
                ).astype(jnp.bfloat16)
                for part in range(8):
                    sums[part] = sums[part] + jnp.where(
                        index_row == targets[part], value_row, zero
                    )
            block = jnp.concatenate(sums, axis=0)
            block_ref[slot] = block
            col_sums.append(dot_across(ones, block))
        for inside in range(GROUP):
            row_block, col_block = place_of(spots_ref, index * GROUP + inside, col_blocks)
            row_ref[row_block] += row_sums[inside]
            col_ref[col_block] += col_sums[inside]
        return 0

    lax.fori_loop(0, groups, build_group, 0)
    for ahead, out in enumerate(row_outs):
        first = lax.rem(lax.axis_index("row") + ahead, row_count) * per_seg
        for part in range(per_seg):
            out[part : part + 1] = jnp.sum(row_ref[first + part], axis=0, keepdims=True)
    for col_block in range(col_blocks):
        col_out_ref[col_block : col_block + 1] = col_ref[col_block][:1]


SCALARS = pl.BlockSpec(memory_space=pltpu.SMEM)
IN_HBM = pl.BlockSpec(memory_space=pltpu.HBM)
IN_VMEM = pl.BlockSpec(memory_space=pltpu.VMEM)


def build_blocks(spots, live, index_table, value_table, row_count, col_count, per_seg):
    slots = index_table.shape[0]
    groups = slots // GROUP
    sum_shapes = [(per_seg, 128)] * row_count + [(col_count * per_seg, 128)]
    return pl.pallas_call(
        functools.partial(build_kernel, row_count),
        in_specs=[SCALARS, SCALARS, IN_HBM, IN_HBM],
        out_specs=[IN_VMEM] * (1 + len(sum_shapes)),
        out_shape=[jax.ShapeDtypeStruct((slots, 128, 128), jnp.bfloat16)]
        + [jax.ShapeDtypeStruct(shape, jnp.float32) for shape in sum_shapes],
        scratch_shapes=[
            pltpu.VMEM(index_table.shape, index_table.dtype),
            pltpu.VMEM(value_table.shape, value_table.dtype),
            pltpu.VMEM((GROUP, 16, 128), jnp.float32),
            pltpu.VMEM((row_count * per_seg, 8, 128), jnp.float32),
            pltpu.VMEM((col_count * per_seg, 8, 128), jnp.float32),
            pltpu.SemaphoreType.DMA((groups,)),
            pltpu.SemaphoreType.DMA((groups,)),
        ],
        compiler_params=pltpu.CompilerParams(vmem_limit_bytes=VMEM_LIMIT),
        name="build_blocks",
    )(spots, live, index_table, value_table)


def each_group(live_ref, run_group):
    def one_group(index, _):
        run_group(index * BATCH)
        return 0

    lax.fori_loop(0, group_count(live_ref, BATCH), one_group, 0)


def add_products(dot, places, first_slot, block_ref, dir_ref, total_refs):
    sums = []
    for inside in range(BATCH):
        slot = first_slot + inside
        sums.append(dot(dir_ref[places(slot)[0]], block_ref[slot]))
    for inside in range(BATCH):
        total_ref = total_refs[inside % len(total_refs)]
        total_ref[places(first_slot + inside)[1]] += sums[inside]


def fill_directions(pieces, dir_ref, mine, per_seg):
    for behind, piece in enumerate(pieces):
        first = lax.rem(mine + (len(pieces) - behind), len(pieces)) * per_seg
        for part in range(per_seg):
            dir_ref[first + part] = piece[part]


def add_gram(total, values, high, directions):
    low = (values - high.astype(jnp.float32)).astype(high.dtype)
    return total + dot_across(jnp.concatenate([high, low], axis=0), tall(directions))


def backward_kernel(row_count, spots_ref, live_ref, block_ref, *refs):
    row_pieces = refs[:row_count]
    gram_refs = refs[row_count:-4]
    col_out_ref, row_dir_ref, even_ref, odd_ref = refs[-4:]
    per_seg, size, _ = row_pieces[0].shape
    col_blocks = even_ref.shape[0]
    col_count, sent = col_out_ref.shape[:2]
    even_ref[...] = jnp.zeros_like(even_ref)
    odd_ref[...] = jnp.zeros_like(odd_ref)
    fill_directions(row_pieces, row_dir_ref, lax.axis_index("row"), per_seg)

    def run_group(first_slot):
        add_products(
            dot_across,
            lambda slot: place_of(spots_ref, slot, col_blocks),
            first_slot,
            block_ref,
            row_dir_ref,
            [even_ref, odd_ref],
        )

    each_group(live_ref, run_group)

    def send_segment(segment, gram):
        for part in range(per_seg):
            col_block = segment * per_seg + part
            values = even_ref[col_block] + odd_ref[col_block]
            high = values.astype(col_out_ref.dtype)
            col_out_ref[segment, part] = high
            if gram_refs:
                gram = add_gram(gram, values, high, gram_refs[0][col_block])
        return gram

    gram = lax.fori_loop(0, col_count, send_segment, jnp.zeros((2 * size, 128), jnp.float32))
    if gram_refs:
        gram = gram_refs[1][...] + pltpu.roll(gram[:size] + gram[size:], 3 * size, 1)
        for term in range(GRAM_TERMS):
            rounded = gram.astype(col_out_ref.dtype)
            gram = gram - rounded.astype(jnp.float32)
            for segment in range(col_count):
                col_out_ref[segment, per_seg + term] = rounded


def forward_kernel(spots_ref, live_ref, block_ref, col_dir_ref, *refs):
    *row_outs, even_ref, odd_ref = refs
    per_seg = row_outs[0].shape[0]
    col_blocks = col_dir_ref.shape[0]
    even_ref[...] = jnp.zeros_like(even_ref)
    odd_ref[...] = jnp.zeros_like(odd_ref)

    def run_group(first_slot):
        add_products(
            dot_plain,
            lambda slot: place_of(spots_ref, slot, col_blocks)[::-1],
            first_slot,
            block_ref,
            col_dir_ref,
            [even_ref, odd_ref],
        )

    each_group(live_ref, run_group)
    for ahead, out in enumerate(row_outs):
        first = lax.rem(lax.axis_index("row") + ahead, len(row_outs)) * per_seg
        for part in range(per_seg):
            values = even_ref[first + part] + odd_ref[first + part]
            out[part] = values.astype(out.dtype)


def over_blocks(kernel, name, places, blocks, inputs, outputs, scratch):
    slots = blocks.shape[0]
    return pl.pallas_call(
        kernel,
        in_specs=[SCALARS, SCALARS] + [IN_VMEM] * (1 + len(inputs)),
        out_specs=[IN_VMEM] * len(outputs),
        out_shape=outputs,
        scratch_shapes=scratch,
        compiler_params=pltpu.CompilerParams(vmem_limit_bytes=VMEM_LIMIT),
        cost_estimate=pl.CostEstimate(
            flops=2 * slots * 32 * 128 * 128, bytes_accessed=2 * blocks.size, transcendentals=0
        ),
        name=name,
    )(*places, blocks, *inputs)


def backward_product(places, blocks, row_pieces, col_count, grams=()):
    per_seg, rows, lanes = row_pieces[0].shape
    sent = per_seg + (GRAM_TERMS if grams else 0)
    col_shape = (col_count * per_seg, rows, lanes)
    (total,) = over_blocks(
        functools.partial(backward_kernel, len(row_pieces)),
        "backward_product",
        places,
        blocks,
        [*row_pieces, *grams],
        [jax.ShapeDtypeStruct((col_count, sent, rows, lanes), jnp.bfloat16)],
        [
            pltpu.VMEM((len(row_pieces) * per_seg, rows, lanes), jnp.bfloat16),
            pltpu.VMEM(col_shape, jnp.float32),
            pltpu.VMEM(col_shape, jnp.float32),
        ],
    )
    return total


def forward_product(places, blocks, col_dirs, row_count, piece):
    row_shape = (row_count * piece[0],) + piece[1:]
    return over_blocks(
        forward_kernel,
        "forward_product",
        places,
        blocks,
        [col_dirs],
        [jax.ShapeDtypeStruct(piece, jnp.bfloat16)] * row_count,
        [pltpu.VMEM(row_shape, jnp.float32), pltpu.VMEM(row_shape, jnp.float32)],
    )


def total_of(values):
    total = values[0].astype(jnp.float32)
    for value in values[1:]:
        total = total + value.astype(jnp.float32)
    return total


def leading(ref):
    return [ref.at[index] for index in range(ref.shape[0])]


def start_kernel(*refs):
    *row_refs, col_ref, query_ref, scaling_ref, scaled_ref, copies_ref = refs
    degree = 1.0 + 0.5 * total_of([ref[...] for ref in [*row_refs, *leading(col_ref)]])
    scaling = 1.0 / jnp.sqrt(degree)
    scaling_ref[...] = scaling
    for part in range(scaling.shape[0]):
        scaled = (
            scaling[part : part + 1] * query_ref[:, part * 128 : part * 128 + 128]
        ).astype(jnp.bfloat16)
        scaled_ref[part] = scaled
        for copy in range(copies_ref.shape[0]):
            copies_ref[copy, part] = scaled


def scaled_sum(row_refs, col_ref, scaling_ref, part):
    scaling = scaling_ref[part : part + 1]
    total = total_of([ref[part] for ref in [*row_refs, *leading(col_ref)]])
    return scaling * (0.5 * total)


def middle_kernel(*refs):
    *row_refs, col_ref, scaling_ref, query_ref, first_ref, scaled_ref, copies_ref, gram_ref = refs
    size = query_ref.shape[0]
    pair_gram = jnp.zeros((2 * size, 128), jnp.float32)
    for part in range(scaling_ref.shape[0]):
        first = scaled_sum(row_refs, col_ref, scaling_ref, part)
        first_ref[part] = first
        scaled = (scaling_ref[part : part + 1] * first).astype(jnp.bfloat16)
        scaled_ref[part] = scaled
        for copy in range(copies_ref.shape[0]):
            copies_ref[copy, part] = scaled
        pair = jnp.concatenate(
            [query_ref[:, part * 128 : part * 128 + 128], first], axis=0
        )
        pair_gram += exact_across(pair, tall(pair))
    gram_ref[...] = beside(
        pair_gram[:size], pltpu.roll(window(pair_gram[size:], 1), size, 1)
    )


def tall(flat):
    rest = flat.shape[1] - flat.shape[0]
    return jnp.concatenate([flat, jnp.zeros((rest, flat.shape[1]), flat.dtype)], axis=0)


def flipped(flat):
    return tall(flat).T[: flat.shape[0]]


def times(left, right):
    return exact_plain(left, tall(right))


def beside(left, right):
    return left + pltpu.roll(right, left.shape[0], 1)


def stacked(upper, lower):
    rest = jnp.zeros((upper.shape[1] - 2 * upper.shape[0], upper.shape[1]), upper.dtype)
    return jnp.concatenate([upper, lower, rest], axis=0)


def sandwich(rows, middle):
    return exact_across(exact_plain(rows, middle), tall(rows))


def symmetric(flat):
    return 0.5 * (flat + flipped(flat))


def window(flat, place):
    size = flat.shape[0]
    if place:
        flat = pltpu.roll(flat, flat.shape[1] - place * size, 1)
    lanes = lax.broadcasted_iota(jnp.int32, flat.shape, 1)
    return jnp.where(lanes < size, flat, 0.0)


def solve_many(pairs):
    size = pairs[0][0].shape[0]
    systems = [matrix + pltpu.roll(side, size, 1) for matrix, side in pairs]
    sublanes = lax.broadcasted_iota(jnp.int32, systems[0].shape, 0)
    for pivot in range(size):
        updated = []
        for system in systems:
            column = system[:, pivot : pivot + 1]
            row = system[pivot : pivot + 1, :] / column[pivot : pivot + 1, :]
            updated.append(jnp.where(sublanes == pivot, row, system - column * row))
        systems = updated
    return [window(system, 1) for system in systems]


def close_kernel(*refs):
    row_count = (len(refs) - 6) // 2
    row_refs = refs[:row_count]
    gram_refs = refs[row_count : 2 * row_count]
    col_ref, scaling_ref, query_ref, first_ref, solution_ref, residual_ref = refs[-6:]
    size = query_ref.shape[0]
    weight = graph_weight
    total = total_of([ref[...] for ref in gram_refs])
    g00 = symmetric(window(total, 0))
    g01 = window(total, 1)
    g11 = symmetric(window(total, 2))
    g12 = symmetric(window(total, 3))
    eye = (
        lax.broadcasted_iota(jnp.int32, total.shape, 0)
        == lax.broadcasted_iota(jnp.int32, total.shape, 1)
    ).astype(jnp.float32)
    curve = symmetric(g00 - weight * g01)
    steps, inverse = solve_many([(curve, g00), (g00, eye)])
    steps_t = flipped(steps)
    plain_gram = stacked(beside(g00, g01), beside(flipped(g01), g11))
    through_gram = stacked(beside(g01, g11), beside(g11, g12))
    after_first = beside(eye - steps_t, weight * steps_t)
    new_gram = symmetric(sandwich(after_first, plain_gram))
    mixing = times(inverse, new_gram)
    direction = after_first + flipped(mixing)
    curve = symmetric(sandwich(direction, plain_gram - weight * through_gram))
    (steps,) = solve_many([(curve, new_gram)])
    steps_t2 = flipped(steps)
    applied = direction - weight * pltpu.roll(direction, size, 1)
    solution_rows = exact_plain(beside(eye, steps_t2), stacked(steps_t, direction))
    residual_rows = exact_plain(beside(eye, -steps_t2), stacked(after_first, applied))
    rows = jnp.concatenate([solution_rows, residual_rows], axis=0)
    for part in range(first_ref.shape[0]):
        lanes = slice(part * 128, part * 128 + 128)
        basis = jnp.concatenate(
            [
                query_ref[:, lanes],
                first_ref[part],
                scaled_sum(row_refs, col_ref, scaling_ref, part),
                jnp.zeros_like(eye),
            ],
            axis=0,
        )
        values = exact_plain(rows, basis)
        solution_ref[:, lanes] = values[:size]
        residual_ref[:, lanes] = values[size:]


def pass_around(pieces, axis):
    count = len(pieces)
    return [pieces[0]] + [
        lax.ppermute(pieces[ahead], axis, [(at, (at + ahead) % count) for at in range(count)])
        for ahead in range(1, count)
    ]


def exchange(pieces, axis):
    return lax.all_to_all(pieces, axis, 0, 0, tiled=True)


def simple_call(kernel, shapes, name, *operands):
    return pl.pallas_call(
        kernel,
        out_shape=shapes,
        compiler_params=pltpu.CompilerParams(vmem_limit_bytes=VMEM_LIMIT),
        name=name,
    )(*operands)


def sum_kernel(col_ref, total_ref):
    col_count, sent = col_ref.shape[:2]
    total_ref[...] = total_of(
        [
            col_ref[segment, sent - GRAM_TERMS + term]
            for term in range(GRAM_TERMS)
            for segment in range(col_count)
        ]
    )


def body(queries, block_spots, live_blocks, neighbor_cols, neighbor_sims):
    row_count = lax.axis_size("row")
    col_count = lax.axis_size("col")
    query_rows, seg_len = queries.shape
    per_seg = seg_len // 128
    places = (block_spots, live_blocks)
    piece = (per_seg, query_rows, 128)
    wide = jax.ShapeDtypeStruct(piece, jnp.float32)
    narrow = jax.ShapeDtypeStruct(piece, jnp.bfloat16)
    copies = jax.ShapeDtypeStruct((col_count,) + piece, jnp.bfloat16)
    gram_shape = jax.ShapeDtypeStruct((query_rows, 128), jnp.float32)

    blocks, *row_sums, col_sums = build_blocks(
        *places, neighbor_cols[0, 0], neighbor_sims[0, 0], row_count, col_count, per_seg
    )
    col_part = exchange(col_sums.reshape(col_count, per_seg, 128), "col")
    row_parts = pass_around(row_sums, "row")
    scaling, scaled, scaled_copies = simple_call(
        start_kernel,
        [jax.ShapeDtypeStruct((per_seg, 128), jnp.float32), narrow, copies],
        "start",
        *row_parts,
        col_part,
        queries,
    )

    def product(vectors, vector_copies, *grams):
        col_dirs = exchange(vector_copies, "col").reshape((col_count * per_seg,) + piece[1:])
        row_pieces = pass_around([vectors] * row_count, "row")
        if grams:
            grams = (col_dirs, *grams)
        total = backward_product(places, blocks, row_pieces, col_count, grams)
        col_part = exchange(total, "col")
        totals = forward_product(places, blocks, col_dirs, row_count, piece)
        return pass_around(totals, "row"), col_part

    row_parts, col_part = product(scaled, scaled_copies)
    first, scaled, scaled_copies, gram = simple_call(
        middle_kernel,
        [wide, narrow, copies, gram_shape],
        "middle",
        *row_parts,
        col_part,
        scaling,
        queries,
    )
    row_parts, col_part = product(scaled, scaled_copies, gram)
    (gram,) = simple_call(sum_kernel, [gram_shape], "gram_sum", col_part)
    flat = jax.ShapeDtypeStruct(queries.shape, jnp.float32)
    return tuple(
        simple_call(
            close_kernel,
            [flat, flat],
            "close",
            *row_parts,
            *pass_around([gram] * row_count, "row"),
            col_part,
            scaling,
            queries,
            first,
        )
    )


def solution(mesh):
    placed = (
        P(None, ("row", "col")),
        P("row", "col", None),
        P("row", "col"),
        P("row", "col", None, None, None),
        P("row", "col", None, None, None),
    )
    return jax.shard_map(
        body,
        mesh=mesh,
        in_specs=placed,
        out_specs=(P(None, ("row", "col")), P(None, ("row", "col"))),
        check_vma=False,
    )
```

```python
import functools

import jax
import jax.numpy as jnp
from jax import lax
from jax.experimental import pallas as pl
from jax.experimental.pallas import tpu as pltpu
from jax.sharding import PartitionSpec as P

graph_weight = 0.95
GROUP = 16
BATCH = 32
AHEAD = 3
GRAM_TERMS = 3
LARGE_GRANT = 60 * 1024 * 1024
SMALL_GRANT = 24 * 1024 * 1024


def dot_plain(left, right, **kwargs):
    return lax.dot_general(
        left, right, (((1,), (0,)), ((), ())), preferred_element_type=jnp.float32, **kwargs
    )


def dot_across(left, right, **kwargs):
    return lax.dot_general(
        left, right, (((1,), (1,)), ((), ())), preferred_element_type=jnp.float32, **kwargs
    )


exact_plain = functools.partial(dot_plain, precision=lax.Precision.HIGHEST)
exact_across = functools.partial(dot_across, precision=lax.Precision.HIGHEST)


def place_of(spots_ref, slot, col_blocks):
    spot = spots_ref[0, 0, slot]
    if col_blocks & (col_blocks - 1):
        return lax.div(spot, col_blocks), lax.rem(spot, col_blocks)
    return spot >> (col_blocks.bit_length() - 1), spot & (col_blocks - 1)


def group_count(live_ref, group):
    return (live_ref[0, 0] + group - 1) // group


def group_copy(source, target, sems, index, group):
    window = pl.ds(index * group, group)
    return pltpu.make_async_copy(source.at[window], target.at[window], sems.at[index])


def build_kernel(row_count, spots_ref, live_ref, index_hbm, value_hbm, block_hbm, *refs):
    row_outs = refs[:row_count]
    (
        col_out_ref,
        index_ref,
        value_ref,
        block_ref,
        row_ref,
        col_ref,
        index_sems,
        value_sems,
        block_sems,
    ) = refs[row_count:]
    per_seg = row_outs[0].shape[0]
    col_blocks = col_out_ref.shape[0]
    groups = group_count(live_ref, BATCH) * (BATCH // GROUP)

    def start_copies(index, _):
        group_copy(index_hbm, index_ref, index_sems, index, GROUP).start()
        group_copy(value_hbm, value_ref, value_sems, index, GROUP).start()
        return 0

    lax.fori_loop(0, groups, start_copies, 0)
    row_ref[...] = jnp.zeros_like(row_ref)
    col_ref[...] = jnp.zeros_like(col_ref)
    rows_16 = lax.broadcasted_iota(jnp.int32, (16, 128), 0)
    ones = jnp.ones((128, 128), jnp.bfloat16)
    zero = jnp.zeros((16, 128), jnp.bfloat16)

    def build_group(index, _):
        group_copy(index_hbm, index_ref, index_sems, index, GROUP).wait()
        group_copy(value_hbm, value_ref, value_sems, index, GROUP).wait()
        targets = [(rows_16 + 16 * part).astype(jnp.int16) for part in range(8)]
        for inside in range(GROUP):
            slot = index * GROUP + inside
            row_block, col_block = place_of(spots_ref, slot, col_blocks)
            active = (slot < live_ref[0, 0]).astype(jnp.float32)
            index_i32 = index_ref[slot]
            value_f32 = value_ref[slot].astype(jnp.float32) * active
            sums = [zero] * 8
            for entry in range(16):
                index_row = jnp.broadcast_to(index_i32[entry : entry + 1], (16, 128)).astype(
                    jnp.int16
                )
                value_row = jnp.broadcast_to(value_f32[entry : entry + 1], (16, 128)).astype(
                    jnp.bfloat16
                )
                for part in range(8):
                    sums[part] = sums[part] + jnp.where(
                        index_row == targets[part], value_row, zero
                    )
            block = jnp.concatenate(sums, axis=0)
            block_ref[slot] = block
            row_ref[row_block] += value_f32[:8] + value_f32[8:]
            col_ref[col_block] += dot_plain(block, ones)
        group_copy(block_ref, block_hbm, block_sems, index, GROUP).start()
        return 0

    lax.fori_loop(0, groups, build_group, 0)
    for ahead, out in enumerate(row_outs):
        first = lax.rem(lax.axis_index("row") + ahead, row_count) * per_seg
        for part in range(per_seg):
            out[part : part + 1] = jnp.sum(row_ref[first + part], axis=0, keepdims=True)
    diagonal = lax.broadcasted_iota(jnp.int32, (128, 128), 0) == lax.broadcasted_iota(
        jnp.int32, (128, 128), 1
    )
    for col_block in range(col_blocks):
        col_out_ref[col_block : col_block + 1] = jnp.sum(
            jnp.where(diagonal, col_ref[col_block], 0.0), axis=0, keepdims=True
        )

    def finish_copies(index, _):
        group_copy(block_ref, block_hbm, block_sems, index, GROUP).wait()
        return 0

    lax.fori_loop(0, groups, finish_copies, 0)


SCALARS = pl.BlockSpec(memory_space=pltpu.SMEM)
ANYWHERE = pl.BlockSpec(memory_space=pl.ANY)
IN_VMEM = pl.BlockSpec(memory_space=pltpu.VMEM)


def build_blocks(spots, live, index_table, value_table, row_count, col_count, per_seg):
    slots = index_table.shape[0]
    groups = slots // GROUP
    sum_shapes = [(per_seg, 128)] * row_count + [(col_count * per_seg, 128)]
    return pl.pallas_call(
        functools.partial(build_kernel, row_count),
        in_specs=[SCALARS, SCALARS, ANYWHERE, ANYWHERE],
        out_specs=[ANYWHERE] + [IN_VMEM] * len(sum_shapes),
        out_shape=[jax.ShapeDtypeStruct((slots, 128, 128), jnp.bfloat16)]
        + [jax.ShapeDtypeStruct(shape, jnp.float32) for shape in sum_shapes],
        scratch_shapes=[
            pltpu.VMEM(index_table.shape, index_table.dtype),
            pltpu.VMEM(value_table.shape, value_table.dtype),
            pltpu.VMEM((slots, 128, 128), jnp.bfloat16),
            pltpu.VMEM((row_count * per_seg, 8, 128), jnp.float32),
            pltpu.VMEM((col_count * per_seg, 128, 128), jnp.float32),
            pltpu.SemaphoreType.DMA((groups,)),
            pltpu.SemaphoreType.DMA((groups,)),
            pltpu.SemaphoreType.DMA((groups,)),
        ],
        compiler_params=pltpu.CompilerParams(vmem_limit_bytes=LARGE_GRANT),
        name="build_blocks",
    )(spots, live, index_table, value_table)


def each_group(live_ref, block_hbm, block_ref, sems, prepare, run_group):
    groups = group_count(live_ref, BATCH)

    def start_copy(index):
        @pl.when(index < groups)
        def _():
            group_copy(block_hbm, block_ref, sems, index, BATCH).start()

    for index in range(min(AHEAD, block_ref.shape[0] // BATCH)):
        start_copy(index)
    prepare()

    def one_group(index, _):
        group_copy(block_hbm, block_ref, sems, index, BATCH).wait()
        start_copy(index + AHEAD)
        run_group(index * BATCH)
        return 0

    lax.fori_loop(0, groups, one_group, 0)


def add_products(dot, places, first_slot, block_ref, dir_ref, total_refs):
    sums = []
    for inside in range(BATCH):
        slot = first_slot + inside
        sums.append(dot(dir_ref[places(slot)[0]], block_ref[slot]))
    for inside in range(BATCH):
        total_ref = total_refs[inside % len(total_refs)]
        total_ref[places(first_slot + inside)[1]] += sums[inside]


def fill_directions(pieces, dir_ref, mine, per_seg):
    for behind, piece in enumerate(pieces):
        first = lax.rem(mine + (len(pieces) - behind), len(pieces)) * per_seg
        for part in range(per_seg):
            dir_ref[first + part] = piece[part]


def add_gram(total, values, high, directions):
    low = (values - high.astype(jnp.float32)).astype(high.dtype)
    return total + dot_across(jnp.concatenate([high, low], axis=0), tall(directions))


def backward_kernel(row_count, spots_ref, live_ref, block_hbm, *refs):
    row_pieces = refs[:row_count]
    gram_refs = refs[row_count:-6]
    col_out_ref, block_ref, sems, row_dir_ref, even_ref, odd_ref = refs[-6:]
    per_seg, size, _ = row_pieces[0].shape
    col_blocks = even_ref.shape[0]
    col_count, sent = col_out_ref.shape[:2]

    def prepare():
        even_ref[...] = jnp.zeros_like(even_ref)
        odd_ref[...] = jnp.zeros_like(odd_ref)
        fill_directions(row_pieces, row_dir_ref, lax.axis_index("row"), per_seg)

    def run_group(first_slot):
        add_products(
            dot_across,
            lambda slot: place_of(spots_ref, slot, col_blocks),
            first_slot,
            block_ref,
            row_dir_ref,
            [even_ref, odd_ref],
        )

    each_group(live_ref, block_hbm, block_ref, sems, prepare, run_group)

    def send_segment(segment, gram):
        for part in range(per_seg):
            col_block = segment * per_seg + part
            values = even_ref[col_block] + odd_ref[col_block]
            high = values.astype(col_out_ref.dtype)
            col_out_ref[segment, part] = high
            if gram_refs:
                gram = add_gram(gram, values, high, gram_refs[0][col_block])
        return gram

    gram = lax.fori_loop(0, col_count, send_segment, jnp.zeros((2 * size, 128), jnp.float32))
    if gram_refs:
        gram = gram_refs[1][...] + pltpu.roll(gram[:size] + gram[size:], 3 * size, 1)
        for term in range(GRAM_TERMS):
            rounded = gram.astype(col_out_ref.dtype)
            gram = gram - rounded.astype(jnp.float32)
            for segment in range(col_count):
                col_out_ref[segment, per_seg + term] = rounded


def forward_kernel(spots_ref, live_ref, block_hbm, col_dir_ref, *refs):
    *row_outs, block_ref, sems, even_ref, odd_ref = refs
    per_seg = row_outs[0].shape[0]
    col_blocks = col_dir_ref.shape[0]

    def prepare():
        even_ref[...] = jnp.zeros_like(even_ref)
        odd_ref[...] = jnp.zeros_like(odd_ref)

    def run_group(first_slot):
        add_products(
            dot_plain,
            lambda slot: place_of(spots_ref, slot, col_blocks)[::-1],
            first_slot,
            block_ref,
            col_dir_ref,
            [even_ref, odd_ref],
        )

    each_group(live_ref, block_hbm, block_ref, sems, prepare, run_group)
    for ahead, out in enumerate(row_outs):
        first = lax.rem(lax.axis_index("row") + ahead, len(row_outs)) * per_seg
        for part in range(per_seg):
            values = even_ref[first + part] + odd_ref[first + part]
            out[part] = values.astype(out.dtype)


def over_blocks(kernel, name, places, blocks, inputs, outputs, scratch):
    slots = blocks.shape[0]
    return pl.pallas_call(
        kernel,
        in_specs=[SCALARS, SCALARS, ANYWHERE] + [IN_VMEM] * len(inputs),
        out_specs=[IN_VMEM] * len(outputs),
        out_shape=outputs,
        scratch_shapes=[
            pltpu.VMEM(blocks.shape, blocks.dtype),
            pltpu.SemaphoreType.DMA((slots // BATCH,)),
        ]
        + scratch,
        compiler_params=pltpu.CompilerParams(vmem_limit_bytes=LARGE_GRANT),
        cost_estimate=pl.CostEstimate(
            flops=2 * slots * 32 * 128 * 128, bytes_accessed=2 * blocks.size, transcendentals=0
        ),
        name=name,
    )(*places, blocks, *inputs)


def backward_product(places, blocks, row_pieces, col_count, grams=()):
    per_seg, rows, lanes = row_pieces[0].shape
    sent = per_seg + (GRAM_TERMS if grams else 0)
    col_shape = (col_count * per_seg, rows, lanes)
    (total,) = over_blocks(
        functools.partial(backward_kernel, len(row_pieces)),
        "backward_product",
        places,
        blocks,
        [*row_pieces, *grams],
        [jax.ShapeDtypeStruct((col_count, sent, rows, lanes), jnp.bfloat16)],
        [
            pltpu.VMEM((len(row_pieces) * per_seg, rows, lanes), jnp.bfloat16),
            pltpu.VMEM(col_shape, jnp.float32),
            pltpu.VMEM(col_shape, jnp.float32),
        ],
    )
    return total


def forward_product(places, blocks, col_dirs, row_count, piece):
    row_shape = (row_count * piece[0],) + piece[1:]
    return over_blocks(
        forward_kernel,
        "forward_product",
        places,
        blocks,
        [col_dirs],
        [jax.ShapeDtypeStruct(piece, jnp.bfloat16)] * row_count,
        [pltpu.VMEM(row_shape, jnp.float32), pltpu.VMEM(row_shape, jnp.float32)],
    )


def total_of(values):
    total = values[0].astype(jnp.float32)
    for value in values[1:]:
        total = total + value.astype(jnp.float32)
    return total


def leading(ref):
    return [ref.at[index] for index in range(ref.shape[0])]


def start_kernel(*refs):
    *row_refs, col_ref, query_ref, scaling_ref, scaled_ref, copies_ref = refs
    degree = 1.0 + 0.5 * total_of([ref[...] for ref in [*row_refs, *leading(col_ref)]])
    scaling = 1.0 / jnp.sqrt(degree)
    scaling_ref[...] = scaling
    for part in range(scaling.shape[0]):
        scaled = (
            scaling[part : part + 1] * query_ref[:, part * 128 : part * 128 + 128]
        ).astype(jnp.bfloat16)
        scaled_ref[part] = scaled
        for copy in range(copies_ref.shape[0]):
            copies_ref[copy, part] = scaled


def scaled_sum(row_refs, col_ref, scaling_ref, part):
    scaling = scaling_ref[part : part + 1]
    total = total_of([ref[part] for ref in [*row_refs, *leading(col_ref)]])
    return scaling * (0.5 * total)


def middle_kernel(*refs):
    *row_refs, col_ref, scaling_ref, query_ref, first_ref, scaled_ref, copies_ref, gram_ref = refs
    size = query_ref.shape[0]
    pair_gram = jnp.zeros((2 * size, 128), jnp.float32)
    for part in range(scaling_ref.shape[0]):
        first = scaled_sum(row_refs, col_ref, scaling_ref, part)
        first_ref[part] = first
        scaled = (scaling_ref[part : part + 1] * first).astype(jnp.bfloat16)
        scaled_ref[part] = scaled
        for copy in range(copies_ref.shape[0]):
            copies_ref[copy, part] = scaled
        pair = jnp.concatenate(
            [query_ref[:, part * 128 : part * 128 + 128], first], axis=0
        )
        pair_gram += exact_across(pair, tall(pair))
    gram_ref[...] = beside(
        pair_gram[:size], pltpu.roll(window(pair_gram[size:], 1), size, 1)
    )


def tall(flat):
    rest = flat.shape[1] - flat.shape[0]
    return jnp.concatenate([flat, jnp.zeros((rest, flat.shape[1]), flat.dtype)], axis=0)


def flipped(flat):
    return tall(flat).T[: flat.shape[0]]


def times(left, right):
    return exact_plain(left, tall(right))


def beside(left, right):
    return left + pltpu.roll(right, left.shape[0], 1)


def stacked(upper, lower):
    rest = jnp.zeros((upper.shape[1] - 2 * upper.shape[0], upper.shape[1]), upper.dtype)
    return jnp.concatenate([upper, lower, rest], axis=0)


def sandwich(rows, middle):
    return exact_across(exact_plain(rows, middle), tall(rows))


def symmetric(flat):
    return 0.5 * (flat + flipped(flat))


def window(flat, place):
    size = flat.shape[0]
    if place:
        flat = pltpu.roll(flat, flat.shape[1] - place * size, 1)
    lanes = lax.broadcasted_iota(jnp.int32, flat.shape, 1)
    return jnp.where(lanes < size, flat, 0.0)


def solve_many(pairs):
    size = pairs[0][0].shape[0]
    systems = [matrix + pltpu.roll(side, size, 1) for matrix, side in pairs]
    sublanes = lax.broadcasted_iota(jnp.int32, systems[0].shape, 0)
    for pivot in range(size):
        updated = []
        for system in systems:
            column = system[:, pivot : pivot + 1]
            row = system[pivot : pivot + 1, :] / column[pivot : pivot + 1, :]
            updated.append(jnp.where(sublanes == pivot, row, system - column * row))
        systems = updated
    return [window(system, 1) for system in systems]


def close_kernel(*refs):
    row_count = (len(refs) - 6) // 2
    row_refs = refs[:row_count]
    gram_refs = refs[row_count : 2 * row_count]
    col_ref, scaling_ref, query_ref, first_ref, solution_ref, residual_ref = refs[-6:]
    size = query_ref.shape[0]
    weight = graph_weight
    total = total_of([ref[...] for ref in gram_refs])
    g00 = symmetric(window(total, 0))
    g01 = window(total, 1)
    g11 = symmetric(window(total, 2))
    g12 = symmetric(window(total, 3))
    eye = (
        lax.broadcasted_iota(jnp.int32, total.shape, 0)
        == lax.broadcasted_iota(jnp.int32, total.shape, 1)
    ).astype(jnp.float32)
    curve = symmetric(g00 - weight * g01)
    steps, inverse = solve_many([(curve, g00), (g00, eye)])
    steps_t = flipped(steps)
    plain_gram = stacked(beside(g00, g01), beside(flipped(g01), g11))
    through_gram = stacked(beside(g01, g11), beside(g11, g12))
    after_first = beside(eye - steps_t, weight * steps_t)
    new_gram = symmetric(sandwich(after_first, plain_gram))
    mixing = times(inverse, new_gram)
    direction = after_first + flipped(mixing)
    curve = symmetric(sandwich(direction, plain_gram - weight * through_gram))
    (steps,) = solve_many([(curve, new_gram)])
    steps_t2 = flipped(steps)
    applied = direction - weight * pltpu.roll(direction, size, 1)
    solution_rows = exact_plain(beside(eye, steps_t2), stacked(steps_t, direction))
    residual_rows = exact_plain(beside(eye, -steps_t2), stacked(after_first, applied))
    rows = jnp.concatenate([solution_rows, residual_rows], axis=0)
    for part in range(first_ref.shape[0]):
        lanes = slice(part * 128, part * 128 + 128)
        basis = jnp.concatenate(
            [
                query_ref[:, lanes],
                first_ref[part],
                scaled_sum(row_refs, col_ref, scaling_ref, part),
                jnp.zeros_like(eye),
            ],
            axis=0,
        )
        values = exact_plain(rows, basis)
        solution_ref[:, lanes] = values[:size]
        residual_ref[:, lanes] = values[size:]


def pass_around(pieces, axis):
    count = len(pieces)
    return [pieces[0]] + [
        lax.ppermute(pieces[ahead], axis, [(at, (at + ahead) % count) for at in range(count)])
        for ahead in range(1, count)
    ]


def exchange(pieces, axis):
    return lax.all_to_all(pieces, axis, 0, 0, tiled=True)


def simple_call(kernel, shapes, name, *operands):
    return pl.pallas_call(
        kernel,
        out_shape=shapes,
        compiler_params=pltpu.CompilerParams(vmem_limit_bytes=SMALL_GRANT),
        name=name,
    )(*operands)


def sum_kernel(col_ref, total_ref):
    col_count, sent = col_ref.shape[:2]
    total_ref[...] = total_of(
        [
            col_ref[segment, sent - GRAM_TERMS + term]
            for term in range(GRAM_TERMS)
            for segment in range(col_count)
        ]
    )


def body(queries, block_spots, live_blocks, neighbor_cols, neighbor_sims):
    row_count = lax.axis_size("row")
    col_count = lax.axis_size("col")
    query_rows, seg_len = queries.shape
    per_seg = seg_len // 128
    places = (block_spots, live_blocks)
    piece = (per_seg, query_rows, 128)
    wide = jax.ShapeDtypeStruct(piece, jnp.float32)
    narrow = jax.ShapeDtypeStruct(piece, jnp.bfloat16)
    copies = jax.ShapeDtypeStruct((col_count,) + piece, jnp.bfloat16)
    gram_shape = jax.ShapeDtypeStruct((query_rows, 128), jnp.float32)

    blocks, *row_sums, col_sums = build_blocks(
        *places, neighbor_cols[0, 0], neighbor_sims[0, 0], row_count, col_count, per_seg
    )
    col_part = exchange(col_sums.reshape(col_count, per_seg, 128), "col")
    row_parts = pass_around(row_sums, "row")
    scaling, scaled, scaled_copies = simple_call(
        start_kernel,
        [jax.ShapeDtypeStruct((per_seg, 128), jnp.float32), narrow, copies],
        "start",
        *row_parts,
        col_part,
        queries,
    )

    def product(vectors, vector_copies, *grams):
        col_dirs = exchange(vector_copies, "col").reshape((col_count * per_seg,) + piece[1:])
        row_pieces = pass_around([vectors] * row_count, "row")
        if grams:
            grams = (col_dirs, *grams)
        total = backward_product(places, blocks, row_pieces, col_count, grams)
        col_part = exchange(total, "col")
        totals = forward_product(places, blocks, col_dirs, row_count, piece)
        return pass_around(totals, "row"), col_part

    row_parts, col_part = product(scaled, scaled_copies)
    first, scaled, scaled_copies, gram = simple_call(
        middle_kernel,
        [wide, narrow, copies, gram_shape],
        "middle",
        *row_parts,
        col_part,
        scaling,
        queries,
    )
    row_parts, col_part = product(scaled, scaled_copies, gram)
    (gram,) = simple_call(sum_kernel, [gram_shape], "gram_sum", col_part)
    flat = jax.ShapeDtypeStruct(queries.shape, jnp.float32)
    return tuple(
        simple_call(
            close_kernel,
            [flat, flat],
            "close",
            *row_parts,
            *pass_around([gram] * row_count, "row"),
            col_part,
            scaling,
            queries,
            first,
        )
    )


def solution(mesh):
    placed = (
        P(None, ("row", "col")),
        P("row", "col", None),
        P("row", "col"),
        P("row", "col", None, None, None),
        P("row", "col", None, None, None),
    )
    return jax.shard_map(
        body,
        mesh=mesh,
        in_specs=placed,
        out_specs=(P(None, ("row", "col")), P(None, ("row", "col"))),
        check_vma=False,
    )
```

```python
import functools

import jax
import jax.numpy as jnp
from jax import lax
from jax.experimental import pallas as pl
from jax.experimental.pallas import tpu as pltpu
from jax.sharding import PartitionSpec as P

graph_weight = 0.95
GROUP = 16
BATCH = 32
GRAM_TERMS = 3
BUILD_GRANT = 60 * 1024 * 1024
PRODUCT_GRANT = 57 * 1024 * 1024
SMALL_GRANT = 24 * 1024 * 1024


def dot_plain(left, right, **kwargs):
    return lax.dot_general(
        left, right, (((1,), (0,)), ((), ())), preferred_element_type=jnp.float32, **kwargs
    )


def dot_across(left, right, **kwargs):
    return lax.dot_general(
        left, right, (((1,), (1,)), ((), ())), preferred_element_type=jnp.float32, **kwargs
    )


exact_plain = functools.partial(dot_plain, precision=lax.Precision.HIGHEST)
exact_across = functools.partial(dot_across, precision=lax.Precision.HIGHEST)


def place_of(spots_ref, slot, col_blocks):
    spot = spots_ref[0, 0, slot]
    if col_blocks & (col_blocks - 1):
        return lax.div(spot, col_blocks), lax.rem(spot, col_blocks)
    return spot >> (col_blocks.bit_length() - 1), spot & (col_blocks - 1)


def group_count(live_ref, group):
    return (live_ref[0, 0] + group - 1) // group


def group_copy(source, target, sems, index, group):
    window = pl.ds(index * group, group)
    return pltpu.make_async_copy(source.at[window], target.at[window], sems.at[index])


def build_kernel(row_count, spots_ref, live_ref, index_hbm, value_hbm, block_hbm, *refs):
    row_outs = refs[:row_count]
    (
        col_out_ref,
        index_ref,
        value_ref,
        block_ref,
        row_ref,
        col_ref,
        index_sems,
        value_sems,
        block_sems,
    ) = refs[row_count:]
    per_seg = row_outs[0].shape[0]
    col_blocks = col_out_ref.shape[0]
    groups = group_count(live_ref, BATCH) * (BATCH // GROUP)

    def start_copies(index, _):
        group_copy(index_hbm, index_ref, index_sems, index, GROUP).start()
        group_copy(value_hbm, value_ref, value_sems, index, GROUP).start()
        return 0

    lax.fori_loop(0, groups, start_copies, 0)
    row_ref[...] = jnp.zeros_like(row_ref)
    col_ref[...] = jnp.zeros_like(col_ref)
    rows_16 = lax.broadcasted_iota(jnp.int32, (16, 128), 0)
    ones = jnp.ones((128, 128), jnp.bfloat16)
    zero = jnp.zeros((16, 128), jnp.bfloat16)
    one = jnp.ones((16, 128), jnp.bfloat16)

    def build_group(index, _):
        group_copy(index_hbm, index_ref, index_sems, index, GROUP).wait()
        group_copy(value_hbm, value_ref, value_sems, index, GROUP).wait()
        targets = [(rows_16 + 16 * half).astype(jnp.int16) for half in range(2)]
        for inside in range(GROUP):
            slot = index * GROUP + inside
            row_block, col_block = place_of(spots_ref, slot, col_blocks)
            active = (slot < live_ref[0, 0]).astype(jnp.float32)
            index_i32 = index_ref[slot]
            value_f32 = value_ref[slot].astype(jnp.float32) * active
            quarter = index_i32 >> 5
            within = index_i32 & 31
            quarter_values = [jnp.where(quarter == part, value_f32, 0.0) for part in range(4)]
            sums = [zero] * 8
            for entry in range(16):
                row = slice(entry, entry + 1)
                within_row = jnp.broadcast_to(within[row], (16, 128)).astype(jnp.int16)
                hits = [jnp.where(within_row == target, one, zero) for target in targets]
                for part in range(4):
                    value_row = jnp.broadcast_to(quarter_values[part][row], (16, 128)).astype(
                        jnp.bfloat16
                    )
                    for half in range(2):
                        place = 2 * part + half
                        sums[place] = sums[place] + hits[half] * value_row
            block = jnp.concatenate(sums, axis=0)
            block_ref[slot] = block
            row_ref[row_block] += value_f32[:8] + value_f32[8:]
            col_ref[col_block] += dot_plain(block, ones)
        group_copy(block_ref, block_hbm, block_sems, index, GROUP).start()
        return 0

    lax.fori_loop(0, groups, build_group, 0)
    for ahead, out in enumerate(row_outs):
        first = lax.rem(lax.axis_index("row") + ahead, row_count) * per_seg
        for part in range(per_seg):
            out[part : part + 1] = jnp.sum(row_ref[first + part], axis=0, keepdims=True)
    diagonal = lax.broadcasted_iota(jnp.int32, (128, 128), 0) == lax.broadcasted_iota(
        jnp.int32, (128, 128), 1
    )
    for col_block in range(col_blocks):
        col_out_ref[col_block : col_block + 1] = jnp.sum(
            jnp.where(diagonal, col_ref[col_block], 0.0), axis=0, keepdims=True
        )

    def finish_copies(index, _):
        group_copy(block_ref, block_hbm, block_sems, index, GROUP).wait()
        return 0

    lax.fori_loop(0, groups, finish_copies, 0)


SCALARS = pl.BlockSpec(memory_space=pltpu.SMEM)
ANYWHERE = pl.BlockSpec(memory_space=pl.ANY)
IN_VMEM = pl.BlockSpec(memory_space=pltpu.VMEM)


def build_blocks(spots, live, index_table, value_table, row_count, col_count, per_seg):
    slots = index_table.shape[0]
    groups = slots // GROUP
    sum_shapes = [(per_seg, 128)] * row_count + [(col_count * per_seg, 128)]
    return pl.pallas_call(
        functools.partial(build_kernel, row_count),
        in_specs=[SCALARS, SCALARS, ANYWHERE, ANYWHERE],
        out_specs=[ANYWHERE] + [IN_VMEM] * len(sum_shapes),
        out_shape=[jax.ShapeDtypeStruct((slots, 128, 128), jnp.bfloat16)]
        + [jax.ShapeDtypeStruct(shape, jnp.float32) for shape in sum_shapes],
        scratch_shapes=[
            pltpu.VMEM(index_table.shape, index_table.dtype),
            pltpu.VMEM(value_table.shape, value_table.dtype),
            pltpu.VMEM((slots, 128, 128), jnp.bfloat16),
            pltpu.VMEM((row_count * per_seg, 8, 128), jnp.float32),
            pltpu.VMEM((col_count * per_seg, 128, 128), jnp.float32),
            pltpu.SemaphoreType.DMA((groups,)),
            pltpu.SemaphoreType.DMA((groups,)),
            pltpu.SemaphoreType.DMA((groups,)),
        ],
        compiler_params=pltpu.CompilerParams(vmem_limit_bytes=BUILD_GRANT),
        name="build_blocks",
    )(spots, live, index_table, value_table)


def each_group(live_ref, block_hbm, block_ref, sems, prepare, run_group):
    groups = group_count(live_ref, BATCH)

    def start_copy(index, _):
        group_copy(block_hbm, block_ref, sems, index, BATCH).start()
        return 0

    lax.fori_loop(0, groups, start_copy, 0)
    prepare()

    def one_group(index, _):
        group_copy(block_hbm, block_ref, sems, index, BATCH).wait()
        run_group(index * BATCH)
        return 0

    lax.fori_loop(0, groups, one_group, 0)


def add_products(dot, places, first_slot, block_ref, dir_ref, total_refs):
    sums = []
    for inside in range(BATCH):
        slot = first_slot + inside
        sums.append(dot(dir_ref[places(slot)[0]], block_ref[slot]))
    for inside in range(BATCH):
        total_ref = total_refs[inside % len(total_refs)]
        total_ref[places(first_slot + inside)[1]] += sums[inside]


def fill_directions(pieces, dir_ref, mine, per_seg):
    for behind, piece in enumerate(pieces):
        first = lax.rem(mine + (len(pieces) - behind), len(pieces)) * per_seg
        for part in range(per_seg):
            dir_ref[first + part] = piece[part]


def backward_kernel(row_count, spots_ref, live_ref, block_hbm, *refs):
    row_pieces = refs[:row_count]
    col_out_ref, block_ref, sems, row_dir_ref, even_ref, odd_ref = refs[row_count:]
    per_seg = row_pieces[0].shape[0]
    col_blocks = even_ref.shape[0]

    def prepare():
        even_ref[...] = jnp.zeros_like(even_ref)
        odd_ref[...] = jnp.zeros_like(odd_ref)
        fill_directions(row_pieces, row_dir_ref, lax.axis_index("row"), per_seg)

    def run_group(first_slot):
        add_products(
            dot_across,
            lambda slot: place_of(spots_ref, slot, col_blocks),
            first_slot,
            block_ref,
            row_dir_ref,
            [even_ref, odd_ref],
        )

    each_group(live_ref, block_hbm, block_ref, sems, prepare, run_group)
    for segment in range(col_out_ref.shape[0]):
        for part in range(per_seg):
            col_block = segment * per_seg + part
            values = even_ref[col_block] + odd_ref[col_block]
            col_out_ref[segment, part] = values.astype(col_out_ref.dtype)


def attach_kernel(col_dir_ref, gram_ref, total_ref, message_ref):
    col_count, sent, size, _ = message_ref.shape
    per_seg = sent - GRAM_TERMS
    def add_segment(segment, gram):
        for part in range(per_seg):
            values = total_ref[segment, part]
            message_ref[segment, part] = values
            gram += dot_across(values, tall(col_dir_ref[segment * per_seg + part]))
        return gram

    gram = lax.fori_loop(
        0, col_count, add_segment, jnp.zeros((size, 128), jnp.float32), unroll=4
    )
    gram = gram_ref[...] + pltpu.roll(gram, 3 * size, 1)
    for term in range(GRAM_TERMS):
        rounded = gram.astype(message_ref.dtype)
        gram = gram - rounded.astype(jnp.float32)
        for segment in range(col_count):
            message_ref[segment, per_seg + term] = rounded


def forward_kernel(spots_ref, live_ref, block_hbm, col_dir_ref, *refs):
    *row_outs, block_ref, sems, even_ref, odd_ref = refs
    per_seg = row_outs[0].shape[0]
    col_blocks = col_dir_ref.shape[0]

    def prepare():
        even_ref[...] = jnp.zeros_like(even_ref)
        odd_ref[...] = jnp.zeros_like(odd_ref)

    def run_group(first_slot):
        add_products(
            dot_plain,
            lambda slot: place_of(spots_ref, slot, col_blocks)[::-1],
            first_slot,
            block_ref,
            col_dir_ref,
            [even_ref, odd_ref],
        )

    each_group(live_ref, block_hbm, block_ref, sems, prepare, run_group)
    for ahead, out in enumerate(row_outs):
        first = lax.rem(lax.axis_index("row") + ahead, len(row_outs)) * per_seg
        for part in range(per_seg):
            values = even_ref[first + part] + odd_ref[first + part]
            out[part] = values.astype(out.dtype)


def over_blocks(kernel, name, places, blocks, inputs, outputs, scratch):
    slots = blocks.shape[0]
    return pl.pallas_call(
        kernel,
        in_specs=[SCALARS, SCALARS, ANYWHERE] + [IN_VMEM] * len(inputs),
        out_specs=[IN_VMEM] * len(outputs),
        out_shape=outputs,
        scratch_shapes=[
            pltpu.VMEM(blocks.shape, blocks.dtype),
            pltpu.SemaphoreType.DMA((slots // BATCH,)),
        ]
        + scratch,
        compiler_params=pltpu.CompilerParams(vmem_limit_bytes=PRODUCT_GRANT),
        cost_estimate=pl.CostEstimate(
            flops=2 * slots * 32 * 128 * 128, bytes_accessed=2 * blocks.size, transcendentals=0
        ),
        name=name,
    )(*places, blocks, *inputs)


def backward_product(places, blocks, row_pieces, col_count):
    per_seg, rows, lanes = row_pieces[0].shape
    col_shape = (col_count * per_seg, rows, lanes)
    (total,) = over_blocks(
        functools.partial(backward_kernel, len(row_pieces)),
        "backward_product",
        places,
        blocks,
        row_pieces,
        [jax.ShapeDtypeStruct((col_count, per_seg, rows, lanes), jnp.bfloat16)],
        [
            pltpu.VMEM((len(row_pieces) * per_seg, rows, lanes), jnp.bfloat16),
            pltpu.VMEM(col_shape, jnp.float32),
            pltpu.VMEM(col_shape, jnp.float32),
        ],
    )
    return total


def forward_product(places, blocks, col_dirs, row_count, piece):
    row_shape = (row_count * piece[0],) + piece[1:]
    return over_blocks(
        forward_kernel,
        "forward_product",
        places,
        blocks,
        [col_dirs],
        [jax.ShapeDtypeStruct(piece, jnp.bfloat16)] * row_count,
        [pltpu.VMEM(row_shape, jnp.float32), pltpu.VMEM(row_shape, jnp.float32)],
    )


def total_of(values):
    total = values[0].astype(jnp.float32)
    for value in values[1:]:
        total = total + value.astype(jnp.float32)
    return total


def leading(ref):
    return [ref.at[index] for index in range(ref.shape[0])]


def start_kernel(*refs):
    *row_refs, col_ref, query_ref, scaling_ref, scaled_ref, copies_ref = refs
    degree = 1.0 + 0.5 * total_of([ref[...] for ref in [*row_refs, *leading(col_ref)]])
    scaling = 1.0 / jnp.sqrt(degree)
    scaling_ref[...] = scaling
    for part in range(scaling.shape[0]):
        scaled = (
            scaling[part : part + 1] * query_ref[:, part * 128 : part * 128 + 128]
        ).astype(jnp.bfloat16)
        scaled_ref[part] = scaled
        for copy in range(copies_ref.shape[0]):
            copies_ref[copy, part] = scaled


def scaled_sum(row_refs, col_ref, scaling_ref, part):
    scaling = scaling_ref[part : part + 1]
    total = total_of([ref[part] for ref in [*row_refs, *leading(col_ref)]])
    return scaling * (0.5 * total)


def middle_kernel(*refs):
    *row_refs, col_ref, scaling_ref, query_ref, first_ref, scaled_ref, copies_ref, gram_ref = refs
    size = query_ref.shape[0]
    pair_gram = jnp.zeros((2 * size, 128), jnp.float32)
    for part in range(scaling_ref.shape[0]):
        first = scaled_sum(row_refs, col_ref, scaling_ref, part)
        first_ref[part] = first
        scaled = (scaling_ref[part : part + 1] * first).astype(jnp.bfloat16)
        scaled_ref[part] = scaled
        for copy in range(copies_ref.shape[0]):
            copies_ref[copy, part] = scaled
        pair = jnp.concatenate(
            [query_ref[:, part * 128 : part * 128 + 128], first], axis=0
        )
        pair_gram += exact_across(pair, tall(pair))
    gram_ref[...] = beside(
        pair_gram[:size], pltpu.roll(window(pair_gram[size:], 1), size, 1)
    )


def tall(flat):
    rest = flat.shape[1] - flat.shape[0]
    return jnp.concatenate([flat, jnp.zeros((rest, flat.shape[1]), flat.dtype)], axis=0)


def flipped(flat):
    return tall(flat).T[: flat.shape[0]]


def times(left, right):
    return exact_plain(left, tall(right))


def beside(left, right):
    return left + pltpu.roll(right, left.shape[0], 1)


def stacked(upper, lower):
    rest = jnp.zeros((upper.shape[1] - 2 * upper.shape[0], upper.shape[1]), upper.dtype)
    return jnp.concatenate([upper, lower, rest], axis=0)


def sandwich(rows, middle):
    return exact_across(exact_plain(rows, middle), tall(rows))


def symmetric(flat):
    return 0.5 * (flat + flipped(flat))


def window(flat, place):
    size = flat.shape[0]
    if place:
        flat = pltpu.roll(flat, flat.shape[1] - place * size, 1)
    lanes = lax.broadcasted_iota(jnp.int32, flat.shape, 1)
    return jnp.where(lanes < size, flat, 0.0)


def solve_many(pairs):
    size = pairs[0][0].shape[0]
    systems = [matrix + pltpu.roll(side, size, 1) for matrix, side in pairs]
    sublanes = lax.broadcasted_iota(jnp.int32, systems[0].shape, 0)
    for pivot in range(size):
        updated = []
        for system in systems:
            column = system[:, pivot : pivot + 1]
            row = system[pivot : pivot + 1, :] / column[pivot : pivot + 1, :]
            updated.append(jnp.where(sublanes == pivot, row, system - column * row))
        systems = updated
    return [window(system, 1) for system in systems]


def close_kernel(*refs):
    row_count = (len(refs) - 6) // 2
    row_refs = refs[:row_count]
    gram_refs = refs[row_count : 2 * row_count]
    col_ref, scaling_ref, query_ref, first_ref, solution_ref, residual_ref = refs[-6:]
    size = query_ref.shape[0]
    weight = graph_weight
    total = total_of([ref[...] for ref in gram_refs])
    g00 = symmetric(window(total, 0))
    g01 = window(total, 1)
    g11 = symmetric(window(total, 2))
    g12 = symmetric(window(total, 3))
    eye = (
        lax.broadcasted_iota(jnp.int32, total.shape, 0)
        == lax.broadcasted_iota(jnp.int32, total.shape, 1)
    ).astype(jnp.float32)
    curve = symmetric(g00 - weight * g01)
    steps, inverse = solve_many([(curve, g00), (g00, eye)])
    steps_t = flipped(steps)
    plain_gram = stacked(beside(g00, g01), beside(flipped(g01), g11))
    through_gram = stacked(beside(g01, g11), beside(g11, g12))
    after_first = beside(eye - steps_t, weight * steps_t)
    new_gram = symmetric(sandwich(after_first, plain_gram))
    mixing = times(inverse, new_gram)
    direction = after_first + flipped(mixing)
    curve = symmetric(sandwich(direction, plain_gram - weight * through_gram))
    (steps,) = solve_many([(curve, new_gram)])
    steps_t2 = flipped(steps)
    applied = direction - weight * pltpu.roll(direction, size, 1)
    solution_rows = exact_plain(beside(eye, steps_t2), stacked(steps_t, direction))
    residual_rows = exact_plain(beside(eye, -steps_t2), stacked(after_first, applied))
    rows = jnp.concatenate([solution_rows, residual_rows], axis=0)
    for part in range(first_ref.shape[0]):
        lanes = slice(part * 128, part * 128 + 128)
        basis = jnp.concatenate(
            [
                query_ref[:, lanes],
                first_ref[part],
                scaled_sum(row_refs, col_ref, scaling_ref, part),
                jnp.zeros_like(eye),
            ],
            axis=0,
        )
        values = exact_plain(rows, basis)
        solution_ref[:, lanes] = values[:size]
        residual_ref[:, lanes] = values[size:]


def pass_around(pieces, axis):
    count = len(pieces)
    return [pieces[0]] + [
        lax.ppermute(pieces[ahead], axis, [(at, (at + ahead) % count) for at in range(count)])
        for ahead in range(1, count)
    ]


def exchange(pieces, axis):
    return lax.all_to_all(pieces, axis, 0, 0, tiled=True)


def simple_call(kernel, shapes, name, *operands):
    return pl.pallas_call(
        kernel,
        out_shape=shapes,
        compiler_params=pltpu.CompilerParams(vmem_limit_bytes=SMALL_GRANT),
        name=name,
    )(*operands)


def sum_kernel(col_ref, total_ref):
    col_count, sent = col_ref.shape[:2]
    total_ref[...] = total_of(
        [
            col_ref[segment, sent - GRAM_TERMS + term]
            for term in range(GRAM_TERMS)
            for segment in range(col_count)
        ]
    )


def body(queries, block_spots, live_blocks, neighbor_cols, neighbor_sims):
    row_count = lax.axis_size("row")
    col_count = lax.axis_size("col")
    query_rows, seg_len = queries.shape
    per_seg = seg_len // 128
    places = (block_spots, live_blocks)
    piece = (per_seg, query_rows, 128)
    wide = jax.ShapeDtypeStruct(piece, jnp.float32)
    narrow = jax.ShapeDtypeStruct(piece, jnp.bfloat16)
    copies = jax.ShapeDtypeStruct((col_count,) + piece, jnp.bfloat16)
    gram_shape = jax.ShapeDtypeStruct((query_rows, 128), jnp.float32)

    blocks, *row_sums, col_sums = build_blocks(
        *places, neighbor_cols[0, 0], neighbor_sims[0, 0], row_count, col_count, per_seg
    )
    col_part = exchange(col_sums.reshape(col_count, per_seg, 128), "col")
    row_parts = pass_around(row_sums, "row")
    scaling, scaled, scaled_copies = simple_call(
        start_kernel,
        [jax.ShapeDtypeStruct((per_seg, 128), jnp.float32), narrow, copies],
        "start",
        *row_parts,
        col_part,
        queries,
    )

    def product(vectors, vector_copies, *grams):
        col_dirs = exchange(vector_copies, "col").reshape((col_count * per_seg,) + piece[1:])
        row_pieces = pass_around([vectors] * row_count, "row")
        total = backward_product(places, blocks, row_pieces, col_count)
        if grams:
            message = jax.ShapeDtypeStruct(
                (col_count, per_seg + GRAM_TERMS) + piece[1:], jnp.bfloat16
            )
            (total,) = simple_call(attach_kernel, [message], "attach", col_dirs, *grams, total)
        col_part = exchange(total, "col")
        totals = forward_product(places, blocks, col_dirs, row_count, piece)
        return pass_around(totals, "row"), col_part

    row_parts, col_part = product(scaled, scaled_copies)
    first, scaled, scaled_copies, gram = simple_call(
        middle_kernel,
        [wide, narrow, copies, gram_shape],
        "middle",
        *row_parts,
        col_part,
        scaling,
        queries,
    )
    row_parts, col_part = product(scaled, scaled_copies, gram)
    (gram,) = simple_call(sum_kernel, [gram_shape], "gram_sum", col_part)
    flat = jax.ShapeDtypeStruct(queries.shape, jnp.float32)
    return tuple(
        simple_call(
            close_kernel,
            [flat, flat],
            "close",
            *row_parts,
            *pass_around([gram] * row_count, "row"),
            col_part,
            scaling,
            queries,
            first,
        )
    )


def solution(mesh):
    placed = (
        P(None, ("row", "col")),
        P("row", "col", None),
        P("row", "col"),
        P("row", "col", None, None, None),
        P("row", "col", None, None, None),
    )
    return jax.shard_map(
        body,
        mesh=mesh,
        in_specs=placed,
        out_specs=(P(None, ("row", "col")), P(None, ("row", "col"))),
        check_vma=False,
    )
```

```python
import functools

import jax
import jax.numpy as jnp
from jax import lax
from jax.experimental import pallas as pl
from jax.experimental.pallas import tpu as pltpu
from jax.sharding import PartitionSpec as P

graph_weight = 0.95
GROUP = 16
BATCH = 32
SPARE = 4
GRAM_TERMS = 3
PANEL = 8
BUILD_GRANT = 60 * 1024 * 1024
PRODUCT_GRANT = 40 * 1024 * 1024
SMALL_GRANT = 24 * 1024 * 1024


def dot_plain(left, right, **kwargs):
    return lax.dot_general(
        left, right, (((1,), (0,)), ((), ())), preferred_element_type=jnp.float32, **kwargs
    )


def dot_across(left, right, **kwargs):
    return lax.dot_general(
        left, right, (((1,), (1,)), ((), ())), preferred_element_type=jnp.float32, **kwargs
    )


exact_plain = functools.partial(dot_plain, precision=lax.Precision.HIGHEST)
exact_across = functools.partial(dot_across, precision=lax.Precision.HIGHEST)


def divided(number, size):
    if size & (size - 1):
        return lax.div(number, size), lax.rem(number, size)
    return number >> (size.bit_length() - 1), number & (size - 1)


def place_of(spots_ref, slot, col_blocks):
    return divided(spots_ref[0, 0, slot], col_blocks)


def group_count(live_ref, group):
    return (live_ref[0, 0] + group - 1) // group


def group_copy(source, target, sems, index, group):
    window = pl.ds(index * group, group)
    return pltpu.make_async_copy(source.at[window], target.at[window], sems.at[index])


def build_kernel(row_count, spots_ref, live_ref, index_hbm, value_hbm, block_hbm, *refs):
    row_outs = refs[:row_count]
    (
        col_out_ref,
        index_ref,
        value_ref,
        block_ref,
        row_ref,
        col_ref,
        index_sems,
        value_sems,
        block_sems,
    ) = refs[row_count:]
    per_seg = row_outs[0].shape[0]
    col_blocks = col_out_ref.shape[0]
    groups = group_count(live_ref, BATCH) * (BATCH // GROUP)

    def start_copies(index, _):
        group_copy(index_hbm, index_ref, index_sems, index, GROUP).start()
        group_copy(value_hbm, value_ref, value_sems, index, GROUP).start()
        return 0

    lax.fori_loop(0, groups, start_copies, 0)
    row_ref[...] = jnp.zeros_like(row_ref)
    col_ref[...] = jnp.zeros_like(col_ref)
    rows_16 = lax.broadcasted_iota(jnp.int32, (16, 128), 0)
    ones = jnp.ones((128, 128), jnp.bfloat16)
    zero = jnp.zeros((16, 128), jnp.bfloat16)

    def build_group(index, _):
        group_copy(index_hbm, index_ref, index_sems, index, GROUP).wait()
        group_copy(value_hbm, value_ref, value_sems, index, GROUP).wait()
        targets = [(rows_16 + 16 * part).astype(jnp.int16) for part in range(8)]
        for inside in range(GROUP):
            slot = index * GROUP + inside
            row_block, col_block = place_of(spots_ref, slot, col_blocks)
            active = (slot < live_ref[0, 0]).astype(jnp.float32)
            index_i32 = index_ref[slot]
            value_f32 = value_ref[slot].astype(jnp.float32) * active
            sums = [zero] * 8
            for entry in range(16):
                index_row = jnp.broadcast_to(index_i32[entry : entry + 1], (16, 128)).astype(
                    jnp.int16
                )
                value_row = jnp.broadcast_to(value_f32[entry : entry + 1], (16, 128)).astype(
                    jnp.bfloat16
                )
                for part in range(8):
                    sums[part] = sums[part] + jnp.where(
                        index_row == targets[part], value_row, zero
                    )
            block = jnp.concatenate(sums, axis=0)
            block_ref[slot] = block
            row_ref[row_block] += value_f32[:8] + value_f32[8:]
            col_ref[col_block] += dot_plain(block, ones)
        group_copy(block_ref, block_hbm, block_sems, index, GROUP).start()
        return 0

    lax.fori_loop(0, groups, build_group, 0)
    for ahead, out in enumerate(row_outs):
        first = lax.rem(lax.axis_index("row") + ahead, row_count) * per_seg
        for part in range(per_seg):
            out[part : part + 1] = jnp.sum(row_ref[first + part], axis=0, keepdims=True)
    diagonal = lax.broadcasted_iota(jnp.int32, (128, 128), 0) == lax.broadcasted_iota(
        jnp.int32, (128, 128), 1
    )
    for col_block in range(col_blocks):
        col_out_ref[col_block : col_block + 1] = jnp.sum(
            jnp.where(diagonal, col_ref[col_block], 0.0), axis=0, keepdims=True
        )

    def finish_copies(index, _):
        group_copy(block_ref, block_hbm, block_sems, index, GROUP).wait()
        return 0

    lax.fori_loop(0, groups, finish_copies, 0)


SCALARS = pl.BlockSpec(memory_space=pltpu.SMEM)
ANYWHERE = pl.BlockSpec(memory_space=pl.ANY)
IN_VMEM = pl.BlockSpec(memory_space=pltpu.VMEM)


def build_blocks(spots, live, index_table, value_table, row_count, col_count, per_seg):
    slots = index_table.shape[0]
    groups = slots // GROUP
    sum_shapes = [(per_seg, 128)] * row_count + [(col_count * per_seg, 128)]
    return pl.pallas_call(
        functools.partial(build_kernel, row_count),
        in_specs=[SCALARS, SCALARS, ANYWHERE, ANYWHERE],
        out_specs=[ANYWHERE] + [IN_VMEM] * len(sum_shapes),
        out_shape=[jax.ShapeDtypeStruct((SPARE * slots, 128, 128), jnp.bfloat16)]
        + [jax.ShapeDtypeStruct(shape, jnp.float32) for shape in sum_shapes],
        scratch_shapes=[
            pltpu.VMEM(index_table.shape, index_table.dtype),
            pltpu.VMEM(value_table.shape, value_table.dtype),
            pltpu.VMEM((slots, 128, 128), jnp.bfloat16),
            pltpu.VMEM((row_count * per_seg, 8, 128), jnp.float32),
            pltpu.VMEM((col_count * per_seg, 128, 128), jnp.float32),
            pltpu.SemaphoreType.DMA((groups,)),
            pltpu.SemaphoreType.DMA((groups,)),
            pltpu.SemaphoreType.DMA((groups,)),
        ],
        compiler_params=pltpu.CompilerParams(vmem_limit_bytes=BUILD_GRANT),
        name="build_blocks",
    )(spots, live, index_table, value_table)


def each_group(live_ref, block_hbm, block_ref, sems, prepare, run_group):
    groups = group_count(live_ref, BATCH)

    def start_copy(index, _):
        group_copy(block_hbm, block_ref, sems, index, BATCH).start()
        return 0

    lax.fori_loop(0, groups, start_copy, 0)
    prepare()

    def one_group(index, _):
        group_copy(block_hbm, block_ref, sems, index, BATCH).wait()
        run_group(index * BATCH)
        return 0

    lax.fori_loop(0, groups, one_group, 0)


def add_products(dot, places, first_slot, block_ref, direction, total_refs):
    sums = []
    for inside in range(BATCH):
        slot = first_slot + inside
        sums.append(dot(direction(places(slot)[0]), block_ref[slot]))
    for inside in range(BATCH):
        total_ref = total_refs[inside % len(total_refs)]
        total_ref[places(first_slot + inside)[1]] += sums[inside]


def fill_directions(pieces, dir_ref, mine, per_seg):
    for behind, piece in enumerate(pieces):
        first = lax.rem(mine + (len(pieces) - behind), len(pieces)) * per_seg
        for part in range(per_seg):
            dir_ref[first + part] = piece[part]


def backward_kernel(row_count, spots_ref, live_ref, block_hbm, *refs):
    row_pieces = refs[:row_count]
    col_out_ref, block_ref, sems, row_dir_ref, even_ref, odd_ref = refs[row_count:]
    per_seg = row_pieces[0].shape[0]
    col_blocks = even_ref.shape[0]

    def prepare():
        even_ref[...] = jnp.zeros_like(even_ref)
        odd_ref[...] = jnp.zeros_like(odd_ref)
        fill_directions(row_pieces, row_dir_ref, lax.axis_index("row"), per_seg)

    def run_group(first_slot):
        add_products(
            dot_across,
            lambda slot: place_of(spots_ref, slot, col_blocks),
            first_slot,
            block_ref,
            lambda row_block: row_dir_ref[row_block],
            [even_ref, odd_ref],
        )

    each_group(live_ref, block_hbm, block_ref, sems, prepare, run_group)
    for segment in range(col_out_ref.shape[0]):
        for part in range(per_seg):
            col_block = segment * per_seg + part
            values = even_ref[col_block] + odd_ref[col_block]
            col_out_ref[segment, part] = values.astype(col_out_ref.dtype)


def in_terms(values):
    terms = []
    for _ in range(GRAM_TERMS):
        terms.append(values.astype(jnp.bfloat16))
        values = values - terms[-1].astype(jnp.float32)
    return terms


def attach_kernel(col_dir_ref, total_ref, message_ref, gram_ref):
    col_count, per_seg, size, _ = total_ref.shape

    def add_segment(segment, gram):
        for part in range(per_seg):
            values = total_ref[segment, part]
            message_ref[segment, part] = values
            gram += dot_across(values, tall(col_dir_ref[segment, part]))
        return gram

    gram = lax.fori_loop(
        0, col_count, add_segment, jnp.zeros((size, 128), jnp.float32), unroll=4
    )
    together = jnp.zeros((size, 128), jnp.float32)
    for term, values in enumerate(in_terms(gram)):
        together = together + pltpu.roll(values.astype(jnp.float32), term * size, 1)
    for segment in range(col_count):
        message_ref[segment, per_seg] = together.astype(message_ref.dtype)
    gram_ref[...] = total_of(
        [
            col_dir_ref[segment, per_seg + term]
            for term in range(GRAM_TERMS)
            for segment in range(col_count)
        ]
    )


def forward_kernel(spots_ref, live_ref, block_hbm, col_dir_ref, *refs):
    *row_outs, block_ref, sems, even_ref, odd_ref = refs
    per_seg = row_outs[0].shape[0]
    col_blocks = col_dir_ref.shape[0] * per_seg

    def prepare():
        even_ref[...] = jnp.zeros_like(even_ref)
        odd_ref[...] = jnp.zeros_like(odd_ref)

    def run_group(first_slot):
        add_products(
            dot_plain,
            lambda slot: place_of(spots_ref, slot, col_blocks)[::-1],
            first_slot,
            block_ref,
            lambda col_block: col_dir_ref[divided(col_block, per_seg)],
            [even_ref, odd_ref],
        )

    each_group(live_ref, block_hbm, block_ref, sems, prepare, run_group)
    for ahead, out in enumerate(row_outs):
        first = lax.rem(lax.axis_index("row") + ahead, len(row_outs)) * per_seg
        for part in range(per_seg):
            values = even_ref[first + part] + odd_ref[first + part]
            out[part] = values.astype(out.dtype)


def over_blocks(kernel, name, places, blocks, inputs, outputs, scratch):
    slots = blocks.shape[0] // SPARE
    return pl.pallas_call(
        kernel,
        in_specs=[SCALARS, SCALARS, ANYWHERE] + [IN_VMEM] * len(inputs),
        out_specs=[IN_VMEM] * len(outputs),
        out_shape=outputs,
        scratch_shapes=[
            pltpu.VMEM((slots,) + blocks.shape[1:], blocks.dtype),
            pltpu.SemaphoreType.DMA((slots // BATCH,)),
        ]
        + scratch,
        compiler_params=pltpu.CompilerParams(vmem_limit_bytes=PRODUCT_GRANT),
        cost_estimate=pl.CostEstimate(
            flops=2 * slots * 32 * 128 * 128, bytes_accessed=2 * slots * 128 * 128, transcendentals=0
        ),
        name=name,
    )(*places, blocks, *inputs)


def backward_product(places, blocks, row_pieces, col_count):
    per_seg, rows, lanes = row_pieces[0].shape
    col_shape = (col_count * per_seg, rows, lanes)
    (total,) = over_blocks(
        functools.partial(backward_kernel, len(row_pieces)),
        "backward_product",
        places,
        blocks,
        row_pieces,
        [jax.ShapeDtypeStruct((col_count, per_seg, rows, lanes), jnp.bfloat16)],
        [
            pltpu.VMEM((len(row_pieces) * per_seg, rows, lanes), jnp.bfloat16),
            pltpu.VMEM(col_shape, jnp.float32),
            pltpu.VMEM(col_shape, jnp.float32),
        ],
    )
    return total


def forward_product(places, blocks, col_dirs, row_count, piece):
    row_shape = (row_count * piece[0],) + piece[1:]
    return over_blocks(
        forward_kernel,
        "forward_product",
        places,
        blocks,
        [col_dirs],
        [jax.ShapeDtypeStruct(piece, jnp.bfloat16)] * row_count,
        [pltpu.VMEM(row_shape, jnp.float32), pltpu.VMEM(row_shape, jnp.float32)],
    )


def total_of(values):
    total = values[0].astype(jnp.float32)
    for value in values[1:]:
        total = total + value.astype(jnp.float32)
    return total


def leading(ref):
    return [ref.at[index] for index in range(ref.shape[0])]


def start_kernel(*refs):
    *row_refs, col_ref, query_ref, scaling_ref, scaled_ref, copies_ref = refs
    degree = 1.0 + 0.5 * total_of([ref[...] for ref in [*row_refs, *leading(col_ref)]])
    scaling = 1.0 / jnp.sqrt(degree)
    scaling_ref[...] = scaling
    for part in range(scaling.shape[0]):
        scaled = (
            scaling[part : part + 1] * query_ref[:, part * 128 : part * 128 + 128]
        ).astype(jnp.bfloat16)
        scaled_ref[part] = scaled
        for copy in range(copies_ref.shape[0]):
            copies_ref[copy, part] = scaled


def scaled_sum(row_refs, col_ref, scaling_ref, part):
    scaling = scaling_ref[part : part + 1]
    total = total_of([ref[part] for ref in [*row_refs, *leading(col_ref)]])
    return scaling * (0.5 * total)


def middle_kernel(*refs):
    *row_refs, col_ref, scaling_ref, query_ref, first_ref, scaled_ref, copies_ref = refs
    size = query_ref.shape[0]
    pair_gram = jnp.zeros((2 * size, 128), jnp.float32)
    for part in range(scaling_ref.shape[0]):
        first = scaled_sum(row_refs, col_ref, scaling_ref, part)
        first_ref[part] = first
        scaled = (scaling_ref[part : part + 1] * first).astype(jnp.bfloat16)
        scaled_ref[part] = scaled
        for copy in range(copies_ref.shape[0]):
            copies_ref[copy, part] = scaled
        pair = jnp.concatenate(
            [query_ref[:, part * 128 : part * 128 + 128], first], axis=0
        )
        pair_gram += exact_across(pair, tall(pair))
    grams = beside(pair_gram[:size], pltpu.roll(window(pair_gram[size:], 1), size, 1))
    for term, values in enumerate(in_terms(grams)):
        for copy in range(copies_ref.shape[0]):
            copies_ref[copy, scaling_ref.shape[0] + term] = values


def tall(flat):
    rest = flat.shape[1] - flat.shape[0]
    return jnp.concatenate([flat, jnp.zeros((rest, flat.shape[1]), flat.dtype)], axis=0)


def flipped(flat):
    return tall(flat).T[: flat.shape[0]]


def times(left, right):
    return exact_plain(left, tall(right))


def beside(left, right):
    return left + pltpu.roll(right, left.shape[0], 1)


def stacked(upper, lower):
    rest = jnp.zeros((upper.shape[1] - 2 * upper.shape[0], upper.shape[1]), upper.dtype)
    return jnp.concatenate([upper, lower, rest], axis=0)


def sandwich(rows, middle):
    return exact_across(exact_plain(rows, middle), tall(rows))


def symmetric(flat):
    return 0.5 * (flat + flipped(flat))


def window(flat, place):
    size = flat.shape[0]
    if place:
        flat = pltpu.roll(flat, flat.shape[1] - place * size, 1)
    lanes = lax.broadcasted_iota(jnp.int32, flat.shape, 1)
    return jnp.where(lanes < size, flat, 0.0)


def solve_many(pairs):
    size = pairs[0][0].shape[0]
    systems = [matrix + pltpu.roll(side, size, 1) for matrix, side in pairs]
    sublanes = lax.broadcasted_iota(jnp.int32, systems[0].shape, 0)

    def eliminated(values, column, scale, pivot):
        row = values[pivot : pivot + 1, :] * scale
        return jnp.where(sublanes == pivot, row, values - column * row)

    for first in range(0, size, PANEL):
        panels = [
            [jnp.broadcast_to(system[:, at : at + 1], system.shape) for at in range(first, first + PANEL)]
            for system in systems
        ]
        for pivot in range(first, first + PANEL):
            for which, (column, *later) in enumerate(panels):
                scale = 1.0 / column[pivot : pivot + 1, :]
                panels[which] = [eliminated(other, column, scale, pivot) for other in later]
                systems[which] = eliminated(systems[which], column, scale, pivot)
    return [window(system, 1) for system in systems]


def close_kernel(*refs):
    row_count = (len(refs) - 6) // 2
    row_refs = refs[:row_count]
    gram_refs = refs[row_count : 2 * row_count]
    col_ref, scaling_ref, query_ref, first_ref, solution_ref, residual_ref = refs[-6:]
    size = query_ref.shape[0]
    weight = graph_weight
    total = total_of([ref[...] for ref in gram_refs])
    g00 = symmetric(window(total, 0))
    g01 = window(total, 1)
    g11 = symmetric(window(total, 2))
    g12 = symmetric(window(total, 3))
    eye = (
        lax.broadcasted_iota(jnp.int32, total.shape, 0)
        == lax.broadcasted_iota(jnp.int32, total.shape, 1)
    ).astype(jnp.float32)
    curve = symmetric(g00 - weight * g01)
    steps, inverse = solve_many([(curve, g00), (g00, eye)])
    steps_t = flipped(steps)
    plain_gram = stacked(beside(g00, g01), beside(flipped(g01), g11))
    through_gram = stacked(beside(g01, g11), beside(g11, g12))
    after_first = beside(eye - steps_t, weight * steps_t)
    new_gram = symmetric(sandwich(after_first, plain_gram))
    mixing = times(inverse, new_gram)
    direction = after_first + flipped(mixing)
    curve = symmetric(sandwich(direction, plain_gram - weight * through_gram))
    (steps,) = solve_many([(curve, new_gram)])
    steps_t2 = flipped(steps)
    applied = direction - weight * pltpu.roll(direction, size, 1)
    solution_rows = exact_plain(beside(eye, steps_t2), stacked(steps_t, direction))
    residual_rows = exact_plain(beside(eye, -steps_t2), stacked(after_first, applied))
    rows = jnp.concatenate([solution_rows, residual_rows], axis=0)
    for part in range(first_ref.shape[0]):
        lanes = slice(part * 128, part * 128 + 128)
        basis = jnp.concatenate(
            [
                query_ref[:, lanes],
                first_ref[part],
                scaled_sum(row_refs, col_ref, scaling_ref, part),
                jnp.zeros_like(eye),
            ],
            axis=0,
        )
        values = exact_plain(rows, basis)
        solution_ref[:, lanes] = values[:size]
        residual_ref[:, lanes] = values[size:]


def pass_around(pieces, axis):
    count = len(pieces)
    return [pieces[0]] + [
        lax.ppermute(pieces[ahead], axis, [(at, (at + ahead) % count) for at in range(count)])
        for ahead in range(1, count)
    ]


def exchange(pieces, axis):
    return lax.all_to_all(pieces, axis, 0, 0, tiled=True)


def simple_call(kernel, shapes, name, *operands):
    return pl.pallas_call(
        kernel,
        out_shape=shapes,
        compiler_params=pltpu.CompilerParams(vmem_limit_bytes=SMALL_GRANT),
        name=name,
    )(*operands)


def sum_kernel(col_ref, gram_ref, total_ref):
    col_count, sent, size, _ = col_ref.shape
    together = total_of([col_ref[segment, sent - 1] for segment in range(col_count)])
    last = total_of([window(together, term) for term in range(GRAM_TERMS)])
    total_ref[...] = gram_ref[...] + pltpu.roll(last, 3 * size, 1)


def body(queries, block_spots, live_blocks, neighbor_cols, neighbor_sims):
    row_count = lax.axis_size("row")
    col_count = lax.axis_size("col")
    query_rows, seg_len = queries.shape
    per_seg = seg_len // 128
    places = (block_spots, live_blocks)
    piece = (per_seg, query_rows, 128)
    wide = jax.ShapeDtypeStruct(piece, jnp.float32)
    narrow = jax.ShapeDtypeStruct(piece, jnp.bfloat16)
    copies = jax.ShapeDtypeStruct((col_count,) + piece, jnp.bfloat16)
    gram_shape = jax.ShapeDtypeStruct((query_rows, 128), jnp.float32)

    blocks, *row_sums, col_sums = build_blocks(
        *places, neighbor_cols[0, 0], neighbor_sims[0, 0], row_count, col_count, per_seg
    )
    col_part = exchange(col_sums.reshape(col_count, per_seg, 128), "col")
    row_parts = pass_around(row_sums, "row")
    scaling, scaled, scaled_copies = simple_call(
        start_kernel,
        [jax.ShapeDtypeStruct((per_seg, 128), jnp.float32), narrow, copies],
        "start",
        *row_parts,
        col_part,
        queries,
    )

    def product(vectors, vector_copies, with_grams):
        col_dirs = exchange(vector_copies, "col")
        row_pieces = pass_around([vectors] * row_count, "row")
        total = backward_product(places, blocks, row_pieces, col_count)
        gram = None
        if with_grams:
            message = jax.ShapeDtypeStruct((col_count, per_seg + 1) + piece[1:], jnp.bfloat16)
            total, gram = simple_call(
                attach_kernel, [message, gram_shape], "attach", col_dirs, total
            )
        col_part = exchange(total, "col")
        totals = forward_product(places, blocks, col_dirs, row_count, piece)
        return pass_around(totals, "row"), col_part, gram

    row_parts, col_part, _ = product(scaled, scaled_copies, False)
    more_copies = jax.ShapeDtypeStruct(
        (col_count, per_seg + GRAM_TERMS) + piece[1:], jnp.bfloat16
    )
    first, scaled, scaled_copies = simple_call(
        middle_kernel,
        [wide, narrow, more_copies],
        "middle",
        *row_parts,
        col_part,
        scaling,
        queries,
    )
    row_parts, col_part, gram = product(scaled, scaled_copies, True)
    (gram,) = simple_call(sum_kernel, [gram_shape], "gram_sum", col_part, gram)
    flat = jax.ShapeDtypeStruct(queries.shape, jnp.float32)
    return tuple(
        simple_call(
            close_kernel,
            [flat, flat],
            "close",
            *row_parts,
            *pass_around([gram] * row_count, "row"),
            col_part,
            scaling,
            queries,
            first,
        )
    )


def solution(mesh):
    placed = (
        P(None, ("row", "col")),
        P("row", "col", None),
        P("row", "col"),
        P("row", "col", None, None, None),
        P("row", "col", None, None, None),
    )
    return jax.shard_map(
        body,
        mesh=mesh,
        in_specs=placed,
        out_specs=(P(None, ("row", "col")), P(None, ("row", "col"))),
        check_vma=False,
    )
```

```python
import functools

import jax
import jax.numpy as jnp
from jax import lax
from jax.experimental import pallas as pl
from jax.experimental.pallas import tpu as pltpu
from jax.sharding import PartitionSpec as P

graph_weight = 0.95
GROUP = 16
BATCH = 32
SPARE = 4
GRAM_TERMS = 3
PANEL = 8
BUILD_GRANT = 60 * 1024 * 1024
PRODUCT_GRANT = 40 * 1024 * 1024
SMALL_GRANT = 24 * 1024 * 1024


def dot_plain(left, right, **kwargs):
    return lax.dot_general(
        left, right, (((1,), (0,)), ((), ())), preferred_element_type=jnp.float32, **kwargs
    )


def dot_across(left, right, **kwargs):
    return lax.dot_general(
        left, right, (((1,), (1,)), ((), ())), preferred_element_type=jnp.float32, **kwargs
    )


exact_plain = functools.partial(dot_plain, precision=lax.Precision.HIGHEST)
exact_across = functools.partial(dot_across, precision=lax.Precision.HIGHEST)


def divided(number, size):
    if size & (size - 1):
        return lax.div(number, size), lax.rem(number, size)
    return number >> (size.bit_length() - 1), number & (size - 1)


def place_of(spots_ref, slot, col_blocks):
    return divided(spots_ref[0, 0, slot], col_blocks)


def group_count(live_ref, group):
    return (live_ref[0, 0] + group - 1) // group


def group_copy(source, target, sems, index, group):
    window = pl.ds(index * group, group)
    return pltpu.make_async_copy(source.at[window], target.at[window], sems.at[index])


def build_kernel(spots_ref, live_ref, index_hbm, value_hbm, block_hbm, flipped_hbm, *refs):
    (
        *row_outs,
        col_out_ref,
        index_ref,
        value_ref,
        block_ref,
        flipped_ref,
        row_ref,
        col_ref,
        index_sems,
        value_sems,
        block_sems,
        flipped_sems,
    ) = refs
    row_count = len(row_outs) + 1
    per_seg = row_outs[0].shape[0]
    col_blocks = col_out_ref.shape[0]
    groups = group_count(live_ref, BATCH) * (BATCH // GROUP)

    def start_copies(index, _):
        group_copy(index_hbm, index_ref, index_sems, index, GROUP).start()
        group_copy(value_hbm, value_ref, value_sems, index, GROUP).start()
        return 0

    lax.fori_loop(0, groups, start_copies, 0)
    row_ref[...] = jnp.zeros_like(row_ref)
    col_ref[...] = jnp.zeros_like(col_ref)
    rows_16 = lax.broadcasted_iota(jnp.int32, (16, 128), 0)
    diagonal = lax.broadcasted_iota(jnp.int32, (128, 128), 0) == lax.broadcasted_iota(
        jnp.int32, (128, 128), 1
    )
    identity = jnp.where(diagonal, 1.0, 0.0).astype(jnp.bfloat16)
    zero = jnp.zeros((16, 128), jnp.bfloat16)

    def build_group(index, _):
        group_copy(index_hbm, index_ref, index_sems, index, GROUP).wait()
        group_copy(value_hbm, value_ref, value_sems, index, GROUP).wait()
        targets = [(rows_16 + 16 * part).astype(jnp.int16) for part in range(8)]
        for inside in range(GROUP):
            slot = index * GROUP + inside
            row_block, col_block = place_of(spots_ref, slot, col_blocks)
            active = (slot < live_ref[0, 0]).astype(jnp.float32)
            index_i32 = index_ref[slot]
            value_f32 = value_ref[slot].astype(jnp.float32) * active
            sums = [zero] * 8
            for entry in range(16):
                index_row = jnp.broadcast_to(index_i32[entry : entry + 1], (16, 128)).astype(
                    jnp.int16
                )
                value_row = jnp.broadcast_to(value_f32[entry : entry + 1], (16, 128)).astype(
                    jnp.bfloat16
                )
                for part in range(8):
                    sums[part] = sums[part] + jnp.where(
                        index_row == targets[part], value_row, zero
                    )
            block = jnp.concatenate(sums, axis=0)
            block_ref[slot] = block
            row_ref[row_block] += value_f32[:8] + value_f32[8:]
            turned = dot_across(identity, block)
            flipped_ref[slot] = turned.astype(jnp.bfloat16)
            col_ref[col_block] += jnp.sum(turned.reshape(16, 8, 128), axis=0)
        group_copy(block_ref, block_hbm, block_sems, index, GROUP).start()
        group_copy(flipped_ref, flipped_hbm, flipped_sems, index, GROUP).start()
        return 0

    lax.fori_loop(0, groups, build_group, 0)
    for ahead, out in enumerate(row_outs, 1):
        first = lax.rem(lax.axis_index("row") + ahead, row_count) * per_seg
        for part in range(per_seg):
            out[part : part + 1] = jnp.sum(row_ref[first + part], axis=0, keepdims=True)
    for part in range(per_seg):
        own = lax.axis_index("col") * per_seg + part
        col_ref[own] += row_ref[lax.axis_index("row") * per_seg + part]
    for col_block in range(col_blocks):
        col_out_ref[col_block : col_block + 1] = jnp.sum(
            col_ref[col_block], axis=0, keepdims=True
        )

    def finish_copies(index, _):
        group_copy(block_ref, block_hbm, block_sems, index, GROUP).wait()
        group_copy(flipped_ref, flipped_hbm, flipped_sems, index, GROUP).wait()
        return 0

    lax.fori_loop(0, groups, finish_copies, 0)


SCALARS = pl.BlockSpec(memory_space=pltpu.SMEM)
ANYWHERE = pl.BlockSpec(memory_space=pl.ANY)
IN_VMEM = pl.BlockSpec(memory_space=pltpu.VMEM)


def build_blocks(spots, live, index_table, value_table, row_count, col_count, per_seg):
    slots = index_table.shape[0]
    groups = slots // GROUP
    sum_shapes = [(per_seg, 128)] * (row_count - 1) + [(col_count * per_seg, 128)]
    return pl.pallas_call(
        build_kernel,
        in_specs=[SCALARS, SCALARS, ANYWHERE, ANYWHERE],
        out_specs=[ANYWHERE] * 2 + [IN_VMEM] * len(sum_shapes),
        out_shape=[jax.ShapeDtypeStruct((SPARE * slots, 128, 128), jnp.bfloat16)] * 2
        + [jax.ShapeDtypeStruct(shape, jnp.float32) for shape in sum_shapes],
        scratch_shapes=[
            pltpu.VMEM(index_table.shape, index_table.dtype),
            pltpu.VMEM(value_table.shape, value_table.dtype),
            pltpu.VMEM((slots, 128, 128), jnp.bfloat16),
            pltpu.VMEM((slots, 128, 128), jnp.bfloat16),
            pltpu.VMEM((row_count * per_seg, 8, 128), jnp.float32),
            pltpu.VMEM((col_count * per_seg, 8, 128), jnp.float32),
            pltpu.SemaphoreType.DMA((groups,)),
            pltpu.SemaphoreType.DMA((groups,)),
            pltpu.SemaphoreType.DMA((groups,)),
            pltpu.SemaphoreType.DMA((groups,)),
        ],
        compiler_params=pltpu.CompilerParams(vmem_limit_bytes=BUILD_GRANT),
        name="build_blocks",
    )(spots, live, index_table, value_table)


def each_group(live_ref, block_hbm, block_ref, sems, prepare, run_group):
    groups = group_count(live_ref, BATCH)

    def start_copy(index, _):
        group_copy(block_hbm, block_ref, sems, index, BATCH).start()
        return 0

    lax.fori_loop(0, groups, start_copy, 0)
    prepare()

    def one_group(index, _):
        group_copy(block_hbm, block_ref, sems, index, BATCH).wait()
        run_group(index * BATCH)
        return 0

    lax.fori_loop(0, groups, one_group, 0)


def add_products(places, first_slot, block_ref, direction, total_refs):
    sums = []
    for inside in range(BATCH):
        slot = first_slot + inside
        sums.append(dot_plain(direction(places(slot)[0]), block_ref[slot]))
    for inside in range(BATCH):
        total_ref = total_refs[inside % len(total_refs)]
        total_ref[places(first_slot + inside)[1]] += sums[inside]


def fill_directions(pieces, dir_ref, mine, per_seg):
    for behind, piece in enumerate(pieces):
        first = lax.rem(mine + (len(pieces) - behind), len(pieces)) * per_seg
        for part in range(per_seg):
            dir_ref[first + part] = piece[part]


def backward_kernel(row_count, spots_ref, live_ref, block_hbm, *refs):
    row_pieces = refs[:row_count]
    col_out_ref, block_ref, sems, row_dir_ref, even_ref, odd_ref = refs[row_count:]
    per_seg = row_pieces[0].shape[0]
    col_blocks = even_ref.shape[0]

    def prepare():
        even_ref[...] = jnp.zeros_like(even_ref)
        odd_ref[...] = jnp.zeros_like(odd_ref)
        fill_directions(row_pieces, row_dir_ref, lax.axis_index("row"), per_seg)

    def run_group(first_slot):
        add_products(
            lambda slot: place_of(spots_ref, slot, col_blocks),
            first_slot,
            block_ref,
            lambda row_block: row_dir_ref[row_block],
            [even_ref, odd_ref],
        )

    each_group(live_ref, block_hbm, block_ref, sems, prepare, run_group)
    for segment in range(col_out_ref.shape[0]):
        for part in range(per_seg):
            col_block = segment * per_seg + part
            values = even_ref[col_block] + odd_ref[col_block]
            col_out_ref[segment, part] = values.astype(col_out_ref.dtype)


def in_terms(values):
    terms = []
    for _ in range(GRAM_TERMS):
        terms.append(values.astype(jnp.bfloat16))
        values = values - terms[-1].astype(jnp.float32)
    return terms


def attach_kernel(col_dir_ref, total_ref, message_ref, gram_ref):
    col_count, per_seg, size, _ = total_ref.shape

    def add_segment(segment, gram):
        for part in range(per_seg):
            values = total_ref[segment, part]
            message_ref[segment, part] = values
            gram += dot_across(values, tall(col_dir_ref[segment, part]))
        return gram

    gram = lax.fori_loop(
        0, col_count, add_segment, jnp.zeros((size, 128), jnp.float32), unroll=4
    )
    together = jnp.zeros((size, 128), jnp.float32)
    for term, values in enumerate(in_terms(gram)):
        together = together + pltpu.roll(values.astype(jnp.float32), term * size, 1)
    for segment in range(col_count):
        message_ref[segment, per_seg] = together.astype(message_ref.dtype)
    gram_ref[...] = total_of(
        [
            col_dir_ref[segment, per_seg + term]
            for term in range(GRAM_TERMS)
            for segment in range(col_count)
        ]
    )


def forward_kernel(spots_ref, live_ref, block_hbm, col_dir_ref, *refs):
    *row_outs, block_ref, sems, even_ref, odd_ref = refs
    per_seg = row_outs[0].shape[0]
    col_blocks = col_dir_ref.shape[0] * per_seg

    def prepare():
        even_ref[...] = jnp.zeros_like(even_ref)
        odd_ref[...] = jnp.zeros_like(odd_ref)

    def run_group(first_slot):
        add_products(
            lambda slot: place_of(spots_ref, slot, col_blocks)[::-1],
            first_slot,
            block_ref,
            lambda col_block: col_dir_ref[divided(col_block, per_seg)],
            [even_ref, odd_ref],
        )

    each_group(live_ref, block_hbm, block_ref, sems, prepare, run_group)
    for ahead, out in enumerate(row_outs):
        first = lax.rem(lax.axis_index("row") + ahead, len(row_outs)) * per_seg
        for part in range(per_seg):
            values = even_ref[first + part] + odd_ref[first + part]
            out[part] = values.astype(out.dtype)


def over_blocks(kernel, name, places, blocks, inputs, outputs, scratch):
    slots = blocks.shape[0] // SPARE
    return pl.pallas_call(
        kernel,
        in_specs=[SCALARS, SCALARS, ANYWHERE] + [IN_VMEM] * len(inputs),
        out_specs=[IN_VMEM] * len(outputs),
        out_shape=outputs,
        scratch_shapes=[
            pltpu.VMEM((slots,) + blocks.shape[1:], blocks.dtype),
            pltpu.SemaphoreType.DMA((slots // BATCH,)),
        ]
        + scratch,
        compiler_params=pltpu.CompilerParams(vmem_limit_bytes=PRODUCT_GRANT),
        cost_estimate=pl.CostEstimate(
            flops=2 * slots * 32 * 128 * 128, bytes_accessed=2 * slots * 128 * 128, transcendentals=0
        ),
        name=name,
    )(*places, blocks, *inputs)


def backward_product(places, blocks, row_pieces, col_count):
    per_seg, rows, lanes = row_pieces[0].shape
    col_shape = (col_count * per_seg, rows, lanes)
    (total,) = over_blocks(
        functools.partial(backward_kernel, len(row_pieces)),
        "backward_product",
        places,
        blocks,
        row_pieces,
        [jax.ShapeDtypeStruct((col_count, per_seg, rows, lanes), jnp.bfloat16)],
        [
            pltpu.VMEM((len(row_pieces) * per_seg, rows, lanes), jnp.bfloat16),
            pltpu.VMEM(col_shape, jnp.float32),
            pltpu.VMEM(col_shape, jnp.float32),
        ],
    )
    return total


def forward_product(places, blocks, col_dirs, row_count, piece):
    row_shape = (row_count * piece[0],) + piece[1:]
    return over_blocks(
        forward_kernel,
        "forward_product",
        places,
        blocks,
        [col_dirs],
        [jax.ShapeDtypeStruct(piece, jnp.bfloat16)] * row_count,
        [pltpu.VMEM(row_shape, jnp.float32), pltpu.VMEM(row_shape, jnp.float32)],
    )


def total_of(values):
    total = values[0].astype(jnp.float32)
    for value in values[1:]:
        total = total + value.astype(jnp.float32)
    return total


def leading(ref):
    return [ref.at[index] for index in range(ref.shape[0])]


def start_kernel(*refs):
    *row_refs, col_ref, query_ref, scaling_ref, scaled_ref = refs
    degree = 1.0 + 0.5 * total_of([ref[...] for ref in [*row_refs, *leading(col_ref)]])
    scaling = 1.0 / jnp.sqrt(degree)
    scaling_ref[...] = scaling
    for part in range(scaling.shape[0]):
        scaled = (
            scaling[part : part + 1] * query_ref[:, part * 128 : part * 128 + 128]
        ).astype(jnp.bfloat16)
        scaled_ref[part] = scaled


def scaled_sum(row_refs, col_ref, scaling_ref, part):
    scaling = scaling_ref[part : part + 1]
    total = total_of([ref[part] for ref in [*row_refs, *leading(col_ref)]])
    return scaling * (0.5 * total)


def middle_kernel(*refs):
    *row_refs, col_ref, scaling_ref, query_ref, first_ref, scaled_ref, sent_ref = refs
    size = query_ref.shape[0]
    pair_gram = jnp.zeros((2 * size, 128), jnp.float32)
    for part in range(scaling_ref.shape[0]):
        first = scaled_sum(row_refs, col_ref, scaling_ref, part)
        first_ref[part] = first
        scaled = (scaling_ref[part : part + 1] * first).astype(jnp.bfloat16)
        scaled_ref[part] = scaled
        sent_ref[part] = scaled
        pair = jnp.concatenate(
            [query_ref[:, part * 128 : part * 128 + 128], first], axis=0
        )
        pair_gram += exact_across(pair, tall(pair))
    grams = beside(pair_gram[:size], pltpu.roll(window(pair_gram[size:], 1), size, 1))
    for term, values in enumerate(in_terms(grams)):
        sent_ref[scaling_ref.shape[0] + term] = values


def tall(flat):
    rest = flat.shape[1] - flat.shape[0]
    return jnp.concatenate([flat, jnp.zeros((rest, flat.shape[1]), flat.dtype)], axis=0)


def flipped(flat):
    return tall(flat).T[: flat.shape[0]]


def times(left, right):
    return exact_plain(left, tall(right))


def beside(left, right):
    return left + pltpu.roll(right, left.shape[0], 1)


def stacked(upper, lower):
    rest = jnp.zeros((upper.shape[1] - 2 * upper.shape[0], upper.shape[1]), upper.dtype)
    return jnp.concatenate([upper, lower, rest], axis=0)


def sandwich(rows, middle):
    return exact_across(exact_plain(rows, middle), tall(rows))


def symmetric(flat):
    return 0.5 * (flat + flipped(flat))


def window(flat, place):
    size = flat.shape[0]
    if place:
        flat = pltpu.roll(flat, flat.shape[1] - place * size, 1)
    lanes = lax.broadcasted_iota(jnp.int32, flat.shape, 1)
    return jnp.where(lanes < size, flat, 0.0)


def solve_many(pairs):
    size = pairs[0][0].shape[0]
    systems = [matrix + pltpu.roll(side, size, 1) for matrix, side in pairs]
    sublanes = lax.broadcasted_iota(jnp.int32, systems[0].shape, 0)

    def eliminated(values, column, scale, pivot):
        row = values[pivot : pivot + 1, :] * scale
        return jnp.where(sublanes == pivot, row, values - column * row)

    for first in range(0, size, PANEL):
        panels = [
            [jnp.broadcast_to(system[:, at : at + 1], system.shape) for at in range(first, first + PANEL)]
            for system in systems
        ]
        for pivot in range(first, first + PANEL):
            for which, (column, *later) in enumerate(panels):
                scale = 1.0 / column[pivot : pivot + 1, :]
                panels[which] = [eliminated(other, column, scale, pivot) for other in later]
                systems[which] = eliminated(systems[which], column, scale, pivot)
    return [window(system, 1) for system in systems]


def close_kernel(*refs):
    row_count = (len(refs) - 6) // 2
    row_refs = refs[:row_count]
    gram_refs = refs[row_count : 2 * row_count]
    col_ref, scaling_ref, query_ref, first_ref, solution_ref, residual_ref = refs[-6:]
    size = query_ref.shape[0]
    weight = graph_weight
    total = total_of([ref[...] for ref in gram_refs])
    g00 = symmetric(window(total, 0))
    g01 = window(total, 1)
    g11 = symmetric(window(total, 2))
    g12 = symmetric(window(total, 3))
    eye = (
        lax.broadcasted_iota(jnp.int32, total.shape, 0)
        == lax.broadcasted_iota(jnp.int32, total.shape, 1)
    ).astype(jnp.float32)
    curve = symmetric(g00 - weight * g01)
    steps, inverse = solve_many([(curve, g00), (g00, eye)])
    steps_t = flipped(steps)
    plain_gram = stacked(beside(g00, g01), beside(flipped(g01), g11))
    through_gram = stacked(beside(g01, g11), beside(g11, g12))
    after_first = beside(eye - steps_t, weight * steps_t)
    new_gram = symmetric(sandwich(after_first, plain_gram))
    mixing = times(inverse, new_gram)
    direction = after_first + flipped(mixing)
    curve = symmetric(sandwich(direction, plain_gram - weight * through_gram))
    (steps,) = solve_many([(curve, new_gram)])
    steps_t2 = flipped(steps)
    applied = direction - weight * pltpu.roll(direction, size, 1)
    solution_rows = exact_plain(beside(eye, steps_t2), stacked(steps_t, direction))
    residual_rows = exact_plain(beside(eye, -steps_t2), stacked(after_first, applied))
    rows = jnp.concatenate([solution_rows, residual_rows], axis=0)
    for part in range(first_ref.shape[0]):
        lanes = slice(part * 128, part * 128 + 128)
        basis = jnp.concatenate(
            [
                query_ref[:, lanes],
                first_ref[part],
                scaled_sum(row_refs, col_ref, scaling_ref, part),
                jnp.zeros_like(eye),
            ],
            axis=0,
        )
        values = exact_plain(rows, basis)
        solution_ref[:, lanes] = values[:size]
        residual_ref[:, lanes] = values[size:]


def pass_around(pieces, axis):
    count = len(pieces)
    return [pieces[0]] + [
        lax.ppermute(pieces[ahead], axis, [(at, (at + ahead) % count) for at in range(count)])
        for ahead in range(1, count)
    ]


def exchange(pieces, axis):
    return lax.all_to_all(pieces, axis, 0, 0, tiled=True)


def simple_call(kernel, shapes, name, *operands):
    return pl.pallas_call(
        kernel,
        out_shape=shapes,
        compiler_params=pltpu.CompilerParams(vmem_limit_bytes=SMALL_GRANT),
        name=name,
    )(*operands)


def sum_kernel(col_ref, gram_ref, total_ref):
    col_count, sent, size, _ = col_ref.shape
    together = total_of([col_ref[segment, sent - 1] for segment in range(col_count)])
    last = total_of([window(together, term) for term in range(GRAM_TERMS)])
    total_ref[...] = gram_ref[...] + pltpu.roll(last, 3 * size, 1)


def body(queries, block_spots, live_blocks, neighbor_cols, neighbor_sims):
    row_count = lax.axis_size("row")
    col_count = lax.axis_size("col")
    query_rows, seg_len = queries.shape
    per_seg = seg_len // 128
    places = (block_spots, live_blocks)
    piece = (per_seg, query_rows, 128)
    wide = jax.ShapeDtypeStruct(piece, jnp.float32)
    narrow = jax.ShapeDtypeStruct(piece, jnp.bfloat16)
    gram_shape = jax.ShapeDtypeStruct((query_rows, 128), jnp.float32)

    blocks, flipped_blocks, *row_sums, col_sums = build_blocks(
        *places, neighbor_cols[0, 0], neighbor_sims[0, 0], row_count, col_count, per_seg
    )
    col_part = exchange(col_sums.reshape(col_count, per_seg, 128), "col")
    row_parts = pass_around([None, *row_sums], "row")[1:]
    scaling, scaled = simple_call(
        start_kernel,
        [jax.ShapeDtypeStruct((per_seg, 128), jnp.float32), narrow],
        "start",
        *row_parts,
        col_part,
        queries,
    )

    def product(vectors, sent, with_grams):
        row_pieces = pass_around([vectors] * row_count, "row")
        col_dirs = exchange(jnp.broadcast_to(sent[None], (col_count,) + sent.shape), "col")
        total = backward_product(places, flipped_blocks, row_pieces, col_count)
        gram = None
        if with_grams:
            message = jax.ShapeDtypeStruct((col_count, per_seg + 1) + piece[1:], jnp.bfloat16)
            total, gram = simple_call(
                attach_kernel, [message, gram_shape], "attach", col_dirs, total
            )
        col_part = exchange(total, "col")
        totals = forward_product(places, blocks, col_dirs, row_count, piece)
        return pass_around(totals, "row"), col_part, gram

    row_parts, col_part, _ = product(scaled, scaled, False)
    more = jax.ShapeDtypeStruct((per_seg + GRAM_TERMS,) + piece[1:], jnp.bfloat16)
    first, scaled, sent = simple_call(
        middle_kernel,
        [wide, narrow, more],
        "middle",
        *row_parts,
        col_part,
        scaling,
        queries,
    )
    row_parts, col_part, gram = product(scaled, sent, True)
    (gram,) = simple_call(sum_kernel, [gram_shape], "gram_sum", col_part, gram)
    flat = jax.ShapeDtypeStruct(queries.shape, jnp.float32)
    return tuple(
        simple_call(
            close_kernel,
            [flat, flat],
            "close",
            *row_parts,
            *pass_around([gram] * row_count, "row"),
            col_part,
            scaling,
            queries,
            first,
        )
    )


def solution(mesh):
    placed = (
        P(None, ("row", "col")),
        P("row", "col", None),
        P("row", "col"),
        P("row", "col", None, None, None),
        P("row", "col", None, None, None),
    )
    return jax.shard_map(
        body,
        mesh=mesh,
        in_specs=placed,
        out_specs=(P(None, ("row", "col")), P(None, ("row", "col"))),
        check_vma=False,
    )
```

```python
import functools

import jax
import jax.numpy as jnp
from jax import lax
from jax.experimental import pallas as pl
from jax.experimental.pallas import tpu as pltpu
from jax.sharding import PartitionSpec as P

graph_weight = 0.95
GROUP = 16
BATCH = 32
SPARE = 4
PANEL = 8
BUILD_GRANT = 60 * 1024 * 1024
PRODUCT_GRANT = 40 * 1024 * 1024
SMALL_GRANT = 24 * 1024 * 1024


def dot_plain(left, right, **kwargs):
    return lax.dot_general(
        left, right, (((1,), (0,)), ((), ())), preferred_element_type=jnp.float32, **kwargs
    )


def dot_across(left, right, **kwargs):
    return lax.dot_general(
        left, right, (((1,), (1,)), ((), ())), preferred_element_type=jnp.float32, **kwargs
    )


exact_plain = functools.partial(dot_plain, precision=lax.Precision.HIGHEST)
exact_across = functools.partial(dot_across, precision=lax.Precision.HIGHEST)


def divided(number, size):
    if size & (size - 1):
        return lax.div(number, size), lax.rem(number, size)
    return number >> (size.bit_length() - 1), number & (size - 1)


def place_of(spots_ref, slot, col_blocks):
    return divided(spots_ref[0, 0, slot], col_blocks)


def group_count(live_ref, group):
    return (live_ref[0, 0] + group - 1) // group


def group_copy(source, target, sems, index, group):
    window = pl.ds(index * group, group)
    return pltpu.make_async_copy(source.at[window], target.at[window], sems.at[index])


def build_kernel(
    spots_ref, live_ref, index_hbm, value_hbm, query_hbm, block_hbm, flipped_hbm, *refs
):
    (
        *row_outs,
        col_out_ref,
        gram_ref,
        query_ref,
        index_ref,
        value_ref,
        block_ref,
        flipped_ref,
        row_ref,
        col_ref,
        index_sems,
        value_sems,
        block_sems,
        flipped_sems,
        query_sem,
    ) = refs
    row_count = len(row_outs) + 1
    per_seg = row_outs[0].shape[0]
    col_blocks = col_out_ref.shape[0]
    groups = group_count(live_ref, BATCH) * (BATCH // GROUP)

    def start_copies(index, _):
        group_copy(index_hbm, index_ref, index_sems, index, GROUP).start()
        group_copy(value_hbm, value_ref, value_sems, index, GROUP).start()
        return 0

    query_copy = pltpu.make_async_copy(query_hbm, query_ref, query_sem)
    query_copy.start()
    lax.fori_loop(0, groups, start_copies, 0)
    row_ref[...] = jnp.zeros_like(row_ref)
    col_ref[...] = jnp.zeros_like(col_ref)
    rows_16 = lax.broadcasted_iota(jnp.int32, (16, 128), 0)
    diagonal = lax.broadcasted_iota(jnp.int32, (128, 128), 0) == lax.broadcasted_iota(
        jnp.int32, (128, 128), 1
    )
    identity = jnp.where(diagonal, 1.0, 0.0).astype(jnp.bfloat16)
    zero = jnp.zeros((16, 128), jnp.bfloat16)

    def build_group(index, _):
        group_copy(index_hbm, index_ref, index_sems, index, GROUP).wait()
        group_copy(value_hbm, value_ref, value_sems, index, GROUP).wait()
        targets = [(rows_16 + 16 * part).astype(jnp.int16) for part in range(8)]
        for inside in range(0, GROUP, 2):
            slots = [index * GROUP + inside, index * GROUP + inside + 1]
            tables = []
            for slot in slots:
                active = (slot < live_ref[0, 0]).astype(jnp.float32)
                tables.append((index_ref[slot], value_ref[slot].astype(jnp.float32) * active))
            sums = [[zero] * 8 for _ in slots]
            for entry in range(0, 16, 2):
                for which, (indices, values) in enumerate(tables):
                    pair = []
                    for at in (entry, entry + 1):
                        index_row = jnp.broadcast_to(indices[at : at + 1], (16, 128))
                        value_row = jnp.broadcast_to(values[at : at + 1], (16, 128))
                        pair.append((index_row.astype(jnp.int16), value_row.astype(jnp.bfloat16)))
                    for part in range(8):
                        first, second = [
                            jnp.where(index_row == targets[part], value_row, zero)
                            for index_row, value_row in pair
                        ]
                        sums[which][part] = sums[which][part] + (first + second)
            for slot, (_, values), parts in zip(slots, tables, sums):
                row_block, col_block = place_of(spots_ref, slot, col_blocks)
                block = jnp.concatenate(parts, axis=0)
                block_ref[slot] = block
                row_ref[row_block] += values[:8] + values[8:]
                turned = dot_across(identity, block)
                flipped_ref[slot] = turned.astype(jnp.bfloat16)
                col_ref[col_block] += jnp.sum(turned.reshape(16, 8, 128), axis=0)
        group_copy(block_ref, block_hbm, block_sems, index, GROUP).start()
        group_copy(flipped_ref, flipped_hbm, flipped_sems, index, GROUP).start()
        return 0

    query_copy.wait()
    size = query_ref.shape[0]
    gram = jnp.zeros((size, 128), jnp.float32)
    for part in range(per_seg):
        query = query_ref[:, part * 128 : part * 128 + 128]
        gram += exact_across(query, tall(query))
    gram_ref[...] = side_by_side(in_terms(gram, 3))

    lax.fori_loop(0, groups, build_group, 0)
    for ahead, out in enumerate(row_outs, 1):
        first = lax.rem(lax.axis_index("row") + ahead, row_count) * per_seg
        for part in range(per_seg):
            out[part : part + 1] = jnp.sum(row_ref[first + part], axis=0, keepdims=True)
    for part in range(per_seg):
        own = lax.axis_index("col") * per_seg + part
        col_ref[own] += row_ref[lax.axis_index("row") * per_seg + part]
    for col_block in range(col_blocks):
        col_out_ref[col_block : col_block + 1] = jnp.sum(
            col_ref[col_block], axis=0, keepdims=True
        )

    def finish_copies(index, _):
        group_copy(block_ref, block_hbm, block_sems, index, GROUP).wait()
        group_copy(flipped_ref, flipped_hbm, flipped_sems, index, GROUP).wait()
        return 0

    lax.fori_loop(0, groups, finish_copies, 0)


SCALARS = pl.BlockSpec(memory_space=pltpu.SMEM)
ANYWHERE = pl.BlockSpec(memory_space=pl.ANY)
IN_VMEM = pl.BlockSpec(memory_space=pltpu.VMEM)


def build_blocks(
    spots, live, index_table, value_table, queries, row_count, col_count, per_seg
):
    slots = index_table.shape[0]
    groups = slots // GROUP
    sum_shapes = [(per_seg, 128)] * (row_count - 1) + [(col_count * per_seg, 128)]
    gram_shape = (queries.shape[0], 128)
    return pl.pallas_call(
        build_kernel,
        in_specs=[SCALARS, SCALARS, ANYWHERE, ANYWHERE, ANYWHERE],
        out_specs=[ANYWHERE] * 2 + [IN_VMEM] * (len(sum_shapes) + 1),
        out_shape=[jax.ShapeDtypeStruct((SPARE * slots, 128, 128), jnp.bfloat16)] * 2
        + [jax.ShapeDtypeStruct(shape, jnp.float32) for shape in sum_shapes]
        + [jax.ShapeDtypeStruct(gram_shape, jnp.bfloat16)],
        scratch_shapes=[
            pltpu.VMEM(queries.shape, queries.dtype),
            pltpu.VMEM(index_table.shape, index_table.dtype),
            pltpu.VMEM(value_table.shape, value_table.dtype),
            pltpu.VMEM((slots, 128, 128), jnp.bfloat16),
            pltpu.VMEM((slots, 128, 128), jnp.bfloat16),
            pltpu.VMEM((row_count * per_seg, 8, 128), jnp.float32),
            pltpu.VMEM((col_count * per_seg, 8, 128), jnp.float32),
            pltpu.SemaphoreType.DMA((groups,)),
            pltpu.SemaphoreType.DMA((groups,)),
            pltpu.SemaphoreType.DMA((groups,)),
            pltpu.SemaphoreType.DMA((groups,)),
            pltpu.SemaphoreType.DMA(()),
        ],
        compiler_params=pltpu.CompilerParams(vmem_limit_bytes=BUILD_GRANT),
        name="build_blocks",
    )(spots, live, index_table, value_table, queries)


def each_group(live_ref, block_hbm, block_ref, sems, prepare, run_group):
    groups = group_count(live_ref, BATCH)

    def start_copy(index, _):
        group_copy(block_hbm, block_ref, sems, index, BATCH).start()
        return 0

    lax.fori_loop(0, groups, start_copy, 0)
    prepare()

    def one_group(index, _):
        group_copy(block_hbm, block_ref, sems, index, BATCH).wait()
        run_group(index * BATCH)
        return 0

    lax.fori_loop(0, groups, one_group, 0)


def add_products(places, first_slot, block_ref, direction, total_refs):
    sums = []
    for inside in range(BATCH):
        slot = first_slot + inside
        sums.append(dot_plain(direction(places(slot)[0]), block_ref[slot]))
    for inside in range(BATCH):
        total_ref = total_refs[inside % len(total_refs)]
        total_ref[places(first_slot + inside)[1]] += sums[inside]


def fill_directions(pieces, dir_ref, mine, per_seg):
    for behind, piece in enumerate(pieces):
        first = lax.rem(mine + (len(pieces) - behind), len(pieces)) * per_seg
        for part in range(per_seg):
            dir_ref[first + part] = piece[part]


def backward_kernel(row_count, spots_ref, live_ref, block_hbm, *refs):
    row_pieces = refs[:row_count]
    col_out_ref, block_ref, sems, row_dir_ref, even_ref, odd_ref = refs[row_count:]
    per_seg = row_pieces[0].shape[0]
    col_blocks = even_ref.shape[0]

    def prepare():
        even_ref[...] = jnp.zeros_like(even_ref)
        odd_ref[...] = jnp.zeros_like(odd_ref)
        fill_directions(row_pieces, row_dir_ref, lax.axis_index("row"), per_seg)

    def run_group(first_slot):
        add_products(
            lambda slot: place_of(spots_ref, slot, col_blocks),
            first_slot,
            block_ref,
            lambda row_block: row_dir_ref[row_block],
            [even_ref, odd_ref],
        )

    each_group(live_ref, block_hbm, block_ref, sems, prepare, run_group)
    size = even_ref.shape[1]
    for segment in range(col_out_ref.shape[0]):
        for part in range(per_seg):
            col_block = segment * per_seg + part
            values = even_ref[col_block] + odd_ref[col_block]
            col_out_ref[segment, part * size : part * size + size] = values.astype(
                col_out_ref.dtype
            )


def in_terms(values, count):
    terms = []
    for _ in range(count):
        terms.append(values.astype(jnp.bfloat16))
        values = values - terms[-1].astype(jnp.float32)
    return terms


def side_by_side(terms, width=32):
    total = terms[0].astype(jnp.float32)
    for place, term in enumerate(terms[1:], 1):
        total = total + pltpu.roll(term.astype(jnp.float32), place * width, 1)
    return total.astype(jnp.bfloat16)


def attach_kernel(first_dir_ref, col_dir_ref, total_ref, message_ref, gram_ref):
    col_count, sent, size, _ = col_dir_ref.shape
    per_seg = sent - 1

    def add_segment(segment, gram):
        for part in range(per_seg):
            rows = slice(part * size, part * size + size)
            values = total_ref[segment, rows]
            message_ref[segment, rows] = values
            gram += dot_across(values, tall(col_dir_ref[segment, part]))
        return gram

    gram = lax.fori_loop(
        0, col_count, add_segment, jnp.zeros((size, 128), jnp.float32), unroll=4
    )
    half = size // 2
    terms = side_by_side(in_terms(gram, 2)).astype(jnp.float32)
    folded = terms[:half] + pltpu.roll(terms[half:], 64, 1)
    for segment in range(col_count):
        message_ref[segment, per_seg * size :] = folded.astype(message_ref.dtype)
    queries = total_of([first_dir_ref[segment, per_seg] for segment in range(col_count)])
    queries = total_of([window(queries, term) for term in range(3)])
    pairs = total_of([col_dir_ref[segment, per_seg] for segment in range(col_count)])
    lanes = lax.broadcasted_iota(jnp.int32, pairs.shape, 1)
    pairs = jnp.where(lanes < 2 * size, pairs + pltpu.roll(pairs, 128 - 2 * size, 1), 0.0)
    gram_ref[...] = beside(queries, pairs)


def forward_kernel(spots_ref, live_ref, block_hbm, col_dir_ref, *refs):
    *row_outs, block_ref, sems, even_ref, odd_ref = refs
    per_seg = row_outs[0].shape[0]
    col_blocks = col_dir_ref.shape[0] * per_seg

    def prepare():
        even_ref[...] = jnp.zeros_like(even_ref)
        odd_ref[...] = jnp.zeros_like(odd_ref)

    def run_group(first_slot):
        add_products(
            lambda slot: place_of(spots_ref, slot, col_blocks)[::-1],
            first_slot,
            block_ref,
            lambda col_block: col_dir_ref[divided(col_block, per_seg)],
            [even_ref, odd_ref],
        )

    each_group(live_ref, block_hbm, block_ref, sems, prepare, run_group)
    for ahead, out in enumerate(row_outs):
        first = lax.rem(lax.axis_index("row") + ahead, len(row_outs)) * per_seg
        for part in range(per_seg):
            values = even_ref[first + part] + odd_ref[first + part]
            out[part] = values.astype(out.dtype)


def over_blocks(kernel, name, places, blocks, inputs, outputs, scratch):
    slots = blocks.shape[0] // SPARE
    return pl.pallas_call(
        kernel,
        in_specs=[SCALARS, SCALARS, ANYWHERE] + [IN_VMEM] * len(inputs),
        out_specs=[IN_VMEM] * len(outputs),
        out_shape=outputs,
        scratch_shapes=[
            pltpu.VMEM((slots,) + blocks.shape[1:], blocks.dtype),
            pltpu.SemaphoreType.DMA((slots // BATCH,)),
        ]
        + scratch,
        compiler_params=pltpu.CompilerParams(vmem_limit_bytes=PRODUCT_GRANT),
        cost_estimate=pl.CostEstimate(
            flops=2 * slots * 32 * 128 * 128, bytes_accessed=2 * slots * 128 * 128, transcendentals=0
        ),
        name=name,
    )(*places, blocks, *inputs)


def backward_product(places, blocks, row_pieces, col_count):
    per_seg, rows, lanes = row_pieces[0].shape
    col_shape = (col_count * per_seg, rows, lanes)
    (total,) = over_blocks(
        functools.partial(backward_kernel, len(row_pieces)),
        "backward_product",
        places,
        blocks,
        row_pieces,
        [jax.ShapeDtypeStruct((col_count, per_seg * rows, lanes), jnp.bfloat16)],
        [
            pltpu.VMEM((len(row_pieces) * per_seg, rows, lanes), jnp.bfloat16),
            pltpu.VMEM(col_shape, jnp.float32),
            pltpu.VMEM(col_shape, jnp.float32),
        ],
    )
    return total


def forward_product(places, blocks, col_dirs, row_count, piece):
    row_shape = (row_count * piece[0],) + piece[1:]
    return over_blocks(
        forward_kernel,
        "forward_product",
        places,
        blocks,
        [col_dirs],
        [jax.ShapeDtypeStruct(piece, jnp.bfloat16)] * row_count,
        [pltpu.VMEM(row_shape, jnp.float32), pltpu.VMEM(row_shape, jnp.float32)],
    )


def total_of(values):
    total = values[0].astype(jnp.float32)
    for value in values[1:]:
        total = total + value.astype(jnp.float32)
    return total


def leading(ref):
    return [ref.at[index] for index in range(ref.shape[0])]


def start_kernel(*refs):
    *row_refs, col_ref, query_ref, scaling_ref, scaled_ref = refs
    degree = 1.0 + 0.5 * total_of([ref[...] for ref in [*row_refs, *leading(col_ref)]])
    scaling = 1.0 / jnp.sqrt(degree)
    scaling_ref[...] = scaling
    for part in range(scaling.shape[0]):
        scaled = (
            scaling[part : part + 1] * query_ref[:, part * 128 : part * 128 + 128]
        ).astype(jnp.bfloat16)
        scaled_ref[part] = scaled


def spread_kernel(scaled_ref, gram_ref, after_ref, copies_ref):
    for copy in range(copies_ref.shape[0]):
        copies_ref[copy, : scaled_ref.shape[0]] = scaled_ref[...]
        copies_ref[copy, scaled_ref.shape[0]] = gram_ref[...]


def scaled_sum(row_refs, col_ref, scaling_ref, part):
    scaling = scaling_ref[part : part + 1]
    size = row_refs[0].shape[1]
    rows = slice(part * size, part * size + size)
    total = total_of([ref[part] for ref in row_refs] + [ref[rows] for ref in leading(col_ref)])
    return scaling * (0.5 * total)


def middle_kernel(*refs):
    *row_refs, col_ref, scaling_ref, query_ref, first_ref, scaled_ref, copies_ref = refs
    size = query_ref.shape[0]
    per_seg = scaling_ref.shape[0]
    grams = jnp.zeros((size, 128), jnp.float32)
    for part in range(per_seg):
        first = scaled_sum(row_refs, col_ref, scaling_ref, part)
        first_ref[part] = first
        scaled = (scaling_ref[part : part + 1] * first).astype(jnp.bfloat16)
        scaled_ref[part] = scaled
        for copy in range(copies_ref.shape[0]):
            copies_ref[copy, part] = scaled
        query = query_ref[:, part * 128 : part * 128 + 128]
        grams += exact_across(first, stacked(query, first))
    terms = side_by_side(in_terms(grams, 2), 2 * size)
    for copy in range(copies_ref.shape[0]):
        copies_ref[copy, per_seg] = terms


def tall(flat):
    rest = flat.shape[1] - flat.shape[0]
    return jnp.concatenate([flat, jnp.zeros((rest, flat.shape[1]), flat.dtype)], axis=0)


def flipped(flat):
    return tall(flat).T[: flat.shape[0]]


def times(left, right):
    return exact_plain(left, tall(right))


def beside(left, right):
    return left + pltpu.roll(right, left.shape[0], 1)


def stacked(upper, lower):
    rest = jnp.zeros((upper.shape[1] - 2 * upper.shape[0], upper.shape[1]), upper.dtype)
    return jnp.concatenate([upper, lower, rest], axis=0)


def sandwich(rows, middle):
    return exact_across(exact_plain(rows, middle), tall(rows))


def symmetric(flat):
    return 0.5 * (flat + flipped(flat))


def window(flat, place, size=None):
    size = size or flat.shape[0]
    if place:
        flat = pltpu.roll(flat, flat.shape[1] - place * size, 1)
    lanes = lax.broadcasted_iota(jnp.int32, flat.shape, 1)
    return jnp.where(lanes < size, flat, 0.0)


def solve_many(pairs):
    size = pairs[0][0].shape[0]
    systems = [matrix + pltpu.roll(side, size, 1) for matrix, side in pairs]
    sublanes = lax.broadcasted_iota(jnp.int32, systems[0].shape, 0)

    def eliminated(values, column, scale, pivot):
        row = values[pivot : pivot + 1, :] * scale
        return jnp.where(sublanes == pivot, row, values - column * row)

    for first in range(0, size, PANEL):
        panels = [
            [jnp.broadcast_to(system[:, at : at + 1], system.shape) for at in range(first, first + PANEL)]
            for system in systems
        ]
        for pivot in range(first, first + PANEL):
            for which, (column, *later) in enumerate(panels):
                scale = 1.0 / column[pivot : pivot + 1, :]
                panels[which] = [eliminated(other, column, scale, pivot) for other in later]
                systems[which] = eliminated(systems[which], column, scale, pivot)
    return [window(system, 1) for system in systems]


def close_kernel(*refs):
    row_count = (len(refs) - 6) // 2
    row_refs = refs[:row_count]
    gram_refs = refs[row_count : 2 * row_count]
    col_ref, scaling_ref, query_ref, first_ref, solution_ref, residual_ref = refs[-6:]
    size = query_ref.shape[0]
    weight = graph_weight
    total = total_of([ref[...] for ref in gram_refs])
    g00 = symmetric(window(total, 0))
    g01 = flipped(window(total, 1))
    g11 = symmetric(window(total, 2))
    g12 = symmetric(window(total, 3))
    eye = (
        lax.broadcasted_iota(jnp.int32, total.shape, 0)
        == lax.broadcasted_iota(jnp.int32, total.shape, 1)
    ).astype(jnp.float32)
    curve = symmetric(g00 - weight * g01)
    steps, inverse = solve_many([(curve, g00), (g00, eye)])
    steps_t = flipped(steps)
    plain_gram = stacked(beside(g00, g01), beside(flipped(g01), g11))
    through_gram = stacked(beside(g01, g11), beside(g11, g12))
    after_first = beside(eye - steps_t, weight * steps_t)
    new_gram = symmetric(sandwich(after_first, plain_gram))
    mixing = times(inverse, new_gram)
    direction = after_first + flipped(mixing)
    curve = symmetric(sandwich(direction, plain_gram - weight * through_gram))
    (steps,) = solve_many([(curve, new_gram)])
    steps_t2 = flipped(steps)
    applied = direction - weight * pltpu.roll(direction, size, 1)
    solution_rows = exact_plain(beside(eye, steps_t2), stacked(steps_t, direction))
    residual_rows = exact_plain(beside(eye, -steps_t2), stacked(after_first, applied))
    rows = jnp.concatenate([solution_rows, residual_rows], axis=0)
    for part in range(first_ref.shape[0]):
        lanes = slice(part * 128, part * 128 + 128)
        basis = jnp.concatenate(
            [
                query_ref[:, lanes],
                first_ref[part],
                scaled_sum(row_refs, col_ref, scaling_ref, part),
                jnp.zeros_like(eye),
            ],
            axis=0,
        )
        values = exact_plain(rows, basis)
        solution_ref[:, lanes] = values[:size]
        residual_ref[:, lanes] = values[size:]


def pass_around(pieces, axis):
    count = len(pieces)
    return [pieces[0]] + [
        lax.ppermute(pieces[ahead], axis, [(at, (at + ahead) % count) for at in range(count)])
        for ahead in range(1, count)
    ]


def exchange(pieces, axis):
    return lax.all_to_all(pieces, axis, 0, 0, tiled=True)


def simple_call(kernel, shapes, name, *operands):
    return pl.pallas_call(
        kernel,
        out_shape=shapes,
        compiler_params=pltpu.CompilerParams(vmem_limit_bytes=SMALL_GRANT),
        name=name,
    )(*operands)


def sum_kernel(col_ref, gram_ref, total_ref):
    size = gram_ref.shape[0]
    col_count, sent, _ = col_ref.shape
    folded = total_of([col_ref[segment, sent - size // 2 :] for segment in range(col_count)])
    upper = window(folded, 0, size) + window(folded, 1, size)
    lower = window(folded, 2, size) + window(folded, 3, size)
    last = jnp.concatenate([upper, lower], axis=0)
    total_ref[...] = gram_ref[...] + pltpu.roll(last, 3 * size, 1)


def body(queries, block_spots, live_blocks, neighbor_cols, neighbor_sims):
    row_count = lax.axis_size("row")
    col_count = lax.axis_size("col")
    query_rows, seg_len = queries.shape
    per_seg = seg_len // 128
    places = (block_spots, live_blocks)
    piece = (per_seg, query_rows, 128)
    wide = jax.ShapeDtypeStruct(piece, jnp.float32)
    narrow = jax.ShapeDtypeStruct(piece, jnp.bfloat16)
    gram_shape = jax.ShapeDtypeStruct((query_rows, 128), jnp.float32)

    message = jax.ShapeDtypeStruct((col_count, per_seg + 1) + piece[1:], jnp.bfloat16)

    blocks, flipped_blocks, *row_sums, col_sums, query_gram = build_blocks(
        *places,
        neighbor_cols[0, 0],
        neighbor_sims[0, 0],
        queries,
        row_count,
        col_count,
        per_seg,
    )
    col_part = exchange(col_sums.reshape(col_count, per_seg, 128), "col")
    row_parts = pass_around([None, *row_sums], "row")[1:]
    scaling, scaled = simple_call(
        start_kernel,
        [jax.ShapeDtypeStruct((per_seg, 128), jnp.float32), narrow],
        "start",
        *row_parts,
        col_part,
        queries,
    )

    row_pieces = pass_around([scaled] * row_count, "row")
    (copies,) = simple_call(
        spread_kernel, [message], "spread", scaled, query_gram, row_pieces[-1]
    )
    first_dirs = exchange(copies, "col")
    total = backward_product(places, flipped_blocks, row_pieces, col_count)
    col_part = exchange(total, "col")
    totals = forward_product(places, blocks, first_dirs, row_count, piece)
    first, scaled, copies = simple_call(
        middle_kernel,
        [wide, narrow, message],
        "middle",
        *pass_around(totals, "row"),
        col_part,
        scaling,
        queries,
    )

    col_dirs = exchange(copies, "col")
    row_pieces = pass_around([scaled] * row_count, "row")
    total = backward_product(places, flipped_blocks, row_pieces, col_count)
    more = jax.ShapeDtypeStruct(
        (col_count, total.shape[1] + query_rows // 2, 128), jnp.bfloat16
    )
    total, gram = simple_call(
        attach_kernel, [more, gram_shape], "attach", first_dirs, col_dirs, total
    )
    col_part = exchange(total, "col")
    totals = forward_product(places, blocks, col_dirs, row_count, piece)
    row_parts = pass_around(totals, "row")
    (gram,) = simple_call(sum_kernel, [gram_shape], "gram_sum", col_part, gram)
    flat = jax.ShapeDtypeStruct(queries.shape, jnp.float32)
    return tuple(
        simple_call(
            close_kernel,
            [flat, flat],
            "close",
            *row_parts,
            *pass_around([gram] * row_count, "row"),
            col_part,
            scaling,
            queries,
            first,
        )
    )


def solution(mesh):
    placed = (
        P(None, ("row", "col")),
        P("row", "col", None),
        P("row", "col"),
        P("row", "col", None, None, None),
        P("row", "col", None, None, None),
    )
    return jax.shard_map(
        body,
        mesh=mesh,
        in_specs=placed,
        out_specs=(P(None, ("row", "col")), P(None, ("row", "col"))),
        check_vma=False,
    )
```

```python
import functools

import jax
import jax.numpy as jnp
from jax import lax
from jax.experimental import pallas as pl
from jax.experimental.pallas import tpu as pltpu
from jax.sharding import PartitionSpec as P

graph_weight = 0.95
GROUP = 16
BATCH = 32
SPARE = 4
PANEL = 8
BUILD_GRANT = 60 * 1024 * 1024
PRODUCT_GRANT = 40 * 1024 * 1024
SMALL_GRANT = 24 * 1024 * 1024


def dot_plain(left, right, **kwargs):
    return lax.dot_general(
        left, right, (((1,), (0,)), ((), ())), preferred_element_type=jnp.float32, **kwargs
    )


def dot_across(left, right, **kwargs):
    return lax.dot_general(
        left, right, (((1,), (1,)), ((), ())), preferred_element_type=jnp.float32, **kwargs
    )


exact_plain = functools.partial(dot_plain, precision=lax.Precision.HIGHEST)
exact_across = functools.partial(dot_across, precision=lax.Precision.HIGHEST)


def divided(number, size):
    if size & (size - 1):
        return lax.div(number, size), lax.rem(number, size)
    return number >> (size.bit_length() - 1), number & (size - 1)


def place_of(places, slot, col_blocks):
    return divided(places[0][0, 0, slot], col_blocks)


def live_count(places):
    return places[1][0, 0]


def group_count(places, group):
    return (live_count(places) + group - 1) // group


def group_copy(source, target, sems, index, group):
    window = pl.ds(index * group, group)
    return pltpu.make_async_copy(source.at[window], target.at[window], sems.at[index])


def build_kernel(
    spots_ref, live_ref, index_hbm, value_hbm, block_hbm, flipped_hbm, *refs
):
    (
        *row_outs,
        col_out_ref,
        index_ref,
        value_ref,
        block_ref,
        flipped_ref,
        row_ref,
        col_ref,
        index_sems,
        value_sems,
        block_sems,
        flipped_sems,
    ) = refs
    places = (spots_ref, live_ref)
    row_count = len(row_outs) + 1
    per_seg = row_outs[0].shape[0]
    col_blocks = col_out_ref.shape[0]
    groups = group_count(places, BATCH) * (BATCH // GROUP)

    def start_copies(index, _):
        group_copy(index_hbm, index_ref, index_sems, index, GROUP).start()
        group_copy(value_hbm, value_ref, value_sems, index, GROUP).start()
        return 0

    lax.fori_loop(0, groups, start_copies, 0)
    row_ref[...] = jnp.zeros_like(row_ref)
    col_ref[...] = jnp.zeros_like(col_ref)
    rows_16 = lax.broadcasted_iota(jnp.int32, (16, 128), 0)
    diagonal = lax.broadcasted_iota(jnp.int32, (128, 128), 0) == lax.broadcasted_iota(
        jnp.int32, (128, 128), 1
    )
    identity = jnp.where(diagonal, 1.0, 0.0).astype(jnp.bfloat16)
    ones = (lax.broadcasted_iota(jnp.int32, (8, 128), 0) == 0).astype(jnp.bfloat16)
    zero = jnp.zeros((16, 128), jnp.bfloat16)

    def build_group(index, _):
        group_copy(index_hbm, index_ref, index_sems, index, GROUP).wait()
        group_copy(value_hbm, value_ref, value_sems, index, GROUP).wait()
        targets = [(rows_16 + 16 * part).astype(jnp.int16) for part in range(8)]
        for inside in range(0, GROUP, 2):
            slots = [index * GROUP + inside, index * GROUP + inside + 1]
            tables = []
            for slot in slots:
                active = (slot < live_count(places)).astype(jnp.float32)
                tables.append((index_ref[slot], value_ref[slot].astype(jnp.float32) * active))
            sums = [[zero] * 8 for _ in slots]
            for entry in range(0, 16, 2):
                for which, (indices, values) in enumerate(tables):
                    pair = []
                    for at in (entry, entry + 1):
                        index_row = jnp.broadcast_to(indices[at : at + 1], (16, 128))
                        value_row = jnp.broadcast_to(values[at : at + 1], (16, 128))
                        pair.append((index_row.astype(jnp.int16), value_row.astype(jnp.bfloat16)))
                    for part in range(8):
                        first, second = [
                            jnp.where(index_row == targets[part], value_row, zero)
                            for index_row, value_row in pair
                        ]
                        sums[which][part] = sums[which][part] + (first + second)
            for slot, (_, values), parts in zip(slots, tables, sums):
                row_block, col_block = place_of(places, slot, col_blocks)
                block = jnp.concatenate(parts, axis=0)
                block_ref[slot] = block
                row_ref[row_block] += values[:8] + values[8:]
                turned = dot_across(identity, block)
                turned = turned.astype(jnp.bfloat16)
                flipped_ref[slot] = turned
                col_ref[col_block] += dot_plain(ones, turned)
        group_copy(block_ref, block_hbm, block_sems, index, GROUP).start()
        group_copy(flipped_ref, flipped_hbm, flipped_sems, index, GROUP).start()
        return 0

    lax.fori_loop(0, groups, build_group, 0)
    for ahead, out in enumerate(row_outs, 1):
        first = lax.rem(lax.axis_index("row") + ahead, row_count) * per_seg
        for part in range(per_seg):
            out[part : part + 1] = jnp.sum(row_ref[first + part], axis=0, keepdims=True)
    for part in range(per_seg):
        own = lax.axis_index("col") * per_seg + part
        col_ref[own] += row_ref[lax.axis_index("row") * per_seg + part]
    for col_block in range(col_blocks):
        col_out_ref[col_block : col_block + 1] = jnp.sum(
            col_ref[col_block], axis=0, keepdims=True
        )

    def finish_copies(index, _):
        group_copy(block_ref, block_hbm, block_sems, index, GROUP).wait()
        group_copy(flipped_ref, flipped_hbm, flipped_sems, index, GROUP).wait()
        return 0

    lax.fori_loop(0, groups, finish_copies, 0)


SCALARS = pl.BlockSpec(memory_space=pltpu.SMEM)
ANYWHERE = pl.BlockSpec(memory_space=pl.ANY)
IN_VMEM = pl.BlockSpec(memory_space=pltpu.VMEM)


def build_blocks(
    places, index_table, value_table, row_count, col_count, per_seg
):
    slots = index_table.shape[0]
    groups = slots // GROUP
    sum_shapes = [(per_seg, 128)] * (row_count - 1) + [(col_count * per_seg, 128)]
    return pl.pallas_call(
        build_kernel,
        in_specs=[SCALARS, SCALARS, ANYWHERE, ANYWHERE],
        out_specs=[ANYWHERE] * 2 + [IN_VMEM] * len(sum_shapes),
        out_shape=[jax.ShapeDtypeStruct((SPARE * slots, 128, 128), jnp.bfloat16)] * 2
        + [jax.ShapeDtypeStruct(shape, jnp.float32) for shape in sum_shapes],
        scratch_shapes=[
            pltpu.VMEM(index_table.shape, index_table.dtype),
            pltpu.VMEM(value_table.shape, value_table.dtype),
            pltpu.VMEM((slots, 128, 128), jnp.bfloat16),
            pltpu.VMEM((slots, 128, 128), jnp.bfloat16),
            pltpu.VMEM((row_count * per_seg, 8, 128), jnp.float32),
            pltpu.VMEM((col_count * per_seg, 8, 128), jnp.float32),
            pltpu.SemaphoreType.DMA((groups,)),
            pltpu.SemaphoreType.DMA((groups,)),
            pltpu.SemaphoreType.DMA((groups,)),
            pltpu.SemaphoreType.DMA((groups,)),
        ],
        compiler_params=pltpu.CompilerParams(vmem_limit_bytes=BUILD_GRANT),
        name="build_blocks",
    )(*places, index_table, value_table)


def each_group(places, block_hbm, block_ref, sems, prepare, run_group):
    groups = group_count(places, BATCH)

    def start_copy(index, _):
        group_copy(block_hbm, block_ref, sems, index, BATCH).start()
        return 0

    lax.fori_loop(0, groups, start_copy, 0)
    prepare()

    def one_group(index, _):
        group_copy(block_hbm, block_ref, sems, index, BATCH).wait()
        run_group(index * BATCH)
        return 0

    lax.fori_loop(0, groups, one_group, 0)


def add_products(places, first_slot, block_ref, direction, total_refs):
    sums = []
    for inside in range(BATCH):
        slot = first_slot + inside
        sums.append(dot_plain(direction(places(slot)[0]), block_ref[slot]))
    for inside in range(BATCH):
        total_ref = total_refs[inside % len(total_refs)]
        total_ref[places(first_slot + inside)[1]] += sums[inside]


def fill_directions(pieces, dir_ref, mine, per_seg):
    for behind, piece in enumerate(pieces):
        first = lax.rem(mine + (len(pieces) - behind), len(pieces)) * per_seg
        for part in range(per_seg):
            dir_ref[first + part] = piece[part]


def backward_kernel(row_count, spots_ref, live_ref, block_hbm, *refs):
    places = (spots_ref, live_ref)
    row_pieces = refs[:row_count]
    col_out_ref, block_ref, sems, row_dir_ref, even_ref, odd_ref = refs[row_count:]
    per_seg = row_pieces[0].shape[0]
    col_blocks = even_ref.shape[0]

    def prepare():
        even_ref[...] = jnp.zeros_like(even_ref)
        odd_ref[...] = jnp.zeros_like(odd_ref)
        fill_directions(row_pieces, row_dir_ref, lax.axis_index("row"), per_seg)

    def run_group(first_slot):
        add_products(
            lambda slot: place_of(places, slot, col_blocks),
            first_slot,
            block_ref,
            lambda row_block: row_dir_ref[row_block],
            [even_ref, odd_ref],
        )

    each_group(places, block_hbm, block_ref, sems, prepare, run_group)
    size = even_ref.shape[1]
    for segment in range(col_out_ref.shape[0]):
        for part in range(per_seg):
            col_block = segment * per_seg + part
            values = even_ref[col_block] + odd_ref[col_block]
            col_out_ref[segment, part * size : part * size + size] = values.astype(
                col_out_ref.dtype
            )


def in_terms(values, count):
    terms = []
    for _ in range(count):
        terms.append(values.astype(jnp.bfloat16))
        values = values - terms[-1].astype(jnp.float32)
    return terms


def side_by_side(terms, width=32):
    total = terms[0].astype(jnp.float32)
    for place, term in enumerate(terms[1:], 1):
        total = total + pltpu.roll(term.astype(jnp.float32), place * width, 1)
    return total.astype(jnp.bfloat16)


def attach_kernel(first_dir_ref, col_dir_ref, total_ref, message_ref, gram_ref):
    col_count, sent, size, _ = col_dir_ref.shape
    per_seg = sent - 1

    def add_segment(segment, gram):
        for part in range(per_seg):
            rows = slice(part * size, part * size + size)
            values = total_ref[segment, rows]
            message_ref[segment, rows] = values
            gram += dot_across(values, tall(col_dir_ref[segment, part]))
        return gram

    gram = lax.fori_loop(
        0, col_count, add_segment, jnp.zeros((size, 128), jnp.float32), unroll=4
    )
    half = size // 2
    terms = side_by_side(in_terms(gram, 2)).astype(jnp.float32)
    folded = terms[:half] + pltpu.roll(terms[half:], 64, 1)
    for segment in range(col_count):
        message_ref[segment, per_seg * size :] = folded.astype(message_ref.dtype)
    queries = total_of([first_dir_ref[segment, per_seg] for segment in range(col_count)])
    queries = total_of([window(queries, term) for term in range(3)])
    pairs = total_of([col_dir_ref[segment, per_seg] for segment in range(col_count)])
    lanes = lax.broadcasted_iota(jnp.int32, pairs.shape, 1)
    pairs = jnp.where(lanes < 2 * size, pairs + pltpu.roll(pairs, 128 - 2 * size, 1), 0.0)
    gram_ref[...] = beside(queries, pairs)


def forward_kernel(spots_ref, live_ref, block_hbm, col_dir_ref, *refs):
    places = (spots_ref, live_ref)
    *row_outs, block_ref, sems, even_ref, odd_ref = refs
    per_seg = row_outs[0].shape[0]
    col_blocks = col_dir_ref.shape[0] * per_seg

    def prepare():
        even_ref[...] = jnp.zeros_like(even_ref)
        odd_ref[...] = jnp.zeros_like(odd_ref)

    def run_group(first_slot):
        add_products(
            lambda slot: place_of(places, slot, col_blocks)[::-1],
            first_slot,
            block_ref,
            lambda col_block: col_dir_ref[divided(col_block, per_seg)],
            [even_ref, odd_ref],
        )

    each_group(places, block_hbm, block_ref, sems, prepare, run_group)
    for ahead, out in enumerate(row_outs):
        first = lax.rem(lax.axis_index("row") + ahead, len(row_outs)) * per_seg
        for part in range(per_seg):
            values = even_ref[first + part] + odd_ref[first + part]
            out[part] = values.astype(out.dtype)


def over_blocks(kernel, name, places, blocks, inputs, outputs, scratch):
    slots = blocks.shape[0] // SPARE
    return pl.pallas_call(
        kernel,
        in_specs=[SCALARS, SCALARS, ANYWHERE] + [IN_VMEM] * len(inputs),
        out_specs=[IN_VMEM] * len(outputs),
        out_shape=outputs,
        scratch_shapes=[
            pltpu.VMEM((slots,) + blocks.shape[1:], blocks.dtype),
            pltpu.SemaphoreType.DMA((slots // BATCH,)),
        ]
        + scratch,
        compiler_params=pltpu.CompilerParams(vmem_limit_bytes=PRODUCT_GRANT),
        cost_estimate=pl.CostEstimate(
            flops=2 * slots * 32 * 128 * 128, bytes_accessed=2 * slots * 128 * 128, transcendentals=0
        ),
        name=name,
    )(*places, blocks, *inputs)


def backward_product(places, blocks, row_pieces, col_count):
    per_seg, rows, lanes = row_pieces[0].shape
    col_shape = (col_count * per_seg, rows, lanes)
    (total,) = over_blocks(
        functools.partial(backward_kernel, len(row_pieces)),
        "backward_product",
        places,
        blocks,
        row_pieces,
        [jax.ShapeDtypeStruct((col_count, per_seg * rows, lanes), jnp.bfloat16)],
        [
            pltpu.VMEM((len(row_pieces) * per_seg, rows, lanes), jnp.bfloat16),
            pltpu.VMEM(col_shape, jnp.float32),
            pltpu.VMEM(col_shape, jnp.float32),
        ],
    )
    return total


def forward_product(places, blocks, col_dirs, row_count, piece):
    row_shape = (row_count * piece[0],) + piece[1:]
    return over_blocks(
        forward_kernel,
        "forward_product",
        places,
        blocks,
        [col_dirs],
        [jax.ShapeDtypeStruct(piece, jnp.bfloat16)] * row_count,
        [pltpu.VMEM(row_shape, jnp.float32), pltpu.VMEM(row_shape, jnp.float32)],
    )


def total_of(values):
    total = values[0].astype(jnp.float32)
    for value in values[1:]:
        total = total + value.astype(jnp.float32)
    return total


def leading(ref):
    return [ref.at[index] for index in range(ref.shape[0])]


def start_kernel(*refs):
    *row_refs, col_ref, query_ref, scaling_ref, scaled_ref = refs
    degree = 1.0 + 0.5 * total_of([ref[...] for ref in [*row_refs, *leading(col_ref)]])
    scaling = 1.0 / jnp.sqrt(degree)
    scaling_ref[...] = scaling
    for part in range(scaling.shape[0]):
        scaled = (
            scaling[part : part + 1] * query_ref[:, part * 128 : part * 128 + 128]
        ).astype(jnp.bfloat16)
        scaled_ref[part] = scaled


def spread_kernel(scaled_ref, query_ref, copies_ref):
    per_seg, size, _ = scaled_ref.shape
    gram = jnp.zeros((size, 128), jnp.float32)
    for part in range(per_seg):
        query = query_ref[:, part * 128 : part * 128 + 128]
        gram += exact_across(query, tall(query))
    terms = side_by_side(in_terms(gram, 3))
    for copy in range(copies_ref.shape[0]):
        copies_ref[copy, :per_seg] = scaled_ref[...]
        copies_ref[copy, per_seg] = terms


def scaled_sum(row_refs, col_ref, scaling_ref, part):
    scaling = scaling_ref[part : part + 1]
    size = row_refs[0].shape[1]
    rows = slice(part * size, part * size + size)
    total = total_of([ref[part] for ref in row_refs] + [ref[rows] for ref in leading(col_ref)])
    return scaling * (0.5 * total)


def middle_kernel(*refs):
    *row_refs, col_ref, scaling_ref, query_ref, first_ref, scaled_ref, copies_ref = refs
    size = query_ref.shape[0]
    per_seg = scaling_ref.shape[0]
    grams = jnp.zeros((size, 128), jnp.float32)
    for part in range(per_seg):
        first = scaled_sum(row_refs, col_ref, scaling_ref, part)
        first_ref[part] = first
        scaled = (scaling_ref[part : part + 1] * first).astype(jnp.bfloat16)
        scaled_ref[part] = scaled
        for copy in range(copies_ref.shape[0]):
            copies_ref[copy, part] = scaled
        query = query_ref[:, part * 128 : part * 128 + 128]
        grams += exact_across(first, stacked(query, first))
    terms = side_by_side(in_terms(grams, 2), 2 * size)
    for copy in range(copies_ref.shape[0]):
        copies_ref[copy, per_seg] = terms


def tall(flat):
    rest = flat.shape[1] - flat.shape[0]
    return jnp.concatenate([flat, jnp.zeros((rest, flat.shape[1]), flat.dtype)], axis=0)


def flipped(flat):
    return tall(flat).T[: flat.shape[0]]


def times(left, right):
    return exact_plain(left, tall(right))


def beside(left, right):
    return left + pltpu.roll(right, left.shape[0], 1)


def stacked(upper, lower):
    rest = jnp.zeros((upper.shape[1] - 2 * upper.shape[0], upper.shape[1]), upper.dtype)
    return jnp.concatenate([upper, lower, rest], axis=0)


def sandwich(rows, middle):
    return exact_across(exact_plain(rows, middle), tall(rows))


def symmetric(flat):
    return 0.5 * (flat + flipped(flat))


def window(flat, place, size=None):
    size = size or flat.shape[0]
    if place:
        flat = pltpu.roll(flat, flat.shape[1] - place * size, 1)
    lanes = lax.broadcasted_iota(jnp.int32, flat.shape, 1)
    return jnp.where(lanes < size, flat, 0.0)


def solve_many(pairs):
    size = pairs[0][0].shape[0]
    systems = [matrix + pltpu.roll(side, size, 1) for matrix, side in pairs]
    sublanes = lax.broadcasted_iota(jnp.int32, systems[0].shape, 0)

    def eliminated(values, column, scale, pivot):
        row = values[pivot : pivot + 1, :] * scale
        return jnp.where(sublanes == pivot, row, values - column * row)

    for first in range(0, size, PANEL):
        panels = [
            [jnp.broadcast_to(system[:, at : at + 1], system.shape) for at in range(first, first + PANEL)]
            for system in systems
        ]
        for pivot in range(first, first + PANEL):
            for which, (column, *later) in enumerate(panels):
                scale = 1.0 / column[pivot : pivot + 1, :]
                panels[which] = [eliminated(other, column, scale, pivot) for other in later]
                systems[which] = eliminated(systems[which], column, scale, pivot)
    return [window(system, 1) for system in systems]


def close_kernel(*refs):
    row_count = (len(refs) - 6) // 2
    row_refs = refs[:row_count]
    gram_refs = refs[row_count : 2 * row_count]
    col_ref, scaling_ref, query_ref, first_ref, solution_ref, residual_ref = refs[-6:]
    size = query_ref.shape[0]
    weight = graph_weight
    total = total_of([ref[...] for ref in gram_refs])
    g00 = symmetric(window(total, 0))
    g01 = flipped(window(total, 1))
    g11 = symmetric(window(total, 2))
    g12 = symmetric(window(total, 3))
    eye = (
        lax.broadcasted_iota(jnp.int32, total.shape, 0)
        == lax.broadcasted_iota(jnp.int32, total.shape, 1)
    ).astype(jnp.float32)
    curve = symmetric(g00 - weight * g01)
    steps, inverse = solve_many([(curve, g00), (g00, eye)])
    steps_t = flipped(steps)
    plain_gram = stacked(beside(g00, g01), beside(flipped(g01), g11))
    through_gram = stacked(beside(g01, g11), beside(g11, g12))
    after_first = beside(eye - steps_t, weight * steps_t)
    new_gram = symmetric(sandwich(after_first, plain_gram))
    mixing = times(inverse, new_gram)
    direction = after_first + flipped(mixing)
    curve = symmetric(sandwich(direction, plain_gram - weight * through_gram))
    (steps,) = solve_many([(curve, new_gram)])
    steps_t2 = flipped(steps)
    applied = direction - weight * pltpu.roll(direction, size, 1)
    solution_rows = exact_plain(beside(eye, steps_t2), stacked(steps_t, direction))
    residual_rows = exact_plain(beside(eye, -steps_t2), stacked(after_first, applied))
    rows = jnp.concatenate([solution_rows, residual_rows], axis=0)
    for part in range(first_ref.shape[0]):
        lanes = slice(part * 128, part * 128 + 128)
        basis = jnp.concatenate(
            [
                query_ref[:, lanes],
                first_ref[part],
                scaled_sum(row_refs, col_ref, scaling_ref, part),
                jnp.zeros_like(eye),
            ],
            axis=0,
        )
        values = exact_plain(rows, basis)
        solution_ref[:, lanes] = values[:size]
        residual_ref[:, lanes] = values[size:]


def pass_around(pieces, axis):
    count = len(pieces)
    return [pieces[0]] + [
        lax.ppermute(pieces[ahead], axis, [(at, (at + ahead) % count) for at in range(count)])
        for ahead in range(1, count)
    ]


def exchange(pieces, axis):
    return lax.all_to_all(pieces, axis, 0, 0, tiled=True)


def simple_call(kernel, shapes, name, *operands, bytes_accessed=None):
    cost = None
    if bytes_accessed:
        cost = pl.CostEstimate(flops=0, bytes_accessed=bytes_accessed, transcendentals=0)
    return pl.pallas_call(
        kernel,
        out_shape=shapes,
        compiler_params=pltpu.CompilerParams(vmem_limit_bytes=SMALL_GRANT),
        cost_estimate=cost,
        name=name,
    )(*operands)


def sum_kernel(col_ref, gram_ref, total_ref):
    size = gram_ref.shape[0]
    col_count, sent, _ = col_ref.shape
    folded = total_of([col_ref[segment, sent - size // 2 :] for segment in range(col_count)])
    upper = window(folded, 0, size) + window(folded, 1, size)
    lower = window(folded, 2, size) + window(folded, 3, size)
    last = jnp.concatenate([upper, lower], axis=0)
    total_ref[...] = gram_ref[...] + pltpu.roll(last, 3 * size, 1)


def body(queries, block_spots, live_blocks, neighbor_cols, neighbor_sims):
    row_count = lax.axis_size("row")
    col_count = lax.axis_size("col")
    query_rows, seg_len = queries.shape
    per_seg = seg_len // 128
    places = (block_spots, live_blocks)
    piece = (per_seg, query_rows, 128)
    wide = jax.ShapeDtypeStruct(piece, jnp.float32)
    narrow = jax.ShapeDtypeStruct(piece, jnp.bfloat16)
    gram_shape = jax.ShapeDtypeStruct((query_rows, 128), jnp.float32)

    message = jax.ShapeDtypeStruct((col_count, per_seg + 1) + piece[1:], jnp.bfloat16)

    blocks, flipped_blocks, *row_sums, col_sums = build_blocks(
        places,
        neighbor_cols[0, 0],
        neighbor_sims[0, 0],
        row_count,
        col_count,
        per_seg,
    )
    col_part = exchange(col_sums.reshape(col_count, per_seg, 128), "col")
    row_parts = pass_around([None, *row_sums], "row")[1:]
    scaling, scaled = simple_call(
        start_kernel,
        [jax.ShapeDtypeStruct((per_seg, 128), jnp.float32), narrow],
        "start",
        *row_parts,
        col_part,
        queries,
    )

    row_pieces = pass_around([scaled] * row_count, "row")
    (copies,) = simple_call(
        spread_kernel, [message], "spread", scaled, queries, bytes_accessed=16 * 1024 * 1024
    )
    first_dirs = exchange(copies, "col")
    total = backward_product(places, flipped_blocks, row_pieces, col_count)
    col_part = exchange(total, "col")
    totals = forward_product(places, blocks, first_dirs, row_count, piece)
    first, scaled, copies = simple_call(
        middle_kernel,
        [wide, narrow, message],
        "middle",
        *pass_around(totals, "row"),
        col_part,
        scaling,
        queries,
    )

    col_dirs = exchange(copies, "col")
    row_pieces = pass_around([scaled] * row_count, "row")
    total = backward_product(places, flipped_blocks, row_pieces, col_count)
    more = jax.ShapeDtypeStruct(
        (col_count, total.shape[1] + query_rows // 2, 128), jnp.bfloat16
    )
    total, gram = simple_call(
        attach_kernel, [more, gram_shape], "attach", first_dirs, col_dirs, total
    )
    col_part = exchange(total, "col")
    totals = forward_product(places, blocks, col_dirs, row_count, piece)
    row_parts = pass_around(totals, "row")
    (gram,) = simple_call(sum_kernel, [gram_shape], "gram_sum", col_part, gram)
    flat = jax.ShapeDtypeStruct(queries.shape, jnp.float32)
    return tuple(
        simple_call(
            close_kernel,
            [flat, flat],
            "close",
            *row_parts,
            *pass_around([gram] * row_count, "row"),
            col_part,
            scaling,
            queries,
            first,
        )
    )


def solution(mesh):
    placed = (
        P(None, ("row", "col")),
        P("row", "col", None),
        P("row", "col"),
        P("row", "col", None, None, None),
        P("row", "col", None, None, None),
    )
    return jax.shard_map(
        body,
        mesh=mesh,
        in_specs=placed,
        out_specs=(P(None, ("row", "col")), P(None, ("row", "col"))),
        check_vma=False,
    )
```

```python
import functools

import jax
import jax.numpy as jnp
from jax import lax
from jax.experimental import pallas as pl
from jax.experimental.pallas import tpu as pltpu
from jax.sharding import PartitionSpec as P

graph_weight = 0.95
GROUP = 32
BATCH = 32
SPARE = 4
PANEL = 8
BUILD_GRANT = 60 * 1024 * 1024
PRODUCT_GRANT = 40 * 1024 * 1024
SMALL_GRANT = 24 * 1024 * 1024


def dot_plain(left, right, **kwargs):
    return lax.dot_general(
        left, right, (((1,), (0,)), ((), ())), preferred_element_type=jnp.float32, **kwargs
    )


def dot_across(left, right, **kwargs):
    return lax.dot_general(
        left, right, (((1,), (1,)), ((), ())), preferred_element_type=jnp.float32, **kwargs
    )


exact_plain = functools.partial(dot_plain, precision=lax.Precision.HIGHEST)
exact_across = functools.partial(dot_across, precision=lax.Precision.HIGHEST)


def divided(number, size):
    if size & (size - 1):
        return lax.div(number, size), lax.rem(number, size)
    return number >> (size.bit_length() - 1), number & (size - 1)


def place_of(places, slot, col_blocks):
    return divided(places[0][0, 0, slot], col_blocks)


def live_count(places):
    return places[1][0, 0]


def group_count(places, group):
    return (live_count(places) + group - 1) // group


def group_copy(source, target, sems, index, group):
    window = pl.ds(index * group, group)
    return pltpu.make_async_copy(source.at[window], target.at[window], sems.at[index])


def build_kernel(
    spots_ref, live_ref, index_hbm, value_hbm, block_hbm, flipped_hbm, *refs
):
    (
        *row_outs,
        col_out_ref,
        index_ref,
        value_ref,
        block_ref,
        flipped_ref,
        row_ref,
        col_ref,
        index_sems,
        value_sems,
        block_sems,
        flipped_sems,
    ) = refs
    places = (spots_ref, live_ref)
    row_count = len(row_outs) + 1
    per_seg = row_outs[0].shape[0]
    col_blocks = col_out_ref.shape[0]
    groups = group_count(places, BATCH) * (BATCH // GROUP)

    def start_copies(index, _):
        group_copy(index_hbm, index_ref, index_sems, index, GROUP).start()
        group_copy(value_hbm, value_ref, value_sems, index, GROUP).start()
        return 0

    lax.fori_loop(0, groups, start_copies, 0)
    row_ref[...] = jnp.zeros_like(row_ref)
    col_ref[...] = jnp.zeros_like(col_ref)
    rows_16 = lax.broadcasted_iota(jnp.int32, (16, 128), 0)
    diagonal = lax.broadcasted_iota(jnp.int32, (128, 128), 0) == lax.broadcasted_iota(
        jnp.int32, (128, 128), 1
    )
    identity = jnp.where(diagonal, 1.0, 0.0).astype(jnp.bfloat16)
    zero = jnp.zeros((16, 128), jnp.bfloat16)

    def build_group(index, _):
        group_copy(index_hbm, index_ref, index_sems, index, GROUP).wait()
        group_copy(value_hbm, value_ref, value_sems, index, GROUP).wait()
        targets = [(rows_16 + 16 * part).astype(jnp.int16) for part in range(8)]

        def load_pair(inside):
            tables = []
            for slot in (index * GROUP + inside, index * GROUP + inside + 1):
                active = (slot < live_count(places)).astype(jnp.float32)
                values = value_ref[slot].astype(jnp.float32) * active
                tables.append((slot, index_ref[slot], values))
            return tables

        def build_pair(tables):
            sums = [[zero] * 8 for _ in tables]
            for entry in range(0, 16, 2):
                for which, (_, indices, values) in enumerate(tables):
                    pair = []
                    for at in (entry, entry + 1):
                        index_row = jnp.broadcast_to(indices[at : at + 1], (16, 128))
                        value_row = jnp.broadcast_to(values[at : at + 1], (16, 128))
                        pair.append((index_row.astype(jnp.int16), value_row.astype(jnp.bfloat16)))
                    for part in range(8):
                        first, second = [
                            jnp.where(index_row == targets[part], value_row, zero)
                            for index_row, value_row in pair
                        ]
                        sums[which][part] = sums[which][part] + (first + second)
            return [jnp.concatenate(parts, axis=0) for parts in sums]

        def store_turned(tables, turned):
            for (slot, _, values), block in zip(tables, turned):
                row_block, col_block = place_of(places, slot, col_blocks)
                flipped_ref[slot] = block.astype(jnp.bfloat16)
                col_ref[col_block] += jnp.sum(block.reshape(16, 8, 128), axis=0)
                row_ref[row_block] += values[:8] + values[8:]

        tables = load_pair(0)
        waiting = None
        for inside in range(0, GROUP, 2):
            following = load_pair(inside + 2) if inside + 2 < GROUP else None
            blocks = build_pair(tables)
            if waiting:
                store_turned(*waiting)
            for (slot, _, _), block in zip(tables, blocks):
                block_ref[slot] = block
            waiting = (tables, [dot_across(identity, block) for block in blocks])
            tables = following
        store_turned(*waiting)
        group_copy(block_ref, block_hbm, block_sems, index, GROUP).start()
        group_copy(flipped_ref, flipped_hbm, flipped_sems, index, GROUP).start()
        return 0

    lax.fori_loop(0, groups, build_group, 0)
    for ahead, out in enumerate(row_outs, 1):
        first = lax.rem(lax.axis_index("row") + ahead, row_count) * per_seg
        for part in range(per_seg):
            out[part : part + 1] = jnp.sum(row_ref[first + part], axis=0, keepdims=True)
    for part in range(per_seg):
        own = lax.axis_index("col") * per_seg + part
        col_ref[own] += row_ref[lax.axis_index("row") * per_seg + part]
    for col_block in range(col_blocks):
        col_out_ref[col_block : col_block + 1] = jnp.sum(
            col_ref[col_block], axis=0, keepdims=True
        )

    def finish_copies(index, _):
        group_copy(block_ref, block_hbm, block_sems, index, GROUP).wait()
        group_copy(flipped_ref, flipped_hbm, flipped_sems, index, GROUP).wait()
        return 0

    lax.fori_loop(0, groups, finish_copies, 0)


SCALARS = pl.BlockSpec(memory_space=pltpu.SMEM)
ANYWHERE = pl.BlockSpec(memory_space=pl.ANY)
IN_VMEM = pl.BlockSpec(memory_space=pltpu.VMEM)


def build_blocks(
    places, index_table, value_table, row_count, col_count, per_seg
):
    slots = index_table.shape[0]
    groups = slots // GROUP
    sum_shapes = [(per_seg, 128)] * (row_count - 1) + [(col_count * per_seg, 128)]
    return pl.pallas_call(
        build_kernel,
        in_specs=[SCALARS, SCALARS, ANYWHERE, ANYWHERE],
        out_specs=[ANYWHERE] * 2 + [IN_VMEM] * len(sum_shapes),
        out_shape=[jax.ShapeDtypeStruct((SPARE * slots, 128, 128), jnp.bfloat16)] * 2
        + [jax.ShapeDtypeStruct(shape, jnp.float32) for shape in sum_shapes],
        scratch_shapes=[
            pltpu.VMEM(index_table.shape, index_table.dtype),
            pltpu.VMEM(value_table.shape, value_table.dtype),
            pltpu.VMEM((slots, 128, 128), jnp.bfloat16),
            pltpu.VMEM((slots, 128, 128), jnp.bfloat16),
            pltpu.VMEM((row_count * per_seg, 8, 128), jnp.float32),
            pltpu.VMEM((col_count * per_seg, 8, 128), jnp.float32),
            pltpu.SemaphoreType.DMA((groups,)),
            pltpu.SemaphoreType.DMA((groups,)),
            pltpu.SemaphoreType.DMA((groups,)),
            pltpu.SemaphoreType.DMA((groups,)),
        ],
        compiler_params=pltpu.CompilerParams(vmem_limit_bytes=BUILD_GRANT),
        name="build_blocks",
    )(*places, index_table, value_table)


def each_group(places, block_hbm, block_ref, sems, prepare, run_group):
    groups = group_count(places, BATCH)

    def start_copy(index, _):
        group_copy(block_hbm, block_ref, sems, index, BATCH).start()
        return 0

    lax.fori_loop(0, groups, start_copy, 0)
    prepare()

    def one_group(index, _):
        group_copy(block_hbm, block_ref, sems, index, BATCH).wait()
        run_group(index * BATCH)
        return 0

    lax.fori_loop(0, groups, one_group, 0)


def add_products(places, first_slot, block_ref, direction, total_refs):
    sums = []
    for inside in range(BATCH):
        slot = first_slot + inside
        sums.append(dot_plain(direction(places(slot)[0]), block_ref[slot]))
    for inside in range(BATCH):
        total_ref = total_refs[inside % len(total_refs)]
        total_ref[places(first_slot + inside)[1]] += sums[inside]


def fill_directions(pieces, dir_ref, mine, per_seg):
    for behind, piece in enumerate(pieces):
        first = lax.rem(mine + (len(pieces) - behind), len(pieces)) * per_seg
        for part in range(per_seg):
            dir_ref[first + part] = piece[part]


def backward_kernel(row_count, spots_ref, live_ref, block_hbm, *refs):
    places = (spots_ref, live_ref)
    row_pieces = refs[:row_count]
    col_out_ref, block_ref, sems, row_dir_ref, even_ref, odd_ref = refs[row_count:]
    per_seg = row_pieces[0].shape[0]
    col_blocks = even_ref.shape[0]

    def prepare():
        even_ref[...] = jnp.zeros_like(even_ref)
        odd_ref[...] = jnp.zeros_like(odd_ref)
        fill_directions(row_pieces, row_dir_ref, lax.axis_index("row"), per_seg)

    def run_group(first_slot):
        add_products(
            lambda slot: place_of(places, slot, col_blocks),
            first_slot,
            block_ref,
            lambda row_block: row_dir_ref[row_block],
            [even_ref, odd_ref],
        )

    each_group(places, block_hbm, block_ref, sems, prepare, run_group)
    size = even_ref.shape[1]
    for segment in range(col_out_ref.shape[0]):
        for part in range(per_seg):
            col_block = segment * per_seg + part
            values = even_ref[col_block] + odd_ref[col_block]
            col_out_ref[segment, part * size : part * size + size] = values.astype(
                col_out_ref.dtype
            )


def in_terms(values, count):
    terms = []
    for _ in range(count):
        terms.append(values.astype(jnp.bfloat16))
        values = values - terms[-1].astype(jnp.float32)
    return terms


def side_by_side(terms, width=32):
    total = terms[0].astype(jnp.float32)
    for place, term in enumerate(terms[1:], 1):
        total = total + pltpu.roll(term.astype(jnp.float32), place * width, 1)
    return total.astype(jnp.bfloat16)


def attach_kernel(first_dir_ref, col_dir_ref, total_ref, message_ref, gram_ref):
    col_count, sent, size, _ = col_dir_ref.shape
    per_seg = sent - 1

    def add_segment(segment, gram):
        for part in range(per_seg):
            rows = slice(part * size, part * size + size)
            values = total_ref[segment, rows]
            message_ref[segment, rows] = values
            gram += dot_across(values, tall(col_dir_ref[segment, part]))
        return gram

    gram = lax.fori_loop(
        0, col_count, add_segment, jnp.zeros((size, 128), jnp.float32), unroll=4
    )
    half = size // 2
    terms = side_by_side(in_terms(gram, 2)).astype(jnp.float32)
    folded = terms[:half] + pltpu.roll(terms[half:], 64, 1)
    for segment in range(col_count):
        message_ref[segment, per_seg * size :] = folded.astype(message_ref.dtype)
    queries = total_of([first_dir_ref[segment, per_seg] for segment in range(col_count)])
    queries = total_of([window(queries, term) for term in range(3)])
    pairs = total_of([col_dir_ref[segment, per_seg] for segment in range(col_count)])
    lanes = lax.broadcasted_iota(jnp.int32, pairs.shape, 1)
    pairs = jnp.where(lanes < 2 * size, pairs + pltpu.roll(pairs, 128 - 2 * size, 1), 0.0)
    gram_ref[...] = beside(queries, pairs)


def forward_kernel(spots_ref, live_ref, block_hbm, col_dir_ref, *refs):
    places = (spots_ref, live_ref)
    *row_outs, block_ref, sems, even_ref, odd_ref = refs
    per_seg = row_outs[0].shape[0]
    col_blocks = col_dir_ref.shape[0] * per_seg

    def prepare():
        even_ref[...] = jnp.zeros_like(even_ref)
        odd_ref[...] = jnp.zeros_like(odd_ref)

    def run_group(first_slot):
        add_products(
            lambda slot: place_of(places, slot, col_blocks)[::-1],
            first_slot,
            block_ref,
            lambda col_block: col_dir_ref[divided(col_block, per_seg)],
            [even_ref, odd_ref],
        )

    each_group(places, block_hbm, block_ref, sems, prepare, run_group)
    for ahead, out in enumerate(row_outs):
        first = lax.rem(lax.axis_index("row") + ahead, len(row_outs)) * per_seg
        for part in range(per_seg):
            values = even_ref[first + part] + odd_ref[first + part]
            out[part] = values.astype(out.dtype)


def over_blocks(kernel, name, places, blocks, inputs, outputs, scratch):
    slots = blocks.shape[0] // SPARE
    return pl.pallas_call(
        kernel,
        in_specs=[SCALARS, SCALARS, ANYWHERE] + [IN_VMEM] * len(inputs),
        out_specs=[IN_VMEM] * len(outputs),
        out_shape=outputs,
        scratch_shapes=[
            pltpu.VMEM((slots,) + blocks.shape[1:], blocks.dtype),
            pltpu.SemaphoreType.DMA((slots // BATCH,)),
        ]
        + scratch,
        compiler_params=pltpu.CompilerParams(vmem_limit_bytes=PRODUCT_GRANT),
        cost_estimate=pl.CostEstimate(
            flops=2 * slots * 32 * 128 * 128, bytes_accessed=2 * slots * 128 * 128, transcendentals=0
        ),
        name=name,
    )(*places, blocks, *inputs)


def backward_product(places, blocks, row_pieces, col_count):
    per_seg, rows, lanes = row_pieces[0].shape
    col_shape = (col_count * per_seg, rows, lanes)
    (total,) = over_blocks(
        functools.partial(backward_kernel, len(row_pieces)),
        "backward_product",
        places,
        blocks,
        row_pieces,
        [jax.ShapeDtypeStruct((col_count, per_seg * rows, lanes), jnp.bfloat16)],
        [
            pltpu.VMEM((len(row_pieces) * per_seg, rows, lanes), jnp.bfloat16),
            pltpu.VMEM(col_shape, jnp.float32),
            pltpu.VMEM(col_shape, jnp.float32),
        ],
    )
    return total


def forward_product(places, blocks, col_dirs, row_count, piece):
    row_shape = (row_count * piece[0],) + piece[1:]
    return over_blocks(
        forward_kernel,
        "forward_product",
        places,
        blocks,
        [col_dirs],
        [jax.ShapeDtypeStruct(piece, jnp.bfloat16)] * row_count,
        [pltpu.VMEM(row_shape, jnp.float32), pltpu.VMEM(row_shape, jnp.float32)],
    )


def total_of(values):
    total = values[0].astype(jnp.float32)
    for value in values[1:]:
        total = total + value.astype(jnp.float32)
    return total


def leading(ref):
    return [ref.at[index] for index in range(ref.shape[0])]


def start_kernel(*refs):
    *row_refs, col_ref, query_ref, scaling_ref, scaled_ref, copies_ref = refs
    degree = 1.0 + 0.5 * total_of([ref[...] for ref in [*row_refs, *leading(col_ref)]])
    scaling = 1.0 / jnp.sqrt(degree)
    scaling_ref[...] = scaling
    per_seg, size, _ = scaled_ref.shape
    gram = jnp.zeros((size, 128), jnp.float32)
    for part in range(per_seg):
        query = query_ref[:, part * 128 : part * 128 + 128]
        scaled = (scaling[part : part + 1] * query).astype(jnp.bfloat16)
        scaled_ref[part] = scaled
        for copy in range(copies_ref.shape[0]):
            copies_ref[copy, part] = scaled
        gram += exact_across(query, tall(query))
    terms = side_by_side(in_terms(gram, 3))
    for copy in range(copies_ref.shape[0]):
        copies_ref[copy, per_seg] = terms


def scaled_sum(row_refs, col_ref, scaling_ref, part):
    scaling = scaling_ref[part : part + 1]
    size = row_refs[0].shape[1]
    rows = slice(part * size, part * size + size)
    total = total_of([ref[part] for ref in row_refs] + [ref[rows] for ref in leading(col_ref)])
    return scaling * (0.5 * total)


def middle_kernel(*refs):
    *row_refs, col_ref, scaling_ref, query_ref, first_ref, scaled_ref, copies_ref = refs
    size = query_ref.shape[0]
    per_seg = scaling_ref.shape[0]
    grams = jnp.zeros((size, 128), jnp.float32)
    for part in range(per_seg):
        first = scaled_sum(row_refs, col_ref, scaling_ref, part)
        first_ref[part] = first
        scaled = (scaling_ref[part : part + 1] * first).astype(jnp.bfloat16)
        scaled_ref[part] = scaled
        for copy in range(copies_ref.shape[0]):
            copies_ref[copy, part] = scaled
        query = query_ref[:, part * 128 : part * 128 + 128]
        grams += exact_across(first, stacked(query, first))
    terms = side_by_side(in_terms(grams, 2), 2 * size)
    for copy in range(copies_ref.shape[0]):
        copies_ref[copy, per_seg] = terms


def tall(flat):
    rest = flat.shape[1] - flat.shape[0]
    return jnp.concatenate([flat, jnp.zeros((rest, flat.shape[1]), flat.dtype)], axis=0)


def flipped(flat):
    return tall(flat).T[: flat.shape[0]]


def times(left, right):
    return exact_plain(left, tall(right))


def beside(left, right):
    return left + pltpu.roll(right, left.shape[0], 1)


def stacked(upper, lower):
    rest = jnp.zeros((upper.shape[1] - 2 * upper.shape[0], upper.shape[1]), upper.dtype)
    return jnp.concatenate([upper, lower, rest], axis=0)


def sandwich(rows, middle):
    return exact_across(exact_plain(rows, middle), tall(rows))


def symmetric(flat):
    return 0.5 * (flat + flipped(flat))


def window(flat, place, size=None):
    size = size or flat.shape[0]
    if place:
        flat = pltpu.roll(flat, flat.shape[1] - place * size, 1)
    lanes = lax.broadcasted_iota(jnp.int32, flat.shape, 1)
    return jnp.where(lanes < size, flat, 0.0)


def solve_many(pairs):
    size = pairs[0][0].shape[0]
    systems = [matrix + pltpu.roll(side, size, 1) for matrix, side in pairs]
    sublanes = lax.broadcasted_iota(jnp.int32, systems[0].shape, 0)

    def eliminated(values, column, scale, pivot):
        row = values[pivot : pivot + 1, :] * scale
        return jnp.where(sublanes == pivot, row, values - column * row)

    for first in range(0, size, PANEL):
        panels = [
            [jnp.broadcast_to(system[:, at : at + 1], system.shape) for at in range(first, first + PANEL)]
            for system in systems
        ]
        for pivot in range(first, first + PANEL):
            for which, (column, *later) in enumerate(panels):
                scale = 1.0 / column[pivot : pivot + 1, :]
                panels[which] = [eliminated(other, column, scale, pivot) for other in later]
                systems[which] = eliminated(systems[which], column, scale, pivot)
    return [window(system, 1) for system in systems]


def close_kernel(*refs):
    row_count = (len(refs) - 6) // 2
    row_refs = refs[:row_count]
    gram_refs = refs[row_count : 2 * row_count]
    col_ref, scaling_ref, query_ref, first_ref, solution_ref, residual_ref = refs[-6:]
    size = query_ref.shape[0]
    weight = graph_weight
    total = total_of([ref[...] for ref in gram_refs])
    g00 = symmetric(window(total, 0))
    g01 = flipped(window(total, 1))
    g11 = symmetric(window(total, 2))
    g12 = symmetric(window(total, 3))
    eye = (
        lax.broadcasted_iota(jnp.int32, total.shape, 0)
        == lax.broadcasted_iota(jnp.int32, total.shape, 1)
    ).astype(jnp.float32)
    curve = symmetric(g00 - weight * g01)
    steps, inverse = solve_many([(curve, g00), (g00, eye)])
    steps_t = flipped(steps)
    plain_gram = stacked(beside(g00, g01), beside(flipped(g01), g11))
    through_gram = stacked(beside(g01, g11), beside(g11, g12))
    after_first = beside(eye - steps_t, weight * steps_t)
    new_gram = symmetric(sandwich(after_first, plain_gram))
    mixing = times(inverse, new_gram)
    direction = after_first + flipped(mixing)
    curve = symmetric(sandwich(direction, plain_gram - weight * through_gram))
    (steps,) = solve_many([(curve, new_gram)])
    steps_t2 = flipped(steps)
    applied = direction - weight * pltpu.roll(direction, size, 1)
    solution_rows = exact_plain(beside(eye, steps_t2), stacked(steps_t, direction))
    residual_rows = exact_plain(beside(eye, -steps_t2), stacked(after_first, applied))
    rows = jnp.concatenate([solution_rows, residual_rows], axis=0)
    for part in range(first_ref.shape[0]):
        lanes = slice(part * 128, part * 128 + 128)
        basis = jnp.concatenate(
            [
                query_ref[:, lanes],
                first_ref[part],
                scaled_sum(row_refs, col_ref, scaling_ref, part),
                jnp.zeros_like(eye),
            ],
            axis=0,
        )
        values = exact_plain(rows, basis)
        solution_ref[:, lanes] = values[:size]
        residual_ref[:, lanes] = values[size:]


def pass_around(pieces, axis):
    count = len(pieces)
    return [pieces[0]] + [
        lax.ppermute(pieces[ahead], axis, [(at, (at + ahead) % count) for at in range(count)])
        for ahead in range(1, count)
    ]


def exchange(pieces, axis):
    return lax.all_to_all(pieces, axis, 0, 0, tiled=True)


def simple_call(kernel, shapes, name, *operands):
    return pl.pallas_call(
        kernel,
        out_shape=shapes,
        compiler_params=pltpu.CompilerParams(vmem_limit_bytes=SMALL_GRANT),
        name=name,
    )(*operands)


def sum_kernel(col_ref, gram_ref, total_ref):
    size = gram_ref.shape[0]
    col_count, sent, _ = col_ref.shape
    folded = total_of([col_ref[segment, sent - size // 2 :] for segment in range(col_count)])
    upper = window(folded, 0, size) + window(folded, 1, size)
    lower = window(folded, 2, size) + window(folded, 3, size)
    last = jnp.concatenate([upper, lower], axis=0)
    total_ref[...] = gram_ref[...] + pltpu.roll(last, 3 * size, 1)


def body(queries, block_spots, live_blocks, neighbor_cols, neighbor_sims):
    row_count = lax.axis_size("row")
    col_count = lax.axis_size("col")
    query_rows, seg_len = queries.shape
    per_seg = seg_len // 128
    places = (block_spots, live_blocks)
    piece = (per_seg, query_rows, 128)
    wide = jax.ShapeDtypeStruct(piece, jnp.float32)
    narrow = jax.ShapeDtypeStruct(piece, jnp.bfloat16)
    gram_shape = jax.ShapeDtypeStruct((query_rows, 128), jnp.float32)

    message = jax.ShapeDtypeStruct((col_count, per_seg + 1) + piece[1:], jnp.bfloat16)

    blocks, flipped_blocks, *row_sums, col_sums = build_blocks(
        places,
        neighbor_cols[0, 0],
        neighbor_sims[0, 0],
        row_count,
        col_count,
        per_seg,
    )
    col_part = exchange(col_sums.reshape(col_count, per_seg, 128), "col")
    row_parts = pass_around([None, *row_sums], "row")[1:]
    scaling, scaled, copies = simple_call(
        start_kernel,
        [jax.ShapeDtypeStruct((per_seg, 128), jnp.float32), narrow, message],
        "start",
        *row_parts,
        col_part,
        queries,
    )

    first_dirs = exchange(copies, "col")
    row_pieces = pass_around([scaled] * row_count, "row")
    total = backward_product(places, flipped_blocks, row_pieces, col_count)
    col_part = exchange(total, "col")
    totals = forward_product(places, blocks, first_dirs, row_count, piece)
    first, scaled, copies = simple_call(
        middle_kernel,
        [wide, narrow, message],
        "middle",
        *pass_around(totals, "row"),
        col_part,
        scaling,
        queries,
    )

    col_dirs = exchange(copies, "col")
    row_pieces = pass_around([scaled] * row_count, "row")
    total = backward_product(places, flipped_blocks, row_pieces, col_count)
    more = jax.ShapeDtypeStruct(
        (col_count, total.shape[1] + query_rows // 2, 128), jnp.bfloat16
    )
    total, gram = simple_call(
        attach_kernel, [more, gram_shape], "attach", first_dirs, col_dirs, total
    )
    col_part = exchange(total, "col")
    totals = forward_product(places, blocks, col_dirs, row_count, piece)
    row_parts = pass_around(totals, "row")
    (gram,) = simple_call(sum_kernel, [gram_shape], "gram_sum", col_part, gram)
    flat = jax.ShapeDtypeStruct(queries.shape, jnp.float32)
    return tuple(
        simple_call(
            close_kernel,
            [flat, flat],
            "close",
            *row_parts,
            *pass_around([gram] * row_count, "row"),
            col_part,
            scaling,
            queries,
            first,
        )
    )


def solution(mesh):
    placed = (
        P(None, ("row", "col")),
        P("row", "col", None),
        P("row", "col"),
        P("row", "col", None, None, None),
        P("row", "col", None, None, None),
    )
    return jax.shard_map(
        body,
        mesh=mesh,
        in_specs=placed,
        out_specs=(P(None, ("row", "col")), P(None, ("row", "col"))),
        check_vma=False,
    )
```

```python
import functools

import jax
import jax.numpy as jnp
from jax import lax
from jax.experimental import pallas as pl
from jax.experimental.pallas import tpu as pltpu
from jax.sharding import PartitionSpec as P

graph_weight = 0.95
GROUP = 16
BATCH = 32
SPARE = 4
PANEL = 8
BUILD_GRANT = 60 * 1024 * 1024
PRODUCT_GRANT = 40 * 1024 * 1024
SMALL_GRANT = 24 * 1024 * 1024


def dot_plain(left, right, **kwargs):
    return lax.dot_general(
        left, right, (((1,), (0,)), ((), ())), preferred_element_type=jnp.float32, **kwargs
    )


def dot_across(left, right, **kwargs):
    return lax.dot_general(
        left, right, (((1,), (1,)), ((), ())), preferred_element_type=jnp.float32, **kwargs
    )


exact_plain = functools.partial(dot_plain, precision=lax.Precision.HIGHEST)
exact_across = functools.partial(dot_across, precision=lax.Precision.HIGHEST)


def divided(number, size):
    if size & (size - 1):
        return lax.div(number, size), lax.rem(number, size)
    return number >> (size.bit_length() - 1), number & (size - 1)


def place_of(places, slot, col_blocks):
    return divided(places[0][0, 0, slot], col_blocks)


def live_count(places):
    return places[1][0, 0]


def group_count(places, group):
    return (live_count(places) + group - 1) // group


def group_copy(source, target, sems, index, group):
    window = pl.ds(index * group, group)
    return pltpu.make_async_copy(source.at[window], target.at[window], sems.at[index])


def build_kernel(
    spots_ref, live_ref, index_hbm, value_hbm, block_hbm, flipped_hbm, *refs
):
    (
        *row_outs,
        col_out_ref,
        index_ref,
        value_ref,
        block_ref,
        flipped_ref,
        row_ref,
        col_ref,
        index_sems,
        value_sems,
        block_sems,
        flipped_sems,
    ) = refs
    places = (spots_ref, live_ref)
    row_count = len(row_outs) + 1
    per_seg = row_outs[0].shape[0]
    col_blocks = col_out_ref.shape[0]
    groups = group_count(places, BATCH) * (BATCH // GROUP)

    def start_copies(index, _):
        group_copy(index_hbm, index_ref, index_sems, index, GROUP).start()
        group_copy(value_hbm, value_ref, value_sems, index, GROUP).start()
        return 0

    lax.fori_loop(0, groups, start_copies, 0)
    row_ref[...] = jnp.zeros_like(row_ref)
    col_ref[...] = jnp.zeros_like(col_ref)
    rows_16 = lax.broadcasted_iota(jnp.int32, (16, 128), 0)
    diagonal = lax.broadcasted_iota(jnp.int32, (128, 128), 0) == lax.broadcasted_iota(
        jnp.int32, (128, 128), 1
    )
    identity = jnp.where(diagonal, 1.0, 0.0).astype(jnp.bfloat16)
    zero = jnp.zeros((16, 128), jnp.bfloat16)

    def build_group(index, _):
        group_copy(index_hbm, index_ref, index_sems, index, GROUP).wait()
        group_copy(value_hbm, value_ref, value_sems, index, GROUP).wait()
        targets = [(rows_16 + 16 * part).astype(jnp.int16) for part in range(8)]

        def load_pair(inside):
            tables = []
            for slot in (index * GROUP + inside, index * GROUP + inside + 1):
                active = (slot < live_count(places)).astype(jnp.float32)
                values = value_ref[slot].astype(jnp.float32) * active
                indices = index_ref[slot].astype(jnp.int16)
                tables.append((slot, indices, values, values.astype(jnp.bfloat16)))
            return tables

        def build_pair(tables):
            sums = [[zero] * 8 for _ in tables]
            for entry in range(0, 16, 2):
                for which, (_, indices, _, narrow) in enumerate(tables):
                    pair = []
                    for at in (entry, entry + 1):
                        index_row = jnp.broadcast_to(indices[at : at + 1], (16, 128))
                        value_row = jnp.broadcast_to(narrow[at : at + 1], (16, 128))
                        pair.append((index_row, value_row))
                    for part in range(8):
                        first, second = [
                            jnp.where(index_row == targets[part], value_row, zero)
                            for index_row, value_row in pair
                        ]
                        sums[which][part] = sums[which][part] + (first + second)
            return [jnp.concatenate(parts, axis=0) for parts in sums]

        def store_turned(tables, turned):
            for (slot, _, values, _), block in zip(tables, turned):
                row_block, col_block = place_of(places, slot, col_blocks)
                flipped_ref[slot] = block.astype(jnp.bfloat16)
                col_ref[col_block] += jnp.sum(block.reshape(16, 8, 128), axis=0)
                row_ref[row_block] += values[:8] + values[8:]

        tables = load_pair(0)
        waiting = None
        for inside in range(0, GROUP, 2):
            following = load_pair(inside + 2) if inside + 2 < GROUP else None
            blocks = build_pair(tables)
            if waiting:
                store_turned(*waiting)
            for (slot, *_), block in zip(tables, blocks):
                block_ref[slot] = block
            waiting = (tables, [dot_across(identity, block) for block in blocks])
            tables = following
        store_turned(*waiting)
        group_copy(block_ref, block_hbm, block_sems, index, GROUP).start()
        group_copy(flipped_ref, flipped_hbm, flipped_sems, index, GROUP).start()
        return 0

    lax.fori_loop(0, groups, build_group, 0)
    for ahead, out in enumerate(row_outs, 1):
        first = lax.rem(lax.axis_index("row") + ahead, row_count) * per_seg
        for part in range(per_seg):
            out[part : part + 1] = jnp.sum(row_ref[first + part], axis=0, keepdims=True)
    for part in range(per_seg):
        own = lax.axis_index("col") * per_seg + part
        col_ref[own] += row_ref[lax.axis_index("row") * per_seg + part]
    for col_block in range(col_blocks):
        col_out_ref[col_block : col_block + 1] = jnp.sum(
            col_ref[col_block], axis=0, keepdims=True
        )

    def finish_copies(index, _):
        group_copy(block_ref, block_hbm, block_sems, index, GROUP).wait()
        group_copy(flipped_ref, flipped_hbm, flipped_sems, index, GROUP).wait()
        return 0

    lax.fori_loop(0, groups, finish_copies, 0)


SCALARS = pl.BlockSpec(memory_space=pltpu.SMEM)
ANYWHERE = pl.BlockSpec(memory_space=pl.ANY)
IN_VMEM = pl.BlockSpec(memory_space=pltpu.VMEM)


def build_blocks(
    places, index_table, value_table, row_count, col_count, per_seg
):
    slots = index_table.shape[0]
    groups = slots // GROUP
    sum_shapes = [(per_seg, 128)] * (row_count - 1) + [(col_count * per_seg, 128)]
    return pl.pallas_call(
        build_kernel,
        in_specs=[SCALARS, SCALARS, ANYWHERE, ANYWHERE],
        out_specs=[ANYWHERE] * 2 + [IN_VMEM] * len(sum_shapes),
        out_shape=[jax.ShapeDtypeStruct((SPARE * slots, 128, 128), jnp.bfloat16)] * 2
        + [jax.ShapeDtypeStruct(shape, jnp.float32) for shape in sum_shapes],
        scratch_shapes=[
            pltpu.VMEM(index_table.shape, index_table.dtype),
            pltpu.VMEM(value_table.shape, value_table.dtype),
            pltpu.VMEM((slots, 128, 128), jnp.bfloat16),
            pltpu.VMEM((slots, 128, 128), jnp.bfloat16),
            pltpu.VMEM((row_count * per_seg, 8, 128), jnp.float32),
            pltpu.VMEM((col_count * per_seg, 8, 128), jnp.float32),
            pltpu.SemaphoreType.DMA((groups,)),
            pltpu.SemaphoreType.DMA((groups,)),
            pltpu.SemaphoreType.DMA((groups,)),
            pltpu.SemaphoreType.DMA((groups,)),
        ],
        compiler_params=pltpu.CompilerParams(vmem_limit_bytes=BUILD_GRANT),
        name="build_blocks",
    )(*places, index_table, value_table)


def each_group(places, block_hbm, block_ref, sems, prepare, run_group):
    groups = group_count(places, BATCH)

    def start_copy(index, _):
        group_copy(block_hbm, block_ref, sems, index, BATCH).start()
        return 0

    lax.fori_loop(0, groups, start_copy, 0)
    prepare()

    def one_group(index, _):
        group_copy(block_hbm, block_ref, sems, index, BATCH).wait()
        run_group(index * BATCH)
        return 0

    lax.fori_loop(0, groups, one_group, 0)


def add_products(places, first_slot, block_ref, direction, total_refs):
    sums = []
    for inside in range(BATCH):
        slot = first_slot + inside
        sums.append(dot_plain(direction(places(slot)[0]), block_ref[slot]))
    for inside in range(BATCH):
        total_ref = total_refs[inside % len(total_refs)]
        total_ref[places(first_slot + inside)[1]] += sums[inside]


def fill_directions(pieces, dir_ref, mine, per_seg):
    for behind, piece in enumerate(pieces):
        first = lax.rem(mine + (len(pieces) - behind), len(pieces)) * per_seg
        for part in range(per_seg):
            dir_ref[first + part] = piece[part]


def backward_kernel(row_count, spots_ref, live_ref, block_hbm, *refs):
    places = (spots_ref, live_ref)
    row_pieces = refs[:row_count]
    col_out_ref, block_ref, sems, row_dir_ref, even_ref, odd_ref = refs[row_count:]
    per_seg = row_pieces[0].shape[0]
    col_blocks = even_ref.shape[0]

    def prepare():
        even_ref[...] = jnp.zeros_like(even_ref)
        odd_ref[...] = jnp.zeros_like(odd_ref)
        fill_directions(row_pieces, row_dir_ref, lax.axis_index("row"), per_seg)

    def run_group(first_slot):
        add_products(
            lambda slot: place_of(places, slot, col_blocks),
            first_slot,
            block_ref,
            lambda row_block: row_dir_ref[row_block],
            [even_ref, odd_ref],
        )

    each_group(places, block_hbm, block_ref, sems, prepare, run_group)
    size = even_ref.shape[1]
    for segment in range(col_out_ref.shape[0]):
        for part in range(per_seg):
            col_block = segment * per_seg + part
            values = even_ref[col_block] + odd_ref[col_block]
            col_out_ref[segment, part * size : part * size + size] = values.astype(
                col_out_ref.dtype
            )


def in_terms(values, count):
    terms = []
    for _ in range(count):
        terms.append(values.astype(jnp.bfloat16))
        values = values - terms[-1].astype(jnp.float32)
    return terms


def side_by_side(terms, width=32):
    total = terms[0].astype(jnp.float32)
    for place, term in enumerate(terms[1:], 1):
        total = total + pltpu.roll(term.astype(jnp.float32), place * width, 1)
    return total.astype(jnp.bfloat16)


def attach_kernel(first_dir_ref, col_dir_ref, total_ref, message_ref, gram_ref):
    col_count, sent, size, _ = col_dir_ref.shape
    per_seg = sent - 1

    def add_segment(segment, gram):
        for part in range(per_seg):
            rows = slice(part * size, part * size + size)
            values = total_ref[segment, rows]
            message_ref[segment, rows] = values
            gram += dot_across(values, tall(col_dir_ref[segment, part]))
        return gram

    gram = lax.fori_loop(
        0, col_count, add_segment, jnp.zeros((size, 128), jnp.float32), unroll=4
    )
    half = size // 2
    terms = side_by_side(in_terms(gram, 2)).astype(jnp.float32)
    folded = terms[:half] + pltpu.roll(terms[half:], 64, 1)
    for segment in range(col_count):
        message_ref[segment, per_seg * size :] = folded.astype(message_ref.dtype)
    queries = total_of([first_dir_ref[segment, per_seg] for segment in range(col_count)])
    queries = total_of([window(queries, term) for term in range(3)])
    pairs = total_of([col_dir_ref[segment, per_seg] for segment in range(col_count)])
    lanes = lax.broadcasted_iota(jnp.int32, pairs.shape, 1)
    pairs = jnp.where(lanes < 2 * size, pairs + pltpu.roll(pairs, 128 - 2 * size, 1), 0.0)
    gram_ref[...] = beside(queries, pairs)


def forward_kernel(spots_ref, live_ref, block_hbm, col_dir_ref, *refs):
    places = (spots_ref, live_ref)
    *row_outs, block_ref, sems, even_ref, odd_ref = refs
    per_seg = row_outs[0].shape[0]
    col_blocks = col_dir_ref.shape[0] * per_seg

    def prepare():
        even_ref[...] = jnp.zeros_like(even_ref)
        odd_ref[...] = jnp.zeros_like(odd_ref)

    def run_group(first_slot):
        add_products(
            lambda slot: place_of(places, slot, col_blocks)[::-1],
            first_slot,
            block_ref,
            lambda col_block: col_dir_ref[divided(col_block, per_seg)],
            [even_ref, odd_ref],
        )

    each_group(places, block_hbm, block_ref, sems, prepare, run_group)
    for ahead, out in enumerate(row_outs):
        first = lax.rem(lax.axis_index("row") + ahead, len(row_outs)) * per_seg
        for part in range(per_seg):
            values = even_ref[first + part] + odd_ref[first + part]
            out[part] = values.astype(out.dtype)


def over_blocks(kernel, name, places, blocks, inputs, outputs, scratch):
    slots = blocks.shape[0] // SPARE
    return pl.pallas_call(
        kernel,
        in_specs=[SCALARS, SCALARS, ANYWHERE] + [IN_VMEM] * len(inputs),
        out_specs=[IN_VMEM] * len(outputs),
        out_shape=outputs,
        scratch_shapes=[
            pltpu.VMEM((slots,) + blocks.shape[1:], blocks.dtype),
            pltpu.SemaphoreType.DMA((slots // BATCH,)),
        ]
        + scratch,
        compiler_params=pltpu.CompilerParams(vmem_limit_bytes=PRODUCT_GRANT),
        cost_estimate=pl.CostEstimate(
            flops=2 * slots * 32 * 128 * 128, bytes_accessed=2 * slots * 128 * 128, transcendentals=0
        ),
        name=name,
    )(*places, blocks, *inputs)


def backward_product(places, blocks, row_pieces, col_count):
    per_seg, rows, lanes = row_pieces[0].shape
    col_shape = (col_count * per_seg, rows, lanes)
    (total,) = over_blocks(
        functools.partial(backward_kernel, len(row_pieces)),
        "backward_product",
        places,
        blocks,
        row_pieces,
        [jax.ShapeDtypeStruct((col_count, per_seg * rows, lanes), jnp.bfloat16)],
        [
            pltpu.VMEM((len(row_pieces) * per_seg, rows, lanes), jnp.bfloat16),
            pltpu.VMEM(col_shape, jnp.float32),
            pltpu.VMEM(col_shape, jnp.float32),
        ],
    )
    return total


def forward_product(places, blocks, col_dirs, row_count, piece):
    row_shape = (row_count * piece[0],) + piece[1:]
    return over_blocks(
        forward_kernel,
        "forward_product",
        places,
        blocks,
        [col_dirs],
        [jax.ShapeDtypeStruct(piece, jnp.bfloat16)] * row_count,
        [pltpu.VMEM(row_shape, jnp.float32), pltpu.VMEM(row_shape, jnp.float32)],
    )


def total_of(values):
    total = values[0].astype(jnp.float32)
    for value in values[1:]:
        total = total + value.astype(jnp.float32)
    return total


def leading(ref):
    return [ref.at[index] for index in range(ref.shape[0])]


def start_kernel(*refs):
    *row_refs, col_ref, query_ref, scaling_ref, scaled_ref, copies_ref = refs
    degree = 1.0 + 0.5 * total_of([ref[...] for ref in [*row_refs, *leading(col_ref)]])
    scaling = 1.0 / jnp.sqrt(degree)
    scaling_ref[...] = scaling
    per_seg, size, _ = scaled_ref.shape
    gram = jnp.zeros((size, 128), jnp.float32)
    for part in range(per_seg):
        query = query_ref[:, part * 128 : part * 128 + 128]
        scaled = (scaling[part : part + 1] * query).astype(jnp.bfloat16)
        scaled_ref[part] = scaled
        for copy in range(copies_ref.shape[0]):
            copies_ref[copy, part] = scaled
        gram += exact_across(query, tall(query))
    terms = side_by_side(in_terms(gram, 3))
    for copy in range(copies_ref.shape[0]):
        copies_ref[copy, per_seg] = terms


def scaled_sum(row_refs, col_ref, scaling_ref, part):
    scaling = scaling_ref[part : part + 1]
    size = row_refs[0].shape[1]
    rows = slice(part * size, part * size + size)
    total = total_of([ref[part] for ref in row_refs] + [ref[rows] for ref in leading(col_ref)])
    return scaling * (0.5 * total)


def middle_kernel(*refs):
    *row_refs, col_ref, scaling_ref, query_ref, first_ref, scaled_ref, copies_ref = refs
    size = query_ref.shape[0]
    per_seg = scaling_ref.shape[0]
    grams = jnp.zeros((size, 128), jnp.float32)
    for part in range(per_seg):
        first = scaled_sum(row_refs, col_ref, scaling_ref, part)
        first_ref[part] = first
        scaled = (scaling_ref[part : part + 1] * first).astype(jnp.bfloat16)
        scaled_ref[part] = scaled
        for copy in range(copies_ref.shape[0]):
            copies_ref[copy, part] = scaled
        query = query_ref[:, part * 128 : part * 128 + 128]
        grams += exact_across(first, stacked(query, first))
    terms = side_by_side(in_terms(grams, 2), 2 * size)
    for copy in range(copies_ref.shape[0]):
        copies_ref[copy, per_seg] = terms


def tall(flat):
    rest = flat.shape[1] - flat.shape[0]
    return jnp.concatenate([flat, jnp.zeros((rest, flat.shape[1]), flat.dtype)], axis=0)


def flipped(flat):
    return tall(flat).T[: flat.shape[0]]


def times(left, right):
    return exact_plain(left, tall(right))


def beside(left, right):
    return left + pltpu.roll(right, left.shape[0], 1)


def stacked(upper, lower):
    rest = jnp.zeros((upper.shape[1] - 2 * upper.shape[0], upper.shape[1]), upper.dtype)
    return jnp.concatenate([upper, lower, rest], axis=0)


def sandwich(rows, middle):
    return exact_across(exact_plain(rows, middle), tall(rows))


def symmetric(flat):
    return 0.5 * (flat + flipped(flat))


def window(flat, place, size=None):
    size = size or flat.shape[0]
    if place:
        flat = pltpu.roll(flat, flat.shape[1] - place * size, 1)
    lanes = lax.broadcasted_iota(jnp.int32, flat.shape, 1)
    return jnp.where(lanes < size, flat, 0.0)


def solve_many(pairs):
    size = pairs[0][0].shape[0]
    systems = [matrix + pltpu.roll(side, size, 1) for matrix, side in pairs]
    sublanes = lax.broadcasted_iota(jnp.int32, systems[0].shape, 0)

    def eliminated(values, column, scale, pivot):
        row = values[pivot : pivot + 1, :] * scale
        return jnp.where(sublanes == pivot, row, values - column * row)

    for first in range(0, size, PANEL):
        panels = [
            [jnp.broadcast_to(system[:, at : at + 1], system.shape) for at in range(first, first + PANEL)]
            for system in systems
        ]
        for pivot in range(first, first + PANEL):
            for which, (column, *later) in enumerate(panels):
                scale = 1.0 / column[pivot : pivot + 1, :]
                panels[which] = [eliminated(other, column, scale, pivot) for other in later]
                systems[which] = eliminated(systems[which], column, scale, pivot)
    return [window(system, 1) for system in systems]


def close_kernel(*refs):
    row_count = (len(refs) - 6) // 2
    row_refs = refs[:row_count]
    gram_refs = refs[row_count : 2 * row_count]
    col_ref, scaling_ref, query_ref, first_ref, solution_ref, residual_ref = refs[-6:]
    size = query_ref.shape[0]
    weight = graph_weight
    total = total_of([ref[...] for ref in gram_refs])
    g00 = symmetric(window(total, 0))
    g01 = flipped(window(total, 1))
    g11 = symmetric(window(total, 2))
    g12 = symmetric(window(total, 3))
    eye = (
        lax.broadcasted_iota(jnp.int32, total.shape, 0)
        == lax.broadcasted_iota(jnp.int32, total.shape, 1)
    ).astype(jnp.float32)
    curve = symmetric(g00 - weight * g01)
    steps, inverse = solve_many([(curve, g00), (g00, eye)])
    steps_t = flipped(steps)
    plain_gram = stacked(beside(g00, g01), beside(flipped(g01), g11))
    through_gram = stacked(beside(g01, g11), beside(g11, g12))
    after_first = beside(eye - steps_t, weight * steps_t)
    new_gram = symmetric(sandwich(after_first, plain_gram))
    mixing = times(inverse, new_gram)
    direction = after_first + flipped(mixing)
    curve = symmetric(sandwich(direction, plain_gram - weight * through_gram))
    (steps,) = solve_many([(curve, new_gram)])
    steps_t2 = flipped(steps)
    applied = direction - weight * pltpu.roll(direction, size, 1)
    solution_rows = exact_plain(beside(eye, steps_t2), stacked(steps_t, direction))
    residual_rows = exact_plain(beside(eye, -steps_t2), stacked(after_first, applied))
    rows = jnp.concatenate([solution_rows, residual_rows], axis=0)
    for part in range(first_ref.shape[0]):
        lanes = slice(part * 128, part * 128 + 128)
        basis = jnp.concatenate(
            [
                query_ref[:, lanes],
                first_ref[part],
                scaled_sum(row_refs, col_ref, scaling_ref, part),
                jnp.zeros_like(eye),
            ],
            axis=0,
        )
        values = exact_plain(rows, basis)
        solution_ref[:, lanes] = values[:size]
        residual_ref[:, lanes] = values[size:]


def pass_around(pieces, axis):
    count = len(pieces)
    return [pieces[0]] + [
        lax.ppermute(pieces[ahead], axis, [(at, (at + ahead) % count) for at in range(count)])
        for ahead in range(1, count)
    ]


def exchange(pieces, axis):
    return lax.all_to_all(pieces, axis, 0, 0, tiled=True)


def simple_call(kernel, shapes, name, *operands):
    return pl.pallas_call(
        kernel,
        out_shape=shapes,
        compiler_params=pltpu.CompilerParams(vmem_limit_bytes=SMALL_GRANT),
        name=name,
    )(*operands)


def sum_kernel(col_ref, gram_ref, total_ref):
    size = gram_ref.shape[0]
    col_count, sent, _ = col_ref.shape
    folded = total_of([col_ref[segment, sent - size // 2 :] for segment in range(col_count)])
    upper = window(folded, 0, size) + window(folded, 1, size)
    lower = window(folded, 2, size) + window(folded, 3, size)
    last = jnp.concatenate([upper, lower], axis=0)
    total_ref[...] = gram_ref[...] + pltpu.roll(last, 3 * size, 1)


def body(queries, block_spots, live_blocks, neighbor_cols, neighbor_sims):
    row_count = lax.axis_size("row")
    col_count = lax.axis_size("col")
    query_rows, seg_len = queries.shape
    per_seg = seg_len // 128
    places = (block_spots, live_blocks)
    piece = (per_seg, query_rows, 128)
    wide = jax.ShapeDtypeStruct(piece, jnp.float32)
    narrow = jax.ShapeDtypeStruct(piece, jnp.bfloat16)
    gram_shape = jax.ShapeDtypeStruct((query_rows, 128), jnp.float32)

    message = jax.ShapeDtypeStruct((col_count, per_seg + 1) + piece[1:], jnp.bfloat16)

    blocks, flipped_blocks, *row_sums, col_sums = build_blocks(
        places,
        neighbor_cols[0, 0],
        neighbor_sims[0, 0],
        row_count,
        col_count,
        per_seg,
    )
    col_part = exchange(col_sums.reshape(col_count, per_seg, 128), "col")
    row_parts = pass_around([None, *row_sums], "row")[1:]
    scaling, scaled, copies = simple_call(
        start_kernel,
        [jax.ShapeDtypeStruct((per_seg, 128), jnp.float32), narrow, message],
        "start",
        *row_parts,
        col_part,
        queries,
    )

    first_dirs = exchange(copies, "col")
    row_pieces = pass_around([scaled] * row_count, "row")
    total = backward_product(places, flipped_blocks, row_pieces, col_count)
    col_part = exchange(total, "col")
    totals = forward_product(places, blocks, first_dirs, row_count, piece)
    first, scaled, copies = simple_call(
        middle_kernel,
        [wide, narrow, message],
        "middle",
        *pass_around(totals, "row"),
        col_part,
        scaling,
        queries,
    )

    col_dirs = exchange(copies, "col")
    row_pieces = pass_around([scaled] * row_count, "row")
    total = backward_product(places, flipped_blocks, row_pieces, col_count)
    more = jax.ShapeDtypeStruct(
        (col_count, total.shape[1] + query_rows // 2, 128), jnp.bfloat16
    )
    total, gram = simple_call(
        attach_kernel, [more, gram_shape], "attach", first_dirs, col_dirs, total
    )
    col_part = exchange(total, "col")
    totals = forward_product(places, blocks, col_dirs, row_count, piece)
    row_parts = pass_around(totals, "row")
    (gram,) = simple_call(sum_kernel, [gram_shape], "gram_sum", col_part, gram)
    flat = jax.ShapeDtypeStruct(queries.shape, jnp.float32)
    return tuple(
        simple_call(
            close_kernel,
            [flat, flat],
            "close",
            *row_parts,
            *pass_around([gram] * row_count, "row"),
            col_part,
            scaling,
            queries,
            first,
        )
    )


def solution(mesh):
    placed = (
        P(None, ("row", "col")),
        P("row", "col", None),
        P("row", "col"),
        P("row", "col", None, None, None),
        P("row", "col", None, None, None),
    )
    return jax.shard_map(
        body,
        mesh=mesh,
        in_specs=placed,
        out_specs=(P(None, ("row", "col")), P(None, ("row", "col"))),
        check_vma=False,
    )
```

```python
import functools

import jax
import jax.numpy as jnp
from jax import lax
from jax.experimental import pallas as pl
from jax.experimental.pallas import tpu as pltpu
from jax.sharding import PartitionSpec as P

graph_weight = 0.95
GROUP = 16
BATCH = 32
SPARE = 4
PANEL = 8
BUILD_GRANT = 60 * 1024 * 1024
PRODUCT_GRANT = 40 * 1024 * 1024
SMALL_GRANT = 24 * 1024 * 1024


def dot_plain(left, right, **kwargs):
    return lax.dot_general(
        left, right, (((1,), (0,)), ((), ())), preferred_element_type=jnp.float32, **kwargs
    )


def dot_across(left, right, **kwargs):
    return lax.dot_general(
        left, right, (((1,), (1,)), ((), ())), preferred_element_type=jnp.float32, **kwargs
    )


exact_plain = functools.partial(dot_plain, precision=lax.Precision.HIGHEST)
exact_across = functools.partial(dot_across, precision=lax.Precision.HIGHEST)


def divided(number, size):
    if size & (size - 1):
        return lax.div(number, size), lax.rem(number, size)
    return number >> (size.bit_length() - 1), number & (size - 1)


def place_of(places, slot, col_blocks):
    return divided(places[0][0, 0, slot], col_blocks)


def live_count(places):
    return places[1][0, 0]


def group_count(places, group):
    return (live_count(places) + group - 1) // group


def group_copy(source, target, sems, index, group):
    window = pl.ds(index * group, group)
    return pltpu.make_async_copy(source.at[window], target.at[window], sems.at[index])


def build_kernel(
    spots_ref, live_ref, index_hbm, value_hbm, block_hbm, flipped_hbm, *refs
):
    (
        *row_outs,
        col_out_ref,
        index_ref,
        value_ref,
        block_ref,
        flipped_ref,
        row_ref,
        col_ref,
        index_sems,
        value_sems,
        block_sems,
        flipped_sems,
    ) = refs
    places = (spots_ref, live_ref)
    row_count = len(row_outs) + 1
    per_seg = row_outs[0].shape[0]
    col_blocks = col_out_ref.shape[0]
    groups = group_count(places, BATCH) * (BATCH // GROUP)

    def start_copies(index, _):
        group_copy(index_hbm, index_ref, index_sems, index, GROUP).start()
        group_copy(value_hbm, value_ref, value_sems, index, GROUP).start()
        return 0

    lax.fori_loop(0, groups, start_copies, 0)
    row_ref[...] = jnp.zeros_like(row_ref)
    col_ref[...] = jnp.zeros_like(col_ref)
    rows_16 = lax.broadcasted_iota(jnp.int32, (16, 128), 0)
    diagonal = lax.broadcasted_iota(jnp.int32, (128, 128), 0) == lax.broadcasted_iota(
        jnp.int32, (128, 128), 1
    )
    identity = jnp.where(diagonal, 1.0, 0.0).astype(jnp.bfloat16)
    zero = jnp.zeros((16, 128), jnp.bfloat16)

    targets = [(rows_16 + 16 * part).astype(jnp.int16) for part in range(8)]

    def turn_pair(first_slot):
        return [dot_across(identity, block_ref[first_slot + which]) for which in range(2)]

    def store_turned(first_slot, turned, started):
        for which, block in enumerate(turned):
            slot = first_slot + which
            flipped_ref[slot] = block.astype(jnp.bfloat16)
            sums = jnp.sum(block.reshape(16, 8, 128), axis=0)
            _, col_block = place_of(places, slot, col_blocks)
            col_ref[col_block] += jnp.where(started, sums, 0.0)

    def build_pair(pair, _):
        first_slot = 2 * pair
        before = 2 * jnp.maximum(pair - 1, 0)
        turned = turn_pair(before)
        tables = []
        for slot in (first_slot, first_slot + 1):
            active = (slot < live_count(places)).astype(jnp.float32)
            values = value_ref[slot].astype(jnp.float32) * active
            tables.append((index_ref[slot].astype(jnp.int16), values.astype(jnp.bfloat16)))
            row_block, _ = place_of(places, slot, col_blocks)
            row_ref[row_block] += values[:8] + values[8:]
        sums = [[zero] * 8 for _ in tables]
        for entry in range(0, 16, 2):
            for which, (indices, values) in enumerate(tables):
                rows = [
                    [jnp.broadcast_to(table[at : at + 1], (16, 128)) for table in (indices, values)]
                    for at in (entry, entry + 1)
                ]
                for part in range(8):
                    first, second = [
                        jnp.where(index_row == targets[part], value_row, zero)
                        for index_row, value_row in rows
                    ]
                    sums[which][part] = sums[which][part] + (first + second)
        for which, parts in enumerate(sums):
            block_ref[first_slot + which] = jnp.concatenate(parts, axis=0)
        store_turned(before, turned, pair > 0)
        return 0

    def build_group(index, _):
        group_copy(index_hbm, index_ref, index_sems, index, GROUP).wait()
        group_copy(value_hbm, value_ref, value_sems, index, GROUP).wait()
        half = GROUP // 2
        lax.fori_loop(index * half, index * half + half, build_pair, 0)
        group_copy(block_ref, block_hbm, block_sems, index, GROUP).start()

        @pl.when(index > 0)
        def _():
            group_copy(flipped_ref, flipped_hbm, flipped_sems, index - 1, GROUP).start()

        return 0

    lax.fori_loop(0, groups, build_group, 0)
    last = groups * GROUP - 2
    store_turned(last, turn_pair(last), True)
    group_copy(flipped_ref, flipped_hbm, flipped_sems, groups - 1, GROUP).start()
    for ahead, out in enumerate(row_outs, 1):
        first = lax.rem(lax.axis_index("row") + ahead, row_count) * per_seg
        for part in range(per_seg):
            out[part : part + 1] = jnp.sum(row_ref[first + part], axis=0, keepdims=True)
    for part in range(per_seg):
        own = lax.axis_index("col") * per_seg + part
        col_ref[own] += row_ref[lax.axis_index("row") * per_seg + part]
    for col_block in range(col_blocks):
        col_out_ref[col_block : col_block + 1] = jnp.sum(
            col_ref[col_block], axis=0, keepdims=True
        )

    def finish_copies(index, _):
        group_copy(block_ref, block_hbm, block_sems, index, GROUP).wait()
        group_copy(flipped_ref, flipped_hbm, flipped_sems, index, GROUP).wait()
        return 0

    lax.fori_loop(0, groups, finish_copies, 0)


SCALARS = pl.BlockSpec(memory_space=pltpu.SMEM)
ANYWHERE = pl.BlockSpec(memory_space=pl.ANY)
IN_VMEM = pl.BlockSpec(memory_space=pltpu.VMEM)


def build_blocks(
    places, index_table, value_table, row_count, col_count, per_seg
):
    slots = index_table.shape[0]
    groups = slots // GROUP
    sum_shapes = [(per_seg, 128)] * (row_count - 1) + [(col_count * per_seg, 128)]
    return pl.pallas_call(
        build_kernel,
        in_specs=[SCALARS, SCALARS, ANYWHERE, ANYWHERE],
        out_specs=[ANYWHERE] * 2 + [IN_VMEM] * len(sum_shapes),
        out_shape=[jax.ShapeDtypeStruct((SPARE * slots, 128, 128), jnp.bfloat16)] * 2
        + [jax.ShapeDtypeStruct(shape, jnp.float32) for shape in sum_shapes],
        scratch_shapes=[
            pltpu.VMEM(index_table.shape, index_table.dtype),
            pltpu.VMEM(value_table.shape, value_table.dtype),
            pltpu.VMEM((slots, 128, 128), jnp.bfloat16),
            pltpu.VMEM((slots, 128, 128), jnp.bfloat16),
            pltpu.VMEM((row_count * per_seg, 8, 128), jnp.float32),
            pltpu.VMEM((col_count * per_seg, 8, 128), jnp.float32),
            pltpu.SemaphoreType.DMA((groups,)),
            pltpu.SemaphoreType.DMA((groups,)),
            pltpu.SemaphoreType.DMA((groups,)),
            pltpu.SemaphoreType.DMA((groups,)),
        ],
        compiler_params=pltpu.CompilerParams(vmem_limit_bytes=BUILD_GRANT),
        name="build_blocks",
    )(*places, index_table, value_table)


def each_group(places, block_hbm, block_ref, sems, prepare, run_group):
    groups = group_count(places, BATCH)

    def start_copy(index, _):
        group_copy(block_hbm, block_ref, sems, index, BATCH).start()
        return 0

    lax.fori_loop(0, groups, start_copy, 0)
    prepare()

    def one_group(index, _):
        group_copy(block_hbm, block_ref, sems, index, BATCH).wait()
        run_group(index * BATCH)
        return 0

    lax.fori_loop(0, groups, one_group, 0)


def add_products(places, first_slot, block_ref, direction, total_refs):
    sums = []
    for inside in range(BATCH):
        slot = first_slot + inside
        sums.append(dot_plain(direction(places(slot)[0]), block_ref[slot]))
    for inside in range(BATCH):
        total_ref = total_refs[inside % len(total_refs)]
        total_ref[places(first_slot + inside)[1]] += sums[inside]


def fill_directions(pieces, dir_ref, mine, per_seg):
    for behind, piece in enumerate(pieces):
        first = lax.rem(mine + (len(pieces) - behind), len(pieces)) * per_seg
        for part in range(per_seg):
            dir_ref[first + part] = piece[part]


def backward_kernel(row_count, spots_ref, live_ref, block_hbm, *refs):
    places = (spots_ref, live_ref)
    row_pieces = refs[:row_count]
    col_out_ref, block_ref, sems, row_dir_ref, even_ref, odd_ref = refs[row_count:]
    per_seg = row_pieces[0].shape[0]
    col_blocks = even_ref.shape[0]

    def prepare():
        even_ref[...] = jnp.zeros_like(even_ref)
        odd_ref[...] = jnp.zeros_like(odd_ref)
        fill_directions(row_pieces, row_dir_ref, lax.axis_index("row"), per_seg)

    def run_group(first_slot):
        add_products(
            lambda slot: place_of(places, slot, col_blocks),
            first_slot,
            block_ref,
            lambda row_block: row_dir_ref[row_block],
            [even_ref, odd_ref],
        )

    each_group(places, block_hbm, block_ref, sems, prepare, run_group)
    size = even_ref.shape[1]
    for segment in range(col_out_ref.shape[0]):
        for part in range(per_seg):
            col_block = segment * per_seg + part
            values = even_ref[col_block] + odd_ref[col_block]
            col_out_ref[segment, part * size : part * size + size] = values.astype(
                col_out_ref.dtype
            )


def in_terms(values, count):
    terms = []
    for _ in range(count):
        terms.append(values.astype(jnp.bfloat16))
        values = values - terms[-1].astype(jnp.float32)
    return terms


def side_by_side(terms, width=32):
    total = terms[0].astype(jnp.float32)
    for place, term in enumerate(terms[1:], 1):
        total = total + pltpu.roll(term.astype(jnp.float32), place * width, 1)
    return total.astype(jnp.bfloat16)


def attach_kernel(first_dir_ref, col_dir_ref, total_ref, message_ref, gram_ref):
    col_count, sent, size, _ = col_dir_ref.shape
    per_seg = sent - 1

    def add_segment(segment, gram):
        for part in range(per_seg):
            rows = slice(part * size, part * size + size)
            values = total_ref[segment, rows]
            message_ref[segment, rows] = values
            gram += dot_across(values, tall(col_dir_ref[segment, part]))
        return gram

    gram = lax.fori_loop(
        0, col_count, add_segment, jnp.zeros((size, 128), jnp.float32), unroll=4
    )
    half = size // 2
    terms = side_by_side(in_terms(gram, 2)).astype(jnp.float32)
    folded = terms[:half] + pltpu.roll(terms[half:], 64, 1)
    for segment in range(col_count):
        message_ref[segment, per_seg * size :] = folded.astype(message_ref.dtype)
    queries = total_of([first_dir_ref[segment, per_seg] for segment in range(col_count)])
    queries = total_of([window(queries, term) for term in range(3)])
    pairs = total_of([col_dir_ref[segment, per_seg] for segment in range(col_count)])
    lanes = lax.broadcasted_iota(jnp.int32, pairs.shape, 1)
    pairs = jnp.where(lanes < 2 * size, pairs + pltpu.roll(pairs, 128 - 2 * size, 1), 0.0)
    gram_ref[...] = beside(queries, pairs)


def forward_kernel(spots_ref, live_ref, block_hbm, col_dir_ref, *refs):
    places = (spots_ref, live_ref)
    *row_outs, block_ref, sems, even_ref, odd_ref = refs
    per_seg = row_outs[0].shape[0]
    col_blocks = col_dir_ref.shape[0] * per_seg

    def prepare():
        even_ref[...] = jnp.zeros_like(even_ref)
        odd_ref[...] = jnp.zeros_like(odd_ref)

    def run_group(first_slot):
        add_products(
            lambda slot: place_of(places, slot, col_blocks)[::-1],
            first_slot,
            block_ref,
            lambda col_block: col_dir_ref[divided(col_block, per_seg)],
            [even_ref, odd_ref],
        )

    each_group(places, block_hbm, block_ref, sems, prepare, run_group)
    for ahead, out in enumerate(row_outs):
        first = lax.rem(lax.axis_index("row") + ahead, len(row_outs)) * per_seg
        for part in range(per_seg):
            values = even_ref[first + part] + odd_ref[first + part]
            out[part] = values.astype(out.dtype)


def over_blocks(kernel, name, places, blocks, inputs, outputs, scratch):
    slots = blocks.shape[0] // SPARE
    return pl.pallas_call(
        kernel,
        in_specs=[SCALARS, SCALARS, ANYWHERE] + [IN_VMEM] * len(inputs),
        out_specs=[IN_VMEM] * len(outputs),
        out_shape=outputs,
        scratch_shapes=[
            pltpu.VMEM((slots,) + blocks.shape[1:], blocks.dtype),
            pltpu.SemaphoreType.DMA((slots // BATCH,)),
        ]
        + scratch,
        compiler_params=pltpu.CompilerParams(vmem_limit_bytes=PRODUCT_GRANT),
        cost_estimate=pl.CostEstimate(
            flops=2 * slots * 32 * 128 * 128, bytes_accessed=2 * slots * 128 * 128, transcendentals=0
        ),
        name=name,
    )(*places, blocks, *inputs)


def backward_product(places, blocks, row_pieces, col_count):
    per_seg, rows, lanes = row_pieces[0].shape
    col_shape = (col_count * per_seg, rows, lanes)
    (total,) = over_blocks(
        functools.partial(backward_kernel, len(row_pieces)),
        "backward_product",
        places,
        blocks,
        row_pieces,
        [jax.ShapeDtypeStruct((col_count, per_seg * rows, lanes), jnp.bfloat16)],
        [
            pltpu.VMEM((len(row_pieces) * per_seg, rows, lanes), jnp.bfloat16),
            pltpu.VMEM(col_shape, jnp.float32),
            pltpu.VMEM(col_shape, jnp.float32),
        ],
    )
    return total


def forward_product(places, blocks, col_dirs, row_count, piece):
    row_shape = (row_count * piece[0],) + piece[1:]
    return over_blocks(
        forward_kernel,
        "forward_product",
        places,
        blocks,
        [col_dirs],
        [jax.ShapeDtypeStruct(piece, jnp.bfloat16)] * row_count,
        [pltpu.VMEM(row_shape, jnp.float32), pltpu.VMEM(row_shape, jnp.float32)],
    )


def total_of(values):
    total = values[0].astype(jnp.float32)
    for value in values[1:]:
        total = total + value.astype(jnp.float32)
    return total


def leading(ref):
    return [ref.at[index] for index in range(ref.shape[0])]


def start_kernel(*refs):
    *row_refs, col_ref, query_ref, scaling_ref, scaled_ref, copies_ref = refs
    degree = 1.0 + 0.5 * total_of([ref[...] for ref in [*row_refs, *leading(col_ref)]])
    scaling = 1.0 / jnp.sqrt(degree)
    scaling_ref[...] = scaling
    per_seg, size, _ = scaled_ref.shape
    gram = jnp.zeros((size, 128), jnp.float32)
    for part in range(per_seg):
        query = query_ref[:, part * 128 : part * 128 + 128]
        scaled = (scaling[part : part + 1] * query).astype(jnp.bfloat16)
        scaled_ref[part] = scaled
        for copy in range(copies_ref.shape[0]):
            copies_ref[copy, part] = scaled
        gram += exact_across(query, tall(query))
    terms = side_by_side(in_terms(gram, 3))
    for copy in range(copies_ref.shape[0]):
        copies_ref[copy, per_seg] = terms


def scaled_sum(row_refs, col_ref, scaling_ref, part):
    scaling = scaling_ref[part : part + 1]
    size = row_refs[0].shape[1]
    rows = slice(part * size, part * size + size)
    total = total_of([ref[part] for ref in row_refs] + [ref[rows] for ref in leading(col_ref)])
    return scaling * (0.5 * total)


def middle_kernel(*refs):
    *row_refs, col_ref, scaling_ref, query_ref, first_ref, scaled_ref, copies_ref = refs
    size = query_ref.shape[0]
    per_seg = scaling_ref.shape[0]
    grams = jnp.zeros((size, 128), jnp.float32)
    for part in range(per_seg):
        first = scaled_sum(row_refs, col_ref, scaling_ref, part)
        first_ref[part] = first
        scaled = (scaling_ref[part : part + 1] * first).astype(jnp.bfloat16)
        scaled_ref[part] = scaled
        for copy in range(copies_ref.shape[0]):
            copies_ref[copy, part] = scaled
        query = query_ref[:, part * 128 : part * 128 + 128]
        grams += exact_across(first, stacked(query, first))
    terms = side_by_side(in_terms(grams, 2), 2 * size)
    for copy in range(copies_ref.shape[0]):
        copies_ref[copy, per_seg] = terms


def tall(flat):
    rest = flat.shape[1] - flat.shape[0]
    return jnp.concatenate([flat, jnp.zeros((rest, flat.shape[1]), flat.dtype)], axis=0)


def flipped(flat):
    return tall(flat).T[: flat.shape[0]]


def times(left, right):
    return exact_plain(left, tall(right))


def beside(left, right):
    return left + pltpu.roll(right, left.shape[0], 1)


def stacked(upper, lower):
    rest = jnp.zeros((upper.shape[1] - 2 * upper.shape[0], upper.shape[1]), upper.dtype)
    return jnp.concatenate([upper, lower, rest], axis=0)


def sandwich(rows, middle):
    return exact_across(exact_plain(rows, middle), tall(rows))


def symmetric(flat):
    return 0.5 * (flat + flipped(flat))


def window(flat, place, size=None):
    size = size or flat.shape[0]
    if place:
        flat = pltpu.roll(flat, flat.shape[1] - place * size, 1)
    lanes = lax.broadcasted_iota(jnp.int32, flat.shape, 1)
    return jnp.where(lanes < size, flat, 0.0)


def solve_many(pairs):
    size = pairs[0][0].shape[0]
    systems = [matrix + pltpu.roll(side, size, 1) for matrix, side in pairs]
    sublanes = lax.broadcasted_iota(jnp.int32, systems[0].shape, 0)

    def eliminated(values, column, scale, pivot):
        row = values[pivot : pivot + 1, :] * scale
        return jnp.where(sublanes == pivot, row, values - column * row)

    for first in range(0, size, PANEL):
        panels = [
            [jnp.broadcast_to(system[:, at : at + 1], system.shape) for at in range(first, first + PANEL)]
            for system in systems
        ]
        for pivot in range(first, first + PANEL):
            for which, (column, *later) in enumerate(panels):
                scale = 1.0 / column[pivot : pivot + 1, :]
                panels[which] = [eliminated(other, column, scale, pivot) for other in later]
                systems[which] = eliminated(systems[which], column, scale, pivot)
    return [window(system, 1) for system in systems]


def close_kernel(*refs):
    row_count = (len(refs) - 6) // 2
    row_refs = refs[:row_count]
    gram_refs = refs[row_count : 2 * row_count]
    col_ref, scaling_ref, query_ref, first_ref, solution_ref, residual_ref = refs[-6:]
    size = query_ref.shape[0]
    weight = graph_weight
    total = total_of([ref[...] for ref in gram_refs])
    g00 = symmetric(window(total, 0))
    g01 = flipped(window(total, 1))
    g11 = symmetric(window(total, 2))
    g12 = symmetric(window(total, 3))
    eye = (
        lax.broadcasted_iota(jnp.int32, total.shape, 0)
        == lax.broadcasted_iota(jnp.int32, total.shape, 1)
    ).astype(jnp.float32)
    curve = symmetric(g00 - weight * g01)
    steps, inverse = solve_many([(curve, g00), (g00, eye)])
    steps_t = flipped(steps)
    plain_gram = stacked(beside(g00, g01), beside(flipped(g01), g11))
    through_gram = stacked(beside(g01, g11), beside(g11, g12))
    after_first = beside(eye - steps_t, weight * steps_t)
    new_gram = symmetric(sandwich(after_first, plain_gram))
    mixing = times(inverse, new_gram)
    direction = after_first + flipped(mixing)
    curve = symmetric(sandwich(direction, plain_gram - weight * through_gram))
    (steps,) = solve_many([(curve, new_gram)])
    steps_t2 = flipped(steps)
    applied = direction - weight * pltpu.roll(direction, size, 1)
    solution_rows = exact_plain(beside(eye, steps_t2), stacked(steps_t, direction))
    residual_rows = exact_plain(beside(eye, -steps_t2), stacked(after_first, applied))
    rows = jnp.concatenate([solution_rows, residual_rows], axis=0)
    for part in range(first_ref.shape[0]):
        lanes = slice(part * 128, part * 128 + 128)
        basis = jnp.concatenate(
            [
                query_ref[:, lanes],
                first_ref[part],
                scaled_sum(row_refs, col_ref, scaling_ref, part),
                jnp.zeros_like(eye),
            ],
            axis=0,
        )
        values = exact_plain(rows, basis)
        solution_ref[:, lanes] = values[:size]
        residual_ref[:, lanes] = values[size:]


def pass_around(pieces, axis):
    count = len(pieces)
    return [pieces[0]] + [
        lax.ppermute(pieces[ahead], axis, [(at, (at + ahead) % count) for at in range(count)])
        for ahead in range(1, count)
    ]


def exchange(pieces, axis):
    return lax.all_to_all(pieces, axis, 0, 0, tiled=True)


def simple_call(kernel, shapes, name, *operands):
    return pl.pallas_call(
        kernel,
        out_shape=shapes,
        compiler_params=pltpu.CompilerParams(vmem_limit_bytes=SMALL_GRANT),
        name=name,
    )(*operands)


def sum_kernel(col_ref, gram_ref, total_ref):
    size = gram_ref.shape[0]
    col_count, sent, _ = col_ref.shape
    folded = total_of([col_ref[segment, sent - size // 2 :] for segment in range(col_count)])
    upper = window(folded, 0, size) + window(folded, 1, size)
    lower = window(folded, 2, size) + window(folded, 3, size)
    last = jnp.concatenate([upper, lower], axis=0)
    total_ref[...] = gram_ref[...] + pltpu.roll(last, 3 * size, 1)


def body(queries, block_spots, live_blocks, neighbor_cols, neighbor_sims):
    row_count = lax.axis_size("row")
    col_count = lax.axis_size("col")
    query_rows, seg_len = queries.shape
    per_seg = seg_len // 128
    places = (block_spots, live_blocks)
    piece = (per_seg, query_rows, 128)
    wide = jax.ShapeDtypeStruct(piece, jnp.float32)
    narrow = jax.ShapeDtypeStruct(piece, jnp.bfloat16)
    gram_shape = jax.ShapeDtypeStruct((query_rows, 128), jnp.float32)

    message = jax.ShapeDtypeStruct((col_count, per_seg + 1) + piece[1:], jnp.bfloat16)

    blocks, flipped_blocks, *row_sums, col_sums = build_blocks(
        places,
        neighbor_cols[0, 0],
        neighbor_sims[0, 0],
        row_count,
        col_count,
        per_seg,
    )
    col_part = exchange(col_sums.reshape(col_count, per_seg, 128), "col")
    row_parts = pass_around([None, *row_sums], "row")[1:]
    scaling, scaled, copies = simple_call(
        start_kernel,
        [jax.ShapeDtypeStruct((per_seg, 128), jnp.float32), narrow, message],
        "start",
        *row_parts,
        col_part,
        queries,
    )

    first_dirs = exchange(copies, "col")
    row_pieces = pass_around([scaled] * row_count, "row")
    total = backward_product(places, flipped_blocks, row_pieces, col_count)
    col_part = exchange(total, "col")
    totals = forward_product(places, blocks, first_dirs, row_count, piece)
    first, scaled, copies = simple_call(
        middle_kernel,
        [wide, narrow, message],
        "middle",
        *pass_around(totals, "row"),
        col_part,
        scaling,
        queries,
    )

    col_dirs = exchange(copies, "col")
    row_pieces = pass_around([scaled] * row_count, "row")
    total = backward_product(places, flipped_blocks, row_pieces, col_count)
    more = jax.ShapeDtypeStruct(
        (col_count, total.shape[1] + query_rows // 2, 128), jnp.bfloat16
    )
    total, gram = simple_call(
        attach_kernel, [more, gram_shape], "attach", first_dirs, col_dirs, total
    )
    col_part = exchange(total, "col")
    totals = forward_product(places, blocks, col_dirs, row_count, piece)
    row_parts = pass_around(totals, "row")
    (gram,) = simple_call(sum_kernel, [gram_shape], "gram_sum", col_part, gram)
    flat = jax.ShapeDtypeStruct(queries.shape, jnp.float32)
    return tuple(
        simple_call(
            close_kernel,
            [flat, flat],
            "close",
            *row_parts,
            *pass_around([gram] * row_count, "row"),
            col_part,
            scaling,
            queries,
            first,
        )
    )


def solution(mesh):
    placed = (
        P(None, ("row", "col")),
        P("row", "col", None),
        P("row", "col"),
        P("row", "col", None, None, None),
        P("row", "col", None, None, None),
    )
    return jax.shard_map(
        body,
        mesh=mesh,
        in_specs=placed,
        out_specs=(P(None, ("row", "col")), P(None, ("row", "col"))),
        check_vma=False,
    )
```

```python
import functools

import jax
import jax.numpy as jnp
from jax import lax
from jax.experimental import pallas as pl
from jax.experimental.pallas import tpu as pltpu
from jax.sharding import PartitionSpec as P

graph_weight = 0.95
GROUP = 32
BATCH = 32
SPARE = 4
PANEL = 8
BUILD_GRANT = 60 * 1024 * 1024
PRODUCT_GRANT = 40 * 1024 * 1024
SMALL_GRANT = 24 * 1024 * 1024


def dot_plain(left, right, **kwargs):
    return lax.dot_general(
        left, right, (((1,), (0,)), ((), ())), preferred_element_type=jnp.float32, **kwargs
    )


def dot_across(left, right, **kwargs):
    return lax.dot_general(
        left, right, (((1,), (1,)), ((), ())), preferred_element_type=jnp.float32, **kwargs
    )


exact_plain = functools.partial(dot_plain, precision=lax.Precision.HIGHEST)
exact_across = functools.partial(dot_across, precision=lax.Precision.HIGHEST)


def divided(number, size):
    if size & (size - 1):
        return lax.div(number, size), lax.rem(number, size)
    return number >> (size.bit_length() - 1), number & (size - 1)


def place_of(places, slot, col_blocks):
    return divided(places[0][0, 0, slot], col_blocks)


def live_count(places):
    return places[1][0, 0]


def group_count(places, group):
    return (live_count(places) + group - 1) // group


def group_copy(source, target, sems, index, group):
    window = pl.ds(index * group, group)
    return pltpu.make_async_copy(source.at[window], target.at[window], sems.at[index])


def build_kernel(
    spots_ref, live_ref, index_hbm, value_hbm, block_hbm, flipped_hbm, *refs
):
    (
        *row_outs,
        col_out_ref,
        index_ref,
        value_ref,
        block_ref,
        flipped_ref,
        row_ref,
        col_ref,
        index_sems,
        value_sems,
        block_sems,
        flipped_sems,
    ) = refs
    places = (spots_ref, live_ref)
    row_count = len(row_outs) + 1
    per_seg = row_outs[0].shape[0]
    col_blocks = col_out_ref.shape[0]
    groups = group_count(places, BATCH) * (BATCH // GROUP)

    def start_copies(index, _):
        group_copy(index_hbm, index_ref, index_sems, index, GROUP).start()
        group_copy(value_hbm, value_ref, value_sems, index, GROUP).start()
        return 0

    lax.fori_loop(0, groups, start_copies, 0)
    row_ref[...] = jnp.zeros_like(row_ref)
    col_ref[...] = jnp.zeros_like(col_ref)
    rows_16 = lax.broadcasted_iota(jnp.int32, (16, 128), 0)
    diagonal = lax.broadcasted_iota(jnp.int32, (128, 128), 0) == lax.broadcasted_iota(
        jnp.int32, (128, 128), 1
    )
    identity = jnp.where(diagonal, 1.0, 0.0).astype(jnp.bfloat16)
    zero = jnp.zeros((16, 128), jnp.bfloat16)

    def build_group(index, _):
        group_copy(index_hbm, index_ref, index_sems, index, GROUP).wait()
        group_copy(value_hbm, value_ref, value_sems, index, GROUP).wait()
        targets = [(rows_16 + 16 * part).astype(jnp.int16) for part in range(8)]

        def load_pair(inside):
            tables = []
            for slot in (index * GROUP + inside, index * GROUP + inside + 1):
                active = (slot < live_count(places)).astype(jnp.float32)
                values = value_ref[slot].astype(jnp.float32) * active
                tables.append((slot, index_ref[slot], values))
            return tables

        def build_pair(tables):
            sums = [[zero] * 8 for _ in tables]
            for entry in range(0, 16, 2):
                for which, (_, indices, values) in enumerate(tables):
                    pair = []
                    for at in (entry, entry + 1):
                        index_row = jnp.broadcast_to(indices[at : at + 1], (16, 128))
                        value_row = jnp.broadcast_to(values[at : at + 1], (16, 128))
                        pair.append((index_row.astype(jnp.int16), value_row.astype(jnp.bfloat16)))
                    for part in range(8):
                        first, second = [
                            jnp.where(index_row == targets[part], value_row, zero)
                            for index_row, value_row in pair
                        ]
                        sums[which][part] = sums[which][part] + (first + second)
            return [jnp.concatenate(parts, axis=0) for parts in sums]

        def store_turned(tables, turned):
            for (slot, _, values), block in zip(tables, turned):
                row_block, col_block = place_of(places, slot, col_blocks)
                flipped_ref[slot] = block.astype(jnp.bfloat16)
                col_ref[col_block] += jnp.sum(block.reshape(16, 8, 128), axis=0)
                row_ref[row_block] += values[:8] + values[8:]

        tables = load_pair(0)
        waiting = None
        for inside in range(0, GROUP, 2):
            following = load_pair(inside + 2) if inside + 2 < GROUP else None
            blocks = build_pair(tables)
            if waiting:
                store_turned(*waiting)
            for (slot, _, _), block in zip(tables, blocks):
                block_ref[slot] = block
            waiting = (tables, [dot_across(identity, block) for block in blocks])
            tables = following
        store_turned(*waiting)
        group_copy(block_ref, block_hbm, block_sems, index, GROUP).start()
        group_copy(flipped_ref, flipped_hbm, flipped_sems, index, GROUP).start()
        return 0

    lax.fori_loop(0, groups, build_group, 0)
    for ahead, out in enumerate(row_outs, 1):
        first = lax.rem(lax.axis_index("row") + ahead, row_count) * per_seg
        for part in range(per_seg):
            out[part : part + 1] = jnp.sum(row_ref[first + part], axis=0, keepdims=True)
    for part in range(per_seg):
        own = lax.axis_index("col") * per_seg + part
        col_ref[own] += row_ref[lax.axis_index("row") * per_seg + part]
    for col_block in range(col_blocks):
        col_out_ref[col_block : col_block + 1] = jnp.sum(
            col_ref[col_block], axis=0, keepdims=True
        )

    def finish_copies(index, _):
        group_copy(block_ref, block_hbm, block_sems, index, GROUP).wait()
        group_copy(flipped_ref, flipped_hbm, flipped_sems, index, GROUP).wait()
        return 0

    lax.fori_loop(0, groups, finish_copies, 0)


SCALARS = pl.BlockSpec(memory_space=pltpu.SMEM)
ANYWHERE = pl.BlockSpec(memory_space=pl.ANY)
IN_VMEM = pl.BlockSpec(memory_space=pltpu.VMEM)


def build_blocks(
    places, index_table, value_table, row_count, col_count, per_seg
):
    slots = index_table.shape[0]
    groups = slots // GROUP
    sum_shapes = [(per_seg, 128)] * (row_count - 1) + [(col_count * per_seg, 128)]
    return pl.pallas_call(
        build_kernel,
        in_specs=[SCALARS, SCALARS, ANYWHERE, ANYWHERE],
        out_specs=[ANYWHERE] * 2 + [IN_VMEM] * len(sum_shapes),
        out_shape=[jax.ShapeDtypeStruct((SPARE * slots, 128, 128), jnp.bfloat16)] * 2
        + [jax.ShapeDtypeStruct(shape, jnp.float32) for shape in sum_shapes],
        scratch_shapes=[
            pltpu.VMEM(index_table.shape, index_table.dtype),
            pltpu.VMEM(value_table.shape, value_table.dtype),
            pltpu.VMEM((slots, 128, 128), jnp.bfloat16),
            pltpu.VMEM((slots, 128, 128), jnp.bfloat16),
            pltpu.VMEM((row_count * per_seg, 8, 128), jnp.float32),
            pltpu.VMEM((col_count * per_seg, 8, 128), jnp.float32),
            pltpu.SemaphoreType.DMA((groups,)),
            pltpu.SemaphoreType.DMA((groups,)),
            pltpu.SemaphoreType.DMA((groups,)),
            pltpu.SemaphoreType.DMA((groups,)),
        ],
        compiler_params=pltpu.CompilerParams(vmem_limit_bytes=BUILD_GRANT),
        name="build_blocks",
    )(*places, index_table, value_table)


def each_group(places, block_hbm, block_ref, sems, prepare, run_group):
    groups = group_count(places, BATCH)

    def start_copy(index, _):
        group_copy(block_hbm, block_ref, sems, index, BATCH).start()
        return 0

    lax.fori_loop(0, groups, start_copy, 0)
    prepare()

    def one_group(index, _):
        group_copy(block_hbm, block_ref, sems, index, BATCH).wait()
        run_group(index * BATCH)
        return 0

    lax.fori_loop(0, groups, one_group, 0)


def add_products(places, first_slot, block_ref, direction, total_refs):
    sums = []
    for inside in range(BATCH):
        slot = first_slot + inside
        sums.append(dot_plain(direction(places(slot)[0]), block_ref[slot]))
    for inside in range(BATCH):
        total_ref = total_refs[inside % len(total_refs)]
        total_ref[places(first_slot + inside)[1]] += sums[inside]


def fill_directions(pieces, dir_ref, mine, per_seg):
    for behind, piece in enumerate(pieces):
        first = lax.rem(mine + (len(pieces) - behind), len(pieces)) * per_seg
        for part in range(per_seg):
            dir_ref[first + part] = piece[part]


def backward_kernel(row_count, spots_ref, live_ref, block_hbm, *refs):
    places = (spots_ref, live_ref)
    row_pieces = refs[:row_count]
    terms_refs = refs[row_count:-6]
    col_out_ref, block_ref, sems, row_dir_ref, even_ref, odd_ref = refs[-6:]
    per_seg = row_pieces[0].shape[0]
    col_blocks = even_ref.shape[0]

    def prepare():
        even_ref[...] = jnp.zeros_like(even_ref)
        odd_ref[...] = jnp.zeros_like(odd_ref)
        fill_directions(row_pieces, row_dir_ref, lax.axis_index("row"), per_seg)

    def run_group(first_slot):
        add_products(
            lambda slot: place_of(places, slot, col_blocks),
            first_slot,
            block_ref,
            lambda row_block: row_dir_ref[row_block],
            [even_ref, odd_ref],
        )

    each_group(places, block_hbm, block_ref, sems, prepare, run_group)
    size = even_ref.shape[1]
    for segment in range(col_out_ref.shape[0]):
        for part in range(per_seg):
            col_block = segment * per_seg + part
            values = even_ref[col_block] + odd_ref[col_block]
            col_out_ref[segment, part * size : part * size + size] = values.astype(
                col_out_ref.dtype
            )
        for terms_ref in terms_refs:
            col_out_ref[segment, per_seg * size :] = terms_ref[...]


def in_terms(values, count):
    terms = []
    for _ in range(count):
        terms.append(values.astype(jnp.bfloat16))
        values = values - terms[-1].astype(jnp.float32)
    return terms


def side_by_side(terms, width=32):
    total = terms[0].astype(jnp.float32)
    for place, term in enumerate(terms[1:], 1):
        total = total + pltpu.roll(term.astype(jnp.float32), place * width, 1)
    return total.astype(jnp.bfloat16)


def attach_kernel(first_col_ref, col_dir_ref, total_ref, message_ref, gram_ref):
    col_count, sent, size, _ = col_dir_ref.shape
    per_seg = sent - 1

    def add_segment(segment, gram):
        for part in range(per_seg):
            rows = slice(part * size, part * size + size)
            values = total_ref[segment, rows]
            message_ref[segment, rows] = values
            gram += dot_across(values, tall(col_dir_ref[segment, part]))
        return gram

    gram = lax.fori_loop(
        0, col_count, add_segment, jnp.zeros((size, 128), jnp.float32), unroll=8
    )
    half = size // 2
    terms = side_by_side(in_terms(gram, 2)).astype(jnp.float32)
    folded = terms[:half] + pltpu.roll(terms[half:], 64, 1)
    for segment in range(col_count):
        message_ref[segment, per_seg * size :] = folded.astype(message_ref.dtype)
    queries = total_of([first_col_ref[segment, per_seg * size :] for segment in range(col_count)])
    queries = total_of([window(queries, term) for term in range(3)])
    pairs = total_of([col_dir_ref[segment, per_seg] for segment in range(col_count)])
    lanes = lax.broadcasted_iota(jnp.int32, pairs.shape, 1)
    pairs = jnp.where(lanes < 2 * size, pairs + pltpu.roll(pairs, 128 - 2 * size, 1), 0.0)
    gram_ref[...] = beside(queries, pairs)


def forward_kernel(spots_ref, live_ref, block_hbm, col_dir_ref, *refs):
    places = (spots_ref, live_ref)
    *row_outs, block_ref, sems, even_ref, odd_ref = refs
    per_seg = row_outs[0].shape[0]
    col_blocks = col_dir_ref.shape[0] * per_seg

    def prepare():
        even_ref[...] = jnp.zeros_like(even_ref)
        odd_ref[...] = jnp.zeros_like(odd_ref)

    def run_group(first_slot):
        add_products(
            lambda slot: place_of(places, slot, col_blocks)[::-1],
            first_slot,
            block_ref,
            lambda col_block: col_dir_ref[divided(col_block, per_seg)],
            [even_ref, odd_ref],
        )

    each_group(places, block_hbm, block_ref, sems, prepare, run_group)
    for ahead, out in enumerate(row_outs):
        first = lax.rem(lax.axis_index("row") + ahead, len(row_outs)) * per_seg
        for part in range(per_seg):
            values = even_ref[first + part] + odd_ref[first + part]
            out[part] = values.astype(out.dtype)


def over_blocks(kernel, name, places, blocks, inputs, outputs, scratch):
    slots = blocks.shape[0] // SPARE
    return pl.pallas_call(
        kernel,
        in_specs=[SCALARS, SCALARS, ANYWHERE] + [IN_VMEM] * len(inputs),
        out_specs=[IN_VMEM] * len(outputs),
        out_shape=outputs,
        scratch_shapes=[
            pltpu.VMEM((slots,) + blocks.shape[1:], blocks.dtype),
            pltpu.SemaphoreType.DMA((slots // BATCH,)),
        ]
        + scratch,
        compiler_params=pltpu.CompilerParams(vmem_limit_bytes=PRODUCT_GRANT),
        cost_estimate=pl.CostEstimate(
            flops=2 * slots * 32 * 128 * 128, bytes_accessed=2 * slots * 128 * 128, transcendentals=0
        ),
        name=name,
    )(*places, blocks, *inputs)


def backward_product(places, blocks, row_pieces, col_count, *terms):
    per_seg, rows, lanes = row_pieces[0].shape
    sent = per_seg + len(terms)
    col_shape = (col_count * per_seg, rows, lanes)
    (total,) = over_blocks(
        functools.partial(backward_kernel, len(row_pieces)),
        "backward_product",
        places,
        blocks,
        [*row_pieces, *terms],
        [jax.ShapeDtypeStruct((col_count, sent * rows, lanes), jnp.bfloat16)],
        [
            pltpu.VMEM((len(row_pieces) * per_seg, rows, lanes), jnp.bfloat16),
            pltpu.VMEM(col_shape, jnp.float32),
            pltpu.VMEM(col_shape, jnp.float32),
        ],
    )
    return total


def forward_product(places, blocks, col_dirs, row_count, piece):
    row_shape = (row_count * piece[0],) + piece[1:]
    return over_blocks(
        forward_kernel,
        "forward_product",
        places,
        blocks,
        [col_dirs],
        [jax.ShapeDtypeStruct(piece, jnp.bfloat16)] * row_count,
        [pltpu.VMEM(row_shape, jnp.float32), pltpu.VMEM(row_shape, jnp.float32)],
    )


def total_of(values):
    total = values[0].astype(jnp.float32)
    for value in values[1:]:
        total = total + value.astype(jnp.float32)
    return total


def leading(ref):
    return [ref.at[index] for index in range(ref.shape[0])]


def start_kernel(*refs):
    *row_refs, col_ref, query_ref, scaling_ref, scaled_ref, copies_ref = refs
    degree = 1.0 + 0.5 * total_of([ref[...] for ref in [*row_refs, *leading(col_ref)]])
    scaling = 1.0 / jnp.sqrt(degree)
    scaling_ref[...] = scaling
    for part in range(scaled_ref.shape[0]):
        query = query_ref[:, part * 128 : part * 128 + 128]
        scaled = (scaling[part : part + 1] * query).astype(jnp.bfloat16)
        scaled_ref[part] = scaled
        for copy in range(copies_ref.shape[0]):
            copies_ref[copy, part] = scaled


def query_gram_kernel(query_ref, terms_ref):
    queries = query_ref[...]
    rest = jnp.zeros((128 - queries.shape[0], queries.shape[1]), queries.dtype)
    gram = exact_across(queries, jnp.concatenate([queries, rest], axis=0))
    terms_ref[...] = side_by_side(in_terms(gram, 3))


def scaled_sum(row_refs, col_ref, scaling_ref, part):
    scaling = scaling_ref[part : part + 1]
    size = row_refs[0].shape[1]
    rows = slice(part * size, part * size + size)
    total = total_of([ref[part] for ref in row_refs] + [ref[rows] for ref in leading(col_ref)])
    return scaling * (0.5 * total)


def middle_kernel(*refs):
    *row_refs, col_ref, scaling_ref, query_ref, first_ref, scaled_ref, copies_ref = refs
    size = query_ref.shape[0]
    per_seg = scaling_ref.shape[0]
    firsts = []
    for part in range(per_seg):
        first = scaled_sum(row_refs, col_ref, scaling_ref, part)
        first_ref[part] = first
        scaled = (scaling_ref[part : part + 1] * first).astype(jnp.bfloat16)
        scaled_ref[part] = scaled
        for copy in range(copies_ref.shape[0]):
            copies_ref[copy, part] = scaled
        firsts.append(first)
    first = jnp.concatenate(firsts, axis=1)
    rest = jnp.zeros((128 - 2 * size, first.shape[1]), first.dtype)
    grams = exact_across(first, jnp.concatenate([query_ref[...], first, rest], axis=0))
    terms = side_by_side(in_terms(grams, 2), 2 * size)
    for copy in range(copies_ref.shape[0]):
        copies_ref[copy, per_seg] = terms


def tall(flat):
    rest = flat.shape[1] - flat.shape[0]
    return jnp.concatenate([flat, jnp.zeros((rest, flat.shape[1]), flat.dtype)], axis=0)


def flipped(flat):
    return tall(flat).T[: flat.shape[0]]


def times(left, right):
    return exact_plain(left, tall(right))


def beside(left, right):
    return left + pltpu.roll(right, left.shape[0], 1)


def stacked(upper, lower):
    rest = jnp.zeros((upper.shape[1] - 2 * upper.shape[0], upper.shape[1]), upper.dtype)
    return jnp.concatenate([upper, lower, rest], axis=0)


def sandwich(rows, middle):
    return exact_across(exact_plain(rows, middle), tall(rows))


def symmetric(flat):
    return 0.5 * (flat + flipped(flat))


def window(flat, place, size=None):
    size = size or flat.shape[0]
    if place:
        flat = pltpu.roll(flat, flat.shape[1] - place * size, 1)
    lanes = lax.broadcasted_iota(jnp.int32, flat.shape, 1)
    return jnp.where(lanes < size, flat, 0.0)


def solve_many(pairs):
    size = pairs[0][0].shape[0]
    systems = [matrix + pltpu.roll(side, size, 1) for matrix, side in pairs]
    sublanes = lax.broadcasted_iota(jnp.int32, systems[0].shape, 0)

    def eliminated(values, column, scale, pivot):
        row = values[pivot : pivot + 1, :] * scale
        return jnp.where(sublanes == pivot, row, values - column * row)

    for first in range(0, size, PANEL):
        panels = [
            [jnp.broadcast_to(system[:, at : at + 1], system.shape) for at in range(first, first + PANEL)]
            for system in systems
        ]
        for pivot in range(first, first + PANEL):
            for which, (column, *later) in enumerate(panels):
                scale = 1.0 / column[pivot : pivot + 1, :]
                panels[which] = [eliminated(other, column, scale, pivot) for other in later]
                systems[which] = eliminated(systems[which], column, scale, pivot)
    return [window(system, 1) for system in systems]


def close_kernel(*refs):
    row_count = (len(refs) - 6) // 2
    row_refs = refs[:row_count]
    gram_refs = refs[row_count : 2 * row_count]
    col_ref, scaling_ref, query_ref, first_ref, solution_ref, residual_ref = refs[-6:]
    size = query_ref.shape[0]
    weight = graph_weight
    total = total_of([ref[...] for ref in gram_refs])
    g00 = symmetric(window(total, 0))
    g01 = flipped(window(total, 1))
    g11 = symmetric(window(total, 2))
    g12 = symmetric(window(total, 3))
    eye = (
        lax.broadcasted_iota(jnp.int32, total.shape, 0)
        == lax.broadcasted_iota(jnp.int32, total.shape, 1)
    ).astype(jnp.float32)
    curve = symmetric(g00 - weight * g01)
    steps, inverse = solve_many([(curve, g00), (g00, eye)])
    steps_t = flipped(steps)
    plain_gram = stacked(beside(g00, g01), beside(flipped(g01), g11))
    through_gram = stacked(beside(g01, g11), beside(g11, g12))
    after_first = beside(eye - steps_t, weight * steps_t)
    new_gram = symmetric(sandwich(after_first, plain_gram))
    mixing = times(inverse, new_gram)
    direction = after_first + flipped(mixing)
    curve = symmetric(sandwich(direction, plain_gram - weight * through_gram))
    (steps,) = solve_many([(curve, new_gram)])
    steps_t2 = flipped(steps)
    applied = direction - weight * pltpu.roll(direction, size, 1)
    solution_rows = exact_plain(beside(eye, steps_t2), stacked(steps_t, direction))
    residual_rows = exact_plain(beside(eye, -steps_t2), stacked(after_first, applied))
    rows = jnp.concatenate([solution_rows, residual_rows], axis=0)
    for part in range(first_ref.shape[0]):
        lanes = slice(part * 128, part * 128 + 128)
        basis = jnp.concatenate(
            [
                query_ref[:, lanes],
                first_ref[part],
                scaled_sum(row_refs, col_ref, scaling_ref, part),
                jnp.zeros_like(eye),
            ],
            axis=0,
        )
        values = exact_plain(rows, basis)
        solution_ref[:, lanes] = values[:size]
        residual_ref[:, lanes] = values[size:]


def pass_around(pieces, axis):
    count = len(pieces)
    return [pieces[0]] + [
        lax.ppermute(pieces[ahead], axis, [(at, (at + ahead) % count) for at in range(count)])
        for ahead in range(1, count)
    ]


def exchange(pieces, axis):
    return lax.all_to_all(pieces, axis, 0, 0, tiled=True)


def simple_call(kernel, shapes, name, *operands):
    return pl.pallas_call(
        kernel,
        out_shape=shapes,
        compiler_params=pltpu.CompilerParams(vmem_limit_bytes=SMALL_GRANT),
        name=name,
    )(*operands)


def sum_kernel(col_ref, gram_ref, total_ref):
    size = gram_ref.shape[0]
    col_count, sent, _ = col_ref.shape
    folded = total_of([col_ref[segment, sent - size // 2 :] for segment in range(col_count)])
    upper = window(folded, 0, size) + window(folded, 1, size)
    lower = window(folded, 2, size) + window(folded, 3, size)
    last = jnp.concatenate([upper, lower], axis=0)
    total_ref[...] = gram_ref[...] + pltpu.roll(last, 3 * size, 1)


def body(queries, block_spots, live_blocks, neighbor_cols, neighbor_sims):
    row_count = lax.axis_size("row")
    col_count = lax.axis_size("col")
    query_rows, seg_len = queries.shape
    per_seg = seg_len // 128
    places = (block_spots, live_blocks)
    piece = (per_seg, query_rows, 128)
    wide = jax.ShapeDtypeStruct(piece, jnp.float32)
    narrow = jax.ShapeDtypeStruct(piece, jnp.bfloat16)
    gram_shape = jax.ShapeDtypeStruct((query_rows, 128), jnp.float32)

    message = jax.ShapeDtypeStruct((col_count, per_seg + 1) + piece[1:], jnp.bfloat16)

    blocks, flipped_blocks, *row_sums, col_sums = build_blocks(
        places,
        neighbor_cols[0, 0],
        neighbor_sims[0, 0],
        row_count,
        col_count,
        per_seg,
    )
    col_part = exchange(col_sums.reshape(col_count, per_seg, 128), "col")
    row_parts = pass_around([None, *row_sums], "row")[1:]
    scaling, scaled, copies = simple_call(
        start_kernel,
        [
            jax.ShapeDtypeStruct((per_seg, 128), jnp.float32),
            narrow,
            jax.ShapeDtypeStruct((col_count,) + piece, jnp.bfloat16),
        ],
        "start",
        *row_parts,
        col_part,
        queries,
    )

    first_dirs = exchange(copies, "col")
    row_pieces = pass_around([scaled] * row_count, "row")
    (terms,) = simple_call(
        query_gram_kernel,
        [jax.ShapeDtypeStruct((query_rows, 128), jnp.bfloat16)],
        "query_gram",
        queries,
    )
    total = backward_product(places, flipped_blocks, row_pieces, col_count, terms)
    first_part = exchange(total, "col")
    totals = forward_product(places, blocks, first_dirs, row_count, piece)
    first, scaled, copies = simple_call(
        middle_kernel,
        [wide, narrow, message],
        "middle",
        *pass_around(totals, "row"),
        first_part,
        scaling,
        queries,
    )

    col_dirs = exchange(copies, "col")
    row_pieces = pass_around([scaled] * row_count, "row")
    total = backward_product(places, flipped_blocks, row_pieces, col_count)
    more = jax.ShapeDtypeStruct(
        (col_count, total.shape[1] + query_rows // 2, 128), jnp.bfloat16
    )
    total, gram = simple_call(
        attach_kernel, [more, gram_shape], "attach", first_part, col_dirs, total
    )
    col_part = exchange(total, "col")
    totals = forward_product(places, blocks, col_dirs, row_count, piece)
    row_parts = pass_around(totals, "row")
    (gram,) = simple_call(sum_kernel, [gram_shape], "gram_sum", col_part, gram)
    flat = jax.ShapeDtypeStruct(queries.shape, jnp.float32)
    return tuple(
        simple_call(
            close_kernel,
            [flat, flat],
            "close",
            *row_parts,
            *pass_around([gram] * row_count, "row"),
            col_part,
            scaling,
            queries,
            first,
        )
    )


def solution(mesh):
    placed = (
        P(None, ("row", "col")),
        P("row", "col", None),
        P("row", "col"),
        P("row", "col", None, None, None),
        P("row", "col", None, None, None),
    )
    return jax.shard_map(
        body,
        mesh=mesh,
        in_specs=placed,
        out_specs=(P(None, ("row", "col")), P(None, ("row", "col"))),
        check_vma=False,
    )
```

```python
import functools

import jax
import jax.numpy as jnp
from jax import lax
from jax.experimental import pallas as pl
from jax.experimental.pallas import tpu as pltpu
from jax.sharding import PartitionSpec as P

graph_weight = 0.95
GROUP = 32
HALF = GROUP // 2
BATCH = 32
SPARE = 4
PANEL = 8
BUILD_GRANT = 60 * 1024 * 1024
PRODUCT_GRANT = 40 * 1024 * 1024
SMALL_GRANT = 24 * 1024 * 1024


def dot_plain(left, right, **kwargs):
    return lax.dot_general(
        left, right, (((1,), (0,)), ((), ())), preferred_element_type=jnp.float32, **kwargs
    )


def dot_across(left, right, **kwargs):
    return lax.dot_general(
        left, right, (((1,), (1,)), ((), ())), preferred_element_type=jnp.float32, **kwargs
    )


exact_plain = functools.partial(dot_plain, precision=lax.Precision.HIGHEST)
exact_across = functools.partial(dot_across, precision=lax.Precision.HIGHEST)


def divided(number, size):
    if size & (size - 1):
        return lax.div(number, size), lax.rem(number, size)
    return number >> (size.bit_length() - 1), number & (size - 1)


def place_of(places, slot, col_blocks):
    return divided(places[0][0, 0, slot], col_blocks)


def live_count(places):
    return places[1][0, 0]


def group_count(places, group):
    return (live_count(places) + group - 1) // group


def group_copy(source, target, sems, index, group):
    window = pl.ds(index * group, group)
    return pltpu.make_async_copy(source.at[window], target.at[window], sems.at[index])


def build_kernel(
    spots_ref, live_ref, index_hbm, value_hbm, block_hbm, flipped_hbm, *refs
):
    (
        *row_outs,
        col_out_ref,
        index_ref,
        value_ref,
        block_ref,
        flipped_ref,
        row_ref,
        col_ref,
        index_sems,
        value_sems,
        block_sems,
        flipped_sems,
    ) = refs
    places = (spots_ref, live_ref)
    row_count = len(row_outs) + 1
    per_seg = row_outs[0].shape[0]
    col_blocks = col_out_ref.shape[0]
    groups = group_count(places, BATCH) * (BATCH // GROUP)

    def start_copies(index, _):
        group_copy(index_hbm, index_ref, index_sems, index, GROUP).start()
        group_copy(value_hbm, value_ref, value_sems, index, GROUP).start()
        return 0

    lax.fori_loop(0, groups, start_copies, 0)
    row_ref[...] = jnp.zeros_like(row_ref)
    col_ref[...] = jnp.zeros_like(col_ref)
    rows_16 = lax.broadcasted_iota(jnp.int32, (16, 128), 0)
    diagonal = lax.broadcasted_iota(jnp.int32, (128, 128), 0) == lax.broadcasted_iota(
        jnp.int32, (128, 128), 1
    )
    identity = jnp.where(diagonal, 1.0, 0.0).astype(jnp.bfloat16)
    zero = jnp.zeros((16, 128), jnp.bfloat16)

    def build_group(index, _):
        group_copy(index_hbm, index_ref, index_sems, index, GROUP).wait()
        group_copy(value_hbm, value_ref, value_sems, index, GROUP).wait()
        targets = [(rows_16 + 16 * part).astype(jnp.int16) for part in range(8)]

        def load_pair(inside):
            tables = []
            for slot in (index * GROUP + inside, index * GROUP + inside + 1):
                active = (slot < live_count(places)).astype(jnp.float32)
                values = value_ref[slot].astype(jnp.float32) * active
                tables.append((slot, index_ref[slot], values))
            return tables

        def build_pair(tables):
            sums = [[zero] * 8 for _ in tables]
            for entry in range(0, 16, 2):
                for which, (_, indices, values) in enumerate(tables):
                    pair = []
                    for at in (entry, entry + 1):
                        index_row = jnp.broadcast_to(indices[at : at + 1], (16, 128))
                        value_row = jnp.broadcast_to(values[at : at + 1], (16, 128))
                        pair.append((index_row.astype(jnp.int16), value_row.astype(jnp.bfloat16)))
                    for part in range(8):
                        first, second = [
                            jnp.where(index_row == targets[part], value_row, zero)
                            for index_row, value_row in pair
                        ]
                        sums[which][part] = sums[which][part] + (first + second)
            return [jnp.concatenate(parts, axis=0) for parts in sums]

        def store_turned(tables, turned):
            for (slot, _, values), block in zip(tables, turned):
                row_block, col_block = place_of(places, slot, col_blocks)
                flipped_ref[slot] = block.astype(jnp.bfloat16)
                col_ref[col_block] += jnp.sum(block.reshape(16, 8, 128), axis=0)
                row_ref[row_block] += values[:8] + values[8:]

        tables = load_pair(0)
        waiting = None
        for inside in range(0, GROUP, 2):
            following = load_pair(inside + 2) if inside + 2 < GROUP else None
            blocks = build_pair(tables)
            if waiting:
                store_turned(*waiting)
            if inside == HALF:
                group_copy(block_ref, block_hbm, block_sems, 2 * index, HALF).start()
                group_copy(flipped_ref, flipped_hbm, flipped_sems, 2 * index, HALF).start()
            for (slot, _, _), block in zip(tables, blocks):
                block_ref[slot] = block
            waiting = (tables, [dot_across(identity, block) for block in blocks])
            tables = following
        store_turned(*waiting)
        group_copy(block_ref, block_hbm, block_sems, 2 * index + 1, HALF).start()
        group_copy(flipped_ref, flipped_hbm, flipped_sems, 2 * index + 1, HALF).start()
        return 0

    lax.fori_loop(0, groups, build_group, 0)
    for ahead, out in enumerate(row_outs, 1):
        first = lax.rem(lax.axis_index("row") + ahead, row_count) * per_seg
        for part in range(per_seg):
            out[part : part + 1] = jnp.sum(row_ref[first + part], axis=0, keepdims=True)
    for part in range(per_seg):
        own = lax.axis_index("col") * per_seg + part
        col_ref[own] += row_ref[lax.axis_index("row") * per_seg + part]
    for col_block in range(col_blocks):
        col_out_ref[col_block : col_block + 1] = jnp.sum(
            col_ref[col_block], axis=0, keepdims=True
        )

    def finish_copies(index, _):
        group_copy(block_ref, block_hbm, block_sems, index, HALF).wait()
        group_copy(flipped_ref, flipped_hbm, flipped_sems, index, HALF).wait()
        return 0

    lax.fori_loop(0, 2 * groups, finish_copies, 0)


SCALARS = pl.BlockSpec(memory_space=pltpu.SMEM)
ANYWHERE = pl.BlockSpec(memory_space=pl.ANY)
IN_VMEM = pl.BlockSpec(memory_space=pltpu.VMEM)


def build_blocks(
    places, index_table, value_table, row_count, col_count, per_seg
):
    slots = index_table.shape[0]
    groups = slots // GROUP
    sum_shapes = [(per_seg, 128)] * (row_count - 1) + [(col_count * per_seg, 128)]
    return pl.pallas_call(
        build_kernel,
        in_specs=[SCALARS, SCALARS, ANYWHERE, ANYWHERE],
        out_specs=[ANYWHERE] * 2 + [IN_VMEM] * len(sum_shapes),
        out_shape=[jax.ShapeDtypeStruct((SPARE * slots, 128, 128), jnp.bfloat16)] * 2
        + [jax.ShapeDtypeStruct(shape, jnp.float32) for shape in sum_shapes],
        scratch_shapes=[
            pltpu.VMEM(index_table.shape, index_table.dtype),
            pltpu.VMEM(value_table.shape, value_table.dtype),
            pltpu.VMEM((slots, 128, 128), jnp.bfloat16),
            pltpu.VMEM((slots, 128, 128), jnp.bfloat16),
            pltpu.VMEM((row_count * per_seg, 8, 128), jnp.float32),
            pltpu.VMEM((col_count * per_seg, 8, 128), jnp.float32),
            pltpu.SemaphoreType.DMA((groups,)),
            pltpu.SemaphoreType.DMA((groups,)),
            pltpu.SemaphoreType.DMA((2 * groups,)),
            pltpu.SemaphoreType.DMA((2 * groups,)),
        ],
        compiler_params=pltpu.CompilerParams(vmem_limit_bytes=BUILD_GRANT),
        name="build_blocks",
    )(*places, index_table, value_table)


def each_group(places, block_hbm, block_ref, sems, prepare, run_group):
    groups = group_count(places, BATCH)

    def start_copy(index, _):
        group_copy(block_hbm, block_ref, sems, index, BATCH).start()
        return 0

    lax.fori_loop(0, groups, start_copy, 0)
    prepare()

    def one_group(index, _):
        group_copy(block_hbm, block_ref, sems, index, BATCH).wait()
        run_group(index * BATCH)
        return 0

    lax.fori_loop(0, groups, one_group, 0)


def add_products(places, first_slot, block_ref, direction, total_refs):
    sums = []
    for inside in range(BATCH):
        slot = first_slot + inside
        sums.append(dot_plain(direction(places(slot)[0]), block_ref[slot]))
    for inside in range(BATCH):
        total_ref = total_refs[inside % len(total_refs)]
        total_ref[places(first_slot + inside)[1]] += sums[inside]


def fill_directions(pieces, dir_ref, mine, per_seg):
    for behind, piece in enumerate(pieces):
        first = lax.rem(mine + (len(pieces) - behind), len(pieces)) * per_seg
        for part in range(per_seg):
            dir_ref[first + part] = piece[part]


def backward_kernel(row_count, spots_ref, live_ref, block_hbm, *refs):
    places = (spots_ref, live_ref)
    row_pieces = refs[:row_count]
    col_out_ref, block_ref, sems, row_dir_ref, even_ref, odd_ref = refs[row_count:]
    per_seg = row_pieces[0].shape[0]
    col_blocks = even_ref.shape[0]

    def prepare():
        even_ref[...] = jnp.zeros_like(even_ref)
        odd_ref[...] = jnp.zeros_like(odd_ref)
        fill_directions(row_pieces, row_dir_ref, lax.axis_index("row"), per_seg)

    def run_group(first_slot):
        add_products(
            lambda slot: place_of(places, slot, col_blocks),
            first_slot,
            block_ref,
            lambda row_block: row_dir_ref[row_block],
            [even_ref, odd_ref],
        )

    each_group(places, block_hbm, block_ref, sems, prepare, run_group)
    size = even_ref.shape[1]
    for segment in range(col_out_ref.shape[0]):
        for part in range(per_seg):
            col_block = segment * per_seg + part
            values = even_ref[col_block] + odd_ref[col_block]
            col_out_ref[segment, part * size : part * size + size] = values.astype(
                col_out_ref.dtype
            )


def in_terms(values, count):
    terms = []
    for _ in range(count):
        terms.append(values.astype(jnp.bfloat16))
        values = values - terms[-1].astype(jnp.float32)
    return terms


def side_by_side(terms, width=32):
    total = terms[0].astype(jnp.float32)
    for place, term in enumerate(terms[1:], 1):
        total = total + pltpu.roll(term.astype(jnp.float32), place * width, 1)
    return total.astype(jnp.bfloat16)


def attach_kernel(first_dir_ref, col_dir_ref, total_ref, message_ref, gram_ref):
    col_count, sent, size, _ = col_dir_ref.shape
    per_seg = sent - 1

    def add_segment(segment, gram):
        for part in range(per_seg):
            rows = slice(part * size, part * size + size)
            values = total_ref[segment, rows]
            message_ref[segment, rows] = values
            gram += dot_across(values, tall(col_dir_ref[segment, part]))
        return gram

    gram = lax.fori_loop(
        0, col_count, add_segment, jnp.zeros((size, 128), jnp.float32), unroll=4
    )
    half = size // 2
    terms = side_by_side(in_terms(gram, 2)).astype(jnp.float32)
    folded = terms[:half] + pltpu.roll(terms[half:], 64, 1)
    for segment in range(col_count):
        message_ref[segment, per_seg * size :] = folded.astype(message_ref.dtype)
    queries = total_of([first_dir_ref[segment, per_seg] for segment in range(col_count)])
    queries = total_of([window(queries, term) for term in range(3)])
    pairs = total_of([col_dir_ref[segment, per_seg] for segment in range(col_count)])
    lanes = lax.broadcasted_iota(jnp.int32, pairs.shape, 1)
    pairs = jnp.where(lanes < 2 * size, pairs + pltpu.roll(pairs, 128 - 2 * size, 1), 0.0)
    gram_ref[...] = beside(queries, pairs)


def forward_kernel(spots_ref, live_ref, block_hbm, col_dir_ref, *refs):
    places = (spots_ref, live_ref)
    *row_outs, block_ref, sems, even_ref, odd_ref = refs
    per_seg = row_outs[0].shape[0]
    col_blocks = col_dir_ref.shape[0] * per_seg

    def prepare():
        even_ref[...] = jnp.zeros_like(even_ref)
        odd_ref[...] = jnp.zeros_like(odd_ref)

    def run_group(first_slot):
        add_products(
            lambda slot: place_of(places, slot, col_blocks)[::-1],
            first_slot,
            block_ref,
            lambda col_block: col_dir_ref[divided(col_block, per_seg)],
            [even_ref, odd_ref],
        )

    each_group(places, block_hbm, block_ref, sems, prepare, run_group)
    for ahead, out in enumerate(row_outs):
        first = lax.rem(lax.axis_index("row") + ahead, len(row_outs)) * per_seg
        for part in range(per_seg):
            values = even_ref[first + part] + odd_ref[first + part]
            out[part] = values.astype(out.dtype)


def over_blocks(kernel, name, places, blocks, inputs, outputs, scratch):
    slots = blocks.shape[0] // SPARE
    return pl.pallas_call(
        kernel,
        in_specs=[SCALARS, SCALARS, ANYWHERE] + [IN_VMEM] * len(inputs),
        out_specs=[IN_VMEM] * len(outputs),
        out_shape=outputs,
        scratch_shapes=[
            pltpu.VMEM((slots,) + blocks.shape[1:], blocks.dtype),
            pltpu.SemaphoreType.DMA((slots // BATCH,)),
        ]
        + scratch,
        compiler_params=pltpu.CompilerParams(vmem_limit_bytes=PRODUCT_GRANT),
        cost_estimate=pl.CostEstimate(
            flops=2 * slots * 32 * 128 * 128, bytes_accessed=2 * slots * 128 * 128, transcendentals=0
        ),
        name=name,
    )(*places, blocks, *inputs)


def backward_product(places, blocks, row_pieces, col_count):
    per_seg, rows, lanes = row_pieces[0].shape
    col_shape = (col_count * per_seg, rows, lanes)
    (total,) = over_blocks(
        functools.partial(backward_kernel, len(row_pieces)),
        "backward_product",
        places,
        blocks,
        row_pieces,
        [jax.ShapeDtypeStruct((col_count, per_seg * rows, lanes), jnp.bfloat16)],
        [
            pltpu.VMEM((len(row_pieces) * per_seg, rows, lanes), jnp.bfloat16),
            pltpu.VMEM(col_shape, jnp.float32),
            pltpu.VMEM(col_shape, jnp.float32),
        ],
    )
    return total


def forward_product(places, blocks, col_dirs, row_count, piece):
    row_shape = (row_count * piece[0],) + piece[1:]
    return over_blocks(
        forward_kernel,
        "forward_product",
        places,
        blocks,
        [col_dirs],
        [jax.ShapeDtypeStruct(piece, jnp.bfloat16)] * row_count,
        [pltpu.VMEM(row_shape, jnp.float32), pltpu.VMEM(row_shape, jnp.float32)],
    )


def total_of(values):
    total = values[0].astype(jnp.float32)
    for value in values[1:]:
        total = total + value.astype(jnp.float32)
    return total


def leading(ref):
    return [ref.at[index] for index in range(ref.shape[0])]


def start_kernel(*refs):
    *row_refs, col_ref, query_ref, scaling_ref, scaled_ref, copies_ref = refs
    degree = 1.0 + 0.5 * total_of([ref[...] for ref in [*row_refs, *leading(col_ref)]])
    scaling = 1.0 / jnp.sqrt(degree)
    scaling_ref[...] = scaling
    per_seg, size, _ = scaled_ref.shape
    gram = jnp.zeros((size, 128), jnp.float32)
    for part in range(per_seg):
        query = query_ref[:, part * 128 : part * 128 + 128]
        scaled = (scaling[part : part + 1] * query).astype(jnp.bfloat16)
        scaled_ref[part] = scaled
        for copy in range(copies_ref.shape[0]):
            copies_ref[copy, part] = scaled
        gram += exact_across(query, tall(query))
    terms = side_by_side(in_terms(gram, 3))
    for copy in range(copies_ref.shape[0]):
        copies_ref[copy, per_seg] = terms


def scaled_sum(row_refs, col_ref, scaling_ref, part):
    scaling = scaling_ref[part : part + 1]
    size = row_refs[0].shape[1]
    rows = slice(part * size, part * size + size)
    total = total_of([ref[part] for ref in row_refs] + [ref[rows] for ref in leading(col_ref)])
    return scaling * (0.5 * total)


def middle_kernel(*refs):
    *row_refs, col_ref, scaling_ref, query_ref, first_ref, scaled_ref, copies_ref = refs
    size = query_ref.shape[0]
    per_seg = scaling_ref.shape[0]
    grams = jnp.zeros((size, 128), jnp.float32)
    for part in range(per_seg):
        first = scaled_sum(row_refs, col_ref, scaling_ref, part)
        first_ref[part] = first
        scaled = (scaling_ref[part : part + 1] * first).astype(jnp.bfloat16)
        scaled_ref[part] = scaled
        for copy in range(copies_ref.shape[0]):
            copies_ref[copy, part] = scaled
        query = query_ref[:, part * 128 : part * 128 + 128]
        grams += exact_across(first, stacked(query, first))
    terms = side_by_side(in_terms(grams, 2), 2 * size)
    for copy in range(copies_ref.shape[0]):
        copies_ref[copy, per_seg] = terms


def tall(flat):
    rest = flat.shape[1] - flat.shape[0]
    return jnp.concatenate([flat, jnp.zeros((rest, flat.shape[1]), flat.dtype)], axis=0)


def flipped(flat):
    return tall(flat).T[: flat.shape[0]]


def times(left, right):
    return exact_plain(left, tall(right))


def beside(left, right):
    return left + pltpu.roll(right, left.shape[0], 1)


def stacked(upper, lower):
    rest = jnp.zeros((upper.shape[1] - 2 * upper.shape[0], upper.shape[1]), upper.dtype)
    return jnp.concatenate([upper, lower, rest], axis=0)


def sandwich(rows, middle):
    return exact_across(exact_plain(rows, middle), tall(rows))


def symmetric(flat):
    return 0.5 * (flat + flipped(flat))


def window(flat, place, size=None):
    size = size or flat.shape[0]
    if place:
        flat = pltpu.roll(flat, flat.shape[1] - place * size, 1)
    lanes = lax.broadcasted_iota(jnp.int32, flat.shape, 1)
    return jnp.where(lanes < size, flat, 0.0)


def solve_many(pairs):
    size = pairs[0][0].shape[0]
    systems = [matrix + pltpu.roll(side, size, 1) for matrix, side in pairs]
    sublanes = lax.broadcasted_iota(jnp.int32, systems[0].shape, 0)

    def eliminated(values, column, scale, pivot):
        row = values[pivot : pivot + 1, :] * scale
        return jnp.where(sublanes == pivot, row, values - column * row)

    for first in range(0, size, PANEL):
        panels = [
            [jnp.broadcast_to(system[:, at : at + 1], system.shape) for at in range(first, first + PANEL)]
            for system in systems
        ]
        for pivot in range(first, first + PANEL):
            for which, (column, *later) in enumerate(panels):
                scale = 1.0 / column[pivot : pivot + 1, :]
                panels[which] = [eliminated(other, column, scale, pivot) for other in later]
                systems[which] = eliminated(systems[which], column, scale, pivot)
    return [window(system, 1) for system in systems]


def close_kernel(*refs):
    row_count = (len(refs) - 6) // 2
    row_refs = refs[:row_count]
    gram_refs = refs[row_count : 2 * row_count]
    col_ref, scaling_ref, query_ref, first_ref, solution_ref, residual_ref = refs[-6:]
    size = query_ref.shape[0]
    weight = graph_weight
    total = total_of([ref[...] for ref in gram_refs])
    g00 = symmetric(window(total, 0))
    g01 = flipped(window(total, 1))
    g11 = symmetric(window(total, 2))
    g12 = symmetric(window(total, 3))
    eye = (
        lax.broadcasted_iota(jnp.int32, total.shape, 0)
        == lax.broadcasted_iota(jnp.int32, total.shape, 1)
    ).astype(jnp.float32)
    curve = symmetric(g00 - weight * g01)
    steps, inverse = solve_many([(curve, g00), (g00, eye)])
    steps_t = flipped(steps)
    plain_gram = stacked(beside(g00, g01), beside(flipped(g01), g11))
    through_gram = stacked(beside(g01, g11), beside(g11, g12))
    after_first = beside(eye - steps_t, weight * steps_t)
    new_gram = symmetric(sandwich(after_first, plain_gram))
    mixing = times(inverse, new_gram)
    direction = after_first + flipped(mixing)
    curve = symmetric(sandwich(direction, plain_gram - weight * through_gram))
    (steps,) = solve_many([(curve, new_gram)])
    steps_t2 = flipped(steps)
    applied = direction - weight * pltpu.roll(direction, size, 1)
    solution_rows = exact_plain(beside(eye, steps_t2), stacked(steps_t, direction))
    residual_rows = exact_plain(beside(eye, -steps_t2), stacked(after_first, applied))
    rows = jnp.concatenate([solution_rows, residual_rows], axis=0)
    for part in range(first_ref.shape[0]):
        lanes = slice(part * 128, part * 128 + 128)
        basis = jnp.concatenate(
            [
                query_ref[:, lanes],
                first_ref[part],
                scaled_sum(row_refs, col_ref, scaling_ref, part),
                jnp.zeros_like(eye),
            ],
            axis=0,
        )
        values = exact_plain(rows, basis)
        solution_ref[:, lanes] = values[:size]
        residual_ref[:, lanes] = values[size:]


def pass_around(pieces, axis):
    count = len(pieces)
    return [pieces[0]] + [
        lax.ppermute(pieces[ahead], axis, [(at, (at + ahead) % count) for at in range(count)])
        for ahead in range(1, count)
    ]


def exchange(pieces, axis):
    return lax.all_to_all(pieces, axis, 0, 0, tiled=True)


def simple_call(kernel, shapes, name, *operands):
    return pl.pallas_call(
        kernel,
        out_shape=shapes,
        compiler_params=pltpu.CompilerParams(vmem_limit_bytes=SMALL_GRANT),
        name=name,
    )(*operands)


def sum_kernel(col_ref, gram_ref, total_ref):
    size = gram_ref.shape[0]
    col_count, sent, _ = col_ref.shape
    folded = total_of([col_ref[segment, sent - size // 2 :] for segment in range(col_count)])
    upper = window(folded, 0, size) + window(folded, 1, size)
    lower = window(folded, 2, size) + window(folded, 3, size)
    last = jnp.concatenate([upper, lower], axis=0)
    total_ref[...] = gram_ref[...] + pltpu.roll(last, 3 * size, 1)


def body(queries, block_spots, live_blocks, neighbor_cols, neighbor_sims):
    row_count = lax.axis_size("row")
    col_count = lax.axis_size("col")
    query_rows, seg_len = queries.shape
    per_seg = seg_len // 128
    places = (block_spots, live_blocks)
    piece = (per_seg, query_rows, 128)
    wide = jax.ShapeDtypeStruct(piece, jnp.float32)
    narrow = jax.ShapeDtypeStruct(piece, jnp.bfloat16)
    gram_shape = jax.ShapeDtypeStruct((query_rows, 128), jnp.float32)

    message = jax.ShapeDtypeStruct((col_count, per_seg + 1) + piece[1:], jnp.bfloat16)

    blocks, flipped_blocks, *row_sums, col_sums = build_blocks(
        places,
        neighbor_cols[0, 0],
        neighbor_sims[0, 0],
        row_count,
        col_count,
        per_seg,
    )
    col_part = exchange(col_sums.reshape(col_count, per_seg, 128), "col")
    row_parts = pass_around([None, *row_sums], "row")[1:]
    scaling, scaled, copies = simple_call(
        start_kernel,
        [jax.ShapeDtypeStruct((per_seg, 128), jnp.float32), narrow, message],
        "start",
        *row_parts,
        col_part,
        queries,
    )

    first_dirs = exchange(copies, "col")
    row_pieces = pass_around([scaled] * row_count, "row")
    total = backward_product(places, flipped_blocks, row_pieces, col_count)
    col_part = exchange(total, "col")
    totals = forward_product(places, blocks, first_dirs, row_count, piece)
    first, scaled, copies = simple_call(
        middle_kernel,
        [wide, narrow, message],
        "middle",
        *pass_around(totals, "row"),
        col_part,
        scaling,
        queries,
    )

    col_dirs = exchange(copies, "col")
    row_pieces = pass_around([scaled] * row_count, "row")
    total = backward_product(places, flipped_blocks, row_pieces, col_count)
    more = jax.ShapeDtypeStruct(
        (col_count, total.shape[1] + query_rows // 2, 128), jnp.bfloat16
    )
    total, gram = simple_call(
        attach_kernel, [more, gram_shape], "attach", first_dirs, col_dirs, total
    )
    col_part = exchange(total, "col")
    totals = forward_product(places, blocks, col_dirs, row_count, piece)
    row_parts = pass_around(totals, "row")
    (gram,) = simple_call(sum_kernel, [gram_shape], "gram_sum", col_part, gram)
    flat = jax.ShapeDtypeStruct(queries.shape, jnp.float32)
    return tuple(
        simple_call(
            close_kernel,
            [flat, flat],
            "close",
            *row_parts,
            *pass_around([gram] * row_count, "row"),
            col_part,
            scaling,
            queries,
            first,
        )
    )


def solution(mesh):
    placed = (
        P(None, ("row", "col")),
        P("row", "col", None),
        P("row", "col"),
        P("row", "col", None, None, None),
        P("row", "col", None, None, None),
    )
    return jax.shard_map(
        body,
        mesh=mesh,
        in_specs=placed,
        out_specs=(P(None, ("row", "col")), P(None, ("row", "col"))),
        check_vma=False,
    )
```

```python
import functools

import jax
import jax.numpy as jnp
from jax import lax
from jax.experimental import pallas as pl
from jax.experimental.pallas import tpu as pltpu
from jax.sharding import PartitionSpec as P

graph_weight = 0.95
GROUP = 32
HALF = GROUP // 2
BATCH = 32
SPARE = 4
PANEL = 8
BUILD_GRANT = 60 * 1024 * 1024
PRODUCT_GRANT = 40 * 1024 * 1024
SMALL_GRANT = 24 * 1024 * 1024


def dot_plain(left, right, **kwargs):
    return lax.dot_general(
        left, right, (((1,), (0,)), ((), ())), preferred_element_type=jnp.float32, **kwargs
    )


def dot_across(left, right, **kwargs):
    return lax.dot_general(
        left, right, (((1,), (1,)), ((), ())), preferred_element_type=jnp.float32, **kwargs
    )


exact_plain = functools.partial(dot_plain, precision=lax.Precision.HIGHEST)
exact_across = functools.partial(dot_across, precision=lax.Precision.HIGHEST)


def divided(number, size):
    if size & (size - 1):
        return lax.div(number, size), lax.rem(number, size)
    return number >> (size.bit_length() - 1), number & (size - 1)


def place_of(places, slot, col_blocks):
    return divided(places[0][0, 0, slot], col_blocks)


def live_count(places):
    return places[1][0, 0]


def group_count(places, group):
    return (live_count(places) + group - 1) // group


def group_copy(source, target, sems, index, group):
    window = pl.ds(index * group, group)
    return pltpu.make_async_copy(source.at[window], target.at[window], sems.at[index])


def build_kernel(
    spots_ref, live_ref, index_hbm, value_hbm, block_hbm, flipped_hbm, *refs
):
    (
        *row_outs,
        col_out_ref,
        index_ref,
        value_ref,
        block_ref,
        flipped_ref,
        row_ref,
        col_ref,
        index_sems,
        value_sems,
        block_sems,
        flipped_sems,
    ) = refs
    places = (spots_ref, live_ref)
    row_count = len(row_outs) + 1
    per_seg = row_outs[0].shape[0]
    col_blocks = col_out_ref.shape[0]
    groups = group_count(places, BATCH) * (BATCH // GROUP)

    def start_copies(index, _):
        group_copy(index_hbm, index_ref, index_sems, index, GROUP).start()
        group_copy(value_hbm, value_ref, value_sems, index, GROUP).start()
        return 0

    lax.fori_loop(0, groups, start_copies, 0)
    row_ref[...] = jnp.zeros_like(row_ref)
    col_ref[...] = jnp.zeros_like(col_ref)
    rows_16 = lax.broadcasted_iota(jnp.int32, (16, 128), 0)
    diagonal = lax.broadcasted_iota(jnp.int32, (128, 128), 0) == lax.broadcasted_iota(
        jnp.int32, (128, 128), 1
    )
    identity = jnp.where(diagonal, 1.0, 0.0).astype(jnp.bfloat16)
    zero = jnp.zeros((16, 128), jnp.bfloat16)

    def build_group(index, _):
        group_copy(index_hbm, index_ref, index_sems, index, GROUP).wait()
        group_copy(value_hbm, value_ref, value_sems, index, GROUP).wait()
        targets = [(rows_16 + 16 * part).astype(jnp.int16) for part in range(8)]

        def load_pair(inside):
            tables = []
            for slot in (index * GROUP + inside, index * GROUP + inside + 1):
                active = (slot < live_count(places)).astype(jnp.float32)
                values = value_ref[slot].astype(jnp.float32) * active
                tables.append((slot, index_ref[slot], values))
            return tables

        def build_pair(tables):
            sums = [[zero] * 8 for _ in tables]
            for entry in range(0, 16, 2):
                for which, (_, indices, values) in enumerate(tables):
                    pair = []
                    for at in (entry, entry + 1):
                        index_row = jnp.broadcast_to(indices[at : at + 1], (16, 128))
                        value_row = jnp.broadcast_to(values[at : at + 1], (16, 128))
                        pair.append((index_row.astype(jnp.int16), value_row.astype(jnp.bfloat16)))
                    for part in range(8):
                        first, second = [
                            jnp.where(index_row == targets[part], value_row, zero)
                            for index_row, value_row in pair
                        ]
                        sums[which][part] = sums[which][part] + (first + second)
            return [jnp.concatenate(parts, axis=0) for parts in sums]

        def store_turned(tables, turned):
            for (slot, _, values), block in zip(tables, turned):
                row_block, col_block = place_of(places, slot, col_blocks)
                flipped_ref[slot] = block.astype(jnp.bfloat16)
                col_ref[col_block] += jnp.sum(block.reshape(16, 8, 128), axis=0)
                row_ref[row_block] += values[:8] + values[8:]

        tables = load_pair(0)
        waiting = None
        for inside in range(0, GROUP, 2):
            following = load_pair(inside + 2) if inside + 2 < GROUP else None
            blocks = build_pair(tables)
            if waiting:
                store_turned(*waiting)
            if inside == HALF:
                group_copy(block_ref, block_hbm, block_sems, 2 * index, HALF).start()
                group_copy(flipped_ref, flipped_hbm, flipped_sems, 2 * index, HALF).start()
            for (slot, _, _), block in zip(tables, blocks):
                block_ref[slot] = block
            waiting = (tables, [dot_across(identity, block) for block in blocks])
            tables = following
        store_turned(*waiting)
        group_copy(block_ref, block_hbm, block_sems, 2 * index + 1, HALF).start()
        group_copy(flipped_ref, flipped_hbm, flipped_sems, 2 * index + 1, HALF).start()
        return 0

    lax.fori_loop(0, groups, build_group, 0)
    for ahead, out in enumerate(row_outs, 1):
        first = lax.rem(lax.axis_index("row") + ahead, row_count) * per_seg
        for part in range(per_seg):
            out[part : part + 1] = jnp.sum(row_ref[first + part], axis=0, keepdims=True)
    for part in range(per_seg):
        own = lax.axis_index("col") * per_seg + part
        col_ref[own] += row_ref[lax.axis_index("row") * per_seg + part]
    for col_block in range(col_blocks):
        col_out_ref[col_block : col_block + 1] = jnp.sum(
            col_ref[col_block], axis=0, keepdims=True
        )

    def finish_copies(index, _):
        group_copy(block_ref, block_hbm, block_sems, index, HALF).wait()
        group_copy(flipped_ref, flipped_hbm, flipped_sems, index, HALF).wait()
        return 0

    lax.fori_loop(0, 2 * groups, finish_copies, 0)


SCALARS = pl.BlockSpec(memory_space=pltpu.SMEM)
ANYWHERE = pl.BlockSpec(memory_space=pl.ANY)
IN_VMEM = pl.BlockSpec(memory_space=pltpu.VMEM)


def build_blocks(
    places, index_table, value_table, row_count, col_count, per_seg
):
    slots = index_table.shape[0]
    groups = slots // GROUP
    sum_shapes = [(per_seg, 128)] * (row_count - 1) + [(col_count * per_seg, 128)]
    return pl.pallas_call(
        build_kernel,
        in_specs=[SCALARS, SCALARS, ANYWHERE, ANYWHERE],
        out_specs=[ANYWHERE] * 2 + [IN_VMEM] * len(sum_shapes),
        out_shape=[jax.ShapeDtypeStruct((SPARE * slots, 128, 128), jnp.bfloat16)] * 2
        + [jax.ShapeDtypeStruct(shape, jnp.float32) for shape in sum_shapes],
        scratch_shapes=[
            pltpu.VMEM(index_table.shape, index_table.dtype),
            pltpu.VMEM(value_table.shape, value_table.dtype),
            pltpu.VMEM((slots, 128, 128), jnp.bfloat16),
            pltpu.VMEM((slots, 128, 128), jnp.bfloat16),
            pltpu.VMEM((row_count * per_seg, 8, 128), jnp.float32),
            pltpu.VMEM((col_count * per_seg, 8, 128), jnp.float32),
            pltpu.SemaphoreType.DMA((groups,)),
            pltpu.SemaphoreType.DMA((groups,)),
            pltpu.SemaphoreType.DMA((2 * groups,)),
            pltpu.SemaphoreType.DMA((2 * groups,)),
        ],
        compiler_params=pltpu.CompilerParams(vmem_limit_bytes=BUILD_GRANT),
        name="build_blocks",
    )(*places, index_table, value_table)


def each_group(places, block_hbm, block_ref, sems, prepare, run_group):
    groups = group_count(places, BATCH)

    def start_copy(index, _):
        group_copy(block_hbm, block_ref, sems, index, BATCH).start()
        return 0

    lax.fori_loop(0, groups, start_copy, 0)
    prepare()

    def one_group(index, _):
        group_copy(block_hbm, block_ref, sems, index, BATCH).wait()
        run_group(index * BATCH)
        return 0

    lax.fori_loop(0, groups, one_group, 0)


def add_products(places, first_slot, block_ref, direction, total_refs):
    sums = []
    for inside in range(BATCH):
        slot = first_slot + inside
        sums.append(dot_plain(direction(places(slot)[0]), block_ref[slot]))
    for inside in range(BATCH):
        total_ref = total_refs[inside % len(total_refs)]
        total_ref[places(first_slot + inside)[1]] += sums[inside]


def fill_directions(pieces, dir_ref, mine, per_seg):
    for behind, piece in enumerate(pieces):
        first = lax.rem(mine + (len(pieces) - behind), len(pieces)) * per_seg
        for part in range(per_seg):
            dir_ref[first + part] = piece[part]


def backward_kernel(row_count, spots_ref, live_ref, block_hbm, *refs):
    places = (spots_ref, live_ref)
    row_pieces = refs[:row_count]
    terms_refs = refs[row_count:-6]
    col_out_ref, block_ref, sems, row_dir_ref, even_ref, odd_ref = refs[-6:]
    per_seg = row_pieces[0].shape[0]
    col_blocks = even_ref.shape[0]

    def prepare():
        even_ref[...] = jnp.zeros_like(even_ref)
        odd_ref[...] = jnp.zeros_like(odd_ref)
        fill_directions(row_pieces, row_dir_ref, lax.axis_index("row"), per_seg)

    def run_group(first_slot):
        add_products(
            lambda slot: place_of(places, slot, col_blocks),
            first_slot,
            block_ref,
            lambda row_block: row_dir_ref[row_block],
            [even_ref, odd_ref],
        )

    each_group(places, block_hbm, block_ref, sems, prepare, run_group)
    size = even_ref.shape[1]
    for segment in range(col_out_ref.shape[0]):
        for part in range(per_seg):
            col_block = segment * per_seg + part
            values = even_ref[col_block] + odd_ref[col_block]
            col_out_ref[segment, part * size : part * size + size] = values.astype(
                col_out_ref.dtype
            )
        for terms_ref in terms_refs:
            col_out_ref[segment, per_seg * size :] = terms_ref[...]


def in_terms(values, count):
    terms = []
    for _ in range(count):
        terms.append(values.astype(jnp.bfloat16))
        values = values - terms[-1].astype(jnp.float32)
    return terms


def side_by_side(terms, width=32):
    total = terms[0].astype(jnp.float32)
    for place, term in enumerate(terms[1:], 1):
        total = total + pltpu.roll(term.astype(jnp.float32), place * width, 1)
    return total.astype(jnp.bfloat16)


def attach_kernel(first_col_ref, col_dir_ref, total_ref, message_ref, gram_ref):
    col_count, sent, size, _ = col_dir_ref.shape
    per_seg = sent - 1

    def add_segment(segment, gram):
        for part in range(per_seg):
            rows = slice(part * size, part * size + size)
            values = total_ref[segment, rows]
            message_ref[segment, rows] = values
            gram += dot_across(values, tall(col_dir_ref[segment, part]))
        return gram

    gram = lax.fori_loop(
        0, col_count, add_segment, jnp.zeros((size, 128), jnp.float32), unroll=8
    )
    half = size // 2
    terms = side_by_side(in_terms(gram, 2)).astype(jnp.float32)
    folded = terms[:half] + pltpu.roll(terms[half:], 64, 1)
    for segment in range(col_count):
        message_ref[segment, per_seg * size :] = folded.astype(message_ref.dtype)
    queries = total_of([first_col_ref[segment, per_seg * size :] for segment in range(col_count)])
    queries = total_of([window(queries, term) for term in range(3)])
    pairs = total_of([col_dir_ref[segment, per_seg] for segment in range(col_count)])
    lanes = lax.broadcasted_iota(jnp.int32, pairs.shape, 1)
    pairs = jnp.where(lanes < 2 * size, pairs + pltpu.roll(pairs, 128 - 2 * size, 1), 0.0)
    gram_ref[...] = beside(queries, pairs)


def forward_kernel(spots_ref, live_ref, block_hbm, col_dir_ref, *refs):
    places = (spots_ref, live_ref)
    *row_outs, block_ref, sems, even_ref, odd_ref = refs
    per_seg = row_outs[0].shape[0]
    col_blocks = col_dir_ref.shape[0] * per_seg

    def prepare():
        even_ref[...] = jnp.zeros_like(even_ref)
        odd_ref[...] = jnp.zeros_like(odd_ref)

    def run_group(first_slot):
        add_products(
            lambda slot: place_of(places, slot, col_blocks)[::-1],
            first_slot,
            block_ref,
            lambda col_block: col_dir_ref[divided(col_block, per_seg)],
            [even_ref, odd_ref],
        )

    each_group(places, block_hbm, block_ref, sems, prepare, run_group)
    for ahead, out in enumerate(row_outs):
        first = lax.rem(lax.axis_index("row") + ahead, len(row_outs)) * per_seg
        for part in range(per_seg):
            values = even_ref[first + part] + odd_ref[first + part]
            out[part] = values.astype(out.dtype)


def over_blocks(kernel, name, places, blocks, inputs, outputs, scratch):
    slots = blocks.shape[0] // SPARE
    return pl.pallas_call(
        kernel,
        in_specs=[SCALARS, SCALARS, ANYWHERE] + [IN_VMEM] * len(inputs),
        out_specs=[IN_VMEM] * len(outputs),
        out_shape=outputs,
        scratch_shapes=[
            pltpu.VMEM((slots,) + blocks.shape[1:], blocks.dtype),
            pltpu.SemaphoreType.DMA((slots // BATCH,)),
        ]
        + scratch,
        compiler_params=pltpu.CompilerParams(vmem_limit_bytes=PRODUCT_GRANT),
        cost_estimate=pl.CostEstimate(
            flops=2 * slots * 32 * 128 * 128, bytes_accessed=2 * slots * 128 * 128, transcendentals=0
        ),
        name=name,
    )(*places, blocks, *inputs)


def backward_product(places, blocks, row_pieces, col_count, *terms):
    per_seg, rows, lanes = row_pieces[0].shape
    sent = per_seg + len(terms)
    col_shape = (col_count * per_seg, rows, lanes)
    (total,) = over_blocks(
        functools.partial(backward_kernel, len(row_pieces)),
        "backward_product",
        places,
        blocks,
        [*row_pieces, *terms],
        [jax.ShapeDtypeStruct((col_count, sent * rows, lanes), jnp.bfloat16)],
        [
            pltpu.VMEM((len(row_pieces) * per_seg, rows, lanes), jnp.bfloat16),
            pltpu.VMEM(col_shape, jnp.float32),
            pltpu.VMEM(col_shape, jnp.float32),
        ],
    )
    return total


def forward_product(places, blocks, col_dirs, row_count, piece):
    row_shape = (row_count * piece[0],) + piece[1:]
    return over_blocks(
        forward_kernel,
        "forward_product",
        places,
        blocks,
        [col_dirs],
        [jax.ShapeDtypeStruct(piece, jnp.bfloat16)] * row_count,
        [pltpu.VMEM(row_shape, jnp.float32), pltpu.VMEM(row_shape, jnp.float32)],
    )


def total_of(values):
    total = values[0].astype(jnp.float32)
    for value in values[1:]:
        total = total + value.astype(jnp.float32)
    return total


def leading(ref):
    return [ref.at[index] for index in range(ref.shape[0])]


def start_kernel(*refs):
    *row_refs, col_ref, query_ref, scaling_ref, scaled_ref, copies_ref = refs
    degree = 1.0 + 0.5 * total_of([ref[...] for ref in [*row_refs, *leading(col_ref)]])
    scaling = 1.0 / jnp.sqrt(degree)
    scaling_ref[...] = scaling
    for part in range(scaled_ref.shape[0]):
        query = query_ref[:, part * 128 : part * 128 + 128]
        scaled = (scaling[part : part + 1] * query).astype(jnp.bfloat16)
        scaled_ref[part] = scaled
        for copy in range(copies_ref.shape[0]):
            copies_ref[copy, part] = scaled


def query_gram_kernel(query_ref, terms_ref):
    queries = query_ref[...]
    rest = jnp.zeros((128 - queries.shape[0], queries.shape[1]), queries.dtype)
    gram = exact_across(queries, jnp.concatenate([queries, rest], axis=0))
    terms_ref[...] = side_by_side(in_terms(gram, 3))


def scaled_sum(row_refs, col_ref, scaling_ref, part):
    scaling = scaling_ref[part : part + 1]
    size = row_refs[0].shape[1]
    rows = slice(part * size, part * size + size)
    total = total_of([ref[part] for ref in row_refs] + [ref[rows] for ref in leading(col_ref)])
    return scaling * (0.5 * total)


def middle_kernel(*refs):
    *row_refs, col_ref, scaling_ref, query_ref, first_ref, scaled_ref, copies_ref = refs
    size = query_ref.shape[0]
    per_seg = scaling_ref.shape[0]
    firsts = []
    for part in range(per_seg):
        first = scaled_sum(row_refs, col_ref, scaling_ref, part)
        first_ref[part] = first
        scaled = (scaling_ref[part : part + 1] * first).astype(jnp.bfloat16)
        scaled_ref[part] = scaled
        for copy in range(copies_ref.shape[0]):
            copies_ref[copy, part] = scaled
        firsts.append(first)
    first = jnp.concatenate(firsts, axis=1)
    rest = jnp.zeros((128 - 2 * size, first.shape[1]), first.dtype)
    grams = exact_across(first, jnp.concatenate([query_ref[...], first, rest], axis=0))
    terms = side_by_side(in_terms(grams, 2), 2 * size)
    for copy in range(copies_ref.shape[0]):
        copies_ref[copy, per_seg] = terms


def tall(flat):
    rest = flat.shape[1] - flat.shape[0]
    return jnp.concatenate([flat, jnp.zeros((rest, flat.shape[1]), flat.dtype)], axis=0)


def flipped(flat):
    return tall(flat).T[: flat.shape[0]]


def times(left, right):
    return exact_plain(left, tall(right))


def beside(left, right):
    return left + pltpu.roll(right, left.shape[0], 1)


def stacked(upper, lower):
    rest = jnp.zeros((upper.shape[1] - 2 * upper.shape[0], upper.shape[1]), upper.dtype)
    return jnp.concatenate([upper, lower, rest], axis=0)


def sandwich(rows, middle):
    return exact_across(exact_plain(rows, middle), tall(rows))


def symmetric(flat):
    return 0.5 * (flat + flipped(flat))


def window(flat, place, size=None):
    size = size or flat.shape[0]
    if place:
        flat = pltpu.roll(flat, flat.shape[1] - place * size, 1)
    lanes = lax.broadcasted_iota(jnp.int32, flat.shape, 1)
    return jnp.where(lanes < size, flat, 0.0)


def solve_many(pairs):
    size = pairs[0][0].shape[0]
    systems = [matrix + pltpu.roll(side, size, 1) for matrix, side in pairs]
    sublanes = lax.broadcasted_iota(jnp.int32, systems[0].shape, 0)

    def eliminated(values, column, scale, pivot):
        row = values[pivot : pivot + 1, :] * scale
        return jnp.where(sublanes == pivot, row, values - column * row)

    for first in range(0, size, PANEL):
        panels = [
            [jnp.broadcast_to(system[:, at : at + 1], system.shape) for at in range(first, first + PANEL)]
            for system in systems
        ]
        for pivot in range(first, first + PANEL):
            for which, (column, *later) in enumerate(panels):
                scale = 1.0 / column[pivot : pivot + 1, :]
                panels[which] = [eliminated(other, column, scale, pivot) for other in later]
                systems[which] = eliminated(systems[which], column, scale, pivot)
    return [window(system, 1) for system in systems]


def close_kernel(*refs):
    row_count = (len(refs) - 6) // 2
    row_refs = refs[:row_count]
    gram_refs = refs[row_count : 2 * row_count]
    col_ref, scaling_ref, query_ref, first_ref, solution_ref, residual_ref = refs[-6:]
    size = query_ref.shape[0]
    weight = graph_weight
    total = total_of([ref[...] for ref in gram_refs])
    g00 = symmetric(window(total, 0))
    g01 = flipped(window(total, 1))
    g11 = symmetric(window(total, 2))
    g12 = symmetric(window(total, 3))
    eye = (
        lax.broadcasted_iota(jnp.int32, total.shape, 0)
        == lax.broadcasted_iota(jnp.int32, total.shape, 1)
    ).astype(jnp.float32)
    curve = symmetric(g00 - weight * g01)
    steps, inverse = solve_many([(curve, g00), (g00, eye)])
    steps_t = flipped(steps)
    plain_gram = stacked(beside(g00, g01), beside(flipped(g01), g11))
    through_gram = stacked(beside(g01, g11), beside(g11, g12))
    after_first = beside(eye - steps_t, weight * steps_t)
    new_gram = symmetric(sandwich(after_first, plain_gram))
    mixing = times(inverse, new_gram)
    direction = after_first + flipped(mixing)
    curve = symmetric(sandwich(direction, plain_gram - weight * through_gram))
    (steps,) = solve_many([(curve, new_gram)])
    steps_t2 = flipped(steps)
    applied = direction - weight * pltpu.roll(direction, size, 1)
    solution_rows = exact_plain(beside(eye, steps_t2), stacked(steps_t, direction))
    residual_rows = exact_plain(beside(eye, -steps_t2), stacked(after_first, applied))
    rows = jnp.concatenate([solution_rows, residual_rows], axis=0)
    for part in range(first_ref.shape[0]):
        lanes = slice(part * 128, part * 128 + 128)
        basis = jnp.concatenate(
            [
                query_ref[:, lanes],
                first_ref[part],
                scaled_sum(row_refs, col_ref, scaling_ref, part),
                jnp.zeros_like(eye),
            ],
            axis=0,
        )
        values = exact_plain(rows, basis)
        solution_ref[:, lanes] = values[:size]
        residual_ref[:, lanes] = values[size:]


def pass_around(pieces, axis):
    count = len(pieces)
    return [pieces[0]] + [
        lax.ppermute(pieces[ahead], axis, [(at, (at + ahead) % count) for at in range(count)])
        for ahead in range(1, count)
    ]


def exchange(pieces, axis):
    return lax.all_to_all(pieces, axis, 0, 0, tiled=True)


def simple_call(kernel, shapes, name, *operands):
    return pl.pallas_call(
        kernel,
        out_shape=shapes,
        compiler_params=pltpu.CompilerParams(vmem_limit_bytes=SMALL_GRANT),
        name=name,
    )(*operands)


def sum_kernel(col_ref, gram_ref, total_ref):
    size = gram_ref.shape[0]
    col_count, sent, _ = col_ref.shape
    folded = total_of([col_ref[segment, sent - size // 2 :] for segment in range(col_count)])
    upper = window(folded, 0, size) + window(folded, 1, size)
    lower = window(folded, 2, size) + window(folded, 3, size)
    last = jnp.concatenate([upper, lower], axis=0)
    total_ref[...] = gram_ref[...] + pltpu.roll(last, 3 * size, 1)


def body(queries, block_spots, live_blocks, neighbor_cols, neighbor_sims):
    row_count = lax.axis_size("row")
    col_count = lax.axis_size("col")
    query_rows, seg_len = queries.shape
    per_seg = seg_len // 128
    places = (block_spots, live_blocks)
    piece = (per_seg, query_rows, 128)
    wide = jax.ShapeDtypeStruct(piece, jnp.float32)
    narrow = jax.ShapeDtypeStruct(piece, jnp.bfloat16)
    gram_shape = jax.ShapeDtypeStruct((query_rows, 128), jnp.float32)

    message = jax.ShapeDtypeStruct((col_count, per_seg + 1) + piece[1:], jnp.bfloat16)

    blocks, flipped_blocks, *row_sums, col_sums = build_blocks(
        places,
        neighbor_cols[0, 0],
        neighbor_sims[0, 0],
        row_count,
        col_count,
        per_seg,
    )
    col_part = exchange(col_sums.reshape(col_count, per_seg, 128), "col")
    row_parts = pass_around([None, *row_sums], "row")[1:]
    scaling, scaled, copies = simple_call(
        start_kernel,
        [
            jax.ShapeDtypeStruct((per_seg, 128), jnp.float32),
            narrow,
            jax.ShapeDtypeStruct((col_count,) + piece, jnp.bfloat16),
        ],
        "start",
        *row_parts,
        col_part,
        queries,
    )

    first_dirs = exchange(copies, "col")
    row_pieces = pass_around([scaled] * row_count, "row")
    (terms,) = simple_call(
        query_gram_kernel,
        [jax.ShapeDtypeStruct((query_rows, 128), jnp.bfloat16)],
        "query_gram",
        queries,
    )
    total = backward_product(places, flipped_blocks, row_pieces, col_count, terms)
    first_part = exchange(total, "col")
    totals = forward_product(places, blocks, first_dirs, row_count, piece)
    first, scaled, copies = simple_call(
        middle_kernel,
        [wide, narrow, message],
        "middle",
        *pass_around(totals, "row"),
        first_part,
        scaling,
        queries,
    )

    col_dirs = exchange(copies, "col")
    row_pieces = pass_around([scaled] * row_count, "row")
    total = backward_product(places, flipped_blocks, row_pieces, col_count)
    more = jax.ShapeDtypeStruct(
        (col_count, total.shape[1] + query_rows // 2, 128), jnp.bfloat16
    )
    total, gram = simple_call(
        attach_kernel, [more, gram_shape], "attach", first_part, col_dirs, total
    )
    col_part = exchange(total, "col")
    totals = forward_product(places, blocks, col_dirs, row_count, piece)
    row_parts = pass_around(totals, "row")
    (gram,) = simple_call(sum_kernel, [gram_shape], "gram_sum", col_part, gram)
    flat = jax.ShapeDtypeStruct(queries.shape, jnp.float32)
    return tuple(
        simple_call(
            close_kernel,
            [flat, flat],
            "close",
            *row_parts,
            *pass_around([gram] * row_count, "row"),
            col_part,
            scaling,
            queries,
            first,
        )
    )


def solution(mesh):
    placed = (
        P(None, ("row", "col")),
        P("row", "col", None),
        P("row", "col"),
        P("row", "col", None, None, None),
        P("row", "col", None, None, None),
    )
    return jax.shard_map(
        body,
        mesh=mesh,
        in_specs=placed,
        out_specs=(P(None, ("row", "col")), P(None, ("row", "col"))),
        check_vma=False,
    )
```
